32 devices in a mesh: segment: 4 (over y, core), space: 8 (over z, x).
Axes of the slice: x: 2, y: 2, z: 4, core: 2. Of those that a mesh axis runs over, the one named last changes fastest.
Arguments:
- x_in: bfloat16 [2, 16, 16, 256], P(None, 'space'), may hold values from -17 to 17
- out_cotangent: bfloat16 [2, 16, 16, 256], P(None, 'space'), may hold values from -17 to 17, as said below
- timesteps: int32 [2], replicated, may hold values from 0 to 999
- labels: int32 [2], replicated, may hold values from 0 to 999
- time_weight: bfloat16 [128, 512], replicated, may hold values from -0.5 to 0.5
- label_table: bfloat16 [1000, 512], replicated, may hold values from -5 to 5
- conv_weight: bfloat16 [4, 3, 3, 256, 256], P('segment'), may hold values from -0.125 to 0.125
- mod_weight: bfloat16 [4, 512, 512], P('segment'), may hold values from -0.25 to 0.25
- mod_bias: float32 [4, 512], P('segment'), may hold values from -3 to 3
- norm_gain: float32 [4, 256], P('segment'), may hold values from 0.25 to 1.75
Outputs:
- segment_grads: bfloat16 [4, 2, 16, 16, 256], P('segment', None, 'space')
- conv_grad: float32 [4, 2304, 256], P('segment', 'space')
- mod_grad: float32 [4, 512, 512], P('segment')
The draws below stay inside these ranges and needn't reach their ends.
Inputs may be any that keep to these rules, and one draw needn't show every extreme that they name: `out_cotangent`: cotangent from the layers after the chain.
All inputs are finite; a program needn't handle non-finite values.
Results may differ from the reference program's by a relative error of at most 0.0076.
Values may be sent and summed in bfloat16 or wider, within the bound.
No kernel may reach another device: no remote copies, remote signals or barrier semaphores. Data moves between devices by JAX's collectives and lax.ppermute only.
A program may use at most 64 MiB of HBM per device.

```python
import math
import jax
import jax.numpy as jnp
from jax import lax

C = 256
E = 512
BASE = 128
CLASSES = 1000
GROUPS = 32
MICRO = 2
HEIGHT = 16
COLS = 16
N_SEGMENT = 4


def ramp_field(key, low_end):
    normal_part = jnp.clip(jax.random.normal(key, (MICRO, HEIGHT, COLS, C), jnp.float32), -4.0, 4.0)
    rough_part = jax.random.uniform(jax.random.fold_in(key, 1), (MICRO, HEIGHT, 1, C), jnp.float32, 0.5, 1.5)
    level_row = low_end + jnp.arange(HEIGHT, dtype=jnp.float32) / HEIGHT
    return normal_part * rough_part * level_row[None, :, None, None]


def draw_x_in(key, part):
    key = jax.random.fold_in(key, 11)
    draw_field = ramp_field(key, 0.5)
    return draw_field.astype(jnp.bfloat16)


def draw_out_cotangent(key, part):
    key = jax.random.fold_in(key, 23)
    draw_field = ramp_field(key, 0.5)
    return draw_field.astype(jnp.bfloat16)


def levels(stream_key, shape, cuts, smallest, largest):
    level, own = 1.0, jax.random.fold_in(stream_key, 6)
    for position, parts in cuts:
        steps = jnp.exp(jax.random.uniform(jax.random.fold_in(own, position), (parts,), jnp.float32, smallest / len(cuts), largest / len(cuts)))
        level = level * jnp.repeat(steps, shape[position] // parts).reshape([-1 if axis == position else 1 for axis in range(len(shape))])
    return level


def bell_draw(own_key, dims, scale, bound, cuts=(), held_as=jnp.bfloat16):
    gain = levels(own_key, dims, cuts, -0.22, 0.18) if cuts else 1.0
    drawn = jax.random.normal(own_key, dims, jnp.float32) * scale * gain
    return jnp.minimum(jnp.maximum(drawn, -bound), bound).astype(held_as)


def setup_inputs(seed: int = 0) -> dict:
    key_list = jax.random.split(jax.random.key(seed), 11)
    return {
        "x_in": draw_x_in(jax.random.fold_in(key_list[10], 71), 0),
        "out_cotangent": draw_out_cotangent(jax.random.fold_in(key_list[10], 71), 0),
        "timesteps": jax.random.randint(key_list[2], (MICRO,), 0, 1000).astype(jnp.int32),
        "labels": jax.random.randint(key_list[3], (MICRO,), 0, CLASSES).astype(jnp.int32),
        "time_weight": bell_draw(key_list[4], (BASE, E), BASE ** -0.5, 0.5),
        "label_table": bell_draw(key_list[5], (CLASSES, E), 1.0, 5.0),
        "conv_weight": bell_draw(key_list[6], (N_SEGMENT, 3, 3, C, C), (9 * C) ** -0.5, 0.125, ((0, 4),)),
        "mod_weight": bell_draw(key_list[7], (N_SEGMENT, E, 2 * C), E ** -0.5, 0.25, ((0, 4),)),
        "mod_bias": bell_draw(key_list[8], (N_SEGMENT, 2 * C), 0.5, 3.0, ((0, 4),), jnp.float32),
        "norm_gain": jnp.clip(1.0 + 0.15 * jax.random.normal(key_list[9], (N_SEGMENT, C), jnp.float32), 0.25, 1.75),
    }


EPSILON = 1e-05

def embed(timesteps, label_rows, time_weight):
    half_base = time_weight.shape[0] // 2
    frequency = jnp.exp(-math.log(10000.0) * jnp.arange(half_base, dtype=jnp.float32) / half_base)
    angles = timesteps.astype(jnp.float32)[:, None] * frequency[None, :]
    sinusoid = jnp.concatenate([jnp.cos(angles), jnp.sin(angles)], axis=1).astype(jnp.bfloat16)
    timed = jnp.dot(sinusoid, time_weight, preferred_element_type=jnp.float32)
    return jax.nn.silu(timed + label_rows).astype(jnp.bfloat16)

def patches(padded, row_count, col_count):
    pieces = [padded[row_off:row_off + row_count, col_off:col_off + col_count] for row_off in range(3) for col_off in range(3)]
    return jnp.concatenate(pieces, axis=-1).reshape(row_count * col_count, -1)

def group_total(values):
    return lax.optimization_barrier(jnp.sum(values.reshape(GROUPS, -1), axis=1))

def normalize(inputs_f, group_mean, inv_std, gain_vec, scale_row, shift_row, group_width):
    normed = (inputs_f - jnp.repeat(group_mean, group_width)) * jnp.repeat(inv_std, group_width)
    factor = gain_vec * (1.0 + scale_row)
    return (normed, normed * factor + shift_row, factor)

def reference(x_in, out_cotangent, timesteps, labels, time_weight, label_table, conv_weight, mod_weight, mod_bias, norm_gain):
    embedded = embed(timesteps, label_table[labels].astype(jnp.float32), time_weight)
    group_width = C // GROUPS
    entries = HEIGHT * COLS * group_width
    records = []
    current = [x_in[micro_id] for micro_id in range(MICRO)]
    for segment_id in range(N_SEGMENT):
        flat_weight = conv_weight[segment_id].reshape(9 * C, C)
        modulation = jnp.dot(embedded, mod_weight[segment_id], preferred_element_type=jnp.float32) + mod_bias[segment_id]
        segment_record = []
        following = []
        for micro_id in range(MICRO):
            inputs = current[micro_id]
            inputs_f = inputs.astype(jnp.float32)
            shaped = inputs_f.reshape(HEIGHT, COLS, GROUPS, group_width)
            group_mean = lax.optimization_barrier(jnp.sum(shaped, axis=(0, 1, 3))) / entries
            inv_std = lax.rsqrt(lax.optimization_barrier(jnp.sum(shaped * shaped, axis=(0, 1, 3))) / entries - group_mean * group_mean + EPSILON)
            normed, pre, factor = normalize(inputs_f, group_mean, inv_std, norm_gain[segment_id], modulation[micro_id, :C], modulation[micro_id, C:], group_width)
            activation = jax.nn.silu(pre).astype(jnp.bfloat16)
            padded = jnp.pad(activation, ((1, 1), (1, 1), (0, 0)))
            conv_out = jnp.dot(patches(padded, HEIGHT, COLS), flat_weight, preferred_element_type=jnp.float32).reshape(HEIGHT, COLS, C)
            following.append((inputs_f + conv_out).astype(jnp.bfloat16))
            segment_record.append((inputs, group_mean, inv_std))
        records.append((modulation, segment_record))
        current = following
    flows = [out_cotangent[micro_id] for micro_id in range(MICRO)]
    grad_list = [None] * N_SEGMENT
    conv_list = [None] * N_SEGMENT
    mod_list = [None] * N_SEGMENT
    for segment_id in reversed(range(N_SEGMENT)):
        kernel = conv_weight[segment_id]
        flip_weight = jnp.swapaxes(kernel[::-1, ::-1], 2, 3).reshape(9 * C, C)
        modulation, segment_record = records[segment_id]
        weight_acc = jnp.zeros((9 * C, C), jnp.float32)
        mod_rows = []
        backs = []
        for micro_id in range(MICRO):
            inputs, group_mean, inv_std = segment_record[micro_id]
            upstream = flows[micro_id]
            normed, pre, factor = normalize(inputs.astype(jnp.float32), group_mean, inv_std, norm_gain[segment_id], modulation[micro_id, :C], modulation[micro_id, C:], group_width)
            activation = jax.nn.silu(pre).astype(jnp.bfloat16)
            padded = jnp.pad(activation, ((1, 1), (1, 1), (0, 0)))
            up_pad = jnp.pad(upstream, ((1, 1), (1, 1), (0, 0)))
            act_grad = jnp.dot(patches(up_pad, HEIGHT, COLS), flip_weight, preferred_element_type=jnp.float32).reshape(HEIGHT, COLS, C)
            sigma = jax.nn.sigmoid(pre)
            pre_grad = act_grad * (sigma * (1.0 + pre * (1.0 - sigma)))
            sum_grad = lax.optimization_barrier(jnp.sum(pre_grad, axis=(0, 1)))
            sum_cross = lax.optimization_barrier(jnp.sum(pre_grad * normed, axis=(0, 1)))
            center = jnp.repeat(group_total(factor * sum_grad), group_width) / entries
            tilt = jnp.repeat(group_total(factor * sum_cross), group_width) / entries
            back = (upstream.astype(jnp.float32) + jnp.repeat(inv_std, group_width) * (factor * pre_grad - center - normed * tilt)).astype(jnp.bfloat16)
            backs.append(back)
            act_cols = patches(padded, HEIGHT, COLS)
            weight_acc = weight_acc + jnp.dot(act_cols.T, upstream.reshape(-1, C), preferred_element_type=jnp.float32)
            mod_rows.append(jnp.concatenate([norm_gain[segment_id] * sum_cross, sum_grad]))
        grad_list[segment_id] = jnp.stack(backs)
        conv_list[segment_id] = weight_acc
        mod_list[segment_id] = jnp.dot(embedded.astype(jnp.float32).T, jnp.stack(mod_rows), precision=lax.Precision.HIGHEST, preferred_element_type=jnp.float32)
        flows = backs
    return (jnp.stack(grad_list), jnp.stack(conv_list), jnp.stack(mod_list))
```

```python
import functools

import jax
import jax.numpy as jnp
import numpy as np
from jax import lax
from jax.experimental import pallas as pl
from jax.experimental.pallas import tpu as pltpu
from jax.sharding import PartitionSpec as P

GROUPS = 32
EPSILON = 1e-05
PAIR = 2
VMEM = pl.BlockSpec(memory_space=pltpu.VMEM)
SMEM = pl.BlockSpec(memory_space=pltpu.SMEM)
HBM = pl.BlockSpec(memory_space=pl.ANY)


def sigmoid(values):
    return 1.0 / (1.0 + jnp.exp(-values))


def over_chunks(count, body):
    if count == 1:
        body(0)
    else:

        def step(i, carry):
            body(i)
            return carry

        lax.fori_loop(0, count, step, 0)


def chunk_start(i, size):
    return 0 if isinstance(i, int) else pl.multiple_of(i * size, size)


def fold_rows(values):
    return jnp.sum(values.reshape(values.shape[0] // 8, 8, values.shape[1]), axis=0)


def column(rows):
    return jnp.sum(rows, axis=0, keepdims=True)


def group_sums(rows, width):
    lanes = lax.broadcasted_iota(jnp.int32, rows.shape, 1)
    size = rows.shape[1]
    step = 1
    while step < width:
        ahead = pltpu.roll(rows, size - step, 1)
        behind = pltpu.roll(rows, step, 1)
        rows = rows + jnp.where((lanes & step) == 0, ahead, behind)
        step *= 2
    return rows


def stack_rows(first, second):
    spot = lax.broadcasted_iota(jnp.int32, (8, first.shape[1]), 0)
    return jnp.where(spot == 0, first, jnp.where(spot == 1, second, 0.0))


class Shape:
    def __init__(self, height, cols, channels, space_count):
        self.cols, self.channels = cols, channels
        self.pixels = height * cols
        self.chunk = cols * max(1, min(self.pixels, 256) // cols)
        self.chunks = self.pixels // self.chunk
        self.width = channels // GROUPS
        self.entries = float(self.pixels * self.width)
        self.padded = self.pixels + 2 * cols
        self.own_rows = height // space_count * cols
        self.slab = 9 * channels // space_count
        self.taps = min(9, (self.slab - 1) // channels + 2)
        self.pack = self.slab + self.own_rows + 8
        self.limit = (12 << 20) + self.pixels * channels * 40


def statistics(sh, x_ref):
    zero = jnp.zeros((8, sh.channels), jnp.float32)

    def add(i, sums):
        part = x_ref[pl.ds(chunk_start(i, sh.chunk), sh.chunk), :].astype(jnp.float32)
        return (sums[0] + fold_rows(part), sums[1] + fold_rows(part * part))

    if sh.chunks == 1:
        one, two = add(0, (zero, zero))
    else:
        one, two = lax.fori_loop(0, sh.chunks, add, (zero, zero))
    total = group_sums(stack_rows(column(one), column(two)), sh.width) / sh.entries
    mean = total[0:1]
    return (mean, lax.rsqrt(total[1:2] - mean * mean + EPSILON))


def clear_edges(sh, padded_ref):
    zero = jnp.zeros((3, sh.cols, sh.channels), padded_ref.dtype)
    padded_ref[:, 0 : sh.cols, :] = zero
    padded_ref[:, sh.pixels + sh.cols : sh.padded, :] = zero


def spread(sh, padded_ref, start, values):
    place = pl.ds(start + sh.cols, sh.chunk)
    spot = lax.broadcasted_iota(jnp.int32, values.shape, 0) % sh.cols
    padded_ref[0, place, :] = jnp.where(spot == 0, 0.0, pltpu.roll(values, 1, 0)).astype(jnp.bfloat16)
    padded_ref[1, place, :] = values.astype(jnp.bfloat16)
    padded_ref[2, place, :] = jnp.where(
        spot == sh.cols - 1, 0.0, pltpu.roll(values, sh.chunk - 1, 0)
    ).astype(jnp.bfloat16)


def convolve(sh, padded_ref, start, weight_ref, unit, backward):
    total = None
    for p in range(3):
        for q in range(3):
            row, col = (2 - p, 2 - q) if backward else (p, q)
            block = padded_ref[col, pl.ds(start + row * sh.cols, sh.chunk), :]
            tap = (3 * p + q) * sh.channels
            weight = weight_ref[unit, tap : tap + sh.channels, :]
            part = lax.dot_general(
                block,
                weight,
                (((1,), (1 if backward else 0,)), ((), ())),
                preferred_element_type=jnp.float32,
            )
            total = part if total is None else total + part
    return total


def forward_unit(sh, x_ref, out_ref, params, padded_ref, weight_ref, unit):
    factor, shift = params
    mean, inv_std = statistics(sh, x_ref)

    def activate(i):
        start = chunk_start(i, sh.chunk)
        normed = (x_ref[pl.ds(start, sh.chunk), :].astype(jnp.float32) - mean) * inv_std
        pre = normed * factor + shift
        spread(sh, padded_ref, start, pre * sigmoid(pre))

    def produce(i):
        start = chunk_start(i, sh.chunk)
        inputs = x_ref[pl.ds(start, sh.chunk), :].astype(jnp.float32)
        z = convolve(sh, padded_ref, start, weight_ref, unit, False)
        out_ref[pl.ds(start, sh.chunk), :] = (inputs + z).astype(jnp.bfloat16)

    over_chunks(sh.chunks, activate)
    over_chunks(sh.chunks, produce)


def backward_unit(sh, x_ref, up_ref, grad_ref, params, scratch, weight_ref, unit, keep_ref, send_ref, core):
    padded_ref, act_ref, slope_ref, pre_grad_ref, slab_ref = scratch
    factor, shift = params
    space = lax.axis_index("space")
    mean, inv_std = statistics(sh, x_ref)
    zero = jnp.zeros((8, sh.channels), jnp.float32)

    def activate(i):
        start = chunk_start(i, sh.chunk)
        rows = pl.ds(start, sh.chunk)
        spread(sh, padded_ref, start, up_ref[rows, :].astype(jnp.float32))
        pre = (x_ref[rows, :].astype(jnp.float32) - mean) * inv_std * factor + shift
        sigma = sigmoid(pre)
        act_ref[rows, :] = (pre * sigma).astype(jnp.bfloat16)
        slope_ref[rows, :] = sigma * (1.0 + pre * (1.0 - sigma))

    def differentiate(i, sums):
        start = chunk_start(i, sh.chunk)
        rows = pl.ds(start, sh.chunk)
        normed = (x_ref[rows, :].astype(jnp.float32) - mean) * inv_std
        pre_grad = convolve(sh, padded_ref, start, weight_ref, unit, True) * slope_ref[rows, :]
        pre_grad_ref[rows, :] = pre_grad
        return (sums[0] + fold_rows(pre_grad), sums[1] + fold_rows(pre_grad * normed))

    over_chunks(sh.chunks, activate)
    if sh.chunks == 1:
        sums = differentiate(0, (zero, zero))
    else:
        sums = lax.fori_loop(0, sh.chunks, differentiate, (zero, zero))
    sum_grad, sum_cross = column(sums[0]), column(sums[1])
    means = group_sums(stack_rows(factor * sum_grad, factor * sum_cross), sh.width) / sh.entries
    center, tilt = means[0:1], means[1:2]

    def finish(i):
        rows = pl.ds(chunk_start(i, sh.chunk), sh.chunk)
        normed = (x_ref[rows, :].astype(jnp.float32) - mean) * inv_std
        back = factor * pre_grad_ref[rows, :] - center - normed * tilt
        grad_ref[rows, :] = (up_ref[rows, :].astype(jnp.float32) + inv_std * back).astype(jnp.bfloat16)

    over_chunks(sh.chunks, finish)
    first_row = space * sh.slab
    first_tap = jnp.minimum(first_row // sh.channels, 9 - sh.taps)
    offset = pl.multiple_of(first_row - first_tap * sh.channels, 8)
    for t in range(sh.taps):
        tap = first_tap + t
        row, col = 2 - tap // 3, 2 - tap % 3
        place = pl.ds(t * sh.channels, sh.channels)

        def product(i):
            start = chunk_start(i, sh.chunk)
            block = padded_ref[col, pl.ds(pl.multiple_of(start + row * sh.cols, 16), sh.chunk), :]
            return lax.dot_general(
                act_ref[pl.ds(start, sh.chunk), :],
                block,
                (((0,), (0,)), ((), ())),
                preferred_element_type=jnp.float32,
            )

        if sh.chunks == 1:
            slab_ref[place, :] = product(0)
        else:
            slab_ref[place, :] = jnp.zeros((sh.channels, sh.channels), jnp.float32)

            def accumulate(i):
                slab_ref[place, :] += product(i)

            over_chunks(sh.chunks, accumulate)
    mine = slab_ref[pl.ds(offset, sh.slab), :]
    rows = grad_ref[pl.ds(pl.multiple_of(space * sh.own_rows, sh.own_rows), sh.own_rows), :]
    sums = stack_rows(sum_grad, sum_cross)

    def write(ref):
        ref[0 : sh.slab, :] = mine
        ref[sh.slab : sh.slab + sh.own_rows, :] = rows.astype(jnp.float32)
        ref[sh.slab + sh.own_rows : sh.pack, :] = sums

    @pl.when(core == unit)
    def _():
        write(keep_ref)

    @pl.when(core != unit)
    def _():
        write(send_ref)


def place_of():
    index = lax.axis_index("segment")
    return (index // PAIR, index % PAIR)


def unit_params(mod_keep_ref, mod_other_ref, core, unit):
    own = core == unit
    factor = jnp.where(own, mod_keep_ref[0:1, :], mod_other_ref[0:1, :])
    shift = jnp.where(own, mod_keep_ref[1:2, :], mod_other_ref[1:2, :])
    return (factor, shift)


def weight_copies(own_ref, other_ref, weights, sems, core):
    mine = pltpu.make_async_copy(own_ref, weights.at[core], sems.at[0])
    theirs = pltpu.make_async_copy(other_ref, weights.at[1 - core], sems.at[1])
    return (mine, theirs)


def prepare_kernel(
    times_ref,
    labels_ref,
    frequency_ref,
    time_weight_ref,
    table_ref,
    mod_weight_ref,
    mod_bias_ref,
    gain_ref,
    keep_ref,
    send_ref,
    embedded_ref,
):
    core = lax.axis_index("segment") % PAIR
    rows = 16
    spot = lax.broadcasted_iota(jnp.int32, (rows, 1), 0)
    classes = table_ref.shape[0]
    label = jnp.where(spot % 2 == 0, labels_ref[0], labels_ref[1])
    time = jnp.where(spot % 2 == 0, times_ref[0], times_ref[1]).astype(jnp.float32)
    one_hot = (lax.broadcasted_iota(jnp.int32, (rows, classes), 1) == label).astype(jnp.bfloat16)
    label_rows = jnp.dot(one_hot, table_ref[...], preferred_element_type=jnp.float32)
    angles = time * frequency_ref[...]
    lanes = lax.broadcasted_iota(jnp.int32, angles.shape, 1)
    half = angles.shape[1] // 2
    sinusoid = jnp.where(lanes < half, jnp.cos(angles), jnp.sin(angles)).astype(jnp.bfloat16)
    timed = jnp.dot(sinusoid, time_weight_ref[...], preferred_element_type=jnp.float32) + label_rows
    embedded = (timed * sigmoid(timed)).astype(jnp.bfloat16)
    embedded_ref[...] = embedded
    modulation = jnp.dot(embedded, mod_weight_ref[...], preferred_element_type=jnp.float32) + mod_bias_ref[...]
    channels = modulation.shape[1] // 2
    factor = gain_ref[...] * (1.0 + modulation[:, :channels])
    shift = modulation[:, channels:]

    @pl.when(core == 0)
    def _():
        keep_ref[...] = stack_rows(factor[0:1], shift[0:1])
        send_ref[...] = stack_rows(factor[1:2], shift[1:2])

    @pl.when(core != 0)
    def _():
        keep_ref[...] = stack_rows(factor[1:2], shift[1:2])
        send_ref[...] = stack_rows(factor[0:1], shift[0:1])


def forward_kernel(
    sh, active_stage, x_ref, mod_keep_ref, mod_other_ref, own_ref, other_ref, middle_ref, out_ref, weights, padded_ref, sems
):
    stage, core = place_of()

    @pl.when(stage == active_stage)
    def _():
        copies = weight_copies(own_ref, other_ref, weights, sems, core)
        for copy in copies:
            copy.start()
        clear_edges(sh, padded_ref)
        for copy in copies:
            copy.wait()
        params = [unit_params(mod_keep_ref, mod_other_ref, core, unit) for unit in range(PAIR)]
        forward_unit(sh, x_ref, middle_ref, params[0], padded_ref, weights, 0)
        forward_unit(sh, middle_ref, out_ref, params[1], padded_ref, weights, 1)


def backward_kernel(sh, active_stage, first, *refs):
    if first:
        x_ref, up_ref, mod_keep_ref, mod_other_ref, own_ref, other_ref = refs[:6]
        refs = refs[6:]
    else:
        x_ref, middle_ref, up_ref, mod_keep_ref, mod_other_ref, own_ref, other_ref, keep_in, send_in = refs[:9]
        refs = refs[9:]
    grad_ref, keep_ref, send_ref = refs[:3]
    weights, padded_ref, act_ref, slope_ref, pre_grad_ref, slab_ref, between_ref, sems = refs[3:11]
    if first:
        middle_ref = refs[11]
    stage, core = place_of()

    @pl.when(stage == active_stage)
    def _():
        copies = weight_copies(own_ref, other_ref, weights, sems, core)
        for copy in copies:
            copy.start()
        clear_edges(sh, padded_ref)
        for copy in copies:
            copy.wait()
        params = [unit_params(mod_keep_ref, mod_other_ref, core, unit) for unit in range(PAIR)]
        if first:
            forward_unit(sh, x_ref, middle_ref, params[0], padded_ref, weights, 0)
        scratch = (padded_ref, act_ref, slope_ref, pre_grad_ref, slab_ref)
        backward_unit(
            sh, middle_ref, up_ref, between_ref, params[1], scratch, weights, 1, keep_ref, send_ref, core
        )
        backward_unit(
            sh, x_ref, between_ref, grad_ref, params[0], scratch, weights, 0, keep_ref, send_ref, core
        )

    if not first:

        @pl.when(stage != active_stage)
        def _():
            keep_ref[...] = keep_in[...]
            send_ref[...] = send_in[...]


def finish_kernel(sh, keep_ref, other_ref, embedded_ref, gain_ref, grads_ref, conv_ref, mod_ref):
    core = lax.axis_index("segment") % PAIR
    conv_ref[...] = keep_ref[0 : sh.slab, :] + other_ref[0 : sh.slab, :]
    rows = slice(sh.slab, sh.slab + sh.own_rows)
    grads_ref[pl.ds(core, 1)] = keep_ref[rows, :].astype(jnp.bfloat16)[None]
    grads_ref[pl.ds(1 - core, 1)] = other_ref[rows, :].astype(jnp.bfloat16)[None]
    base = sh.slab + sh.own_rows

    def mod_rows(ref):
        return jnp.concatenate([gain_ref[...] * ref[base + 1 : base + 2, :], ref[base : base + 1, :]], axis=1)

    own, other = mod_rows(keep_ref), mod_rows(other_ref)
    spot = lax.broadcasted_iota(jnp.int32, (16, own.shape[1]), 0)
    values = jnp.where(spot % 2 == core, own, other)
    high = values.astype(jnp.bfloat16).astype(jnp.float32)
    rest = values - high
    middle = rest.astype(jnp.bfloat16).astype(jnp.float32)
    low = rest - middle
    part = spot // 2
    pieces = jnp.where(part == 0, high, jnp.where(part == 1, middle, jnp.where(part == 2, low, 0.0)))
    mod_ref[...] = lax.dot_general(
        embedded_ref[...],
        pieces.astype(jnp.bfloat16),
        (((0,), (0,)), ((), ())),
        preferred_element_type=jnp.float32,
    )


def shards(
    x_in,
    out_cotangent,
    timesteps,
    labels,
    time_weight,
    label_table,
    conv_weight,
    mod_weight,
    mod_bias,
    norm_gain,
):
    segments, spaces = lax.axis_size("segment"), lax.axis_size("space")
    stages = segments // PAIR
    stage, core = place_of()
    images, row_count, cols, channels = x_in.shape
    sh = Shape(row_count * spaces, cols, channels, spaces)
    f32, bf16 = jnp.float32, jnp.bfloat16
    params = pltpu.CompilerParams(vmem_limit_bytes=sh.limit)

    def call(body, ins, outs, scratch=()):
        return pl.pallas_call(
            body,
            out_shape=outs,
            in_specs=ins,
            out_specs=[VMEM] * len(outs),
            scratch_shapes=list(scratch),
            compiler_params=params,
        )

    shape = jax.ShapeDtypeStruct
    swap = [(i, i ^ 1) for i in range(segments)]
    weight = conv_weight.reshape(9 * channels, channels)
    ends = jnp.where(stage == 0, x_in, out_cotangent) if stages > 1 else x_in
    mine = lax.dynamic_index_in_dim(ends, core, 0, keepdims=False)
    image = lax.all_gather(mine, "space", axis=0, tiled=True).reshape(sh.pixels, channels)
    other_weight = lax.ppermute(weight, "segment", swap)

    half = time_weight.shape[0] // 2
    frequency = np.exp(-np.log(10000.0) * np.arange(half) / half).astype(np.float32)
    frequency = jnp.asarray(np.concatenate([frequency, frequency])[None])
    mod_keep, mod_send, embedded = call(
        prepare_kernel,
        [SMEM, SMEM] + [VMEM] * 6,
        [shape((8, channels), f32), shape((8, channels), f32), shape((16, time_weight.shape[1]), bf16)],
    )(timesteps, labels, frequency, time_weight, label_table, mod_weight[0], mod_bias, norm_gain)
    mod_other = lax.ppermute(mod_send, "segment", swap)
    own = (mod_keep, mod_other, weight, other_weight)
    own_specs = [VMEM, VMEM, HBM, HBM]

    image_shape = shape((sh.pixels, channels), bf16)
    pack_shape = shape((sh.pack, channels), f32)
    common = [
        pltpu.VMEM((PAIR, 9 * channels, channels), bf16),
        pltpu.VMEM((3, sh.padded, channels), bf16),
    ]
    sems = [pltpu.SemaphoreType.DMA((2,))]

    def hop(value, source, target):
        pairs = [(PAIR * source + k, PAIR * target + k) for k in range(PAIR)]
        return lax.ppermute(value, "segment", pairs)

    entering, middles = [image], []
    for active in range(stages - 1):
        middle, out = call(
            functools.partial(forward_kernel, sh, active),
            [VMEM] + own_specs,
            [image_shape, image_shape],
            common + sems,
        )(entering[active], *own)
        middles.append(middle)
        entering.append(hop(out, active, active + 1))

    scratch = common + [
        pltpu.VMEM((sh.pixels, channels), bf16),
        pltpu.VMEM((sh.pixels, channels), f32),
        pltpu.VMEM((sh.pixels, channels), f32),
        pltpu.VMEM((sh.taps * channels, channels), f32),
        pltpu.VMEM((sh.pixels, channels), bf16),
    ]
    outs = [image_shape, pack_shape, pack_shape]
    grad, keep, send = call(
        functools.partial(backward_kernel, sh, stages - 1, True),
        [VMEM, VMEM] + own_specs,
        outs,
        scratch + sems + [pltpu.VMEM((sh.pixels, channels), bf16)],
    )(entering[stages - 1], image, *own)
    for active in range(stages - 2, -1, -1):
        upstream = hop(grad, active + 1, active)
        grad, keep, send = call(
            functools.partial(backward_kernel, sh, active, False),
            [VMEM, VMEM, VMEM] + own_specs + [VMEM, VMEM],
            outs,
            scratch + sems,
        )(entering[active], middles[active], upstream, *own, keep, send)
    other = lax.ppermute(send, "segment", swap)
    grads, conv_grad, mod_grad = call(
        functools.partial(finish_kernel, sh),
        [VMEM] * 4,
        [
            shape((images, sh.own_rows, channels), bf16),
            shape((sh.slab, channels), f32),
            shape((time_weight.shape[1], 2 * channels), f32),
        ],
    )(keep, other, embedded, norm_gain)
    return (grads.reshape(1, images, row_count, cols, channels), conv_grad[None], mod_grad[None])


def solution(mesh):
    placed = (
        P(None, "space", None, None),
        P(None, "space", None, None),
        P(),
        P(),
        P(),
        P(),
        P("segment", None, None, None, None),
        P("segment", None, None),
        P("segment", None),
        P("segment", None),
    )
    return jax.shard_map(
        shards,
        mesh=mesh,
        in_specs=placed,
        out_specs=(
            P("segment", None, "space", None, None),
            P("segment", "space", None),
            P("segment", None, None),
        ),
        check_vma=False,
    )
```

```python
import functools

import jax
import jax.numpy as jnp
import numpy as np
from jax import lax
from jax.experimental import pallas as pl
from jax.experimental.pallas import tpu as pltpu
from jax.sharding import PartitionSpec as P

GROUPS = 32
EPSILON = 1e-05
PAIR = 2
VMEM = pl.BlockSpec(memory_space=pltpu.VMEM)
SMEM = pl.BlockSpec(memory_space=pltpu.SMEM)
HBM = pl.BlockSpec(memory_space=pl.ANY)


def sigmoid(values):
    return 1.0 / (1.0 + jnp.exp(-values))


def over_chunks(count, body):
    if count == 1:
        body(0)
    else:

        def step(i, carry):
            body(i)
            return carry

        lax.fori_loop(0, count, step, 0)


def chunk_start(i, size):
    return 0 if isinstance(i, int) else pl.multiple_of(i * size, size)


def fold_rows(values):
    return jnp.sum(values.reshape(values.shape[0] // 8, 8, values.shape[1]), axis=0)


def column(rows):
    return jnp.sum(rows, axis=0, keepdims=True)


def group_sums(rows, width):
    lanes = lax.broadcasted_iota(jnp.int32, rows.shape, 1)
    size = rows.shape[1]
    step = 1
    while step < width:
        ahead = pltpu.roll(rows, size - step, 1)
        behind = pltpu.roll(rows, step, 1)
        rows = rows + jnp.where((lanes & step) == 0, ahead, behind)
        step *= 2
    return rows


def stack_rows(first, second):
    spot = lax.broadcasted_iota(jnp.int32, (8, first.shape[1]), 0)
    return jnp.where(spot == 0, first, jnp.where(spot == 1, second, 0.0))


class Shape:
    def __init__(self, height, cols, channels, space_count):
        self.cols, self.channels = cols, channels
        self.pixels = height * cols
        self.chunk = cols * max(1, min(self.pixels, 256) // cols)
        self.chunks = self.pixels // self.chunk
        self.width = channels // GROUPS
        self.entries = float(self.pixels * self.width)
        self.padded = self.pixels + 2 * cols
        self.own_rows = height // space_count * cols
        self.slab = 9 * channels // space_count
        self.taps = min(9, (self.slab - 1) // channels + 2)
        self.pack = self.slab + self.own_rows + 8
        self.limit = (12 << 20) + self.pixels * channels * 40


def statistics(sh, x_ref):
    zero = jnp.zeros((8, sh.channels), jnp.float32)

    def add(i, sums):
        part = x_ref[pl.ds(chunk_start(i, sh.chunk), sh.chunk), :].astype(jnp.float32)
        return (sums[0] + fold_rows(part), sums[1] + fold_rows(part * part))

    if sh.chunks == 1:
        one, two = add(0, (zero, zero))
    else:
        one, two = lax.fori_loop(0, sh.chunks, add, (zero, zero))
    total = group_sums(stack_rows(column(one), column(two)), sh.width) / sh.entries
    mean = total[0:1]
    return (mean, lax.rsqrt(total[1:2] - mean * mean + EPSILON))


def clear_edges(sh, padded_ref):
    zero = jnp.zeros((3, sh.cols, sh.channels), padded_ref.dtype)
    padded_ref[:, 0 : sh.cols, :] = zero
    padded_ref[:, sh.pixels + sh.cols : sh.padded, :] = zero


def spread(sh, padded_ref, start, values):
    place = pl.ds(start + sh.cols, sh.chunk)
    spot = lax.broadcasted_iota(jnp.int32, values.shape, 0) % sh.cols
    padded_ref[0, place, :] = jnp.where(spot == 0, 0.0, pltpu.roll(values, 1, 0)).astype(jnp.bfloat16)
    padded_ref[1, place, :] = values.astype(jnp.bfloat16)
    padded_ref[2, place, :] = jnp.where(
        spot == sh.cols - 1, 0.0, pltpu.roll(values, sh.chunk - 1, 0)
    ).astype(jnp.bfloat16)


def convolve(sh, padded_ref, start, weight_ref, unit, backward):
    total = None
    for p in range(3):
        for q in range(3):
            row, col = (2 - p, 2 - q) if backward else (p, q)
            block = padded_ref[col, pl.ds(start + row * sh.cols, sh.chunk), :]
            tap = (3 * p + q) * sh.channels
            weight = weight_ref[unit, tap : tap + sh.channels, :]
            part = lax.dot_general(
                block,
                weight,
                (((1,), (1 if backward else 0,)), ((), ())),
                preferred_element_type=jnp.float32,
            )
            total = part if total is None else total + part
    return total


def forward_unit(sh, x_ref, out_ref, params, padded_ref, weight_ref, unit):
    factor, shift = params
    mean, inv_std = statistics(sh, x_ref)

    def activate(i):
        start = chunk_start(i, sh.chunk)
        normed = (x_ref[pl.ds(start, sh.chunk), :].astype(jnp.float32) - mean) * inv_std
        pre = normed * factor + shift
        spread(sh, padded_ref, start, pre * sigmoid(pre))

    def produce(i):
        start = chunk_start(i, sh.chunk)
        inputs = x_ref[pl.ds(start, sh.chunk), :].astype(jnp.float32)
        z = convolve(sh, padded_ref, start, weight_ref, unit, False)
        out_ref[pl.ds(start, sh.chunk), :] = (inputs + z).astype(jnp.bfloat16)

    over_chunks(sh.chunks, activate)
    over_chunks(sh.chunks, produce)


def backward_unit(sh, x_ref, up_ref, grad_ref, params, scratch, weight_ref, unit, keep_ref, send_ref, core):
    padded_ref, act_ref, slope_ref, pre_grad_ref, slab_ref = scratch
    factor, shift = params
    space = lax.axis_index("space")
    mean, inv_std = statistics(sh, x_ref)
    zero = jnp.zeros((8, sh.channels), jnp.float32)

    def activate(i):
        start = chunk_start(i, sh.chunk)
        rows = pl.ds(start, sh.chunk)
        spread(sh, padded_ref, start, up_ref[rows, :].astype(jnp.float32))
        pre = (x_ref[rows, :].astype(jnp.float32) - mean) * inv_std * factor + shift
        sigma = sigmoid(pre)
        act_ref[rows, :] = (pre * sigma).astype(jnp.bfloat16)
        slope_ref[rows, :] = sigma * (1.0 + pre * (1.0 - sigma))

    def differentiate(i, sums):
        start = chunk_start(i, sh.chunk)
        rows = pl.ds(start, sh.chunk)
        normed = (x_ref[rows, :].astype(jnp.float32) - mean) * inv_std
        pre_grad = convolve(sh, padded_ref, start, weight_ref, unit, True) * slope_ref[rows, :]
        pre_grad_ref[rows, :] = pre_grad
        return (sums[0] + fold_rows(pre_grad), sums[1] + fold_rows(pre_grad * normed))

    over_chunks(sh.chunks, activate)
    if sh.chunks == 1:
        sums = differentiate(0, (zero, zero))
    else:
        sums = lax.fori_loop(0, sh.chunks, differentiate, (zero, zero))
    sum_grad, sum_cross = column(sums[0]), column(sums[1])
    means = group_sums(stack_rows(factor * sum_grad, factor * sum_cross), sh.width) / sh.entries
    center, tilt = means[0:1], means[1:2]

    def finish(i):
        rows = pl.ds(chunk_start(i, sh.chunk), sh.chunk)
        normed = (x_ref[rows, :].astype(jnp.float32) - mean) * inv_std
        back = factor * pre_grad_ref[rows, :] - center - normed * tilt
        grad_ref[rows, :] = (up_ref[rows, :].astype(jnp.float32) + inv_std * back).astype(jnp.bfloat16)

    over_chunks(sh.chunks, finish)
    first_row = space * sh.slab
    first_tap = jnp.minimum(first_row // sh.channels, 9 - sh.taps)
    offset = pl.multiple_of(first_row - first_tap * sh.channels, 8)
    for t in range(sh.taps):
        tap = first_tap + t
        row, col = 2 - tap // 3, 2 - tap % 3
        place = pl.ds(t * sh.channels, sh.channels)

        def product(i):
            start = chunk_start(i, sh.chunk)
            block = padded_ref[col, pl.ds(pl.multiple_of(start + row * sh.cols, 16), sh.chunk), :]
            return lax.dot_general(
                act_ref[pl.ds(start, sh.chunk), :],
                block,
                (((0,), (0,)), ((), ())),
                preferred_element_type=jnp.float32,
            )

        if sh.chunks == 1:
            slab_ref[place, :] = product(0)
        else:
            slab_ref[place, :] = jnp.zeros((sh.channels, sh.channels), jnp.float32)

            def accumulate(i):
                slab_ref[place, :] += product(i)

            over_chunks(sh.chunks, accumulate)
    mine = slab_ref[pl.ds(offset, sh.slab), :]
    rows = grad_ref[pl.ds(pl.multiple_of(space * sh.own_rows, sh.own_rows), sh.own_rows), :]
    sums = stack_rows(sum_grad, sum_cross)

    def write(ref):
        ref[0 : sh.slab, :] = mine
        ref[sh.slab : sh.slab + sh.own_rows, :] = rows.astype(jnp.float32)
        ref[sh.slab + sh.own_rows : sh.pack, :] = sums

    @pl.when(core == unit)
    def _():
        write(keep_ref)

    @pl.when(core != unit)
    def _():
        write(send_ref)


def place_of():
    index = lax.axis_index("segment")
    return (index // PAIR, index % PAIR)


def unit_params(mod_keep_ref, mod_other_ref, core, unit):
    own = core == unit
    factor = jnp.where(own, mod_keep_ref[0:1, :], mod_other_ref[0:1, :])
    shift = jnp.where(own, mod_keep_ref[1:2, :], mod_other_ref[1:2, :])
    return (factor, shift)


def weight_copies(own_ref, other_ref, weights, sems, core):
    mine = pltpu.make_async_copy(own_ref, weights.at[core], sems.at[0])
    theirs = pltpu.make_async_copy(other_ref, weights.at[1 - core], sems.at[1])
    return (mine, theirs)


def prepare_kernel(
    times_ref,
    labels_ref,
    frequency_hbm,
    time_weight_hbm,
    table_hbm,
    mod_weight_hbm,
    mod_bias_hbm,
    gain_hbm,
    keep_ref,
    send_ref,
    embedded_ref,
    frequency_ref,
    time_weight_ref,
    table_ref,
    mod_weight_ref,
    mod_bias_ref,
    gain_ref,
    sems,
):
    core = lax.axis_index("segment") % PAIR
    sources = (frequency_hbm, time_weight_hbm, table_hbm, mod_weight_hbm, mod_bias_hbm, gain_hbm)
    targets = (frequency_ref, time_weight_ref, table_ref, mod_weight_ref, mod_bias_ref, gain_ref)
    copies = [pltpu.make_async_copy(a, b, sems.at[i]) for i, (a, b) in enumerate(zip(sources, targets))]
    for copy in copies:
        copy.start()
    for copy in copies:
        copy.wait()
    rows = 16
    spot = lax.broadcasted_iota(jnp.int32, (rows, 1), 0)
    classes = table_ref.shape[0]
    label = jnp.where(spot % 2 == 0, labels_ref[0], labels_ref[1])
    time = jnp.where(spot % 2 == 0, times_ref[0], times_ref[1]).astype(jnp.float32)
    one_hot = (lax.broadcasted_iota(jnp.int32, (rows, classes), 1) == label).astype(jnp.bfloat16)
    label_rows = jnp.dot(one_hot, table_ref[...], preferred_element_type=jnp.float32)
    angles = time * frequency_ref[...]
    lanes = lax.broadcasted_iota(jnp.int32, angles.shape, 1)
    half = angles.shape[1] // 2
    sinusoid = jnp.where(lanes < half, jnp.cos(angles), jnp.sin(angles)).astype(jnp.bfloat16)
    timed = jnp.dot(sinusoid, time_weight_ref[...], preferred_element_type=jnp.float32) + label_rows
    embedded = (timed * sigmoid(timed)).astype(jnp.bfloat16)
    embedded_ref[...] = embedded
    modulation = jnp.dot(embedded, mod_weight_ref[...], preferred_element_type=jnp.float32) + mod_bias_ref[...]
    channels = modulation.shape[1] // 2
    factor = gain_ref[...] * (1.0 + modulation[:, :channels])
    shift = modulation[:, channels:]

    @pl.when(core == 0)
    def _():
        keep_ref[...] = stack_rows(factor[0:1], shift[0:1])
        send_ref[...] = stack_rows(factor[1:2], shift[1:2])

    @pl.when(core != 0)
    def _():
        keep_ref[...] = stack_rows(factor[1:2], shift[1:2])
        send_ref[...] = stack_rows(factor[0:1], shift[0:1])


def assemble(sh, blocks_ref, order, image_ref):
    space = lax.axis_index("space")
    for k, bits in enumerate(order):
        start = pl.multiple_of((space ^ bits) * sh.own_rows, sh.own_rows)
        image_ref[pl.ds(start, sh.own_rows), :] = blocks_ref[k]


def forward_kernel(sh, active_stage, orders, *refs):
    if orders:
        near_ref, far_ref, mod_keep_ref, mod_other_ref, own_ref, other_ref = refs[:6]
        x_ref, middle_ref, out_ref, weights, padded_ref, sems = refs[6:]
        assemble(sh, near_ref, orders[0], x_ref)
        assemble(sh, far_ref, orders[1], x_ref)
    else:
        x_ref, mod_keep_ref, mod_other_ref, own_ref, other_ref = refs[:5]
        middle_ref, out_ref, weights, padded_ref, sems = refs[5:]
    stage, core = place_of()

    @pl.when(stage == active_stage)
    def _():
        copies = weight_copies(own_ref, other_ref, weights, sems, core)
        for copy in copies:
            copy.start()
        clear_edges(sh, padded_ref)
        for copy in copies:
            copy.wait()
        params = [unit_params(mod_keep_ref, mod_other_ref, core, unit) for unit in range(PAIR)]
        forward_unit(sh, x_ref, middle_ref, params[0], padded_ref, weights, 0)
        forward_unit(sh, middle_ref, out_ref, params[1], padded_ref, weights, 1)


def backward_kernel(sh, active_stage, first, *refs):
    if first:
        x_ref, up_ref, mod_keep_ref, mod_other_ref, own_ref, other_ref = refs[:6]
        refs = refs[6:]
    else:
        x_ref, middle_ref, up_ref, mod_keep_ref, mod_other_ref, own_ref, other_ref, keep_in, send_in = refs[:9]
        refs = refs[9:]
    grad_ref, keep_ref, send_ref = refs[:3]
    weights, padded_ref, act_ref, slope_ref, pre_grad_ref, slab_ref, between_ref, sems = refs[3:11]
    if first:
        middle_ref = refs[11]
    stage, core = place_of()

    @pl.when(stage == active_stage)
    def _():
        copies = weight_copies(own_ref, other_ref, weights, sems, core)
        for copy in copies:
            copy.start()
        clear_edges(sh, padded_ref)
        for copy in copies:
            copy.wait()
        params = [unit_params(mod_keep_ref, mod_other_ref, core, unit) for unit in range(PAIR)]
        if first:
            forward_unit(sh, x_ref, middle_ref, params[0], padded_ref, weights, 0)
        scratch = (padded_ref, act_ref, slope_ref, pre_grad_ref, slab_ref)
        backward_unit(
            sh, middle_ref, up_ref, between_ref, params[1], scratch, weights, 1, keep_ref, send_ref, core
        )
        backward_unit(
            sh, x_ref, between_ref, grad_ref, params[0], scratch, weights, 0, keep_ref, send_ref, core
        )

    if not first:

        @pl.when(stage != active_stage)
        def _():
            keep_ref[...] = keep_in[...]
            send_ref[...] = send_in[...]


def finish_kernel(sh, keep_ref, other_ref, embedded_ref, gain_ref, grads_ref, conv_ref, mod_ref):
    core = lax.axis_index("segment") % PAIR
    conv_ref[...] = keep_ref[0 : sh.slab, :] + other_ref[0 : sh.slab, :]
    rows = slice(sh.slab, sh.slab + sh.own_rows)
    grads_ref[pl.ds(core, 1)] = keep_ref[rows, :].astype(jnp.bfloat16)[None]
    grads_ref[pl.ds(1 - core, 1)] = other_ref[rows, :].astype(jnp.bfloat16)[None]
    base = sh.slab + sh.own_rows

    def mod_rows(ref):
        return jnp.concatenate([gain_ref[...] * ref[base + 1 : base + 2, :], ref[base : base + 1, :]], axis=1)

    own, other = mod_rows(keep_ref), mod_rows(other_ref)
    spot = lax.broadcasted_iota(jnp.int32, (16, own.shape[1]), 0)
    values = jnp.where(spot % 2 == core, own, other)
    high = values.astype(jnp.bfloat16).astype(jnp.float32)
    rest = values - high
    middle = rest.astype(jnp.bfloat16).astype(jnp.float32)
    low = rest - middle
    part = spot // 2
    pieces = jnp.where(part == 0, high, jnp.where(part == 1, middle, jnp.where(part == 2, low, 0.0)))
    mod_ref[...] = lax.dot_general(
        embedded_ref[...],
        pieces.astype(jnp.bfloat16),
        (((0,), (0,)), ((), ())),
        preferred_element_type=jnp.float32,
    )


def shards(
    x_in,
    out_cotangent,
    timesteps,
    labels,
    time_weight,
    label_table,
    conv_weight,
    mod_weight,
    mod_bias,
    norm_gain,
):
    segments, spaces = lax.axis_size("segment"), lax.axis_size("space")
    stages = segments // PAIR
    stage, core = place_of()
    images, row_count, cols, channels = x_in.shape
    sh = Shape(row_count * spaces, cols, channels, spaces)
    f32, bf16 = jnp.float32, jnp.bfloat16

    def call(body, ins, outs, scratch=(), limit=sh.limit, cost=None):
        return pl.pallas_call(
            body,
            out_shape=outs,
            in_specs=ins,
            out_specs=[VMEM] * len(outs),
            scratch_shapes=list(scratch),
            compiler_params=pltpu.CompilerParams(vmem_limit_bytes=limit),
            cost_estimate=cost,
        )

    shape = jax.ShapeDtypeStruct
    swap = [(i, i ^ 1) for i in range(segments)]
    weight = conv_weight.reshape(9 * channels, channels)
    ends = jnp.where(stage == 0, x_in, out_cotangent)
    near = lax.dynamic_index_in_dim(ends, core, 0, keepdims=False).reshape(1, sh.own_rows, channels)
    order, bit = [0], spaces // 2
    while True:
        far = lax.ppermute(near, "space", [(i, i ^ bit) for i in range(spaces)])
        far_order = [k ^ bit for k in order]
        if bit == 1:
            break
        near = jnp.concatenate([near, far])
        order, bit = order + far_order, bit // 2
    other_weight = lax.ppermute(weight, "segment", swap)

    half = time_weight.shape[0] // 2
    frequency = np.exp(-np.log(10000.0) * np.arange(half) / half).astype(np.float32)
    frequency = jnp.asarray(np.concatenate([frequency, frequency])[None])
    operands = (frequency, time_weight, label_table, mod_weight[0], mod_bias, norm_gain)
    mod_keep, mod_send, embedded = call(
        prepare_kernel,
        [SMEM, SMEM] + [HBM] * 6,
        [shape((8, channels), f32), shape((8, channels), f32), shape((16, time_weight.shape[1]), bf16)],
        [pltpu.VMEM(a.shape, a.dtype) for a in operands] + [pltpu.SemaphoreType.DMA((len(operands),))],
        60 << 20,
        pl.CostEstimate(flops=1 << 27, bytes_accessed=2 << 20, transcendentals=0),
    )(timesteps, labels, *operands)
    mod_other = lax.ppermute(mod_send, "segment", swap)
    own = (mod_keep, mod_other, weight, other_weight)
    own_specs = [VMEM, VMEM, HBM, HBM]

    image_shape = shape((sh.pixels, channels), bf16)
    pack_shape = shape((sh.pack, channels), f32)
    common = [
        pltpu.VMEM((PAIR, 9 * channels, channels), bf16),
        pltpu.VMEM((3, sh.padded, channels), bf16),
    ]
    sems = [pltpu.SemaphoreType.DMA((2,))]

    def hop(value, source, target):
        pairs = [(PAIR * source + k, PAIR * target + k) for k in range(PAIR)]
        return lax.ppermute(value, "segment", pairs)

    image, middle, out = call(
        functools.partial(forward_kernel, sh, 0, (order, far_order)),
        [VMEM, VMEM] + own_specs,
        [image_shape] * 3,
        common + sems,
    )(near, far, *own)
    entering, middles = [image, hop(out, 0, 1)], [middle]
    for active in range(1, stages - 1):
        middle, out = call(
            functools.partial(forward_kernel, sh, active, None),
            [VMEM] + own_specs,
            [image_shape, image_shape],
            common + sems,
        )(entering[active], *own)
        middles.append(middle)
        entering.append(hop(out, active, active + 1))

    scratch = common + [
        pltpu.VMEM((sh.pixels, channels), bf16),
        pltpu.VMEM((sh.pixels, channels), f32),
        pltpu.VMEM((sh.pixels, channels), f32),
        pltpu.VMEM((sh.taps * channels, channels), f32),
        pltpu.VMEM((sh.pixels, channels), bf16),
    ]
    outs = [image_shape, pack_shape, pack_shape]
    grad, keep, send = call(
        functools.partial(backward_kernel, sh, stages - 1, True),
        [VMEM, VMEM] + own_specs,
        outs,
        scratch + sems + [pltpu.VMEM((sh.pixels, channels), bf16)],
    )(entering[stages - 1], image, *own)
    for active in range(stages - 2, -1, -1):
        upstream = hop(grad, active + 1, active)
        grad, keep, send = call(
            functools.partial(backward_kernel, sh, active, False),
            [VMEM, VMEM, VMEM] + own_specs + [VMEM, VMEM],
            outs,
            scratch + sems,
        )(entering[active], middles[active], upstream, *own, keep, send)
    other = lax.ppermute(send, "segment", swap)
    grads, conv_grad, mod_grad = call(
        functools.partial(finish_kernel, sh),
        [VMEM] * 4,
        [
            shape((images, sh.own_rows, channels), bf16),
            shape((sh.slab, channels), f32),
            shape((time_weight.shape[1], 2 * channels), f32),
        ],
    )(keep, other, embedded, norm_gain)
    return (grads.reshape(1, images, row_count, cols, channels), conv_grad[None], mod_grad[None])


def solution(mesh):
    placed = (
        P(None, "space", None, None),
        P(None, "space", None, None),
        P(),
        P(),
        P(),
        P(),
        P("segment", None, None, None, None),
        P("segment", None, None),
        P("segment", None),
        P("segment", None),
    )
    return jax.shard_map(
        shards,
        mesh=mesh,
        in_specs=placed,
        out_specs=(
            P("segment", None, "space", None, None),
            P("segment", "space", None),
            P("segment", None, None),
        ),
        check_vma=False,
    )
```

```python
import functools

import jax
import jax.numpy as jnp
import numpy as np
from jax import lax
from jax.experimental import pallas as pl
from jax.experimental.pallas import tpu as pltpu
from jax.sharding import PartitionSpec as P

GROUPS = 32
EPSILON = 1e-05
PAIR = 2
VMEM = pl.BlockSpec(memory_space=pltpu.VMEM)
SMEM = pl.BlockSpec(memory_space=pltpu.SMEM)
HBM = pl.BlockSpec(memory_space=pl.ANY)


def sigmoid(values):
    return 1.0 / (1.0 + jnp.exp(-values))


def over_chunks(count, body):
    if count == 1:
        body(0)
    else:

        def step(i, carry):
            body(i)
            return carry

        lax.fori_loop(0, count, step, 0)


def chunk_start(i, size):
    return 0 if isinstance(i, int) else pl.multiple_of(i * size, size)


def fold_rows(values):
    return jnp.sum(values.reshape(values.shape[0] // 8, 8, values.shape[1]), axis=0)


def column(rows):
    return jnp.sum(rows, axis=0, keepdims=True)


def group_sums(rows, width):
    lanes = lax.broadcasted_iota(jnp.int32, rows.shape, 1)
    size = rows.shape[1]
    step = 1
    while step < width:
        ahead = pltpu.roll(rows, size - step, 1)
        behind = pltpu.roll(rows, step, 1)
        rows = rows + jnp.where((lanes & step) == 0, ahead, behind)
        step *= 2
    return rows


def stack_rows(first, second):
    spot = lax.broadcasted_iota(jnp.int32, (8, first.shape[1]), 0)
    return jnp.where(spot == 0, first, jnp.where(spot == 1, second, 0.0))


class Shape:
    def __init__(self, height, cols, channels, space_count):
        self.cols, self.channels = cols, channels
        self.pixels = height * cols
        self.chunk = cols * max(1, min(self.pixels, 256) // cols)
        self.chunks = self.pixels // self.chunk
        self.width = channels // GROUPS
        self.entries = float(self.pixels * self.width)
        self.padded = self.pixels + 2 * cols
        self.own_rows = height // space_count * cols
        self.slab = 9 * channels // space_count
        self.taps = min(9, (self.slab - 1) // channels + 2)
        self.pack = self.slab + self.own_rows + 8
        self.limit = (12 << 20) + self.pixels * channels * 40


def statistics(sh, x_ref):
    zero = jnp.zeros((8, sh.channels), jnp.float32)

    def add(i, sums):
        part = x_ref[pl.ds(chunk_start(i, sh.chunk), sh.chunk), :].astype(jnp.float32)
        return (sums[0] + fold_rows(part), sums[1] + fold_rows(part * part))

    if sh.chunks == 1:
        one, two = add(0, (zero, zero))
    else:
        one, two = lax.fori_loop(0, sh.chunks, add, (zero, zero))
    total = group_sums(stack_rows(column(one), column(two)), sh.width) / sh.entries
    mean = total[0:1]
    return (mean, lax.rsqrt(total[1:2] - mean * mean + EPSILON))


def clear_edges(sh, padded_ref):
    zero = jnp.zeros((3, sh.cols, sh.channels), padded_ref.dtype)
    padded_ref[:, 0 : sh.cols, :] = zero
    padded_ref[:, sh.pixels + sh.cols : sh.padded, :] = zero


def spread(sh, padded_ref, start, values):
    place = pl.ds(start + sh.cols, sh.chunk)
    spot = lax.broadcasted_iota(jnp.int32, values.shape, 0) % sh.cols
    padded_ref[0, place, :] = jnp.where(spot == 0, 0.0, pltpu.roll(values, 1, 0)).astype(jnp.bfloat16)
    padded_ref[1, place, :] = values.astype(jnp.bfloat16)
    padded_ref[2, place, :] = jnp.where(
        spot == sh.cols - 1, 0.0, pltpu.roll(values, sh.chunk - 1, 0)
    ).astype(jnp.bfloat16)


def convolve(sh, padded_ref, start, weight_ref, unit, backward):
    total = None
    for p in range(3):
        for q in range(3):
            row, col = (2 - p, 2 - q) if backward else (p, q)
            block = padded_ref[col, pl.ds(start + row * sh.cols, sh.chunk), :]
            tap = (3 * p + q) * sh.channels
            weight = weight_ref[unit, tap : tap + sh.channels, :]
            part = lax.dot_general(
                block,
                weight,
                (((1,), (1 if backward else 0,)), ((), ())),
                preferred_element_type=jnp.float32,
            )
            total = part if total is None else total + part
    return total


def forward_unit(sh, x_ref, out_ref, params, padded_ref, weight_ref, unit):
    factor, shift = params
    mean, inv_std = statistics(sh, x_ref)

    def activate(i):
        start = chunk_start(i, sh.chunk)
        normed = (x_ref[pl.ds(start, sh.chunk), :].astype(jnp.float32) - mean) * inv_std
        pre = normed * factor + shift
        spread(sh, padded_ref, start, pre * sigmoid(pre))

    def produce(i):
        start = chunk_start(i, sh.chunk)
        inputs = x_ref[pl.ds(start, sh.chunk), :].astype(jnp.float32)
        z = convolve(sh, padded_ref, start, weight_ref, unit, False)
        out_ref[pl.ds(start, sh.chunk), :] = (inputs + z).astype(jnp.bfloat16)

    over_chunks(sh.chunks, activate)
    over_chunks(sh.chunks, produce)


def backward_unit(sh, x_ref, up_ref, grad_ref, params, scratch, weight_ref, unit, keep_ref, send_ref, core):
    padded_ref, act_ref, slope_ref, pre_grad_ref, slab_ref = scratch
    factor, shift = params
    space = lax.axis_index("space")
    mean, inv_std = statistics(sh, x_ref)
    zero = jnp.zeros((8, sh.channels), jnp.float32)

    def activate(i):
        start = chunk_start(i, sh.chunk)
        rows = pl.ds(start, sh.chunk)
        spread(sh, padded_ref, start, up_ref[rows, :].astype(jnp.float32))
        pre = (x_ref[rows, :].astype(jnp.float32) - mean) * inv_std * factor + shift
        sigma = sigmoid(pre)
        act_ref[rows, :] = (pre * sigma).astype(jnp.bfloat16)
        slope_ref[rows, :] = sigma * (1.0 + pre * (1.0 - sigma))

    def differentiate(i, sums):
        start = chunk_start(i, sh.chunk)
        rows = pl.ds(start, sh.chunk)
        normed = (x_ref[rows, :].astype(jnp.float32) - mean) * inv_std
        pre_grad = convolve(sh, padded_ref, start, weight_ref, unit, True) * slope_ref[rows, :]
        pre_grad_ref[rows, :] = pre_grad
        return (sums[0] + fold_rows(pre_grad), sums[1] + fold_rows(pre_grad * normed))

    over_chunks(sh.chunks, activate)
    if sh.chunks == 1:
        sums = differentiate(0, (zero, zero))
    else:
        sums = lax.fori_loop(0, sh.chunks, differentiate, (zero, zero))
    sum_grad, sum_cross = column(sums[0]), column(sums[1])
    means = group_sums(stack_rows(factor * sum_grad, factor * sum_cross), sh.width) / sh.entries
    center, tilt = means[0:1], means[1:2]

    def finish(i):
        rows = pl.ds(chunk_start(i, sh.chunk), sh.chunk)
        normed = (x_ref[rows, :].astype(jnp.float32) - mean) * inv_std
        back = factor * pre_grad_ref[rows, :] - center - normed * tilt
        grad_ref[rows, :] = (up_ref[rows, :].astype(jnp.float32) + inv_std * back).astype(jnp.bfloat16)

    over_chunks(sh.chunks, finish)
    first_row = space * sh.slab
    first_tap = jnp.minimum(first_row // sh.channels, 9 - sh.taps)
    offset = pl.multiple_of(first_row - first_tap * sh.channels, 8)
    for t in range(sh.taps):
        tap = first_tap + t
        row, col = 2 - tap // 3, 2 - tap % 3
        place = pl.ds(t * sh.channels, sh.channels)

        def product(i):
            start = chunk_start(i, sh.chunk)
            block = padded_ref[col, pl.ds(pl.multiple_of(start + row * sh.cols, 16), sh.chunk), :]
            return lax.dot_general(
                act_ref[pl.ds(start, sh.chunk), :],
                block,
                (((0,), (0,)), ((), ())),
                preferred_element_type=jnp.float32,
            )

        if sh.chunks == 1:
            slab_ref[place, :] = product(0)
        else:
            slab_ref[place, :] = jnp.zeros((sh.channels, sh.channels), jnp.float32)

            def accumulate(i):
                slab_ref[place, :] += product(i)

            over_chunks(sh.chunks, accumulate)
    mine = slab_ref[pl.ds(offset, sh.slab), :]
    rows = grad_ref[pl.ds(pl.multiple_of(space * sh.own_rows, sh.own_rows), sh.own_rows), :]
    sums = stack_rows(sum_grad, sum_cross)

    def write(ref):
        ref[0 : sh.slab, :] = mine
        ref[sh.slab : sh.slab + sh.own_rows, :] = rows.astype(jnp.float32)
        ref[sh.slab + sh.own_rows : sh.pack, :] = sums

    @pl.when(core == unit)
    def _():
        write(keep_ref)

    @pl.when(core != unit)
    def _():
        write(send_ref)


def place_of():
    index = lax.axis_index("segment")
    return (index // PAIR, index % PAIR)


def unit_params(params_ref, unit):
    return (params_ref[2 * unit : 2 * unit + 1, :], params_ref[2 * unit + 1 : 2 * unit + 2, :])


def layout_kernel(own_hbm, other_hbm, mod_keep_hbm, mod_other_hbm, weights_ref, params_ref, mods_ref, sems):
    core = lax.axis_index("segment") % PAIR
    copies = [
        pltpu.make_async_copy(mod_keep_hbm, mods_ref.at[core], sems.at[0]),
        pltpu.make_async_copy(mod_other_hbm, mods_ref.at[1 - core], sems.at[1]),
        pltpu.make_async_copy(own_hbm, weights_ref.at[core], sems.at[2]),
        pltpu.make_async_copy(other_hbm, weights_ref.at[1 - core], sems.at[3]),
    ]
    for copy in copies:
        copy.start()
    for copy in copies[:2]:
        copy.wait()
    params_ref[0:2, :] = mods_ref[0, 0:2, :]
    params_ref[2:4, :] = mods_ref[1, 0:2, :]
    params_ref[4:8, :] = jnp.zeros((4, params_ref.shape[1]), jnp.float32)
    for copy in copies[2:]:
        copy.wait()


def prepare_kernel(
    times_ref,
    labels_ref,
    frequency_hbm,
    time_weight_hbm,
    table_hbm,
    mod_weight_hbm,
    mod_bias_hbm,
    gain_hbm,
    keep_ref,
    send_ref,
    embedded_ref,
    frequency_ref,
    time_weight_ref,
    table_ref,
    mod_weight_ref,
    mod_bias_ref,
    gain_ref,
    sems,
):
    core = lax.axis_index("segment") % PAIR
    sources = (frequency_hbm, time_weight_hbm, mod_weight_hbm, mod_bias_hbm, gain_hbm)
    targets = (frequency_ref, time_weight_ref, mod_weight_ref, mod_bias_ref, gain_ref)
    copies = [pltpu.make_async_copy(a, b, sems.at[i]) for i, (a, b) in enumerate(zip(sources, targets))]
    for image in range(PAIR):
        block = table_hbm.at[pl.ds(labels_ref[image] // 8, 1)]
        copies.append(pltpu.make_async_copy(block, table_ref.at[pl.ds(image, 1)], sems.at[len(copies)]))
    for copy in copies:
        copy.start()
    for copy in copies:
        copy.wait()
    rows = 16
    spot = lax.broadcasted_iota(jnp.int32, (rows, 1), 0)
    time = jnp.where(spot % 2 == 0, times_ref[0], times_ref[1]).astype(jnp.float32)

    def label_row(image):
        block = table_ref[image].astype(jnp.float32)
        row = lax.broadcasted_iota(jnp.int32, block.shape, 0)
        return column(jnp.where(row == labels_ref[image] % 8, block, 0.0))

    label_rows = jnp.where(spot % 2 == 0, label_row(0), label_row(1))
    angles = time * frequency_ref[...]
    lanes = lax.broadcasted_iota(jnp.int32, angles.shape, 1)
    half = angles.shape[1] // 2
    sinusoid = jnp.where(lanes < half, jnp.cos(angles), jnp.sin(angles)).astype(jnp.bfloat16)
    timed = jnp.dot(sinusoid, time_weight_ref[...], preferred_element_type=jnp.float32) + label_rows
    embedded = (timed * sigmoid(timed)).astype(jnp.bfloat16)
    embedded_ref[...] = embedded
    modulation = jnp.dot(embedded, mod_weight_ref[...], preferred_element_type=jnp.float32) + mod_bias_ref[...]
    channels = modulation.shape[1] // 2
    factor = gain_ref[...] * (1.0 + modulation[:, :channels])
    shift = modulation[:, channels:]

    @pl.when(core == 0)
    def _():
        keep_ref[...] = stack_rows(factor[0:1], shift[0:1])
        send_ref[...] = stack_rows(factor[1:2], shift[1:2])

    @pl.when(core != 0)
    def _():
        keep_ref[...] = stack_rows(factor[1:2], shift[1:2])
        send_ref[...] = stack_rows(factor[0:1], shift[0:1])


def forward_kernel(sh, active_stage, x_ref, params_ref, weights, middle_ref, out_ref, padded_ref):
    stage, _ = place_of()

    @pl.when(stage == active_stage)
    def _():
        clear_edges(sh, padded_ref)
        forward_unit(sh, x_ref, middle_ref, unit_params(params_ref, 0), padded_ref, weights, 0)
        forward_unit(sh, middle_ref, out_ref, unit_params(params_ref, 1), padded_ref, weights, 1)


def backward_kernel(sh, active_stage, first, *refs):
    if first:
        x_ref, up_ref, params_ref, weights = refs[:4]
        refs = refs[4:]
    else:
        x_ref, middle_ref, up_ref, params_ref, weights, keep_in, send_in = refs[:7]
        refs = refs[7:]
    grad_ref, keep_ref, send_ref = refs[:3]
    padded_ref, act_ref, slope_ref, pre_grad_ref, slab_ref, between_ref = refs[3:9]
    if first:
        middle_ref = refs[9]
    stage, core = place_of()

    @pl.when(stage == active_stage)
    def _():
        clear_edges(sh, padded_ref)
        params = [unit_params(params_ref, unit) for unit in range(PAIR)]
        if first:
            forward_unit(sh, x_ref, middle_ref, params[0], padded_ref, weights, 0)
        scratch = (padded_ref, act_ref, slope_ref, pre_grad_ref, slab_ref)
        backward_unit(
            sh, middle_ref, up_ref, between_ref, params[1], scratch, weights, 1, keep_ref, send_ref, core
        )
        backward_unit(
            sh, x_ref, between_ref, grad_ref, params[0], scratch, weights, 0, keep_ref, send_ref, core
        )

    if not first:

        @pl.when(stage != active_stage)
        def _():
            keep_ref[...] = keep_in[...]
            send_ref[...] = send_in[...]


def finish_kernel(sh, keep_ref, other_ref, embedded_ref, gain_ref, grads_ref, conv_ref, mod_ref):
    core = lax.axis_index("segment") % PAIR
    conv_ref[...] = keep_ref[0 : sh.slab, :] + other_ref[0 : sh.slab, :]
    rows = slice(sh.slab, sh.slab + sh.own_rows)
    grads_ref[pl.ds(core, 1)] = keep_ref[rows, :].astype(jnp.bfloat16)[None]
    grads_ref[pl.ds(1 - core, 1)] = other_ref[rows, :].astype(jnp.bfloat16)[None]
    base = sh.slab + sh.own_rows

    def mod_rows(ref):
        return jnp.concatenate([gain_ref[...] * ref[base + 1 : base + 2, :], ref[base : base + 1, :]], axis=1)

    own, other = mod_rows(keep_ref), mod_rows(other_ref)
    spot = lax.broadcasted_iota(jnp.int32, (16, own.shape[1]), 0)
    values = jnp.where(spot % 2 == core, own, other)
    high = values.astype(jnp.bfloat16).astype(jnp.float32)
    rest = values - high
    middle = rest.astype(jnp.bfloat16).astype(jnp.float32)
    low = rest - middle
    part = spot // 2
    pieces = jnp.where(part == 0, high, jnp.where(part == 1, middle, jnp.where(part == 2, low, 0.0)))
    mod_ref[...] = lax.dot_general(
        embedded_ref[...],
        pieces.astype(jnp.bfloat16),
        (((0,), (0,)), ((), ())),
        preferred_element_type=jnp.float32,
    )


def shards(
    x_in,
    out_cotangent,
    timesteps,
    labels,
    time_weight,
    label_table,
    conv_weight,
    mod_weight,
    mod_bias,
    norm_gain,
):
    segments, spaces = lax.axis_size("segment"), lax.axis_size("space")
    stages = segments // PAIR
    stage, core = place_of()
    images, row_count, cols, channels = x_in.shape
    sh = Shape(row_count * spaces, cols, channels, spaces)
    f32, bf16 = jnp.float32, jnp.bfloat16

    def call(body, ins, outs, scratch=(), limit=sh.limit, cost=None):
        return pl.pallas_call(
            body,
            out_shape=outs,
            in_specs=ins,
            out_specs=[VMEM] * len(outs),
            scratch_shapes=list(scratch),
            compiler_params=pltpu.CompilerParams(vmem_limit_bytes=limit),
            cost_estimate=cost,
        )

    shape = jax.ShapeDtypeStruct
    swap = [(i, i ^ 1) for i in range(segments)]
    weight = conv_weight.reshape(9 * channels, channels)
    ends = jnp.where(stage == 0, x_in, out_cotangent)
    near = lax.dynamic_index_in_dim(ends, core, 0, keepdims=False).reshape(1, sh.own_rows, channels)
    copies = jnp.broadcast_to(near, (spaces, sh.own_rows, channels))
    image = lax.all_to_all(copies, "space", 0, 0).reshape(sh.pixels, channels)
    other_weight = lax.ppermute(weight, "segment", swap)

    half = time_weight.shape[0] // 2
    frequency = np.exp(-np.log(10000.0) * np.arange(half) / half).astype(np.float32)
    frequency = jnp.asarray(np.concatenate([frequency, frequency])[None])
    table = label_table.reshape(-1, 8, label_table.shape[1])
    operands = (frequency, time_weight, table, mod_weight[0], mod_bias, norm_gain)
    mod_keep, mod_send, embedded = call(
        prepare_kernel,
        [SMEM, SMEM] + [HBM] * 6,
        [shape((8, channels), f32), shape((8, channels), f32), shape((16, time_weight.shape[1]), bf16)],
        [pltpu.VMEM(a.shape if a.ndim == 2 else (PAIR, *a.shape[1:]), a.dtype) for a in operands]
        + [pltpu.SemaphoreType.DMA((len(operands) + 1,))],
        60 << 20,
        pl.CostEstimate(flops=1 << 27, bytes_accessed=2 << 20, transcendentals=0),
    )(timesteps, labels, *operands)
    mod_other = lax.ppermute(mod_send, "segment", swap)
    weights, params = call(
        layout_kernel,
        [HBM] * 4,
        [shape((PAIR, 9 * channels, channels), bf16), shape((8, channels), f32)],
        [pltpu.VMEM((PAIR, 8, channels), f32), pltpu.SemaphoreType.DMA((4,))],
    )(weight, other_weight, mod_keep, mod_other)

    image_shape = shape((sh.pixels, channels), bf16)
    pack_shape = shape((sh.pack, channels), f32)
    common = [pltpu.VMEM((3, sh.padded, channels), bf16)]

    def hop(value, source, target):
        pairs = [(PAIR * source + k, PAIR * target + k) for k in range(PAIR)]
        return lax.ppermute(value, "segment", pairs)

    entering, middles = [image], []
    for active in range(stages - 1):
        middle, out = call(
            functools.partial(forward_kernel, sh, active),
            [VMEM] * 3,
            [image_shape, image_shape],
            common,
        )(entering[active], params, weights)
        middles.append(middle)
        entering.append(hop(out, active, active + 1))

    scratch = common + [
        pltpu.VMEM((sh.pixels, channels), bf16),
        pltpu.VMEM((sh.pixels, channels), f32),
        pltpu.VMEM((sh.pixels, channels), f32),
        pltpu.VMEM((sh.taps * channels, channels), f32),
        pltpu.VMEM((sh.pixels, channels), bf16),
    ]
    outs = [image_shape, pack_shape, pack_shape]
    grad, keep, send = call(
        functools.partial(backward_kernel, sh, stages - 1, True),
        [VMEM] * 4,
        outs,
        scratch + [pltpu.VMEM((sh.pixels, channels), bf16)],
    )(entering[stages - 1], image, params, weights)
    for active in range(stages - 2, -1, -1):
        upstream = hop(grad, active + 1, active)
        grad, keep, send = call(
            functools.partial(backward_kernel, sh, active, False),
            [VMEM] * 7,
            outs,
            scratch,
        )(entering[active], middles[active], upstream, params, weights, keep, send)
    other = lax.ppermute(send, "segment", swap)
    grads, conv_grad, mod_grad = call(
        functools.partial(finish_kernel, sh),
        [VMEM] * 4,
        [
            shape((images, sh.own_rows, channels), bf16),
            shape((sh.slab, channels), f32),
            shape((time_weight.shape[1], 2 * channels), f32),
        ],
    )(keep, other, embedded, norm_gain)
    return (grads.reshape(1, images, row_count, cols, channels), conv_grad[None], mod_grad[None])


def solution(mesh):
    placed = (
        P(None, "space", None, None),
        P(None, "space", None, None),
        P(),
        P(),
        P(),
        P(),
        P("segment", None, None, None, None),
        P("segment", None, None),
        P("segment", None),
        P("segment", None),
    )
    return jax.shard_map(
        shards,
        mesh=mesh,
        in_specs=placed,
        out_specs=(
            P("segment", None, "space", None, None),
            P("segment", "space", None),
            P("segment", None, None),
        ),
        check_vma=False,
    )
```

```python
import functools
import math

import jax
import jax.numpy as jnp
from jax import lax
from jax.experimental import pallas as pl
from jax.experimental.pallas import tpu as pltpu
from jax.sharding import PartitionSpec as P

GROUPS = 32
EPSILON = 1e-05
PAIR = 2
VMEM = pl.BlockSpec(memory_space=pltpu.VMEM)
SMEM = pl.BlockSpec(memory_space=pltpu.SMEM)
ANY = pl.BlockSpec(memory_space=pl.ANY)


def sigmoid(values):
    return 1.0 / (1.0 + jnp.exp(-values))


def over_chunks(count, body):
    if count == 1:
        body(0)
    else:

        def step(i, carry):
            body(i)
            return carry

        lax.fori_loop(0, count, step, 0)


def chunk_start(i, size):
    return 0 if isinstance(i, int) else pl.multiple_of(i * size, size)


def fold_rows(values):
    return jnp.sum(values.reshape(values.shape[0] // 8, 8, values.shape[1]), axis=0)


def column(rows):
    return jnp.sum(rows, axis=0, keepdims=True)


def group_sums(rows, width):
    lanes = lax.broadcasted_iota(jnp.int32, rows.shape, 1)
    size = rows.shape[1]
    step = 1
    while step < width:
        ahead = pltpu.roll(rows, size - step, 1)
        behind = pltpu.roll(rows, step, 1)
        rows = rows + jnp.where((lanes & step) == 0, ahead, behind)
        step *= 2
    return rows


def stack_rows(first, second):
    spot = lax.broadcasted_iota(jnp.int32, (8, first.shape[1]), 0)
    return jnp.where(spot == 0, first, jnp.where(spot == 1, second, 0.0))


class Shape:
    def __init__(self, height, cols, channels, space_count):
        self.cols, self.channels = cols, channels
        self.pixels = height * cols
        self.chunk = cols * max(1, min(self.pixels, 256) // cols)
        self.chunks = self.pixels // self.chunk
        self.width = channels // GROUPS
        self.entries = float(self.pixels * self.width)
        self.padded = self.pixels + 2 * cols
        self.own_rows = height // space_count * cols
        self.slab = 9 * channels // space_count
        self.taps = min(9, (self.slab - 1) // channels + 2)
        self.pack = self.slab + self.own_rows + 8
        self.limit = (12 << 20) + self.pixels * channels * 40


def statistics(sh, x_ref):
    zero = jnp.zeros((8, sh.channels), jnp.float32)

    def add(i, sums):
        part = x_ref[pl.ds(chunk_start(i, sh.chunk), sh.chunk), :].astype(jnp.float32)
        return (sums[0] + fold_rows(part), sums[1] + fold_rows(part * part))

    if sh.chunks == 1:
        one, two = add(0, (zero, zero))
    else:
        one, two = lax.fori_loop(0, sh.chunks, add, (zero, zero))
    total = group_sums(stack_rows(column(one), column(two)), sh.width) / sh.entries
    mean = total[0:1]
    return (mean, lax.rsqrt(total[1:2] - mean * mean + EPSILON))


def clear_edges(sh, padded_ref):
    zero = jnp.zeros((3, sh.cols, sh.channels), padded_ref.dtype)
    padded_ref[:, 0 : sh.cols, :] = zero
    padded_ref[:, sh.pixels + sh.cols : sh.padded, :] = zero


def spread(sh, padded_ref, start, values):
    place = pl.ds(start + sh.cols, sh.chunk)
    spot = lax.broadcasted_iota(jnp.int32, values.shape, 0) % sh.cols
    padded_ref[0, place, :] = jnp.where(spot == 0, 0.0, pltpu.roll(values, 1, 0)).astype(jnp.bfloat16)
    padded_ref[1, place, :] = values.astype(jnp.bfloat16)
    padded_ref[2, place, :] = jnp.where(
        spot == sh.cols - 1, 0.0, pltpu.roll(values, sh.chunk - 1, 0)
    ).astype(jnp.bfloat16)


def convolve(sh, padded_ref, start, weight_ref, unit, backward):
    total = None
    for p in range(3):
        for q in range(3):
            row, col = (2 - p, 2 - q) if backward else (p, q)
            block = padded_ref[col, pl.ds(start + row * sh.cols, sh.chunk), :]
            tap = (3 * p + q) * sh.channels
            weight = weight_ref[unit, tap : tap + sh.channels, :]
            part = lax.dot_general(
                block,
                weight,
                (((1,), (1 if backward else 0,)), ((), ())),
                preferred_element_type=jnp.float32,
            )
            total = part if total is None else total + part
    return total


def forward_unit(sh, x_ref, out_ref, params, padded_ref, weight_ref, unit):
    factor, shift = params
    mean, inv_std = statistics(sh, x_ref)

    def activate(i):
        start = chunk_start(i, sh.chunk)
        normed = (x_ref[pl.ds(start, sh.chunk), :].astype(jnp.float32) - mean) * inv_std
        pre = normed * factor + shift
        spread(sh, padded_ref, start, pre * sigmoid(pre))

    def produce(i):
        start = chunk_start(i, sh.chunk)
        inputs = x_ref[pl.ds(start, sh.chunk), :].astype(jnp.float32)
        z = convolve(sh, padded_ref, start, weight_ref, unit, False)
        out_ref[pl.ds(start, sh.chunk), :] = (inputs + z).astype(jnp.bfloat16)

    over_chunks(sh.chunks, activate)
    over_chunks(sh.chunks, produce)


def backward_unit(sh, x_ref, up_ref, grad_ref, params, scratch, weight_ref, unit, keep_ref, send_ref, core):
    padded_ref, act_ref, slope_ref, pre_grad_ref, slab_ref = scratch
    factor, shift = params
    space = lax.axis_index("space")
    mean, inv_std = statistics(sh, x_ref)
    zero = jnp.zeros((8, sh.channels), jnp.float32)

    def activate(i):
        start = chunk_start(i, sh.chunk)
        rows = pl.ds(start, sh.chunk)
        spread(sh, padded_ref, start, up_ref[rows, :].astype(jnp.float32))
        pre = (x_ref[rows, :].astype(jnp.float32) - mean) * inv_std * factor + shift
        sigma = sigmoid(pre)
        act_ref[rows, :] = (pre * sigma).astype(jnp.bfloat16)
        slope_ref[rows, :] = sigma * (1.0 + pre * (1.0 - sigma))

    def differentiate(i, sums):
        start = chunk_start(i, sh.chunk)
        rows = pl.ds(start, sh.chunk)
        normed = (x_ref[rows, :].astype(jnp.float32) - mean) * inv_std
        pre_grad = convolve(sh, padded_ref, start, weight_ref, unit, True) * slope_ref[rows, :]
        pre_grad_ref[rows, :] = pre_grad
        return (sums[0] + fold_rows(pre_grad), sums[1] + fold_rows(pre_grad * normed))

    over_chunks(sh.chunks, activate)
    if sh.chunks == 1:
        sums = differentiate(0, (zero, zero))
    else:
        sums = lax.fori_loop(0, sh.chunks, differentiate, (zero, zero))
    sum_grad, sum_cross = column(sums[0]), column(sums[1])
    means = group_sums(stack_rows(factor * sum_grad, factor * sum_cross), sh.width) / sh.entries
    center, tilt = means[0:1], means[1:2]

    def finish(i):
        rows = pl.ds(chunk_start(i, sh.chunk), sh.chunk)
        normed = (x_ref[rows, :].astype(jnp.float32) - mean) * inv_std
        back = factor * pre_grad_ref[rows, :] - center - normed * tilt
        grad_ref[rows, :] = (up_ref[rows, :].astype(jnp.float32) + inv_std * back).astype(jnp.bfloat16)

    over_chunks(sh.chunks, finish)
    first_row = space * sh.slab
    first_tap = jnp.minimum(first_row // sh.channels, 9 - sh.taps)
    offset = pl.multiple_of(first_row - first_tap * sh.channels, 8)
    for t in range(sh.taps):
        tap = first_tap + t
        row, col = 2 - tap // 3, 2 - tap % 3
        place = pl.ds(t * sh.channels, sh.channels)

        def product(i):
            start = chunk_start(i, sh.chunk)
            block = padded_ref[col, pl.ds(pl.multiple_of(start + row * sh.cols, 16), sh.chunk), :]
            return lax.dot_general(
                act_ref[pl.ds(start, sh.chunk), :],
                block,
                (((0,), (0,)), ((), ())),
                preferred_element_type=jnp.float32,
            )

        if sh.chunks == 1:
            slab_ref[place, :] = product(0)
        else:
            slab_ref[place, :] = jnp.zeros((sh.channels, sh.channels), jnp.float32)

            def accumulate(i):
                slab_ref[place, :] += product(i)

            over_chunks(sh.chunks, accumulate)
    mine = slab_ref[pl.ds(offset, sh.slab), :]
    rows = grad_ref[pl.ds(pl.multiple_of(space * sh.own_rows, sh.own_rows), sh.own_rows), :]
    sums = stack_rows(sum_grad, sum_cross)

    def write(ref):
        ref[0 : sh.slab, :] = mine
        ref[sh.slab : sh.slab + sh.own_rows, :] = rows.astype(jnp.float32)
        ref[sh.slab + sh.own_rows : sh.pack, :] = sums

    @pl.when(core == unit)
    def _():
        write(keep_ref)

    @pl.when(core != unit)
    def _():
        write(send_ref)


def place_of():
    index = lax.axis_index("segment")
    return (index // PAIR, index % PAIR)


def unit_params(params_ref, unit):
    return (params_ref[2 * unit : 2 * unit + 1, :], params_ref[2 * unit + 1 : 2 * unit + 2, :])


def copies_kernel(block_ref, out_hbm, sems):
    copies = [
        pltpu.make_async_copy(block_ref, out_hbm.at[pl.ds(i, 1)], sems.at[i]) for i in range(out_hbm.shape[0])
    ]
    for copy in copies:
        copy.start()
    for copy in copies:
        copy.wait()


def prepare_kernel(
    times_ref,
    labels_ref,
    table_any,
    own_any,
    other_any,
    time_weight_ref,
    mod_weight_ref,
    mod_weight_other_ref,
    mod_bias_ref,
    mod_bias_other_ref,
    gain_ref,
    gain_other_ref,
    weights_ref,
    params_ref,
    embedded_ref,
    table_ref,
    sems,
):
    core = lax.axis_index("segment") % PAIR
    pairs = [(table_any.at[pl.ds(labels_ref[i] // 8, 1)], table_ref.at[pl.ds(i, 1)]) for i in range(PAIR)]
    pairs += [(own_any, weights_ref.at[core]), (other_any, weights_ref.at[1 - core])]
    copies = [pltpu.make_async_copy(a, b, sems.at[i]) for i, (a, b) in enumerate(pairs)]
    for copy in copies:
        copy.start()
    rows = 16
    spot = lax.broadcasted_iota(jnp.int32, (rows, 1), 0)
    time = jnp.where(spot % 2 == 0, times_ref[0], times_ref[1]).astype(jnp.float32)
    base = time_weight_ref.shape[0]
    half = base // 2
    lanes = lax.broadcasted_iota(jnp.int32, (rows, base), 1)
    power = jnp.where(lanes < half, lanes, lanes - half).astype(jnp.float32)
    angles = time * jnp.exp(-math.log(10000.0) * power / half)
    sinusoid = jnp.where(lanes < half, jnp.cos(angles), jnp.sin(angles)).astype(jnp.bfloat16)

    def label_row(image):
        block = table_ref[image].astype(jnp.float32)
        row = lax.broadcasted_iota(jnp.int32, block.shape, 0)
        return column(jnp.where(row == labels_ref[image] % 8, block, 0.0))

    timed = jnp.dot(sinusoid, time_weight_ref[...], preferred_element_type=jnp.float32)
    for copy in copies[:PAIR]:
        copy.wait()
    timed = timed + jnp.where(spot % 2 == 0, label_row(0), label_row(1))
    embedded = (timed * sigmoid(timed)).astype(jnp.bfloat16)
    embedded_ref[...] = embedded
    channels = gain_ref.shape[1]

    def factor_and_shift(weight, bias, gain):
        modulation = jnp.dot(embedded, weight[...], preferred_element_type=jnp.float32) + bias[...]
        modulation = jnp.where(core == 0, modulation[0:1], modulation[1:2])
        return (gain[...] * (1.0 + modulation[:, :channels]), modulation[:, channels:])

    own = factor_and_shift(mod_weight_ref, mod_bias_ref, gain_ref)
    other = factor_and_shift(mod_weight_other_ref, mod_bias_other_ref, gain_other_ref)
    row = lax.broadcasted_iota(jnp.int32, params_ref.shape, 0)
    factor = jnp.where(row // 2 == core, own[0], other[0])
    shift = jnp.where(row // 2 == core, own[1], other[1])
    params_ref[...] = jnp.where(row % 2 == 0, factor, shift)
    for copy in copies[PAIR:]:
        copy.wait()


def forward_kernel(sh, active_stage, x_ref, params_ref, weights, middle_ref, out_ref, padded_ref):
    stage, _ = place_of()

    @pl.when(stage == active_stage)
    def _():
        clear_edges(sh, padded_ref)
        forward_unit(sh, x_ref, middle_ref, unit_params(params_ref, 0), padded_ref, weights, 0)
        forward_unit(sh, middle_ref, out_ref, unit_params(params_ref, 1), padded_ref, weights, 1)


def backward_kernel(sh, active_stage, first, *refs):
    if first:
        x_ref, up_ref, params_ref, weights = refs[:4]
        refs = refs[4:]
    else:
        x_ref, middle_ref, up_ref, params_ref, weights, keep_in, send_in = refs[:7]
        refs = refs[7:]
    keep_ref, send_ref, grad_ref = refs[:3]
    padded_ref, act_ref, slope_ref, pre_grad_ref, slab_ref, between_ref = refs[3:9]
    if first:
        middle_ref = refs[9]
    stage, core = place_of()

    @pl.when(stage == active_stage)
    def _():
        clear_edges(sh, padded_ref)
        params = [unit_params(params_ref, unit) for unit in range(PAIR)]
        if first:
            forward_unit(sh, x_ref, middle_ref, params[0], padded_ref, weights, 0)
        scratch = (padded_ref, act_ref, slope_ref, pre_grad_ref, slab_ref)
        backward_unit(
            sh, middle_ref, up_ref, between_ref, params[1], scratch, weights, 1, keep_ref, send_ref, core
        )
        backward_unit(
            sh, x_ref, between_ref, grad_ref, params[0], scratch, weights, 0, keep_ref, send_ref, core
        )

    if not first:

        @pl.when(stage != active_stage)
        def _():
            keep_ref[...] = keep_in[...]
            send_ref[...] = send_in[...]


def finish_kernel(sh, keep_ref, other_ref, embedded_ref, gain_ref, grads_ref, conv_ref, mod_ref):
    core = lax.axis_index("segment") % PAIR
    conv_ref[...] = keep_ref[0 : sh.slab, :] + other_ref[0 : sh.slab, :]
    rows = slice(sh.slab, sh.slab + sh.own_rows)
    grads_ref[pl.ds(core, 1)] = keep_ref[rows, :].astype(jnp.bfloat16)[None]
    grads_ref[pl.ds(1 - core, 1)] = other_ref[rows, :].astype(jnp.bfloat16)[None]
    base = sh.slab + sh.own_rows

    def mod_rows(ref):
        return jnp.concatenate([gain_ref[...] * ref[base + 1 : base + 2, :], ref[base : base + 1, :]], axis=1)

    own, other = mod_rows(keep_ref), mod_rows(other_ref)
    spot = lax.broadcasted_iota(jnp.int32, (16, own.shape[1]), 0)
    values = jnp.where(spot % 2 == core, own, other)
    high = values.astype(jnp.bfloat16).astype(jnp.float32)
    rest = values - high
    middle = rest.astype(jnp.bfloat16).astype(jnp.float32)
    low = rest - middle
    part = spot // 2
    pieces = jnp.where(part == 0, high, jnp.where(part == 1, middle, jnp.where(part == 2, low, 0.0)))
    mod_ref[...] = lax.dot_general(
        embedded_ref[...],
        pieces.astype(jnp.bfloat16),
        (((0,), (0,)), ((), ())),
        preferred_element_type=jnp.float32,
    )


def shards(
    x_in,
    out_cotangent,
    timesteps,
    labels,
    time_weight,
    label_table,
    conv_weight,
    mod_weight,
    mod_bias,
    norm_gain,
):
    segments, spaces = lax.axis_size("segment"), lax.axis_size("space")
    stages = segments // PAIR
    stage, core = place_of()
    images, row_count, cols, channels = x_in.shape
    sh = Shape(row_count * spaces, cols, channels, spaces)
    f32, bf16 = jnp.float32, jnp.bfloat16

    def call(body, ins, outs, scratch=(), limit=sh.limit, cost=None):
        return pl.pallas_call(
            body,
            out_shape=outs,
            in_specs=ins,
            out_specs=[VMEM] * len(outs),
            scratch_shapes=list(scratch),
            compiler_params=pltpu.CompilerParams(vmem_limit_bytes=limit),
            cost_estimate=cost,
        )

    shape = jax.ShapeDtypeStruct
    swap = [(i, i ^ 1) for i in range(segments)]
    weight = conv_weight.reshape(9 * channels, channels)
    ends = jnp.where(stage == 0, x_in, out_cotangent)
    near = lax.dynamic_index_in_dim(ends, core, 0, keepdims=False).reshape(1, sh.own_rows, channels)
    copies = pl.pallas_call(
        copies_kernel,
        out_shape=shape((spaces, sh.own_rows, channels), bf16),
        in_specs=[VMEM],
        out_specs=ANY,
        scratch_shapes=[pltpu.SemaphoreType.DMA((spaces,))],
        cost_estimate=pl.CostEstimate(flops=2 << 34, bytes_accessed=1 << 20, transcendentals=0),
    )(near)
    image = lax.all_to_all(copies, "space", 0, 0).reshape(sh.pixels, channels)
    own = (mod_weight[0], mod_bias, norm_gain, weight)
    theirs = [lax.ppermute(value, "segment", swap) for value in own]
    table = label_table.reshape(-1, 8, label_table.shape[1])
    width = time_weight.shape[1]
    mods = [value for pair in zip(own[:3], theirs[:3]) for value in pair]
    weights, params, embedded = call(
        prepare_kernel,
        [SMEM, SMEM] + [ANY] * 3 + [VMEM] * 7,
        [shape((PAIR, 9 * channels, channels), bf16), shape((8, channels), f32), shape((16, width), bf16)],
        [pltpu.VMEM((PAIR, 8, width), bf16), pltpu.SemaphoreType.DMA((2 * PAIR,))],
        cost=pl.CostEstimate(flops=1 << 24, bytes_accessed=4 << 20, transcendentals=0),
    )(timesteps, labels, table, weight, theirs[3], time_weight, *mods)

    image_shape = shape((sh.pixels, channels), bf16)
    pack_shape = shape((sh.pack, channels), f32)
    common = [pltpu.VMEM((3, sh.padded, channels), bf16)]

    def hop(value, source, target):
        pairs = [(PAIR * source + k, PAIR * target + k) for k in range(PAIR)]
        return lax.ppermute(value, "segment", pairs)

    entering, middles = [image], []
    for active in range(stages - 1):
        middle, out = call(
            functools.partial(forward_kernel, sh, active),
            [VMEM] * 3,
            [image_shape, image_shape],
            common,
        )(entering[active], params, weights)
        middles.append(middle)
        entering.append(hop(out, active, active + 1))

    scratch = common + [
        pltpu.VMEM((sh.pixels, channels), bf16),
        pltpu.VMEM((sh.pixels, channels), f32),
        pltpu.VMEM((sh.pixels, channels), f32),
        pltpu.VMEM((sh.taps * channels, channels), f32),
        pltpu.VMEM((sh.pixels, channels), bf16),
    ]
    outs = [pack_shape, pack_shape, image_shape]
    keep, send, grad = call(
        functools.partial(backward_kernel, sh, stages - 1, True),
        [VMEM] * 4,
        outs,
        scratch + [pltpu.VMEM((sh.pixels, channels), bf16)],
    )(entering[stages - 1], image, params, weights)
    for active in range(stages - 2, -1, -1):
        upstream = hop(grad[0] if isinstance(grad, list) else grad, active + 1, active)
        last = active == 0
        keep, send, *grad = call(
            functools.partial(backward_kernel, sh, active, False),
            [VMEM] * 7,
            outs[:2] if last else outs,
            scratch[-1:] + scratch if last else scratch,
        )(entering[active], middles[active], upstream, params, weights, keep, send)
    other = lax.ppermute(send, "segment", swap)
    grads, conv_grad, mod_grad = call(
        functools.partial(finish_kernel, sh),
        [VMEM] * 4,
        [
            shape((images, sh.own_rows, channels), bf16),
            shape((sh.slab, channels), f32),
            shape((time_weight.shape[1], 2 * channels), f32),
        ],
    )(keep, other, embedded, norm_gain)
    return (grads.reshape(1, images, row_count, cols, channels), conv_grad[None], mod_grad[None])


def solution(mesh):
    placed = (
        P(None, "space", None, None),
        P(None, "space", None, None),
        P(),
        P(),
        P(),
        P(),
        P("segment", None, None, None, None),
        P("segment", None, None),
        P("segment", None),
        P("segment", None),
    )
    return jax.shard_map(
        shards,
        mesh=mesh,
        in_specs=placed,
        out_specs=(
            P("segment", None, "space", None, None),
            P("segment", "space", None),
            P("segment", None, None),
        ),
        check_vma=False,
    )
```

```python
import functools
import math

import jax
import jax.numpy as jnp
from jax import lax
from jax.experimental import pallas as pl
from jax.experimental.pallas import tpu as pltpu
from jax.sharding import PartitionSpec as P

GROUPS = 32
EPSILON = 1e-05
PAIR = 2
PREPARE_LIMIT = 60 << 20
CHAIN_LIMIT = 48 << 20
VMEM = pl.BlockSpec(memory_space=pltpu.VMEM)
SMEM = pl.BlockSpec(memory_space=pltpu.SMEM)
ANY = pl.BlockSpec(memory_space=pl.ANY)


def sigmoid(values):
    return 1.0 / (1.0 + jnp.exp(-values))


def over_chunks(count, body):
    if count == 1:
        body(0)
    else:

        def step(i, carry):
            body(i)
            return carry

        lax.fori_loop(0, count, step, 0)


def chunk_start(i, size):
    return 0 if isinstance(i, int) else pl.multiple_of(i * size, size)


def fold_rows(values):
    return jnp.sum(values.reshape(values.shape[0] // 8, 8, values.shape[1]), axis=0)


def column(rows):
    return jnp.sum(rows, axis=0, keepdims=True)


def group_sums(rows, width):
    lanes = lax.broadcasted_iota(jnp.int32, rows.shape, 1)
    size = rows.shape[1]
    step = 1
    while step < width:
        ahead = pltpu.roll(rows, size - step, 1)
        behind = pltpu.roll(rows, step, 1)
        rows = rows + jnp.where((lanes & step) == 0, ahead, behind)
        step *= 2
    return rows


def stack_rows(first, second):
    spot = lax.broadcasted_iota(jnp.int32, (8, first.shape[1]), 0)
    return jnp.where(spot == 0, first, jnp.where(spot == 1, second, 0.0))


class Shape:
    def __init__(self, height, cols, channels, space_count):
        self.cols, self.channels = cols, channels
        self.pixels = height * cols
        self.chunk = cols * max(1, min(self.pixels, 256) // cols)
        self.chunks = self.pixels // self.chunk
        self.width = channels // GROUPS
        self.entries = float(self.pixels * self.width)
        self.padded = self.pixels + 2 * cols
        self.own_rows = height // space_count * cols
        self.slab = 9 * channels // space_count
        self.taps = min(9, (self.slab - 1) // channels + 2)
        self.pack = self.slab + self.own_rows + 8
        self.limit = (12 << 20) + self.pixels * channels * 40


def statistics(sh, x_ref):
    zero = jnp.zeros((8, sh.channels), jnp.float32)

    def add(i, sums):
        part = x_ref[pl.ds(chunk_start(i, sh.chunk), sh.chunk), :].astype(jnp.float32)
        return (sums[0] + fold_rows(part), sums[1] + fold_rows(part * part))

    if sh.chunks == 1:
        one, two = add(0, (zero, zero))
    else:
        one, two = lax.fori_loop(0, sh.chunks, add, (zero, zero))
    total = group_sums(stack_rows(column(one), column(two)), sh.width) / sh.entries
    mean = total[0:1]
    return (mean, lax.rsqrt(total[1:2] - mean * mean + EPSILON))


def clear_edges(sh, padded_ref):
    zero = jnp.zeros((3, sh.cols, sh.channels), padded_ref.dtype)
    padded_ref[:, 0 : sh.cols, :] = zero
    padded_ref[:, sh.pixels + sh.cols : sh.padded, :] = zero


def spread(sh, padded_ref, start, values):
    place = pl.ds(start + sh.cols, sh.chunk)
    spot = lax.broadcasted_iota(jnp.int32, values.shape, 0) % sh.cols
    padded_ref[0, place, :] = jnp.where(spot == 0, 0.0, pltpu.roll(values, 1, 0)).astype(jnp.bfloat16)
    padded_ref[1, place, :] = values.astype(jnp.bfloat16)
    padded_ref[2, place, :] = jnp.where(
        spot == sh.cols - 1, 0.0, pltpu.roll(values, sh.chunk - 1, 0)
    ).astype(jnp.bfloat16)


def convolve(sh, padded_ref, start, weight_ref, unit, backward):
    total = None
    for p in range(3):
        for q in range(3):
            row, col = (2 - p, 2 - q) if backward else (p, q)
            block = padded_ref[col, pl.ds(start + row * sh.cols, sh.chunk), :]
            tap = (3 * p + q) * sh.channels
            weight = weight_ref[unit, tap : tap + sh.channels, :]
            part = lax.dot_general(
                block,
                weight,
                (((1,), (1 if backward else 0,)), ((), ())),
                preferred_element_type=jnp.float32,
            )
            total = part if total is None else total + part
    return total


def forward_unit(sh, x_ref, out_ref, params, padded_ref, weight_ref, unit, fetch):
    factor, shift = params
    mean, inv_std = statistics(sh, x_ref)

    def activate(i):
        start = chunk_start(i, sh.chunk)
        normed = (x_ref[pl.ds(start, sh.chunk), :].astype(jnp.float32) - mean) * inv_std
        pre = normed * factor + shift
        spread(sh, padded_ref, start, pre * sigmoid(pre))

    def produce(i):
        start = chunk_start(i, sh.chunk)
        inputs = x_ref[pl.ds(start, sh.chunk), :].astype(jnp.float32)
        z = convolve(sh, padded_ref, start, weight_ref, unit, False)
        out_ref[pl.ds(start, sh.chunk), :] = (inputs + z).astype(jnp.bfloat16)

    over_chunks(sh.chunks, activate)
    fetch.ready(unit)
    over_chunks(sh.chunks, produce)


def backward_unit(sh, x_ref, up_ref, grad_ref, params, scratch, weight_ref, unit, keep_ref, send_ref, core, fetch):
    padded_ref, act_ref, slope_ref, pre_grad_ref, slab_ref = scratch
    factor, shift = params
    space = lax.axis_index("space")
    mean, inv_std = statistics(sh, x_ref)
    zero = jnp.zeros((8, sh.channels), jnp.float32)

    def activate(i):
        start = chunk_start(i, sh.chunk)
        rows = pl.ds(start, sh.chunk)
        spread(sh, padded_ref, start, up_ref[rows, :].astype(jnp.float32))
        pre = (x_ref[rows, :].astype(jnp.float32) - mean) * inv_std * factor + shift
        sigma = sigmoid(pre)
        act_ref[rows, :] = (pre * sigma).astype(jnp.bfloat16)
        slope_ref[rows, :] = sigma * (1.0 + pre * (1.0 - sigma))

    def differentiate(i, sums):
        start = chunk_start(i, sh.chunk)
        rows = pl.ds(start, sh.chunk)
        normed = (x_ref[rows, :].astype(jnp.float32) - mean) * inv_std
        pre_grad = convolve(sh, padded_ref, start, weight_ref, unit, True) * slope_ref[rows, :]
        pre_grad_ref[rows, :] = pre_grad
        return (sums[0] + fold_rows(pre_grad), sums[1] + fold_rows(pre_grad * normed))

    over_chunks(sh.chunks, activate)
    if fetch is not None:
        fetch.ready(unit)
    if sh.chunks == 1:
        sums = differentiate(0, (zero, zero))
    else:
        sums = lax.fori_loop(0, sh.chunks, differentiate, (zero, zero))
    sum_grad, sum_cross = column(sums[0]), column(sums[1])
    means = group_sums(stack_rows(factor * sum_grad, factor * sum_cross), sh.width) / sh.entries
    center, tilt = means[0:1], means[1:2]

    def finish(i):
        rows = pl.ds(chunk_start(i, sh.chunk), sh.chunk)
        normed = (x_ref[rows, :].astype(jnp.float32) - mean) * inv_std
        back = factor * pre_grad_ref[rows, :] - center - normed * tilt
        grad_ref[rows, :] = (up_ref[rows, :].astype(jnp.float32) + inv_std * back).astype(jnp.bfloat16)

    over_chunks(sh.chunks, finish)
    first_row = space * sh.slab
    first_tap = jnp.minimum(first_row // sh.channels, 9 - sh.taps)
    offset = pl.multiple_of(first_row - first_tap * sh.channels, 8)
    for t in range(sh.taps):
        tap = first_tap + t
        row, col = 2 - tap // 3, 2 - tap % 3
        place = pl.ds(t * sh.channels, sh.channels)

        def product(i):
            start = chunk_start(i, sh.chunk)
            block = padded_ref[col, pl.ds(pl.multiple_of(start + row * sh.cols, 16), sh.chunk), :]
            return lax.dot_general(
                act_ref[pl.ds(start, sh.chunk), :],
                block,
                (((0,), (0,)), ((), ())),
                preferred_element_type=jnp.float32,
            )

        if sh.chunks == 1:
            slab_ref[place, :] = product(0)
        else:
            slab_ref[place, :] = jnp.zeros((sh.channels, sh.channels), jnp.float32)

            def accumulate(i):
                slab_ref[place, :] += product(i)

            over_chunks(sh.chunks, accumulate)
    mine = slab_ref[pl.ds(offset, sh.slab), :]
    rows = grad_ref[pl.ds(pl.multiple_of(space * sh.own_rows, sh.own_rows), sh.own_rows), :]
    sums = stack_rows(sum_grad, sum_cross)

    def write(ref):
        ref[0 : sh.slab, :] = mine
        ref[sh.slab : sh.slab + sh.own_rows, :] = rows.astype(jnp.float32)
        ref[sh.slab + sh.own_rows : sh.pack, :] = sums

    @pl.when(core == unit)
    def _():
        write(keep_ref)

    @pl.when(core != unit)
    def _():
        write(send_ref)


def place_of():
    index = lax.axis_index("segment")
    return (index // PAIR, index % PAIR)


def sinusoid_of(time, base):
    half = base // 2
    lanes = lax.broadcasted_iota(jnp.int32, (time.shape[0], base), 1)
    power = jnp.where(lanes < half, lanes, lanes - half).astype(jnp.float32)
    angle = time * jnp.exp(-math.log(10000.0) * power / half)
    turns = jnp.floor(angle * (2.0 / math.pi) + 0.5)
    rest = ((angle - turns * 1.5703125) - turns * 4.83751296997e-4) - turns * 7.54978995489e-8
    square = rest * rest
    sine = rest + rest * square * (
        -1.6666654611e-1 + square * (8.3321608736e-3 - square * 1.9515295891e-4)
    )
    cosine = 1.0 - 0.5 * square + square * square * (
        4.166664568298827e-2 + square * (-1.388731625493765e-3 + square * 2.443315711809948e-5)
    )
    quarter = turns.astype(jnp.int32) + jnp.where(lanes < half, 1, 0)
    value = jnp.where(quarter % 2 == 1, cosine, sine)
    return jnp.where((quarter // 2) % 2 == 1, -value, value).astype(jnp.bfloat16)


def prepare_kernel(
    times_ref,
    labels_ref,
    x_hbm,
    cotangent_hbm,
    table_hbm,
    time_weight_hbm,
    mod_weight_hbm,
    bias_hbm,
    gain_hbm,
    out_hbm,
    keep_ref,
    send_ref,
    embedded_ref,
    block_ref,
    table_ref,
    time_weight_ref,
    mod_weight_ref,
    bias_ref,
    gain_ref,
    sems,
    out_sems,
):
    stage, core = place_of()

    @pl.when(stage == 0)
    def _():
        pltpu.make_async_copy(x_hbm.at[core], block_ref, sems.at[0]).start()

    @pl.when(stage != 0)
    def _():
        pltpu.make_async_copy(cotangent_hbm.at[core], block_ref, sems.at[0]).start()

    pairs = [(time_weight_hbm, time_weight_ref)]
    pairs += [(table_hbm.at[pl.ds(labels_ref[i] // 8, 1)], table_ref.at[pl.ds(i, 1)]) for i in range(PAIR)]
    pairs += [(mod_weight_hbm, mod_weight_ref), (bias_hbm, bias_ref), (gain_hbm, gain_ref)]
    copies = [pltpu.make_async_copy(a, b, sems.at[i + 1]) for i, (a, b) in enumerate(pairs)]
    for copy in copies:
        copy.start()
    spot = lax.broadcasted_iota(jnp.int32, (16, 1), 0)
    time = jnp.where(spot % 2 == 0, times_ref[0], times_ref[1]).astype(jnp.float32)
    sinusoid = sinusoid_of(time, time_weight_ref.shape[0])
    pltpu.make_async_copy(x_hbm.at[core], block_ref, sems.at[0]).wait()
    sends = [pltpu.make_async_copy(block_ref, out_hbm.at[i], out_sems.at[i]) for i in range(out_hbm.shape[0])]
    for send in sends:
        send.start()

    def label_row(image):
        block = table_ref[image].astype(jnp.float32)
        row = lax.broadcasted_iota(jnp.int32, block.shape, 0)
        return column(jnp.where(row == labels_ref[image] % 8, block, 0.0))

    copies[0].wait()
    timed = jnp.dot(sinusoid, time_weight_ref[...], preferred_element_type=jnp.float32)
    for copy in copies[1 : PAIR + 1]:
        copy.wait()
    timed = timed + jnp.where(spot % 2 == 0, label_row(0), label_row(1))
    embedded = (timed * sigmoid(timed)).astype(jnp.bfloat16)
    embedded_ref[...] = embedded
    for copy in copies[PAIR + 1 :]:
        copy.wait()
    modulation = jnp.dot(embedded, mod_weight_ref[...], preferred_element_type=jnp.float32) + bias_ref[...]
    channels = gain_ref.shape[1]
    factor = gain_ref[...] * (1.0 + modulation[:, :channels])
    shift = modulation[:, channels:]
    first = stack_rows(factor[0:1], shift[0:1])
    second = stack_rows(factor[1:2], shift[1:2])
    keep_ref[...] = jnp.where(core == 0, first, second)
    send_ref[...] = jnp.where(core == 0, second, first)
    for send in sends:
        send.wait()


def unit_params(mods_ref, unit):
    return (mods_ref[unit, 0:1, :], mods_ref[unit, 1:2, :])


class Fetch:
    def __init__(self, sources, weights_ref, mods_ref, sems):
        core = lax.axis_index("segment") % PAIR
        self.targets = (mods_ref, weights_ref)
        self.sources, self.sems = sources, sems
        for kind in range(2):
            for spot, source in zip((core, 1 - core), sources[kind]):
                self.copy(kind, spot, source).start()

    def copy(self, kind, spot, source):
        return pltpu.make_async_copy(source, self.targets[kind].at[spot], self.sems.at[kind, spot])

    def params(self):
        for unit in range(PAIR):
            self.copy(0, unit, self.sources[0][0]).wait()
        return [unit_params(self.targets[0], unit) for unit in range(PAIR)]

    def ready(self, unit):
        self.copy(1, unit, self.sources[1][0]).wait()


def forward_kernel(sh, active_stage, x_ref, *refs):
    mods, units = refs[0:2], refs[2:4]
    middle_ref, out_ref, padded_ref, weights, mods_ref, sems = refs[4:]
    stage, _ = place_of()

    @pl.when(stage == active_stage)
    def _():
        fetch = Fetch((mods, units), weights, mods_ref, sems)
        clear_edges(sh, padded_ref)
        params = fetch.params()
        forward_unit(sh, x_ref, middle_ref, params[0], padded_ref, weights, 0, fetch)
        forward_unit(sh, middle_ref, out_ref, params[1], padded_ref, weights, 1, fetch)


def backward_kernel(sh, active_stage, first, *refs):
    if first:
        x_ref, up_ref = refs[:2]
        refs = refs[2:]
    else:
        x_ref, middle_ref, up_ref = refs[:3]
        refs = refs[3:]
    mods, units = refs[0:2], refs[2:4]
    refs = refs[4:]
    if not first:
        refs = refs[2:]
    keep_ref, send_ref, grad_ref = refs[:3]
    padded_ref, weights, mods_ref, sems, act_ref, slope_ref, pre_grad_ref, slab_ref, between_ref = refs[3:12]
    if first:
        middle_ref = refs[12]
    stage, core = place_of()

    @pl.when(stage == active_stage)
    def _():
        fetch = Fetch((mods, units), weights, mods_ref, sems)
        clear_edges(sh, padded_ref)
        params = fetch.params()
        if first:
            forward_unit(sh, x_ref, middle_ref, params[0], padded_ref, weights, 0, fetch)
        scratch = (padded_ref, act_ref, slope_ref, pre_grad_ref, slab_ref)
        backward_unit(
            sh, middle_ref, up_ref, between_ref, params[1], scratch, weights, 1, keep_ref, send_ref, core, fetch
        )
        backward_unit(
            sh,
            x_ref,
            between_ref,
            grad_ref,
            params[0],
            scratch,
            weights,
            0,
            keep_ref,
            send_ref,
            core,
            None if first else fetch,
        )


def finish_kernel(sh, keep_ref, other_ref, embedded_ref, gain_ref, grads_ref, conv_ref, mod_ref):
    core = lax.axis_index("segment") % PAIR
    conv_ref[...] = keep_ref[0 : sh.slab, :] + other_ref[0 : sh.slab, :]
    rows = slice(sh.slab, sh.slab + sh.own_rows)
    grads_ref[pl.ds(core, 1)] = keep_ref[rows, :].astype(jnp.bfloat16)[None]
    grads_ref[pl.ds(1 - core, 1)] = other_ref[rows, :].astype(jnp.bfloat16)[None]
    base = sh.slab + sh.own_rows

    def mod_rows(ref):
        return jnp.concatenate([gain_ref[...] * ref[base + 1 : base + 2, :], ref[base : base + 1, :]], axis=1)

    own, other = mod_rows(keep_ref), mod_rows(other_ref)
    spot = lax.broadcasted_iota(jnp.int32, (16, own.shape[1]), 0)
    values = jnp.where(spot % 2 == core, own, other)
    high = values.astype(jnp.bfloat16).astype(jnp.float32)
    rest = values - high
    middle = rest.astype(jnp.bfloat16).astype(jnp.float32)
    low = rest - middle
    part = spot // 2
    pieces = jnp.where(part == 0, high, jnp.where(part == 1, middle, jnp.where(part == 2, low, 0.0)))
    mod_ref[...] = lax.dot_general(
        embedded_ref[...],
        pieces.astype(jnp.bfloat16),
        (((0,), (0,)), ((), ())),
        preferred_element_type=jnp.float32,
    )


def shards(
    x_in,
    out_cotangent,
    timesteps,
    labels,
    time_weight,
    label_table,
    conv_weight,
    mod_weight,
    mod_bias,
    norm_gain,
):
    segments, spaces = lax.axis_size("segment"), lax.axis_size("space")
    stages = segments // PAIR
    images, row_count, cols, channels = x_in.shape
    sh = Shape(row_count * spaces, cols, channels, spaces)
    f32, bf16 = jnp.float32, jnp.bfloat16

    def call(body, ins, outs, scratch=(), limit=sh.limit, out_specs=None, aliases={}):
        return pl.pallas_call(
            body,
            out_shape=outs,
            in_specs=ins,
            out_specs=out_specs or [VMEM] * len(outs),
            scratch_shapes=list(scratch),
            input_output_aliases=aliases,
            compiler_params=pltpu.CompilerParams(vmem_limit_bytes=limit),
        )

    shape = jax.ShapeDtypeStruct
    swap = [(i, i ^ 1) for i in range(segments)]
    weight = conv_weight.reshape(9 * channels, channels)
    other_weight = lax.ppermute(weight, "segment", swap)
    rows = (images, sh.own_rows, channels)
    table = label_table.reshape(-1, 8, label_table.shape[1])
    width = time_weight.shape[1]
    params_shape = shape((8, channels), f32)
    operands = (time_weight, mod_weight[0], mod_bias, norm_gain)
    copies, mod_keep, mod_send, embedded = call(
        prepare_kernel,
        [SMEM, SMEM] + [ANY] * 7,
        [shape((spaces, *rows[1:]), bf16), params_shape, params_shape, shape((16, width), bf16)],
        [pltpu.VMEM(rows[1:], bf16), pltpu.VMEM((PAIR, 8, width), bf16)]
        + [pltpu.VMEM(value.shape, value.dtype) for value in operands]
        + [pltpu.SemaphoreType.DMA((PAIR + 5,)), pltpu.SemaphoreType.DMA((spaces,))],
        PREPARE_LIMIT,
        [ANY] + [VMEM] * 3,
    )(timesteps, labels, x_in.reshape(rows), out_cotangent.reshape(rows), table, *operands)
    mod_other = lax.ppermute(mod_send, "segment", swap)
    image = lax.all_to_all(copies, "space", 0, 0).reshape(sh.pixels, channels)
    units = (mod_keep, mod_other, weight, other_weight)

    image_shape = shape((sh.pixels, channels), bf16)
    pack_shape = shape((sh.pack, channels), f32)
    common = [
        pltpu.VMEM((3, sh.padded, channels), bf16),
        pltpu.VMEM((PAIR, 9 * channels, channels), bf16),
        pltpu.VMEM((PAIR, 8, channels), f32),
        pltpu.SemaphoreType.DMA((2, PAIR)),
    ]

    def hop(value, source, target):
        pairs = [(PAIR * source + k, PAIR * target + k) for k in range(PAIR)]
        return lax.ppermute(value, "segment", pairs)

    entering, middles = [image], []
    for active in range(stages - 1):
        middle, out = call(
            functools.partial(forward_kernel, sh, active),
            [VMEM] + [ANY] * 4,
            [image_shape, image_shape],
            common,
            CHAIN_LIMIT,
        )(entering[active], *units)
        middles.append(middle)
        entering.append(hop(out, active, active + 1))

    scratch = common + [
        pltpu.VMEM((sh.pixels, channels), bf16),
        pltpu.VMEM((sh.pixels, channels), f32),
        pltpu.VMEM((sh.pixels, channels), f32),
        pltpu.VMEM((sh.taps * channels, channels), f32),
        pltpu.VMEM((sh.pixels, channels), bf16),
    ]
    outs = [pack_shape, pack_shape, image_shape]
    keep, send, grad = call(
        functools.partial(backward_kernel, sh, stages - 1, True),
        [VMEM] * 2 + [ANY] * 4,
        outs,
        scratch + [pltpu.VMEM((sh.pixels, channels), bf16)],
        CHAIN_LIMIT,
    )(entering[stages - 1], image, *units)
    for active in range(stages - 2, -1, -1):
        upstream = hop(grad[0] if isinstance(grad, list) else grad, active + 1, active)
        last = active == 0
        keep, send, *grad = call(
            functools.partial(backward_kernel, sh, active, False),
            [VMEM] * 3 + [ANY] * 4 + [VMEM] * 2,
            outs[:2] if last else outs,
            scratch[-1:] + scratch if last else scratch,
            CHAIN_LIMIT,
            aliases={7: 0, 8: 1},
        )(entering[active], middles[active], upstream, *units, keep, send)
    other = lax.ppermute(send, "segment", swap)
    grads, conv_grad, mod_grad = call(
        functools.partial(finish_kernel, sh),
        [VMEM] * 4,
        [
            shape((images, sh.own_rows, channels), bf16),
            shape((sh.slab, channels), f32),
            shape((time_weight.shape[1], 2 * channels), f32),
        ],
    )(keep, other, embedded, norm_gain)
    return (grads.reshape(1, images, row_count, cols, channels), conv_grad[None], mod_grad[None])


def solution(mesh):
    placed = (
        P(None, "space", None, None),
        P(None, "space", None, None),
        P(),
        P(),
        P(),
        P(),
        P("segment", None, None, None, None),
        P("segment", None, None),
        P("segment", None),
        P("segment", None),
    )
    return jax.shard_map(
        shards,
        mesh=mesh,
        in_specs=placed,
        out_specs=(
            P("segment", None, "space", None, None),
            P("segment", "space", None),
            P("segment", None, None),
        ),
        check_vma=False,
    )
```

```python
import functools
import math

import jax
import jax.numpy as jnp
from jax import lax
from jax.experimental import pallas as pl
from jax.experimental.pallas import tpu as pltpu
from jax.sharding import PartitionSpec as P

GROUPS = 32
EPSILON = 1e-05
PAIR = 2
PREPARE_LIMIT = 60 << 20
CHAIN_LIMIT = 48 << 20
VMEM = pl.BlockSpec(memory_space=pltpu.VMEM)
SMEM = pl.BlockSpec(memory_space=pltpu.SMEM)
ANY = pl.BlockSpec(memory_space=pl.ANY)


def sigmoid(values):
    return 1.0 / (1.0 + jnp.exp(-values))


def over_chunks(count, body):
    if count == 1:
        body(0)
    else:

        def step(i, carry):
            body(i)
            return carry

        lax.fori_loop(0, count, step, 0)


def chunk_start(i, size):
    return 0 if isinstance(i, int) else pl.multiple_of(i * size, size)


def fold_rows(values):
    return jnp.sum(values.reshape(values.shape[0] // 8, 8, values.shape[1]), axis=0)


def column(rows):
    return jnp.sum(rows, axis=0, keepdims=True)


def group_sums(rows, width):
    lanes = lax.broadcasted_iota(jnp.int32, rows.shape, 1)
    size = rows.shape[1]
    step = 1
    while step < width:
        ahead = pltpu.roll(rows, size - step, 1)
        behind = pltpu.roll(rows, step, 1)
        rows = rows + jnp.where((lanes & step) == 0, ahead, behind)
        step *= 2
    return rows


def stack_rows(first, second):
    spot = lax.broadcasted_iota(jnp.int32, (8, first.shape[1]), 0)
    return jnp.where(spot == 0, first, jnp.where(spot == 1, second, 0.0))


class Shape:
    def __init__(self, height, cols, channels, space_count):
        self.cols, self.channels = cols, channels
        self.pixels = height * cols
        self.chunk = cols * max(1, min(self.pixels, 256) // cols)
        self.chunks = self.pixels // self.chunk
        self.width = channels // GROUPS
        self.entries = float(self.pixels * self.width)
        self.padded = self.pixels + 2 * cols
        self.own_rows = height // space_count * cols
        self.slab = 9 * channels // space_count
        self.taps = min(9, (self.slab - 1) // channels + 2)
        self.pack = self.slab + self.own_rows + 8
        self.limit = (12 << 20) + self.pixels * channels * 40


def statistics(sh, x_ref):
    zero = jnp.zeros((8, sh.channels), jnp.float32)

    def add(i, sums):
        part = x_ref[pl.ds(chunk_start(i, sh.chunk), sh.chunk), :].astype(jnp.float32)
        return (sums[0] + fold_rows(part), sums[1] + fold_rows(part * part))

    if sh.chunks == 1:
        one, two = add(0, (zero, zero))
    else:
        one, two = lax.fori_loop(0, sh.chunks, add, (zero, zero))
    total = group_sums(stack_rows(column(one), column(two)), sh.width) / sh.entries
    mean = total[0:1]
    return (mean, lax.rsqrt(total[1:2] - mean * mean + EPSILON))


def clear_edges(sh, padded_ref):
    zero = jnp.zeros((3, sh.cols, sh.channels), padded_ref.dtype)
    padded_ref[:, 0 : sh.cols, :] = zero
    padded_ref[:, sh.pixels + sh.cols : sh.padded, :] = zero


def spread(sh, padded_ref, start, values):
    place = pl.ds(start + sh.cols, sh.chunk)
    spot = lax.broadcasted_iota(jnp.int32, values.shape, 0) % sh.cols
    padded_ref[0, place, :] = jnp.where(spot == 0, 0.0, pltpu.roll(values, 1, 0)).astype(jnp.bfloat16)
    padded_ref[1, place, :] = values.astype(jnp.bfloat16)
    padded_ref[2, place, :] = jnp.where(
        spot == sh.cols - 1, 0.0, pltpu.roll(values, sh.chunk - 1, 0)
    ).astype(jnp.bfloat16)


def convolve(sh, padded_ref, start, weight_ref, unit, backward):
    total = None
    for p in range(3):
        for q in range(3):
            row, col = (2 - p, 2 - q) if backward else (p, q)
            block = padded_ref[col, pl.ds(start + row * sh.cols, sh.chunk), :]
            tap = (3 * p + q) * sh.channels
            weight = weight_ref[unit, tap : tap + sh.channels, :]
            part = lax.dot_general(
                block,
                weight,
                (((1,), (1 if backward else 0,)), ((), ())),
                preferred_element_type=jnp.float32,
            )
            total = part if total is None else total + part
    return total


def forward_unit(sh, x_ref, out_ref, params, padded_ref, weight_ref, unit):
    factor, shift = params
    mean, inv_std = statistics(sh, x_ref)

    def activate(i):
        start = chunk_start(i, sh.chunk)
        normed = (x_ref[pl.ds(start, sh.chunk), :].astype(jnp.float32) - mean) * inv_std
        pre = normed * factor + shift
        spread(sh, padded_ref, start, pre * sigmoid(pre))

    def produce(i):
        start = chunk_start(i, sh.chunk)
        inputs = x_ref[pl.ds(start, sh.chunk), :].astype(jnp.float32)
        z = convolve(sh, padded_ref, start, weight_ref, unit, False)
        out_ref[pl.ds(start, sh.chunk), :] = (inputs + z).astype(jnp.bfloat16)

    over_chunks(sh.chunks, activate)
    over_chunks(sh.chunks, produce)


def backward_unit(sh, x_ref, up_ref, grad_ref, params, scratch, weight_ref, unit, keep_ref, send_ref, core):
    padded_ref, act_ref, slope_ref, pre_grad_ref, slab_ref = scratch
    factor, shift = params
    space = lax.axis_index("space")
    mean, inv_std = statistics(sh, x_ref)
    zero = jnp.zeros((8, sh.channels), jnp.float32)

    def activate(i):
        start = chunk_start(i, sh.chunk)
        rows = pl.ds(start, sh.chunk)
        spread(sh, padded_ref, start, up_ref[rows, :].astype(jnp.float32))
        pre = (x_ref[rows, :].astype(jnp.float32) - mean) * inv_std * factor + shift
        sigma = sigmoid(pre)
        act_ref[rows, :] = (pre * sigma).astype(jnp.bfloat16)
        slope_ref[rows, :] = sigma * (1.0 + pre * (1.0 - sigma))

    def differentiate(i, sums):
        start = chunk_start(i, sh.chunk)
        rows = pl.ds(start, sh.chunk)
        normed = (x_ref[rows, :].astype(jnp.float32) - mean) * inv_std
        pre_grad = convolve(sh, padded_ref, start, weight_ref, unit, True) * slope_ref[rows, :]
        pre_grad_ref[rows, :] = pre_grad
        return (sums[0] + fold_rows(pre_grad), sums[1] + fold_rows(pre_grad * normed))

    over_chunks(sh.chunks, activate)
    if sh.chunks == 1:
        sums = differentiate(0, (zero, zero))
    else:
        sums = lax.fori_loop(0, sh.chunks, differentiate, (zero, zero))
    sum_grad, sum_cross = column(sums[0]), column(sums[1])
    means = group_sums(stack_rows(factor * sum_grad, factor * sum_cross), sh.width) / sh.entries
    center, tilt = means[0:1], means[1:2]

    def finish(i):
        rows = pl.ds(chunk_start(i, sh.chunk), sh.chunk)
        normed = (x_ref[rows, :].astype(jnp.float32) - mean) * inv_std
        back = factor * pre_grad_ref[rows, :] - center - normed * tilt
        grad_ref[rows, :] = (up_ref[rows, :].astype(jnp.float32) + inv_std * back).astype(jnp.bfloat16)

    over_chunks(sh.chunks, finish)
    first_row = space * sh.slab
    first_tap = jnp.minimum(first_row // sh.channels, 9 - sh.taps)
    offset = pl.multiple_of(first_row - first_tap * sh.channels, 8)
    for t in range(sh.taps):
        tap = first_tap + t
        row, col = 2 - tap // 3, 2 - tap % 3
        place = pl.ds(t * sh.channels, sh.channels)

        def product(i):
            start = chunk_start(i, sh.chunk)
            block = padded_ref[col, pl.ds(pl.multiple_of(start + row * sh.cols, 16), sh.chunk), :]
            return lax.dot_general(
                act_ref[pl.ds(start, sh.chunk), :],
                block,
                (((0,), (0,)), ((), ())),
                preferred_element_type=jnp.float32,
            )

        if sh.chunks == 1:
            slab_ref[place, :] = product(0)
        else:
            slab_ref[place, :] = jnp.zeros((sh.channels, sh.channels), jnp.float32)

            def accumulate(i):
                slab_ref[place, :] += product(i)

            over_chunks(sh.chunks, accumulate)
    mine = slab_ref[pl.ds(offset, sh.slab), :]
    rows = grad_ref[pl.ds(pl.multiple_of(space * sh.own_rows, sh.own_rows), sh.own_rows), :]
    sums = stack_rows(sum_grad, sum_cross)

    def write(ref):
        ref[0 : sh.slab, :] = mine
        ref[sh.slab : sh.slab + sh.own_rows, :] = rows.astype(jnp.float32)
        ref[sh.slab + sh.own_rows : sh.pack, :] = sums

    @pl.when(core == unit)
    def _():
        write(keep_ref)

    @pl.when(core != unit)
    def _():
        write(send_ref)


def place_of():
    index = lax.axis_index("segment")
    return (index // PAIR, index % PAIR)


def unit_params(params_ref, unit):
    return (params_ref[2 * unit : 2 * unit + 1, :], params_ref[2 * unit + 1 : 2 * unit + 2, :])


def sinusoid_of(time, base):
    half = base // 2
    lanes = lax.broadcasted_iota(jnp.int32, (time.shape[0], base), 1)
    power = jnp.where(lanes < half, lanes, lanes - half).astype(jnp.float32)
    angle = time * jnp.exp(-math.log(10000.0) * power / half)
    turns = jnp.floor(angle * (2.0 / math.pi) + 0.5)
    rest = ((angle - turns * 1.5703125) - turns * 4.83751296997e-4) - turns * 7.54978995489e-8
    square = rest * rest
    sine = rest + rest * square * (
        -1.6666654611e-1 + square * (8.3321608736e-3 - square * 1.9515295891e-4)
    )
    cosine = 1.0 - 0.5 * square + square * square * (
        4.166664568298827e-2 + square * (-1.388731625493765e-3 + square * 2.443315711809948e-5)
    )
    quarter = turns.astype(jnp.int32) + jnp.where(lanes < half, 1, 0)
    value = jnp.where(quarter % 2 == 1, cosine, sine)
    return jnp.where((quarter // 2) % 2 == 1, -value, value).astype(jnp.bfloat16)


def start_all(pairs, sems):
    copies = [pltpu.make_async_copy(a, b, sems.at[i]) for i, (a, b) in enumerate(pairs)]
    for copy in copies:
        copy.start()
    return copies


def embed_kernel(times_ref, labels_ref, table_hbm, time_weight_hbm, embedded_ref, table_ref, time_weight_ref, sems):
    pairs = [(time_weight_hbm, time_weight_ref)]
    pairs += [(table_hbm.at[pl.ds(labels_ref[i] // 8, 1)], table_ref.at[pl.ds(i, 1)]) for i in range(PAIR)]
    copies = start_all(pairs, sems)
    spot = lax.broadcasted_iota(jnp.int32, (16, 1), 0)
    time = jnp.where(spot % 2 == 0, times_ref[0], times_ref[1]).astype(jnp.float32)
    sinusoid = sinusoid_of(time, time_weight_ref.shape[0])

    def label_row(image):
        block = table_ref[image].astype(jnp.float32)
        row = lax.broadcasted_iota(jnp.int32, block.shape, 0)
        return column(jnp.where(row == labels_ref[image] % 8, block, 0.0))

    for copy in copies:
        copy.wait()
    timed = jnp.dot(sinusoid, time_weight_ref[...], preferred_element_type=jnp.float32)
    timed = timed + jnp.where(spot % 2 == 0, label_row(0), label_row(1))
    embedded_ref[...] = (timed * sigmoid(timed)).astype(jnp.bfloat16)


def modulate_kernel(embedded_hbm, mod_weight_hbm, bias_hbm, gain_hbm, keep_ref, send_ref, *scratch):
    embedded_ref, mod_weight_ref, bias_ref, gain_ref, sems = scratch
    core = lax.axis_index("segment") % PAIR
    copies = start_all(zip((embedded_hbm, mod_weight_hbm, bias_hbm, gain_hbm), scratch[:4]), sems)
    for copy in copies:
        copy.wait()
    modulation = jnp.dot(embedded_ref[...], mod_weight_ref[...], preferred_element_type=jnp.float32) + bias_ref[...]
    channels = gain_ref.shape[1]
    factor = gain_ref[...] * (1.0 + modulation[:, :channels])
    shift = modulation[:, channels:]
    first = stack_rows(factor[0:1], shift[0:1])
    second = stack_rows(factor[1:2], shift[1:2])
    keep_ref[...] = jnp.where(core == 0, first, second)
    send_ref[...] = jnp.where(core == 0, second, first)


def layout_kernel(own_any, other_any, mod_keep_any, mod_other_any, weights_ref, params_ref, mods_ref, sems):
    core = lax.axis_index("segment") % PAIR
    pairs = [(mod_keep_any, mods_ref.at[core]), (mod_other_any, mods_ref.at[1 - core])]
    pairs += [(own_any, weights_ref.at[core]), (other_any, weights_ref.at[1 - core])]
    copies = start_all(pairs, sems)
    for copy in copies[:PAIR]:
        copy.wait()
    params_ref[0:2, :] = mods_ref[0, 0:2, :]
    params_ref[2:4, :] = mods_ref[1, 0:2, :]
    params_ref[4:8, :] = jnp.zeros((4, params_ref.shape[1]), jnp.float32)
    for copy in copies[PAIR:]:
        copy.wait()


def assemble(sh, blocks_ref, order, image_ref):
    space = lax.axis_index("space")
    for k, bits in enumerate(order):
        start = pl.multiple_of((space ^ bits) * sh.own_rows, sh.own_rows)
        image_ref[pl.ds(start, sh.own_rows), :] = blocks_ref[k]


def forward_kernel(sh, active_stage, orders, *refs):
    if orders:
        near_ref, far_ref, params_ref, weights, x_ref = refs[:5]
        assemble(sh, near_ref, orders[0], x_ref)
        assemble(sh, far_ref, orders[1], x_ref)
        refs = refs[5:]
    else:
        x_ref, params_ref, weights = refs[:3]
        refs = refs[3:]
    middle_ref, out_ref, padded_ref = refs
    stage, _ = place_of()

    @pl.when(stage == active_stage)
    def _():
        clear_edges(sh, padded_ref)
        forward_unit(sh, x_ref, middle_ref, unit_params(params_ref, 0), padded_ref, weights, 0)
        forward_unit(sh, middle_ref, out_ref, unit_params(params_ref, 1), padded_ref, weights, 1)


def backward_kernel(sh, active_stage, first, *refs):
    if first:
        x_ref, up_ref, params_ref, weights = refs[:4]
        refs = refs[4:]
    else:
        x_ref, middle_ref, up_ref, params_ref, weights = refs[:5]
        refs = refs[7:]
    keep_ref, send_ref, grad_ref = refs[:3]
    padded_ref, act_ref, slope_ref, pre_grad_ref, slab_ref, between_ref = refs[3:9]
    if first:
        middle_ref = refs[9]
    stage, core = place_of()

    @pl.when(stage == active_stage)
    def _():
        clear_edges(sh, padded_ref)
        params = [unit_params(params_ref, unit) for unit in range(PAIR)]
        if first:
            forward_unit(sh, x_ref, middle_ref, params[0], padded_ref, weights, 0)
        scratch = (padded_ref, act_ref, slope_ref, pre_grad_ref, slab_ref)
        backward_unit(
            sh, middle_ref, up_ref, between_ref, params[1], scratch, weights, 1, keep_ref, send_ref, core
        )
        backward_unit(
            sh, x_ref, between_ref, grad_ref, params[0], scratch, weights, 0, keep_ref, send_ref, core
        )


def finish_kernel(sh, keep_ref, other_ref, embedded_ref, gain_ref, grads_ref, conv_ref, mod_ref):
    core = lax.axis_index("segment") % PAIR
    conv_ref[...] = keep_ref[0 : sh.slab, :] + other_ref[0 : sh.slab, :]
    rows = slice(sh.slab, sh.slab + sh.own_rows)
    grads_ref[pl.ds(core, 1)] = keep_ref[rows, :].astype(jnp.bfloat16)[None]
    grads_ref[pl.ds(1 - core, 1)] = other_ref[rows, :].astype(jnp.bfloat16)[None]
    base = sh.slab + sh.own_rows

    def mod_rows(ref):
        return jnp.concatenate([gain_ref[...] * ref[base + 1 : base + 2, :], ref[base : base + 1, :]], axis=1)

    own, other = mod_rows(keep_ref), mod_rows(other_ref)
    spot = lax.broadcasted_iota(jnp.int32, (16, own.shape[1]), 0)
    values = jnp.where(spot % 2 == core, own, other)
    high = values.astype(jnp.bfloat16).astype(jnp.float32)
    rest = values - high
    middle = rest.astype(jnp.bfloat16).astype(jnp.float32)
    low = rest - middle
    part = spot // 2
    pieces = jnp.where(part == 0, high, jnp.where(part == 1, middle, jnp.where(part == 2, low, 0.0)))
    mod_ref[...] = lax.dot_general(
        embedded_ref[...],
        pieces.astype(jnp.bfloat16),
        (((0,), (0,)), ((), ())),
        preferred_element_type=jnp.float32,
    )


def shards(
    x_in,
    out_cotangent,
    timesteps,
    labels,
    time_weight,
    label_table,
    conv_weight,
    mod_weight,
    mod_bias,
    norm_gain,
):
    segments, spaces = lax.axis_size("segment"), lax.axis_size("space")
    stages = segments // PAIR
    stage, core = place_of()
    images, row_count, cols, channels = x_in.shape
    sh = Shape(row_count * spaces, cols, channels, spaces)
    f32, bf16 = jnp.float32, jnp.bfloat16

    def call(body, ins, outs, scratch=(), limit=CHAIN_LIMIT, cost=None, aliases={}):
        return pl.pallas_call(
            body,
            out_shape=outs,
            in_specs=ins,
            out_specs=[VMEM] * len(outs),
            scratch_shapes=list(scratch),
            input_output_aliases=aliases,
            compiler_params=pltpu.CompilerParams(vmem_limit_bytes=limit),
            cost_estimate=cost,
        )

    shape = jax.ShapeDtypeStruct
    swap = [(i, i ^ 1) for i in range(segments)]
    weight = conv_weight.reshape(9 * channels, channels)
    other_weight = lax.ppermute(weight, "segment", swap)
    ends = jnp.where(stage == 0, x_in, out_cotangent)
    near = lax.dynamic_index_in_dim(ends, core, 0, keepdims=False).reshape(1, sh.own_rows, channels)
    table = label_table.reshape(-1, 8, label_table.shape[1])
    width = time_weight.shape[1]
    some = pl.CostEstimate(flops=1 << 20, bytes_accessed=4 << 20, transcendentals=0)
    order, bit = [0], spaces // 2
    waiting = []
    while True:
        far = lax.ppermute(near, "space", [(i, i ^ bit) for i in range(spaces)])
        if not waiting:
            (embedded,) = call(
                embed_kernel,
                [SMEM, SMEM, ANY, ANY],
                [shape((16, width), bf16)],
                [
                    pltpu.VMEM((PAIR, 8, width), bf16),
                    pltpu.VMEM(time_weight.shape, bf16),
                    pltpu.SemaphoreType.DMA((PAIR + 1,)),
                ],
                PREPARE_LIMIT,
                some,
            )(timesteps, labels, table, time_weight)
            waiting = [embedded]
            far, embedded = lax.optimization_barrier((far, embedded))
        elif len(waiting) == 1:
            operands = (embedded, mod_weight[0], mod_bias, norm_gain)
            mod_keep, mod_send = call(
                modulate_kernel,
                [ANY] * 4,
                [shape((8, channels), f32)] * 2,
                [pltpu.VMEM(value.shape, value.dtype) for value in operands] + [pltpu.SemaphoreType.DMA((4,))],
                PREPARE_LIMIT,
                some,
            )(*operands)
            waiting.append(mod_keep)
            far, mod_keep, mod_send = lax.optimization_barrier((far, mod_keep, mod_send))
        far_order = [k ^ bit for k in order]
        if bit == 1:
            break
        near = jnp.concatenate([near, far])
        order, bit = order + far_order, bit // 2
    mod_other = lax.ppermute(mod_send, "segment", swap)
    weights, params = call(
        layout_kernel,
        [ANY] * 4,
        [shape((PAIR, 9 * channels, channels), bf16), shape((8, channels), f32)],
        [pltpu.VMEM((PAIR, 8, channels), f32), pltpu.SemaphoreType.DMA((2 * PAIR,))],
        cost=some,
    )(weight, other_weight, mod_keep, mod_other)

    image_shape = shape((sh.pixels, channels), bf16)
    pack_shape = shape((sh.pack, channels), f32)
    common = [pltpu.VMEM((3, sh.padded, channels), bf16)]

    def hop(value, source, target):
        pairs = [(PAIR * source + k, PAIR * target + k) for k in range(PAIR)]
        return lax.ppermute(value, "segment", pairs)

    image, middle, out = call(
        functools.partial(forward_kernel, sh, 0, (order, far_order)),
        [VMEM] * 4,
        [image_shape] * 3,
        common,
    )(near, far, params, weights)
    entering, middles = [image, hop(out, 0, 1)], [middle]
    for active in range(1, stages - 1):
        middle, out = call(
            functools.partial(forward_kernel, sh, active, None),
            [VMEM] * 3,
            [image_shape, image_shape],
            common,
        )(entering[active], params, weights)
        middles.append(middle)
        entering.append(hop(out, active, active + 1))

    scratch = common + [
        pltpu.VMEM((sh.pixels, channels), bf16),
        pltpu.VMEM((sh.pixels, channels), f32),
        pltpu.VMEM((sh.pixels, channels), f32),
        pltpu.VMEM((sh.taps * channels, channels), f32),
        pltpu.VMEM((sh.pixels, channels), bf16),
    ]
    outs = [pack_shape, pack_shape, image_shape]
    keep, send, grad = call(
        functools.partial(backward_kernel, sh, stages - 1, True),
        [VMEM] * 4,
        outs,
        scratch + [pltpu.VMEM((sh.pixels, channels), bf16)],
    )(entering[stages - 1], image, params, weights)
    for active in range(stages - 2, -1, -1):
        upstream = hop(grad[0] if isinstance(grad, list) else grad, active + 1, active)
        last = active == 0
        keep, send, *grad = call(
            functools.partial(backward_kernel, sh, active, False),
            [VMEM] * 7,
            outs[:2] if last else outs,
            scratch[-1:] + scratch if last else scratch,
            aliases={5: 0, 6: 1},
        )(entering[active], middles[active], upstream, params, weights, keep, send)
    other = lax.ppermute(send, "segment", swap)
    grads, conv_grad, mod_grad = call(
        functools.partial(finish_kernel, sh),
        [VMEM] * 4,
        [
            shape((images, sh.own_rows, channels), bf16),
            shape((sh.slab, channels), f32),
            shape((time_weight.shape[1], 2 * channels), f32),
        ],
    )(keep, other, embedded, norm_gain)
    return (grads.reshape(1, images, row_count, cols, channels), conv_grad[None], mod_grad[None])


def solution(mesh):
    placed = (
        P(None, "space", None, None),
        P(None, "space", None, None),
        P(),
        P(),
        P(),
        P(),
        P("segment", None, None, None, None),
        P("segment", None, None),
        P("segment", None),
        P("segment", None),
    )
    return jax.shard_map(
        shards,
        mesh=mesh,
        in_specs=placed,
        out_specs=(
            P("segment", None, "space", None, None),
            P("segment", "space", None),
            P("segment", None, None),
        ),
        check_vma=False,
    )
```

```python
import functools
import math

import jax
import jax.numpy as jnp
from jax import lax
from jax.experimental import pallas as pl
from jax.experimental.pallas import tpu as pltpu
from jax.sharding import PartitionSpec as P

GROUPS = 32
EPSILON = 1e-05
PAIR = 2
PREPARE_LIMIT = 60 << 20
CHAIN_LIMIT = 48 << 20
VMEM = pl.BlockSpec(memory_space=pltpu.VMEM)
SMEM = pl.BlockSpec(memory_space=pltpu.SMEM)
ANY = pl.BlockSpec(memory_space=pl.ANY)


def sigmoid(values):
    return 1.0 / (1.0 + jnp.exp(-values))


def over_chunks(count, body):
    if count == 1:
        body(0)
    else:

        def step(i, carry):
            body(i)
            return carry

        lax.fori_loop(0, count, step, 0)


def chunk_start(i, size):
    return 0 if isinstance(i, int) else pl.multiple_of(i * size, size)


def fold_rows(values):
    return jnp.sum(values.reshape(values.shape[0] // 8, 8, values.shape[1]), axis=0)


def column(rows):
    return jnp.sum(rows, axis=0, keepdims=True)


def group_sums(rows, width):
    lanes = lax.broadcasted_iota(jnp.int32, rows.shape, 1)
    size = rows.shape[1]
    step = 1
    while step < width:
        ahead = pltpu.roll(rows, size - step, 1)
        behind = pltpu.roll(rows, step, 1)
        rows = rows + jnp.where((lanes & step) == 0, ahead, behind)
        step *= 2
    return rows


def stack_rows(first, second):
    spot = lax.broadcasted_iota(jnp.int32, (8, first.shape[1]), 0)
    return jnp.where(spot == 0, first, jnp.where(spot == 1, second, 0.0))


class Shape:
    def __init__(self, height, cols, channels, space_count):
        self.cols, self.channels = cols, channels
        self.pixels = height * cols
        self.chunk = cols * max(1, min(self.pixels, 256) // cols)
        self.chunks = self.pixels // self.chunk
        self.width = channels // GROUPS
        self.entries = float(self.pixels * self.width)
        self.padded = self.pixels + 2 * cols
        self.own_rows = height // space_count * cols
        self.slab = 9 * channels // space_count
        self.taps = min(9, (self.slab - 1) // channels + 2)
        self.pack = self.slab + self.own_rows + 8
        self.limit = (12 << 20) + self.pixels * channels * 40


def statistics(sh, x_ref):
    zero = jnp.zeros((8, sh.channels), jnp.float32)

    def add(i, sums):
        part = x_ref[pl.ds(chunk_start(i, sh.chunk), sh.chunk), :].astype(jnp.float32)
        return (sums[0] + fold_rows(part), sums[1] + fold_rows(part * part))

    if sh.chunks == 1:
        one, two = add(0, (zero, zero))
    else:
        one, two = lax.fori_loop(0, sh.chunks, add, (zero, zero))
    total = group_sums(stack_rows(column(one), column(two)), sh.width) / sh.entries
    mean = total[0:1]
    return (mean, lax.rsqrt(total[1:2] - mean * mean + EPSILON))


def clear_edges(sh, padded_ref):
    zero = jnp.zeros((3, sh.cols, sh.channels), padded_ref.dtype)
    padded_ref[:, 0 : sh.cols, :] = zero
    padded_ref[:, sh.pixels + sh.cols : sh.padded, :] = zero


def spread(sh, padded_ref, start, values):
    place = pl.ds(start + sh.cols, sh.chunk)
    spot = lax.broadcasted_iota(jnp.int32, values.shape, 0) % sh.cols
    padded_ref[0, place, :] = jnp.where(spot == 0, 0.0, pltpu.roll(values, 1, 0)).astype(jnp.bfloat16)
    padded_ref[1, place, :] = values.astype(jnp.bfloat16)
    padded_ref[2, place, :] = jnp.where(
        spot == sh.cols - 1, 0.0, pltpu.roll(values, sh.chunk - 1, 0)
    ).astype(jnp.bfloat16)


def convolve(sh, padded_ref, start, weight_ref, unit, backward):
    total = None
    for p in range(3):
        for q in range(3):
            row, col = (2 - p, 2 - q) if backward else (p, q)
            block = padded_ref[col, pl.ds(start + row * sh.cols, sh.chunk), :]
            tap = (3 * p + q) * sh.channels
            weight = weight_ref[unit, tap : tap + sh.channels, :]
            part = lax.dot_general(
                block,
                weight,
                (((1,), (1 if backward else 0,)), ((), ())),
                preferred_element_type=jnp.float32,
            )
            total = part if total is None else total + part
    return total


def forward_unit(sh, x_ref, out_ref, params, padded_ref, weight_ref, unit):
    factor, shift = params
    mean, inv_std = statistics(sh, x_ref)

    def activate(i):
        start = chunk_start(i, sh.chunk)
        normed = (x_ref[pl.ds(start, sh.chunk), :].astype(jnp.float32) - mean) * inv_std
        pre = normed * factor + shift
        spread(sh, padded_ref, start, pre * sigmoid(pre))

    def produce(i):
        start = chunk_start(i, sh.chunk)
        inputs = x_ref[pl.ds(start, sh.chunk), :].astype(jnp.float32)
        z = convolve(sh, padded_ref, start, weight_ref, unit, False)
        out_ref[pl.ds(start, sh.chunk), :] = (inputs + z).astype(jnp.bfloat16)

    over_chunks(sh.chunks, activate)
    over_chunks(sh.chunks, produce)


def backward_unit(sh, x_ref, up_ref, grad_ref, params, scratch, weight_ref, unit, keep_ref, send_ref, core):
    padded_ref, act_ref, slope_ref, pre_grad_ref, slab_ref = scratch
    factor, shift = params
    space = lax.axis_index("space")
    mean, inv_std = statistics(sh, x_ref)
    zero = jnp.zeros((8, sh.channels), jnp.float32)

    def activate(i):
        start = chunk_start(i, sh.chunk)
        rows = pl.ds(start, sh.chunk)
        spread(sh, padded_ref, start, up_ref[rows, :].astype(jnp.float32))
        pre = (x_ref[rows, :].astype(jnp.float32) - mean) * inv_std * factor + shift
        sigma = sigmoid(pre)
        act_ref[rows, :] = (pre * sigma).astype(jnp.bfloat16)
        slope_ref[rows, :] = sigma * (1.0 + pre * (1.0 - sigma))

    def differentiate(i, sums):
        start = chunk_start(i, sh.chunk)
        rows = pl.ds(start, sh.chunk)
        normed = (x_ref[rows, :].astype(jnp.float32) - mean) * inv_std
        pre_grad = convolve(sh, padded_ref, start, weight_ref, unit, True) * slope_ref[rows, :]
        pre_grad_ref[rows, :] = pre_grad
        return (sums[0] + fold_rows(pre_grad), sums[1] + fold_rows(pre_grad * normed))

    over_chunks(sh.chunks, activate)
    if sh.chunks == 1:
        sums = differentiate(0, (zero, zero))
    else:
        sums = lax.fori_loop(0, sh.chunks, differentiate, (zero, zero))
    sum_grad, sum_cross = column(sums[0]), column(sums[1])
    means = group_sums(stack_rows(factor * sum_grad, factor * sum_cross), sh.width) / sh.entries
    center, tilt = means[0:1], means[1:2]

    def finish(i):
        rows = pl.ds(chunk_start(i, sh.chunk), sh.chunk)
        normed = (x_ref[rows, :].astype(jnp.float32) - mean) * inv_std
        back = factor * pre_grad_ref[rows, :] - center - normed * tilt
        grad_ref[rows, :] = (up_ref[rows, :].astype(jnp.float32) + inv_std * back).astype(jnp.bfloat16)

    over_chunks(sh.chunks, finish)
    first_row = space * sh.slab
    first_tap = jnp.minimum(first_row // sh.channels, 9 - sh.taps)
    offset = pl.multiple_of(first_row - first_tap * sh.channels, 8)
    for t in range(sh.taps):
        tap = first_tap + t
        row, col = 2 - tap // 3, 2 - tap % 3
        place = pl.ds(t * sh.channels, sh.channels)

        def product(i):
            start = chunk_start(i, sh.chunk)
            block = padded_ref[col, pl.ds(pl.multiple_of(start + row * sh.cols, 16), sh.chunk), :]
            return lax.dot_general(
                act_ref[pl.ds(start, sh.chunk), :],
                block,
                (((0,), (0,)), ((), ())),
                preferred_element_type=jnp.float32,
            )

        if sh.chunks == 1:
            slab_ref[place, :] = product(0)
        else:
            slab_ref[place, :] = jnp.zeros((sh.channels, sh.channels), jnp.float32)

            def accumulate(i):
                slab_ref[place, :] += product(i)

            over_chunks(sh.chunks, accumulate)
    mine = slab_ref[pl.ds(offset, sh.slab), :]
    rows = grad_ref[pl.ds(pl.multiple_of(space * sh.own_rows, sh.own_rows), sh.own_rows), :]
    sums = stack_rows(sum_grad, sum_cross)

    def write(ref):
        ref[0 : sh.slab, :] = mine
        ref[sh.slab : sh.slab + sh.own_rows, :] = rows.astype(jnp.float32)
        ref[sh.slab + sh.own_rows : sh.pack, :] = sums

    @pl.when(core == unit)
    def _():
        write(keep_ref)

    @pl.when(core != unit)
    def _():
        write(send_ref)


def place_of():
    index = lax.axis_index("segment")
    return (index // PAIR, index % PAIR)


def unit_params(params_ref, unit):
    return (params_ref[2 * unit : 2 * unit + 1, :], params_ref[2 * unit + 1 : 2 * unit + 2, :])


def sinusoid_of(time, base):
    half = base // 2
    lanes = lax.broadcasted_iota(jnp.int32, (time.shape[0], base), 1)
    power = jnp.where(lanes < half, lanes, lanes - half).astype(jnp.float32)
    angle = time * jnp.exp(-math.log(10000.0) * power / half)
    turns = jnp.floor(angle * (2.0 / math.pi) + 0.5)
    rest = ((angle - turns * 1.5703125) - turns * 4.83751296997e-4) - turns * 7.54978995489e-8
    square = rest * rest
    sine = rest + rest * square * (
        -1.6666654611e-1 + square * (8.3321608736e-3 - square * 1.9515295891e-4)
    )
    cosine = 1.0 - 0.5 * square + square * square * (
        4.166664568298827e-2 + square * (-1.388731625493765e-3 + square * 2.443315711809948e-5)
    )
    quarter = turns.astype(jnp.int32) + jnp.where(lanes < half, 1, 0)
    value = jnp.where(quarter % 2 == 1, cosine, sine)
    return jnp.where((quarter // 2) % 2 == 1, -value, value).astype(jnp.bfloat16)


def start_all(pairs, sems):
    copies = [pltpu.make_async_copy(a, b, sems.at[i]) for i, (a, b) in enumerate(pairs)]
    for copy in copies:
        copy.start()
    return copies


def embed_kernel(times_ref, labels_ref, table_hbm, time_weight_hbm, embedded_ref, table_ref, time_weight_ref, sems):
    pairs = [(time_weight_hbm, time_weight_ref)]
    pairs += [(table_hbm.at[pl.ds(labels_ref[i] // 8, 1)], table_ref.at[pl.ds(i, 1)]) for i in range(PAIR)]
    copies = start_all(pairs, sems)
    spot = lax.broadcasted_iota(jnp.int32, (16, 1), 0)
    time = jnp.where(spot % 2 == 0, times_ref[0], times_ref[1]).astype(jnp.float32)
    sinusoid = sinusoid_of(time, time_weight_ref.shape[0])

    def label_row(image):
        block = table_ref[image].astype(jnp.float32)
        row = lax.broadcasted_iota(jnp.int32, block.shape, 0)
        return column(jnp.where(row == labels_ref[image] % 8, block, 0.0))

    for copy in copies:
        copy.wait()
    timed = jnp.dot(sinusoid, time_weight_ref[...], preferred_element_type=jnp.float32)
    timed = timed + jnp.where(spot % 2 == 0, label_row(0), label_row(1))
    embedded_ref[...] = (timed * sigmoid(timed)).astype(jnp.bfloat16)


def modulate_kernel(embedded_hbm, mod_weight_hbm, bias_hbm, gain_hbm, keep_ref, send_ref, *scratch):
    embedded_ref, mod_weight_ref, bias_ref, gain_ref, sems = scratch
    core = lax.axis_index("segment") % PAIR
    copies = start_all(zip((embedded_hbm, mod_weight_hbm, bias_hbm, gain_hbm), scratch[:4]), sems)
    for copy in copies:
        copy.wait()
    modulation = jnp.dot(embedded_ref[...], mod_weight_ref[...], preferred_element_type=jnp.float32) + bias_ref[...]
    channels = gain_ref.shape[1]
    factor = gain_ref[...] * (1.0 + modulation[:, :channels])
    shift = modulation[:, channels:]
    first = stack_rows(factor[0:1], shift[0:1])
    second = stack_rows(factor[1:2], shift[1:2])
    keep_ref[...] = jnp.where(core == 0, first, second)
    send_ref[...] = jnp.where(core == 0, second, first)


def layout_kernel(own_any, other_any, mod_keep_any, mod_other_any, weights_ref, params_ref, mods_ref, sems):
    core = lax.axis_index("segment") % PAIR
    pairs = [(mod_keep_any, mods_ref.at[core]), (mod_other_any, mods_ref.at[1 - core])]
    pairs += [(own_any, weights_ref.at[core]), (other_any, weights_ref.at[1 - core])]
    copies = start_all(pairs, sems)
    for copy in copies[:PAIR]:
        copy.wait()
    params_ref[0:2, :] = mods_ref[0, 0:2, :]
    params_ref[2:4, :] = mods_ref[1, 0:2, :]
    params_ref[4:8, :] = jnp.zeros((4, params_ref.shape[1]), jnp.float32)
    for copy in copies[PAIR:]:
        copy.wait()


def assemble(sh, blocks_ref, order, image_ref):
    space = lax.axis_index("space")
    for k, bits in enumerate(order):
        start = pl.multiple_of((space ^ bits) * sh.own_rows, sh.own_rows)
        image_ref[pl.ds(start, sh.own_rows), :] = blocks_ref[k]


def forward_kernel(sh, active_stage, orders, *refs):
    if orders:
        near_ref, far_ref, params_ref, weights, x_ref = refs[:5]
        assemble(sh, near_ref, orders[0], x_ref)
        assemble(sh, far_ref, orders[1], x_ref)
        refs = refs[5:]
    else:
        x_ref, params_ref, weights = refs[:3]
        refs = refs[3:]
    middle_ref, out_ref, padded_ref = refs
    stage, _ = place_of()

    @pl.when(stage == active_stage)
    def _():
        clear_edges(sh, padded_ref)
        forward_unit(sh, x_ref, middle_ref, unit_params(params_ref, 0), padded_ref, weights, 0)
        forward_unit(sh, middle_ref, out_ref, unit_params(params_ref, 1), padded_ref, weights, 1)


def backward_kernel(sh, active_stage, first, *refs):
    if first:
        x_ref, up_ref, params_ref, weights = refs[:4]
        refs = refs[4:]
    else:
        x_ref, middle_ref, up_ref, params_ref, weights = refs[:5]
        refs = refs[7:]
    keep_ref, send_ref, grad_ref = refs[:3]
    padded_ref, act_ref, slope_ref, pre_grad_ref, slab_ref, between_ref = refs[3:9]
    if first:
        middle_ref = refs[9]
    stage, core = place_of()

    @pl.when(stage == active_stage)
    def _():
        clear_edges(sh, padded_ref)
        params = [unit_params(params_ref, unit) for unit in range(PAIR)]
        if first:
            forward_unit(sh, x_ref, middle_ref, params[0], padded_ref, weights, 0)
        scratch = (padded_ref, act_ref, slope_ref, pre_grad_ref, slab_ref)
        backward_unit(
            sh, middle_ref, up_ref, between_ref, params[1], scratch, weights, 1, keep_ref, send_ref, core
        )
        backward_unit(
            sh, x_ref, between_ref, grad_ref, params[0], scratch, weights, 0, keep_ref, send_ref, core
        )


def finish_kernel(sh, keep_ref, other_ref, embedded_ref, gain_ref, grads_ref, conv_ref, mod_ref):
    core = lax.axis_index("segment") % PAIR
    conv_ref[...] = keep_ref[0 : sh.slab, :] + other_ref[0 : sh.slab, :]
    rows = slice(sh.slab, sh.slab + sh.own_rows)
    grads_ref[pl.ds(core, 1)] = keep_ref[rows, :].astype(jnp.bfloat16)[None]
    grads_ref[pl.ds(1 - core, 1)] = other_ref[rows, :].astype(jnp.bfloat16)[None]
    base = sh.slab + sh.own_rows

    def mod_rows(ref):
        return jnp.concatenate([gain_ref[...] * ref[base + 1 : base + 2, :], ref[base : base + 1, :]], axis=1)

    own, other = mod_rows(keep_ref), mod_rows(other_ref)
    spot = lax.broadcasted_iota(jnp.int32, (16, own.shape[1]), 0)
    values = jnp.where(spot % 2 == core, own, other)
    high = values.astype(jnp.bfloat16).astype(jnp.float32)
    rest = values - high
    middle = rest.astype(jnp.bfloat16).astype(jnp.float32)
    low = rest - middle
    part = spot // 2
    pieces = jnp.where(part == 0, high, jnp.where(part == 1, middle, jnp.where(part == 2, low, 0.0)))
    mod_ref[...] = lax.dot_general(
        embedded_ref[...],
        pieces.astype(jnp.bfloat16),
        (((0,), (0,)), ((), ())),
        preferred_element_type=jnp.float32,
    )


def shards(
    x_in,
    out_cotangent,
    timesteps,
    labels,
    time_weight,
    label_table,
    conv_weight,
    mod_weight,
    mod_bias,
    norm_gain,
):
    segments, spaces = lax.axis_size("segment"), lax.axis_size("space")
    stages = segments // PAIR
    stage, core = place_of()
    images, row_count, cols, channels = x_in.shape
    sh = Shape(row_count * spaces, cols, channels, spaces)
    f32, bf16 = jnp.float32, jnp.bfloat16

    def call(body, ins, outs, scratch=(), limit=CHAIN_LIMIT, cost=None, aliases={}):
        return pl.pallas_call(
            body,
            out_shape=outs,
            in_specs=ins,
            out_specs=[VMEM] * len(outs),
            scratch_shapes=list(scratch),
            input_output_aliases=aliases,
            compiler_params=pltpu.CompilerParams(vmem_limit_bytes=limit),
            cost_estimate=cost,
        )

    shape = jax.ShapeDtypeStruct
    swap = [(i, i ^ 1) for i in range(segments)]
    weight = conv_weight.reshape(9 * channels, channels)
    other_weight = lax.ppermute(weight, "segment", swap)
    ends = jnp.where(stage == 0, x_in, out_cotangent)
    near = lax.dynamic_index_in_dim(ends, core, 0, keepdims=False).reshape(1, sh.own_rows, channels)
    table = label_table.reshape(-1, 8, label_table.shape[1])
    width = time_weight.shape[1]
    some = pl.CostEstimate(flops=1 << 20, bytes_accessed=4 << 20, transcendentals=0)
    order, bit = [0], spaces // 2
    waiting = []
    while True:
        far = lax.ppermute(near, "space", [(i, i ^ bit) for i in range(spaces)])
        if not waiting:
            (embedded,) = call(
                embed_kernel,
                [SMEM, SMEM, ANY, ANY],
                [shape((16, width), bf16)],
                [
                    pltpu.VMEM((PAIR, 8, width), bf16),
                    pltpu.VMEM(time_weight.shape, bf16),
                    pltpu.SemaphoreType.DMA((PAIR + 1,)),
                ],
                PREPARE_LIMIT,
                some,
            )(timesteps, labels, table, time_weight)
            waiting = [embedded]
            far, embedded = lax.optimization_barrier((far, embedded))
        elif len(waiting) == 1:
            operands = (embedded, mod_weight[0], mod_bias, norm_gain)
            mod_keep, mod_send = call(
                modulate_kernel,
                [ANY] * 4,
                [shape((8, channels), f32)] * 2,
                [pltpu.VMEM(value.shape, value.dtype) for value in operands] + [pltpu.SemaphoreType.DMA((4,))],
                PREPARE_LIMIT,
                some,
            )(*operands)
            waiting.append(mod_keep)
            far, mod_keep, mod_send = lax.optimization_barrier((far, mod_keep, mod_send))
        far_order = [k ^ bit for k in order]
        if bit == 1:
            break
        near = jnp.concatenate([near, far])
        order, bit = order + far_order, bit // 2
    mod_other = lax.ppermute(mod_send, "segment", swap)
    weights, params = call(
        layout_kernel,
        [ANY] * 4,
        [shape((PAIR, 9 * channels, channels), bf16), shape((8, channels), f32)],
        [pltpu.VMEM((PAIR, 8, channels), f32), pltpu.SemaphoreType.DMA((2 * PAIR,))],
        cost=some,
    )(weight, other_weight, mod_keep, mod_other)

    image_shape = shape((sh.pixels, channels), bf16)
    pack_shape = shape((sh.pack, channels), f32)
    common = [pltpu.VMEM((3, sh.padded, channels), bf16)]

    def hop(value, source, target):
        pairs = [(PAIR * source + k, PAIR * target + k) for k in range(PAIR)]
        return lax.ppermute(value, "segment", pairs + [(b, a) for a, b in pairs])

    image, middle, out = call(
        functools.partial(forward_kernel, sh, 0, (order, far_order)),
        [VMEM] * 4,
        [image_shape] * 3,
        common,
    )(near, far, params, weights)
    entering, middles = [image, hop(out, 0, 1)], [middle]
    for active in range(1, stages - 1):
        middle, out = call(
            functools.partial(forward_kernel, sh, active, None),
            [VMEM] * 3,
            [image_shape, image_shape],
            common,
        )(entering[active], params, weights)
        middles.append(middle)
        entering.append(hop(out, active, active + 1))

    scratch = common + [
        pltpu.VMEM((sh.pixels, channels), bf16),
        pltpu.VMEM((sh.pixels, channels), f32),
        pltpu.VMEM((sh.pixels, channels), f32),
        pltpu.VMEM((sh.taps * channels, channels), f32),
        pltpu.VMEM((sh.pixels, channels), bf16),
    ]
    outs = [pack_shape, pack_shape, image_shape]
    keep, send, grad = call(
        functools.partial(backward_kernel, sh, stages - 1, True),
        [VMEM] * 4,
        outs,
        scratch + [pltpu.VMEM((sh.pixels, channels), bf16)],
    )(entering[stages - 1], image, params, weights)
    for active in range(stages - 2, -1, -1):
        upstream = hop(grad[0] if isinstance(grad, list) else grad, active + 1, active)
        last = active == 0
        keep, send, *grad = call(
            functools.partial(backward_kernel, sh, active, False),
            [VMEM] * 7,
            outs[:2] if last else outs,
            scratch[-1:] + scratch if last else scratch,
            aliases={5: 0, 6: 1},
        )(entering[active], middles[active], upstream, params, weights, keep, send)
    other = lax.ppermute(send, "segment", swap)
    grads, conv_grad, mod_grad = call(
        functools.partial(finish_kernel, sh),
        [VMEM] * 4,
        [
            shape((images, sh.own_rows, channels), bf16),
            shape((sh.slab, channels), f32),
            shape((time_weight.shape[1], 2 * channels), f32),
        ],
    )(keep, other, embedded, norm_gain)
    return (grads.reshape(1, images, row_count, cols, channels), conv_grad[None], mod_grad[None])


def solution(mesh):
    placed = (
        P(None, "space", None, None),
        P(None, "space", None, None),
        P(),
        P(),
        P(),
        P(),
        P("segment", None, None, None, None),
        P("segment", None, None),
        P("segment", None),
        P("segment", None),
    )
    return jax.shard_map(
        shards,
        mesh=mesh,
        in_specs=placed,
        out_specs=(
            P("segment", None, "space", None, None),
            P("segment", "space", None),
            P("segment", None, None),
        ),
        check_vma=False,
    )
```

```python
import functools
import math

import jax
import jax.numpy as jnp
from jax import lax
from jax.experimental import pallas as pl
from jax.experimental.pallas import tpu as pltpu
from jax.sharding import PartitionSpec as P

GROUPS = 32
EPSILON = 1e-05
PAIR = 2
PREPARE_LIMIT = 60 << 20
CHAIN_LIMIT = 48 << 20
VMEM = pl.BlockSpec(memory_space=pltpu.VMEM)
SMEM = pl.BlockSpec(memory_space=pltpu.SMEM)
ANY = pl.BlockSpec(memory_space=pl.ANY)


def sigmoid(values):
    return 1.0 / (1.0 + jnp.exp(-values))


def over_chunks(count, body):
    if count == 1:
        body(0)
    else:

        def step(i, carry):
            body(i)
            return carry

        lax.fori_loop(0, count, step, 0)


def chunk_start(i, size):
    return 0 if isinstance(i, int) else pl.multiple_of(i * size, size)


def fold_rows(values):
    return jnp.sum(values.reshape(values.shape[0] // 8, 8, values.shape[1]), axis=0)


def column(rows):
    return jnp.sum(rows, axis=0, keepdims=True)


def group_sums(rows, width):
    lanes = lax.broadcasted_iota(jnp.int32, rows.shape, 1)
    size = rows.shape[1]
    step = 1
    while step < width:
        ahead = pltpu.roll(rows, size - step, 1)
        behind = pltpu.roll(rows, step, 1)
        rows = rows + jnp.where((lanes & step) == 0, ahead, behind)
        step *= 2
    return rows


def stack_rows(first, second):
    spot = lax.broadcasted_iota(jnp.int32, (8, first.shape[1]), 0)
    return jnp.where(spot == 0, first, jnp.where(spot == 1, second, 0.0))


class Shape:
    def __init__(self, height, cols, channels, space_count):
        self.cols, self.channels = cols, channels
        self.pixels = height * cols
        self.chunk = cols * max(1, min(self.pixels, 256) // cols)
        self.chunks = self.pixels // self.chunk
        self.width = channels // GROUPS
        self.entries = float(self.pixels * self.width)
        self.padded = self.pixels + 2 * cols
        self.own_rows = height // space_count * cols
        self.slab = 9 * channels // space_count
        self.taps = min(9, (self.slab - 1) // channels + 2)
        self.pack = self.slab + self.own_rows + 8
        self.limit = (12 << 20) + self.pixels * channels * 40


def statistics(sh, x_ref):
    zero = jnp.zeros((8, sh.channels), jnp.float32)

    def add(i, sums):
        part = x_ref[pl.ds(chunk_start(i, sh.chunk), sh.chunk), :].astype(jnp.float32)
        return (sums[0] + fold_rows(part), sums[1] + fold_rows(part * part))

    if sh.chunks == 1:
        one, two = add(0, (zero, zero))
    else:
        one, two = lax.fori_loop(0, sh.chunks, add, (zero, zero))
    total = group_sums(stack_rows(column(one), column(two)), sh.width) / sh.entries
    mean = total[0:1]
    return (mean, lax.rsqrt(total[1:2] - mean * mean + EPSILON))


def clear_edges(sh, padded_ref):
    zero = jnp.zeros((3, sh.cols, sh.channels), padded_ref.dtype)
    padded_ref[:, 0 : sh.cols, :] = zero
    padded_ref[:, sh.pixels + sh.cols : sh.padded, :] = zero


def spread(sh, padded_ref, start, values):
    place = pl.ds(start + sh.cols, sh.chunk)
    spot = lax.broadcasted_iota(jnp.int32, values.shape, 0) % sh.cols
    padded_ref[0, place, :] = jnp.where(spot == 0, 0.0, pltpu.roll(values, 1, 0)).astype(jnp.bfloat16)
    padded_ref[1, place, :] = values.astype(jnp.bfloat16)
    padded_ref[2, place, :] = jnp.where(
        spot == sh.cols - 1, 0.0, pltpu.roll(values, sh.chunk - 1, 0)
    ).astype(jnp.bfloat16)


def convolve(sh, padded_ref, start, weight_ref, unit, backward):
    total = None
    for p in range(3):
        for q in range(3):
            row, col = (2 - p, 2 - q) if backward else (p, q)
            block = padded_ref[col, pl.ds(start + row * sh.cols, sh.chunk), :]
            tap = (3 * p + q) * sh.channels
            weight = weight_ref[unit, tap : tap + sh.channels, :]
            part = lax.dot_general(
                block,
                weight,
                (((1,), (1 if backward else 0,)), ((), ())),
                preferred_element_type=jnp.float32,
            )
            total = part if total is None else total + part
    return total


def forward_unit(sh, x_ref, out_ref, params, padded_ref, weight_ref, unit):
    factor, shift = params
    mean, inv_std = statistics(sh, x_ref)

    def activate(i):
        start = chunk_start(i, sh.chunk)
        normed = (x_ref[pl.ds(start, sh.chunk), :].astype(jnp.float32) - mean) * inv_std
        pre = normed * factor + shift
        spread(sh, padded_ref, start, pre * sigmoid(pre))

    def produce(i):
        start = chunk_start(i, sh.chunk)
        inputs = x_ref[pl.ds(start, sh.chunk), :].astype(jnp.float32)
        z = convolve(sh, padded_ref, start, weight_ref, unit, False)
        out_ref[pl.ds(start, sh.chunk), :] = (inputs + z).astype(jnp.bfloat16)

    over_chunks(sh.chunks, activate)
    over_chunks(sh.chunks, produce)


def backward_unit(sh, x_ref, up_ref, grad_ref, params, scratch, weight_ref, unit, keep_ref, send_ref, core):
    padded_ref, act_ref, slope_ref, pre_grad_ref, slab_ref = scratch
    factor, shift = params
    space = lax.axis_index("space")
    mean, inv_std = statistics(sh, x_ref)
    zero = jnp.zeros((8, sh.channels), jnp.float32)

    def activate(i):
        start = chunk_start(i, sh.chunk)
        rows = pl.ds(start, sh.chunk)
        spread(sh, padded_ref, start, up_ref[rows, :].astype(jnp.float32))
        pre = (x_ref[rows, :].astype(jnp.float32) - mean) * inv_std * factor + shift
        sigma = sigmoid(pre)
        act_ref[rows, :] = (pre * sigma).astype(jnp.bfloat16)
        slope_ref[rows, :] = sigma * (1.0 + pre * (1.0 - sigma))

    def differentiate(i, sums):
        start = chunk_start(i, sh.chunk)
        rows = pl.ds(start, sh.chunk)
        normed = (x_ref[rows, :].astype(jnp.float32) - mean) * inv_std
        pre_grad = convolve(sh, padded_ref, start, weight_ref, unit, True) * slope_ref[rows, :]
        pre_grad_ref[rows, :] = pre_grad
        return (sums[0] + fold_rows(pre_grad), sums[1] + fold_rows(pre_grad * normed))

    over_chunks(sh.chunks, activate)
    if sh.chunks == 1:
        sums = differentiate(0, (zero, zero))
    else:
        sums = lax.fori_loop(0, sh.chunks, differentiate, (zero, zero))
    sum_grad, sum_cross = column(sums[0]), column(sums[1])
    means = group_sums(stack_rows(factor * sum_grad, factor * sum_cross), sh.width) / sh.entries
    center, tilt = means[0:1], means[1:2]

    def finish(i):
        rows = pl.ds(chunk_start(i, sh.chunk), sh.chunk)
        normed = (x_ref[rows, :].astype(jnp.float32) - mean) * inv_std
        back = factor * pre_grad_ref[rows, :] - center - normed * tilt
        grad_ref[rows, :] = (up_ref[rows, :].astype(jnp.float32) + inv_std * back).astype(jnp.bfloat16)

    over_chunks(sh.chunks, finish)
    first_row = space * sh.slab
    first_tap = jnp.minimum(first_row // sh.channels, 9 - sh.taps)
    offset = pl.multiple_of(first_row - first_tap * sh.channels, 8)
    for t in range(sh.taps):
        tap = first_tap + t
        row, col = 2 - tap // 3, 2 - tap % 3
        place = pl.ds(t * sh.channels, sh.channels)

        def product(i):
            start = chunk_start(i, sh.chunk)
            block = padded_ref[col, pl.ds(pl.multiple_of(start + row * sh.cols, 16), sh.chunk), :]
            return lax.dot_general(
                act_ref[pl.ds(start, sh.chunk), :],
                block,
                (((0,), (0,)), ((), ())),
                preferred_element_type=jnp.float32,
            )

        if sh.chunks == 1:
            slab_ref[place, :] = product(0)
        else:
            slab_ref[place, :] = jnp.zeros((sh.channels, sh.channels), jnp.float32)

            def accumulate(i):
                slab_ref[place, :] += product(i)

            over_chunks(sh.chunks, accumulate)
    mine = slab_ref[pl.ds(offset, sh.slab), :]
    rows = grad_ref[pl.ds(pl.multiple_of(space * sh.own_rows, sh.own_rows), sh.own_rows), :]
    sums = stack_rows(sum_grad, sum_cross)

    def write(ref):
        ref[0 : sh.slab, :] = mine
        ref[sh.slab : sh.slab + sh.own_rows, :] = rows.astype(jnp.float32)
        ref[sh.slab + sh.own_rows : sh.pack, :] = sums

    @pl.when(core == unit)
    def _():
        write(keep_ref)

    @pl.when(core != unit)
    def _():
        write(send_ref)


def place_of():
    index = lax.axis_index("segment")
    return (index // PAIR, index % PAIR)


def unit_params(params_ref, unit):
    return (params_ref[2 * unit : 2 * unit + 1, :], params_ref[2 * unit + 1 : 2 * unit + 2, :])


def sinusoid_of(time, base):
    half = base // 2
    lanes = lax.broadcasted_iota(jnp.int32, (time.shape[0], base), 1)
    power = jnp.where(lanes < half, lanes, lanes - half).astype(jnp.float32)
    angle = time * jnp.exp(-math.log(10000.0) * power / half)
    turns = jnp.floor(angle * (2.0 / math.pi) + 0.5)
    rest = ((angle - turns * 1.5703125) - turns * 4.83751296997e-4) - turns * 7.54978995489e-8
    square = rest * rest
    sine = rest + rest * square * (
        -1.6666654611e-1 + square * (8.3321608736e-3 - square * 1.9515295891e-4)
    )
    cosine = 1.0 - 0.5 * square + square * square * (
        4.166664568298827e-2 + square * (-1.388731625493765e-3 + square * 2.443315711809948e-5)
    )
    quarter = turns.astype(jnp.int32) + jnp.where(lanes < half, 1, 0)
    value = jnp.where(quarter % 2 == 1, cosine, sine)
    return jnp.where((quarter // 2) % 2 == 1, -value, value).astype(jnp.bfloat16)


def start_all(pairs, sems):
    copies = [pltpu.make_async_copy(a, b, sems.at[i]) for i, (a, b) in enumerate(pairs)]
    for copy in copies:
        copy.start()
    return copies


def prepare_kernel(times_ref, labels_ref, table_hbm, *refs):
    sources, (embedded_ref, keep_ref, send_ref), scratch = refs[:4], refs[4:7], refs[7:]
    time_weight_ref, mod_weight_ref, bias_ref, gain_ref, table_ref, sems = scratch
    core = lax.axis_index("segment") % PAIR
    pairs = [(table_hbm.at[pl.ds(labels_ref[i] // 8, 1)], table_ref.at[pl.ds(i, 1)]) for i in range(PAIR)]
    copies = start_all(pairs + list(zip(sources, scratch[:4])), sems)
    spot = lax.broadcasted_iota(jnp.int32, (16, 1), 0)
    time = jnp.where(spot % 2 == 0, times_ref[0], times_ref[1]).astype(jnp.float32)
    sinusoid = sinusoid_of(time, time_weight_ref.shape[0])

    def label_row(image):
        block = table_ref[image].astype(jnp.float32)
        row = lax.broadcasted_iota(jnp.int32, block.shape, 0)
        return column(jnp.where(row == labels_ref[image] % 8, block, 0.0))

    for copy in copies[: PAIR + 1]:
        copy.wait()
    timed = jnp.dot(sinusoid, time_weight_ref[...], preferred_element_type=jnp.float32)
    timed = timed + jnp.where(spot % 2 == 0, label_row(0), label_row(1))
    embedded = (timed * sigmoid(timed)).astype(jnp.bfloat16)
    embedded_ref[...] = embedded
    for copy in copies[PAIR + 1 :]:
        copy.wait()
    modulation = jnp.dot(embedded, mod_weight_ref[...], preferred_element_type=jnp.float32) + bias_ref[...]
    channels = gain_ref.shape[1]
    factor = gain_ref[...] * (1.0 + modulation[:, :channels])
    shift = modulation[:, channels:]
    first = stack_rows(factor[0:1], shift[0:1])
    second = stack_rows(factor[1:2], shift[1:2])
    keep_ref[...] = jnp.where(core == 0, first, second)
    send_ref[...] = jnp.where(core == 0, second, first)


def layout_kernel(own_any, other_any, mod_keep_any, mod_other_any, weights_ref, params_ref, mods_ref, sems):
    core = lax.axis_index("segment") % PAIR
    pairs = [(mod_keep_any, mods_ref.at[core]), (mod_other_any, mods_ref.at[1 - core])]
    pairs += [(own_any, weights_ref.at[core]), (other_any, weights_ref.at[1 - core])]
    copies = start_all(pairs, sems)
    for copy in copies[:PAIR]:
        copy.wait()
    params_ref[0:2, :] = mods_ref[0, 0:2, :]
    params_ref[2:4, :] = mods_ref[1, 0:2, :]
    params_ref[4:8, :] = jnp.zeros((4, params_ref.shape[1]), jnp.float32)
    for copy in copies[PAIR:]:
        copy.wait()


def assemble(sh, blocks_ref, order, image_ref):
    space = lax.axis_index("space")
    for k, bits in enumerate(order):
        start = pl.multiple_of((space ^ bits) * sh.own_rows, sh.own_rows)
        image_ref[pl.ds(start, sh.own_rows), :] = blocks_ref[k]


def forward_kernel(sh, active_stage, orders, *refs):
    if orders:
        near_ref, far_ref, params_ref, weights, x_ref = refs[:5]
        assemble(sh, near_ref, orders[0], x_ref)
        assemble(sh, far_ref, orders[1], x_ref)
        refs = refs[5:]
    else:
        x_ref, params_ref, weights = refs[:3]
        refs = refs[3:]
    middle_ref, out_ref, padded_ref = refs
    stage, _ = place_of()

    @pl.when(stage == active_stage)
    def _():
        clear_edges(sh, padded_ref)
        forward_unit(sh, x_ref, middle_ref, unit_params(params_ref, 0), padded_ref, weights, 0)
        forward_unit(sh, middle_ref, out_ref, unit_params(params_ref, 1), padded_ref, weights, 1)


def backward_kernel(sh, active_stage, first, *refs):
    if first:
        x_ref, up_ref, params_ref, weights = refs[:4]
        refs = refs[4:]
    else:
        x_ref, middle_ref, up_ref, params_ref, weights = refs[:5]
        refs = refs[7:]
    keep_ref, send_ref, grad_ref = refs[:3]
    padded_ref, act_ref, slope_ref, pre_grad_ref, slab_ref, between_ref = refs[3:9]
    if first:
        middle_ref = refs[9]
    stage, core = place_of()

    @pl.when(stage == active_stage)
    def _():
        clear_edges(sh, padded_ref)
        params = [unit_params(params_ref, unit) for unit in range(PAIR)]
        if first:
            forward_unit(sh, x_ref, middle_ref, params[0], padded_ref, weights, 0)
        scratch = (padded_ref, act_ref, slope_ref, pre_grad_ref, slab_ref)
        backward_unit(
            sh, middle_ref, up_ref, between_ref, params[1], scratch, weights, 1, keep_ref, send_ref, core
        )
        backward_unit(
            sh, x_ref, between_ref, grad_ref, params[0], scratch, weights, 0, keep_ref, send_ref, core
        )


def finish_kernel(sh, keep_ref, other_ref, embedded_ref, gain_ref, grads_ref, conv_ref, mod_ref):
    core = lax.axis_index("segment") % PAIR
    conv_ref[...] = keep_ref[0 : sh.slab, :] + other_ref[0 : sh.slab, :]
    rows = slice(sh.slab, sh.slab + sh.own_rows)
    grads_ref[pl.ds(core, 1)] = keep_ref[rows, :].astype(jnp.bfloat16)[None]
    grads_ref[pl.ds(1 - core, 1)] = other_ref[rows, :].astype(jnp.bfloat16)[None]
    base = sh.slab + sh.own_rows

    def mod_rows(ref):
        return jnp.concatenate([gain_ref[...] * ref[base + 1 : base + 2, :], ref[base : base + 1, :]], axis=1)

    own, other = mod_rows(keep_ref), mod_rows(other_ref)
    spot = lax.broadcasted_iota(jnp.int32, (16, own.shape[1]), 0)
    values = jnp.where(spot % 2 == core, own, other)
    high = values.astype(jnp.bfloat16).astype(jnp.float32)
    rest = values - high
    middle = rest.astype(jnp.bfloat16).astype(jnp.float32)
    low = rest - middle
    part = spot // 2
    pieces = jnp.where(part == 0, high, jnp.where(part == 1, middle, jnp.where(part == 2, low, 0.0)))
    mod_ref[...] = lax.dot_general(
        embedded_ref[...],
        pieces.astype(jnp.bfloat16),
        (((0,), (0,)), ((), ())),
        preferred_element_type=jnp.float32,
    )


def shards(
    x_in,
    out_cotangent,
    timesteps,
    labels,
    time_weight,
    label_table,
    conv_weight,
    mod_weight,
    mod_bias,
    norm_gain,
):
    segments, spaces = lax.axis_size("segment"), lax.axis_size("space")
    stages = segments // PAIR
    stage, core = place_of()
    images, row_count, cols, channels = x_in.shape
    sh = Shape(row_count * spaces, cols, channels, spaces)
    f32, bf16 = jnp.float32, jnp.bfloat16

    def call(body, ins, outs, scratch=(), limit=CHAIN_LIMIT, cost=None, aliases={}):
        return pl.pallas_call(
            body,
            out_shape=outs,
            in_specs=ins,
            out_specs=[VMEM] * len(outs),
            scratch_shapes=list(scratch),
            input_output_aliases=aliases,
            compiler_params=pltpu.CompilerParams(vmem_limit_bytes=limit),
            cost_estimate=cost,
        )

    shape = jax.ShapeDtypeStruct
    swap = [(i, i ^ 1) for i in range(segments)]
    weight = conv_weight.reshape(9 * channels, channels)
    other_weight = lax.ppermute(weight, "segment", swap)
    ends = jnp.where(stage == 0, x_in, out_cotangent)
    near = lax.dynamic_index_in_dim(ends, core, 0, keepdims=False).reshape(1, sh.own_rows, channels)
    table = label_table.reshape(-1, 8, label_table.shape[1])
    width = time_weight.shape[1]
    some = pl.CostEstimate(flops=1 << 20, bytes_accessed=4 << 20, transcendentals=0)
    operands = (time_weight, mod_weight[0], mod_bias, norm_gain)
    embedded, mod_keep, mod_send = call(
        prepare_kernel,
        [SMEM, SMEM] + [ANY] * 5,
        [shape((16, width), bf16)] + [shape((8, channels), f32)] * 2,
        [pltpu.VMEM(value.shape, value.dtype) for value in operands]
        + [pltpu.VMEM((PAIR, 8, width), bf16), pltpu.SemaphoreType.DMA((PAIR + 4,))],
        PREPARE_LIMIT,
        some,
    )(timesteps, labels, table, *operands)

    def exchange(bits):
        return lax.ppermute(near, "space", [(i, i ^ bits) for i in range(spaces)])

    quarter = spaces // 4
    order = [k * quarter for k in (0, 3, 2, 1)]
    fars = [exchange(bits) for bits in order[1:]]
    *fars, mod_keep, mod_send = lax.optimization_barrier((*fars, mod_keep, mod_send))
    bit = quarter // 2
    near = jnp.concatenate([near, *fars])
    while True:
        far, far_order = exchange(bit), [k ^ bit for k in order]
        bit //= 2
        if bit == 0:
            break
        near, order = jnp.concatenate([near, far]), order + far_order
    mod_other = lax.ppermute(mod_send, "segment", swap)
    weights, params = call(
        layout_kernel,
        [ANY] * 4,
        [shape((PAIR, 9 * channels, channels), bf16), shape((8, channels), f32)],
        [pltpu.VMEM((PAIR, 8, channels), f32), pltpu.SemaphoreType.DMA((2 * PAIR,))],
        cost=some,
    )(weight, other_weight, mod_keep, mod_other)

    image_shape = shape((sh.pixels, channels), bf16)
    pack_shape = shape((sh.pack, channels), f32)
    common = [pltpu.VMEM((3, sh.padded, channels), bf16)]

    def hop(value, source, target):
        pairs = [(PAIR * source + k, PAIR * target + k) for k in range(PAIR)]
        return lax.ppermute(value, "segment", pairs + [(b, a) for a, b in pairs])

    image, middle, out = call(
        functools.partial(forward_kernel, sh, 0, (order, far_order)),
        [VMEM] * 4,
        [image_shape] * 3,
        common,
    )(near, far, params, weights)
    entering, middles = [image, hop(out, 0, 1)], [middle]
    for active in range(1, stages - 1):
        middle, out = call(
            functools.partial(forward_kernel, sh, active, None),
            [VMEM] * 3,
            [image_shape, image_shape],
            common,
        )(entering[active], params, weights)
        middles.append(middle)
        entering.append(hop(out, active, active + 1))

    scratch = common + [
        pltpu.VMEM((sh.pixels, channels), bf16),
        pltpu.VMEM((sh.pixels, channels), f32),
        pltpu.VMEM((sh.pixels, channels), f32),
        pltpu.VMEM((sh.taps * channels, channels), f32),
        pltpu.VMEM((sh.pixels, channels), bf16),
    ]
    outs = [pack_shape, pack_shape, image_shape]
    keep, send, grad = call(
        functools.partial(backward_kernel, sh, stages - 1, True),
        [VMEM] * 4,
        outs,
        scratch + [pltpu.VMEM((sh.pixels, channels), bf16)],
    )(entering[stages - 1], image, params, weights)
    for active in range(stages - 2, -1, -1):
        upstream = hop(grad[0] if isinstance(grad, list) else grad, active + 1, active)
        last = active == 0
        keep, send, *grad = call(
            functools.partial(backward_kernel, sh, active, False),
            [VMEM] * 7,
            outs[:2] if last else outs,
            scratch[-1:] + scratch if last else scratch,
            aliases={5: 0, 6: 1},
        )(entering[active], middles[active], upstream, params, weights, keep, send)
    other = lax.ppermute(send, "segment", swap)
    grads, conv_grad, mod_grad = call(
        functools.partial(finish_kernel, sh),
        [VMEM] * 4,
        [
            shape((images, sh.own_rows, channels), bf16),
            shape((sh.slab, channels), f32),
            shape((time_weight.shape[1], 2 * channels), f32),
        ],
    )(keep, other, embedded, norm_gain)
    return (grads.reshape(1, images, row_count, cols, channels), conv_grad[None], mod_grad[None])


def solution(mesh):
    placed = (
        P(None, "space", None, None),
        P(None, "space", None, None),
        P(),
        P(),
        P(),
        P(),
        P("segment", None, None, None, None),
        P("segment", None, None),
        P("segment", None),
        P("segment", None),
    )
    return jax.shard_map(
        shards,
        mesh=mesh,
        in_specs=placed,
        out_specs=(
            P("segment", None, "space", None, None),
            P("segment", "space", None),
            P("segment", None, None),
        ),
        check_vma=False,
    )
```

```python
import functools
import math

import jax
import jax.numpy as jnp
from jax import lax
from jax.experimental import pallas as pl
from jax.experimental.pallas import tpu as pltpu
from jax.sharding import PartitionSpec as P

GROUPS = 32
EPSILON = 1e-05
PAIR = 2
PREPARE_LIMIT = 60 << 20
CHAIN_LIMIT = 48 << 20
VMEM = pl.BlockSpec(memory_space=pltpu.VMEM)
SMEM = pl.BlockSpec(memory_space=pltpu.SMEM)
ANY = pl.BlockSpec(memory_space=pl.ANY)


def sigmoid(values):
    return 1.0 / (1.0 + jnp.exp(-values))


def over_chunks(count, body):
    if count == 1:
        body(0)
    else:

        def step(i, carry):
            body(i)
            return carry

        lax.fori_loop(0, count, step, 0)


def chunk_start(i, size):
    return 0 if isinstance(i, int) else pl.multiple_of(i * size, size)


def fold_rows(values):
    return jnp.sum(values.reshape(values.shape[0] // 8, 8, values.shape[1]), axis=0)


def column(rows):
    return jnp.sum(rows, axis=0, keepdims=True)


def group_sums(rows, width):
    lanes = lax.broadcasted_iota(jnp.int32, rows.shape, 1)
    size = rows.shape[1]
    step = 1
    while step < width:
        ahead = pltpu.roll(rows, size - step, 1)
        behind = pltpu.roll(rows, step, 1)
        rows = rows + jnp.where((lanes & step) == 0, ahead, behind)
        step *= 2
    return rows


def stack_rows(first, second):
    spot = lax.broadcasted_iota(jnp.int32, (8, first.shape[1]), 0)
    return jnp.where(spot == 0, first, jnp.where(spot == 1, second, 0.0))


class Shape:
    def __init__(self, height, cols, channels, space_count):
        self.cols, self.channels = cols, channels
        self.pixels = height * cols
        self.chunk = cols * max(1, min(self.pixels, 256) // cols)
        self.chunks = self.pixels // self.chunk
        self.width = channels // GROUPS
        self.entries = float(self.pixels * self.width)
        self.padded = self.pixels + 2 * cols
        self.own_rows = height // space_count * cols
        self.slab = 9 * channels // space_count
        self.taps = min(9, (self.slab - 1) // channels + 2)
        self.pack = self.slab + self.own_rows + 8
        self.limit = (12 << 20) + self.pixels * channels * 40


def statistics(sh, x_ref):
    zero = jnp.zeros((8, sh.channels), jnp.float32)

    def add(i, sums):
        part = x_ref[pl.ds(chunk_start(i, sh.chunk), sh.chunk), :].astype(jnp.float32)
        return (sums[0] + fold_rows(part), sums[1] + fold_rows(part * part))

    if sh.chunks == 1:
        one, two = add(0, (zero, zero))
    else:
        one, two = lax.fori_loop(0, sh.chunks, add, (zero, zero))
    total = group_sums(stack_rows(column(one), column(two)), sh.width) / sh.entries
    mean = total[0:1]
    return (mean, lax.rsqrt(total[1:2] - mean * mean + EPSILON))


def clear_edges(sh, padded_ref):
    zero = jnp.zeros((3, sh.cols, sh.channels), padded_ref.dtype)
    padded_ref[:, 0 : sh.cols, :] = zero
    padded_ref[:, sh.pixels + sh.cols : sh.padded, :] = zero


def spread(sh, padded_ref, start, values):
    place = pl.ds(start + sh.cols, sh.chunk)
    spot = lax.broadcasted_iota(jnp.int32, values.shape, 0) % sh.cols
    padded_ref[0, place, :] = jnp.where(spot == 0, 0.0, pltpu.roll(values, 1, 0)).astype(jnp.bfloat16)
    padded_ref[1, place, :] = values.astype(jnp.bfloat16)
    padded_ref[2, place, :] = jnp.where(
        spot == sh.cols - 1, 0.0, pltpu.roll(values, sh.chunk - 1, 0)
    ).astype(jnp.bfloat16)


def convolve(sh, padded_ref, start, weight_ref, unit, backward):
    blocks, weights = [], []
    for p in range(3):
        for q in range(3):
            row, col = (2 - p, 2 - q) if backward else (p, q)
            blocks.append(padded_ref[col, pl.ds(start + row * sh.cols, sh.chunk), :])
            tap = (3 * p + q) * sh.channels
            weights.append(weight_ref[unit, tap : tap + sh.channels, :])
    return lax.dot_general(
        jnp.concatenate(blocks, axis=1),
        jnp.concatenate(weights, axis=1 if backward else 0),
        (((1,), (1 if backward else 0,)), ((), ())),
        preferred_element_type=jnp.float32,
    )


def activation(sh, x_ref, place, stats, params):
    (mean, inv_std), (factor, shift) = stats, params
    pre = (x_ref[place, :].astype(jnp.float32) - mean) * inv_std * factor + shift
    sigma = sigmoid(pre)
    return pre * sigma, sigma * (1.0 + pre * (1.0 - sigma))


def note_unit(sh, x_ref, params, act_ref, slope_ref):
    stats = statistics(sh, x_ref)

    def activate(i):
        place = pl.ds(chunk_start(i, sh.chunk), sh.chunk)
        values, slope = activation(sh, x_ref, place, stats, params)
        act_ref[place, :] = values.astype(jnp.bfloat16)
        slope_ref[place, :] = slope

    over_chunks(sh.chunks, activate)
    return stats


def forward_unit(sh, x_ref, out_ref, params, padded_ref, weight_ref, unit, act_ref=None, slope_ref=None):
    stats = statistics(sh, x_ref)

    def activate(i):
        start = chunk_start(i, sh.chunk)
        place = pl.ds(start, sh.chunk)
        values, slope = activation(sh, x_ref, place, stats, params)
        spread(sh, padded_ref, start, values)
        if act_ref is not None:
            act_ref[place, :] = values.astype(jnp.bfloat16)
            slope_ref[place, :] = slope

    def produce(i):
        start = chunk_start(i, sh.chunk)
        inputs = x_ref[pl.ds(start, sh.chunk), :].astype(jnp.float32)
        z = convolve(sh, padded_ref, start, weight_ref, unit, False)
        out_ref[pl.ds(start, sh.chunk), :] = (inputs + z).astype(jnp.bfloat16)

    over_chunks(sh.chunks, activate)
    over_chunks(sh.chunks, produce)
    return stats


def backward_unit(sh, x_ref, up_ref, grad_ref, params, known, scratch, weight_ref, unit, keep_ref, send_ref, core):
    padded_ref, pre_grad_ref, slab_ref = scratch
    act_ref, slope_ref, (mean, inv_std) = known
    factor, _ = params
    space = lax.axis_index("space")
    zero = jnp.zeros((8, sh.channels), jnp.float32)

    def place_upstream(i):
        start = chunk_start(i, sh.chunk)
        spread(sh, padded_ref, start, up_ref[pl.ds(start, sh.chunk), :].astype(jnp.float32))

    def differentiate(i, sums):
        start = chunk_start(i, sh.chunk)
        rows = pl.ds(start, sh.chunk)
        normed = (x_ref[rows, :].astype(jnp.float32) - mean) * inv_std
        pre_grad = convolve(sh, padded_ref, start, weight_ref, unit, True) * slope_ref[rows, :]
        pre_grad_ref[rows, :] = pre_grad
        return (sums[0] + fold_rows(pre_grad), sums[1] + fold_rows(pre_grad * normed))

    over_chunks(sh.chunks, place_upstream)
    if sh.chunks == 1:
        sums = differentiate(0, (zero, zero))
    else:
        sums = lax.fori_loop(0, sh.chunks, differentiate, (zero, zero))
    sum_grad, sum_cross = column(sums[0]), column(sums[1])
    means = group_sums(stack_rows(factor * sum_grad, factor * sum_cross), sh.width) / sh.entries
    center, tilt = means[0:1], means[1:2]

    def finish(i):
        rows = pl.ds(chunk_start(i, sh.chunk), sh.chunk)
        normed = (x_ref[rows, :].astype(jnp.float32) - mean) * inv_std
        back = factor * pre_grad_ref[rows, :] - center - normed * tilt
        grad_ref[rows, :] = (up_ref[rows, :].astype(jnp.float32) + inv_std * back).astype(jnp.bfloat16)

    over_chunks(sh.chunks, finish)
    first_row = space * sh.slab
    first_tap = jnp.minimum(first_row // sh.channels, 9 - sh.taps)
    offset = pl.multiple_of(first_row - first_tap * sh.channels, 8)

    def products(i):
        start = chunk_start(i, sh.chunk)
        blocks = []
        for t in range(sh.taps):
            tap = first_tap + t
            row, col = 2 - tap // 3, 2 - tap % 3
            blocks.append(padded_ref[col, pl.ds(pl.multiple_of(start + row * sh.cols, 16), sh.chunk), :])
        return lax.dot_general(
            act_ref[pl.ds(start, sh.chunk), :],
            jnp.concatenate(blocks, axis=1),
            (((0,), (0,)), ((), ())),
            preferred_element_type=jnp.float32,
        )

    def place_products(i, add):
        values = products(i)
        for t in range(sh.taps):
            place = slice(t * sh.channels, (t + 1) * sh.channels)
            slab_ref[place, :] = values[:, place] + (slab_ref[place, :] if add else 0.0)

    if sh.chunks == 1:
        place_products(0, False)
    else:
        slab_ref[...] = jnp.zeros(slab_ref.shape, jnp.float32)
        over_chunks(sh.chunks, lambda i: place_products(i, True))
    mine = slab_ref[pl.ds(offset, sh.slab), :]
    rows = grad_ref[pl.ds(pl.multiple_of(space * sh.own_rows, sh.own_rows), sh.own_rows), :]
    sums = stack_rows(sum_grad, sum_cross)

    def write(ref):
        ref[0 : sh.slab, :] = mine
        ref[sh.slab : sh.slab + sh.own_rows, :] = rows.astype(jnp.float32)
        ref[sh.slab + sh.own_rows : sh.pack, :] = sums

    @pl.when(core == unit)
    def _():
        write(keep_ref)

    @pl.when(core != unit)
    def _():
        write(send_ref)


def place_of():
    index = lax.axis_index("segment")
    return (index // PAIR, index % PAIR)


def unit_params(params_ref, unit):
    return (params_ref[2 * unit : 2 * unit + 1, :], params_ref[2 * unit + 1 : 2 * unit + 2, :])


def sinusoid_of(time, base):
    half = base // 2
    lanes = lax.broadcasted_iota(jnp.int32, (time.shape[0], base), 1)
    power = jnp.where(lanes < half, lanes, lanes - half).astype(jnp.float32)
    angle = time * jnp.exp(-math.log(10000.0) * power / half)
    turns = jnp.floor(angle * (2.0 / math.pi) + 0.5)
    rest = ((angle - turns * 1.5703125) - turns * 4.83751296997e-4) - turns * 7.54978995489e-8
    square = rest * rest
    sine = rest + rest * square * (
        -1.6666654611e-1 + square * (8.3321608736e-3 - square * 1.9515295891e-4)
    )
    cosine = 1.0 - 0.5 * square + square * square * (
        4.166664568298827e-2 + square * (-1.388731625493765e-3 + square * 2.443315711809948e-5)
    )
    quarter = turns.astype(jnp.int32) + jnp.where(lanes < half, 1, 0)
    value = jnp.where(quarter % 2 == 1, cosine, sine)
    return jnp.where((quarter // 2) % 2 == 1, -value, value).astype(jnp.bfloat16)


def start_all(pairs, sems):
    copies = [pltpu.make_async_copy(a, b, sems.at[i]) for i, (a, b) in enumerate(pairs)]
    for copy in copies:
        copy.start()
    return copies


def embed_kernel(times_ref, labels_ref, table_hbm, time_weight_hbm, embedded_ref, table_ref, time_weight_ref, sems):
    pairs = [(time_weight_hbm, time_weight_ref)]
    pairs += [(table_hbm.at[pl.ds(labels_ref[i] // 8, 1)], table_ref.at[pl.ds(i, 1)]) for i in range(PAIR)]
    copies = start_all(pairs, sems)
    spot = lax.broadcasted_iota(jnp.int32, (16, 1), 0)
    time = jnp.where(spot % 2 == 0, times_ref[0], times_ref[1]).astype(jnp.float32)
    sinusoid = sinusoid_of(time, time_weight_ref.shape[0])

    def label_row(image):
        block = table_ref[image].astype(jnp.float32)
        row = lax.broadcasted_iota(jnp.int32, block.shape, 0)
        return column(jnp.where(row == labels_ref[image] % 8, block, 0.0))

    for copy in copies:
        copy.wait()
    timed = jnp.dot(sinusoid, time_weight_ref[...], preferred_element_type=jnp.float32)
    timed = timed + jnp.where(spot % 2 == 0, label_row(0), label_row(1))
    embedded_ref[...] = (timed * sigmoid(timed)).astype(jnp.bfloat16)


def modulate_kernel(embedded_hbm, mod_weight_hbm, bias_hbm, gain_hbm, keep_ref, send_ref, *scratch):
    embedded_ref, mod_weight_ref, bias_ref, gain_ref, sems = scratch
    core = lax.axis_index("segment") % PAIR
    copies = start_all(zip((embedded_hbm, mod_weight_hbm, bias_hbm, gain_hbm), scratch[:4]), sems)
    for copy in copies:
        copy.wait()
    modulation = jnp.dot(embedded_ref[...], mod_weight_ref[...], preferred_element_type=jnp.float32) + bias_ref[...]
    channels = gain_ref.shape[1]
    factor = gain_ref[...] * (1.0 + modulation[:, :channels])
    shift = modulation[:, channels:]
    first = stack_rows(factor[0:1], shift[0:1])
    second = stack_rows(factor[1:2], shift[1:2])
    keep_ref[...] = jnp.where(core == 0, first, second)
    send_ref[...] = jnp.where(core == 0, second, first)


def layout_kernel(own_any, other_any, mod_keep_any, mod_other_any, weights_ref, params_ref, mods_ref, sems):
    core = lax.axis_index("segment") % PAIR
    pairs = [(mod_keep_any, mods_ref.at[core]), (mod_other_any, mods_ref.at[1 - core])]
    pairs += [(own_any, weights_ref.at[core]), (other_any, weights_ref.at[1 - core])]
    copies = start_all(pairs, sems)
    for copy in copies[:PAIR]:
        copy.wait()
    params_ref[0:2, :] = mods_ref[0, 0:2, :]
    params_ref[2:4, :] = mods_ref[1, 0:2, :]
    params_ref[4:8, :] = jnp.zeros((4, params_ref.shape[1]), jnp.float32)
    for copy in copies[PAIR:]:
        copy.wait()


def assemble(sh, blocks_ref, order, image_ref):
    space = lax.axis_index("space")
    for k, bits in enumerate(order):
        start = pl.multiple_of((space ^ bits) * sh.own_rows, sh.own_rows)
        image_ref[pl.ds(start, sh.own_rows), :] = blocks_ref[k]


def forward_kernel(sh, active_stage, orders, *refs):
    if orders:
        near_ref, far_ref, params_ref, weights, x_ref = refs[:5]
        assemble(sh, near_ref, orders[0], x_ref)
        assemble(sh, far_ref, orders[1], x_ref)
        refs = refs[5:]
    else:
        x_ref, params_ref, weights = refs[:3]
        refs = refs[3:]
    middle_ref, out_ref, padded_ref = refs
    stage, _ = place_of()

    @pl.when(stage == active_stage)
    def _():
        clear_edges(sh, padded_ref)
        forward_unit(sh, x_ref, middle_ref, unit_params(params_ref, 0), padded_ref, weights, 0)
        forward_unit(sh, middle_ref, out_ref, unit_params(params_ref, 1), padded_ref, weights, 1)


def note_kernel(sh, active_stage, x_ref, middle_ref, params_ref, *refs):
    act_ref, slope_ref, stats_ref = refs[-3:]
    stage, _ = place_of()

    @pl.when(stage == active_stage)
    def _():
        for unit, source in enumerate((x_ref, middle_ref)):
            stats = note_unit(sh, source, unit_params(params_ref, unit), act_ref.at[unit], slope_ref.at[unit])
            stats_ref[unit] = stack_rows(*stats)


def backward_kernel(sh, active_stage, first, *refs):
    if first:
        x_ref, up_ref, params_ref, weights = refs[:4]
        refs = refs[4:]
    else:
        x_ref, middle_ref, up_ref, params_ref, weights, act_ref, slope_ref, stats_ref = refs[:8]
        refs = refs[10:]
    keep_ref, send_ref, grad_ref = refs[:3]
    padded_ref, pre_grad_ref, slab_ref, between_ref = refs[3:7]
    if first:
        middle_ref, act_ref, slope_ref = refs[7:]
    stage, core = place_of()

    @pl.when(stage == active_stage)
    def _():
        clear_edges(sh, padded_ref)
        params = [unit_params(params_ref, unit) for unit in range(PAIR)]
        acts, slopes = [[ref.at[unit] for unit in range(PAIR)] for ref in (act_ref, slope_ref)]
        if first:
            early = forward_unit(sh, x_ref, middle_ref, params[0], padded_ref, weights, 0, acts[0], slopes[0])
            stats = [early, note_unit(sh, middle_ref, params[1], acts[1], slopes[1])]
        else:
            stats = [(stats_ref[unit, 0:1, :], stats_ref[unit, 1:2, :]) for unit in range(PAIR)]
        known = list(zip(acts, slopes, stats))
        scratch = (padded_ref, pre_grad_ref, slab_ref)
        outs = (keep_ref, send_ref, core)
        backward_unit(sh, middle_ref, up_ref, between_ref, params[1], known[1], scratch, weights, 1, *outs)
        backward_unit(sh, x_ref, between_ref, grad_ref, params[0], known[0], scratch, weights, 0, *outs)


def finish_kernel(sh, keep_ref, other_ref, embedded_ref, gain_ref, grads_ref, conv_ref, mod_ref):
    core = lax.axis_index("segment") % PAIR
    conv_ref[...] = keep_ref[0 : sh.slab, :] + other_ref[0 : sh.slab, :]
    rows = slice(sh.slab, sh.slab + sh.own_rows)
    grads_ref[pl.ds(core, 1)] = keep_ref[rows, :].astype(jnp.bfloat16)[None]
    grads_ref[pl.ds(1 - core, 1)] = other_ref[rows, :].astype(jnp.bfloat16)[None]
    base = sh.slab + sh.own_rows

    def mod_rows(ref):
        return jnp.concatenate([gain_ref[...] * ref[base + 1 : base + 2, :], ref[base : base + 1, :]], axis=1)

    own, other = mod_rows(keep_ref), mod_rows(other_ref)
    spot = lax.broadcasted_iota(jnp.int32, (16, own.shape[1]), 0)
    values = jnp.where(spot % 2 == core, own, other)
    high = values.astype(jnp.bfloat16).astype(jnp.float32)
    rest = values - high
    middle = rest.astype(jnp.bfloat16).astype(jnp.float32)
    low = rest - middle
    part = spot // 2
    pieces = jnp.where(part == 0, high, jnp.where(part == 1, middle, jnp.where(part == 2, low, 0.0)))
    mod_ref[...] = lax.dot_general(
        embedded_ref[...],
        pieces.astype(jnp.bfloat16),
        (((0,), (0,)), ((), ())),
        preferred_element_type=jnp.float32,
    )


def shards(
    x_in,
    out_cotangent,
    timesteps,
    labels,
    time_weight,
    label_table,
    conv_weight,
    mod_weight,
    mod_bias,
    norm_gain,
):
    segments, spaces = lax.axis_size("segment"), lax.axis_size("space")
    stages = segments // PAIR
    stage, core = place_of()
    images, row_count, cols, channels = x_in.shape
    sh = Shape(row_count * spaces, cols, channels, spaces)
    f32, bf16 = jnp.float32, jnp.bfloat16

    def call(body, ins, outs, scratch=(), limit=CHAIN_LIMIT, cost=None, aliases={}):
        return pl.pallas_call(
            body,
            out_shape=outs,
            in_specs=ins,
            out_specs=[VMEM] * len(outs),
            scratch_shapes=list(scratch),
            input_output_aliases=aliases,
            compiler_params=pltpu.CompilerParams(vmem_limit_bytes=limit),
            cost_estimate=cost,
        )

    shape = jax.ShapeDtypeStruct
    swap = [(i, i ^ 1) for i in range(segments)]
    weight = conv_weight.reshape(9 * channels, channels)
    other_weight = lax.ppermute(weight, "segment", swap)
    ends = jnp.where(stage == 0, x_in, out_cotangent)
    near = lax.dynamic_index_in_dim(ends, core, 0, keepdims=False).reshape(1, sh.own_rows, channels)
    table = label_table.reshape(-1, 8, label_table.shape[1])
    width = time_weight.shape[1]
    some = pl.CostEstimate(flops=1 << 20, bytes_accessed=4 << 20, transcendentals=0)
    order, bit = [0], spaces // 2
    waiting = []
    while True:
        far = lax.ppermute(near, "space", [(i, i ^ bit) for i in range(spaces)])
        if not waiting:
            (embedded,) = call(
                embed_kernel,
                [SMEM, SMEM, ANY, ANY],
                [shape((16, width), bf16)],
                [
                    pltpu.VMEM((PAIR, 8, width), bf16),
                    pltpu.VMEM(time_weight.shape, bf16),
                    pltpu.SemaphoreType.DMA((PAIR + 1,)),
                ],
                PREPARE_LIMIT,
                some,
            )(timesteps, labels, table, time_weight)
            waiting = [embedded]
            far, embedded = lax.optimization_barrier((far, embedded))
        elif len(waiting) == 1:
            operands = (embedded, mod_weight[0], mod_bias, norm_gain)
            mod_keep, mod_send = call(
                modulate_kernel,
                [ANY] * 4,
                [shape((8, channels), f32)] * 2,
                [pltpu.VMEM(value.shape, value.dtype) for value in operands] + [pltpu.SemaphoreType.DMA((4,))],
                PREPARE_LIMIT,
                some,
            )(*operands)
            waiting.append(mod_keep)
            far, mod_keep, mod_send = lax.optimization_barrier((far, mod_keep, mod_send))
        far_order = [k ^ bit for k in order]
        if bit == 1:
            break
        near = jnp.concatenate([near, far])
        order, bit = order + far_order, bit // 2
    mod_other = lax.ppermute(mod_send, "segment", swap)
    weights, params = call(
        layout_kernel,
        [ANY] * 4,
        [shape((PAIR, 9 * channels, channels), bf16), shape((8, channels), f32)],
        [pltpu.VMEM((PAIR, 8, channels), f32), pltpu.SemaphoreType.DMA((2 * PAIR,))],
        cost=some,
    )(weight, other_weight, mod_keep, mod_other)

    image_shape = shape((sh.pixels, channels), bf16)
    pack_shape = shape((sh.pack, channels), f32)
    common = [pltpu.VMEM((3, sh.padded, channels), bf16)]

    def hop(value, source, target):
        pairs = [(PAIR * source + k, PAIR * target + k) for k in range(PAIR)]
        return lax.ppermute(value, "segment", pairs + [(b, a) for a, b in pairs])

    image, middle, out = call(
        functools.partial(forward_kernel, sh, 0, (order, far_order)),
        [VMEM] * 4,
        [image_shape] * 3,
        common,
    )(near, far, params, weights)
    entering, middles = [image, hop(out, 0, 1)], [middle]
    for active in range(1, stages - 1):
        middle, out = call(
            functools.partial(forward_kernel, sh, active, None),
            [VMEM] * 3,
            [image_shape, image_shape],
            common,
        )(entering[active], params, weights)
        middles.append(middle)
        entering.append(hop(out, active, active + 1))

    noted = []
    for active in range(stages - 1):
        noted = call(
            functools.partial(note_kernel, sh, active),
            [VMEM] * (3 + len(noted)),
            [
                shape((PAIR, sh.pixels, channels), bf16),
                shape((PAIR, sh.pixels, channels), f32),
                shape((PAIR, 8, channels), f32),
            ],
            cost=some,
            aliases={3 + k: k for k in range(len(noted))},
        )(entering[active], middles[active], params, *noted)

    scratch = common + [
        pltpu.VMEM((sh.pixels, channels), f32),
        pltpu.VMEM((sh.taps * channels, channels), f32),
        pltpu.VMEM((sh.pixels, channels), bf16),
    ]
    outs = [pack_shape, pack_shape, image_shape]
    keep, send, grad = call(
        functools.partial(backward_kernel, sh, stages - 1, True),
        [VMEM] * 4,
        outs,
        scratch
        + [
            pltpu.VMEM((sh.pixels, channels), bf16),
            pltpu.VMEM((PAIR, sh.pixels, channels), bf16),
            pltpu.VMEM((PAIR, sh.pixels, channels), f32),
        ],
    )(entering[stages - 1], image, params, weights)
    for active in range(stages - 2, -1, -1):
        upstream = hop(grad[0] if isinstance(grad, list) else grad, active + 1, active)
        last = active == 0
        keep, send, *grad = call(
            functools.partial(backward_kernel, sh, active, False),
            [VMEM] * 10,
            outs[:2] if last else outs,
            scratch[-1:] + scratch if last else scratch,
            aliases={8: 0, 9: 1},
        )(entering[active], middles[active], upstream, params, weights, *noted, keep, send)
    other = lax.ppermute(send, "segment", swap)
    grads, conv_grad, mod_grad = call(
        functools.partial(finish_kernel, sh),
        [VMEM] * 4,
        [
            shape((images, sh.own_rows, channels), bf16),
            shape((sh.slab, channels), f32),
            shape((time_weight.shape[1], 2 * channels), f32),
        ],
    )(keep, other, embedded, norm_gain)
    return (grads.reshape(1, images, row_count, cols, channels), conv_grad[None], mod_grad[None])


def solution(mesh):
    placed = (
        P(None, "space", None, None),
        P(None, "space", None, None),
        P(),
        P(),
        P(),
        P(),
        P("segment", None, None, None, None),
        P("segment", None, None),
        P("segment", None),
        P("segment", None),
    )
    return jax.shard_map(
        shards,
        mesh=mesh,
        in_specs=placed,
        out_specs=(
            P("segment", None, "space", None, None),
            P("segment", "space", None),
            P("segment", None, None),
        ),
        check_vma=False,
    )
```

```python
import functools
import math

import jax
import jax.numpy as jnp
from jax import lax
from jax.experimental import pallas as pl
from jax.experimental.pallas import tpu as pltpu
from jax.sharding import PartitionSpec as P

GROUPS = 32
EPSILON = 1e-05
PAIR = 2
MOD_PARTS = 4
PREPARE_LIMIT = 60 << 20
CHAIN_LIMIT = 48 << 20
VMEM = pl.BlockSpec(memory_space=pltpu.VMEM)
SMEM = pl.BlockSpec(memory_space=pltpu.SMEM)
ANY = pl.BlockSpec(memory_space=pl.ANY)


def sigmoid(values):
    return 1.0 / (1.0 + jnp.exp(-values))


def over_chunks(count, body):
    if count == 1:
        body(0)
    else:

        def step(i, carry):
            body(i)
            return carry

        lax.fori_loop(0, count, step, 0)


def chunk_start(i, size):
    return 0 if isinstance(i, int) else pl.multiple_of(i * size, size)


def fold_rows(values):
    return jnp.sum(values.reshape(values.shape[0] // 8, 8, values.shape[1]), axis=0)


def column(rows):
    return jnp.sum(rows, axis=0, keepdims=True)


def group_sums(rows, width):
    lanes = lax.broadcasted_iota(jnp.int32, rows.shape, 1)
    size = rows.shape[1]
    step = 1
    while step < width:
        ahead = pltpu.roll(rows, size - step, 1)
        behind = pltpu.roll(rows, step, 1)
        rows = rows + jnp.where((lanes & step) == 0, ahead, behind)
        step *= 2
    return rows


def stack_rows(first, second):
    spot = lax.broadcasted_iota(jnp.int32, (8, first.shape[1]), 0)
    return jnp.where(spot == 0, first, jnp.where(spot == 1, second, 0.0))


class Shape:
    def __init__(self, height, cols, channels, space_count):
        self.cols, self.channels = cols, channels
        self.pixels = height * cols
        self.chunk = cols * max(1, min(self.pixels, 256) // cols)
        self.chunks = self.pixels // self.chunk
        self.width = channels // GROUPS
        self.entries = float(self.pixels * self.width)
        self.padded = self.pixels + 2 * cols
        self.own_rows = height // space_count * cols
        self.slab = 9 * channels // space_count
        self.taps = min(9, (self.slab - 1) // channels + 2)
        self.pack = self.slab + self.own_rows + 8
        self.limit = (12 << 20) + self.pixels * channels * 40


def statistics(sh, x_ref):
    zero = jnp.zeros((8, sh.channels), jnp.float32)

    def add(i, sums):
        part = x_ref[pl.ds(chunk_start(i, sh.chunk), sh.chunk), :].astype(jnp.float32)
        return (sums[0] + fold_rows(part), sums[1] + fold_rows(part * part))

    if sh.chunks == 1:
        one, two = add(0, (zero, zero))
    else:
        one, two = lax.fori_loop(0, sh.chunks, add, (zero, zero))
    total = group_sums(stack_rows(column(one), column(two)), sh.width) / sh.entries
    mean = total[0:1]
    return (mean, lax.rsqrt(total[1:2] - mean * mean + EPSILON))


def clear_edges(sh, padded_ref):
    zero = jnp.zeros((3, sh.cols, sh.channels), padded_ref.dtype)
    padded_ref[:, 0 : sh.cols, :] = zero
    padded_ref[:, sh.pixels + sh.cols : sh.padded, :] = zero


def spread(sh, padded_ref, start, values):
    place = pl.ds(start + sh.cols, sh.chunk)
    spot = lax.broadcasted_iota(jnp.int32, values.shape, 0) % sh.cols
    padded_ref[0, place, :] = jnp.where(spot == 0, 0.0, pltpu.roll(values, 1, 0)).astype(jnp.bfloat16)
    padded_ref[1, place, :] = values.astype(jnp.bfloat16)
    padded_ref[2, place, :] = jnp.where(
        spot == sh.cols - 1, 0.0, pltpu.roll(values, sh.chunk - 1, 0)
    ).astype(jnp.bfloat16)


def convolve(sh, padded_ref, start, weight_ref, unit, backward):
    total = None
    for p in range(3):
        for q in range(3):
            row, col = (2 - p, 2 - q) if backward else (p, q)
            block = padded_ref[col, pl.ds(start + row * sh.cols, sh.chunk), :]
            tap = (3 * p + q) * sh.channels
            weight = weight_ref[unit, tap : tap + sh.channels, :]
            part = lax.dot_general(
                block,
                weight,
                (((1,), (1 if backward else 0,)), ((), ())),
                preferred_element_type=jnp.float32,
            )
            total = part if total is None else total + part
    return total


def activation(sh, x_ref, place, stats, params):
    (mean, inv_std), (factor, shift) = stats, params
    pre = (x_ref[place, :].astype(jnp.float32) - mean) * inv_std * factor + shift
    sigma = sigmoid(pre)
    return pre * sigma, sigma * (1.0 + pre * (1.0 - sigma))


def note_unit(sh, x_ref, params, act_ref, slope_ref):
    stats = statistics(sh, x_ref)

    def activate(i):
        place = pl.ds(chunk_start(i, sh.chunk), sh.chunk)
        values, slope = activation(sh, x_ref, place, stats, params)
        act_ref[place, :] = values.astype(jnp.bfloat16)
        slope_ref[place, :] = slope

    over_chunks(sh.chunks, activate)
    return stats


def forward_unit(sh, x_ref, out_ref, params, padded_ref, weight_ref, unit, act_ref=None, slope_ref=None):
    stats = statistics(sh, x_ref)

    def activate(i):
        start = chunk_start(i, sh.chunk)
        place = pl.ds(start, sh.chunk)
        values, slope = activation(sh, x_ref, place, stats, params)
        spread(sh, padded_ref, start, values)
        if act_ref is not None:
            act_ref[place, :] = values.astype(jnp.bfloat16)
            slope_ref[place, :] = slope

    def produce(i):
        start = chunk_start(i, sh.chunk)
        inputs = x_ref[pl.ds(start, sh.chunk), :].astype(jnp.float32)
        z = convolve(sh, padded_ref, start, weight_ref, unit, False)
        out_ref[pl.ds(start, sh.chunk), :] = (inputs + z).astype(jnp.bfloat16)

    over_chunks(sh.chunks, activate)
    over_chunks(sh.chunks, produce)
    return stats


def place_upstream(sh, up_ref, padded_ref):
    def place(i):
        start = chunk_start(i, sh.chunk)
        spread(sh, padded_ref, start, up_ref[pl.ds(start, sh.chunk), :].astype(jnp.float32))

    over_chunks(sh.chunks, place)


def backward_unit(sh, x_ref, up_ref, grad_ref, params, known, padded_ref, pre_grad_ref, weight_ref, unit):
    slope_ref, (mean, inv_std) = known
    factor, _ = params
    zero = jnp.zeros((8, sh.channels), jnp.float32)

    def differentiate(i, sums):
        start = chunk_start(i, sh.chunk)
        rows = pl.ds(start, sh.chunk)
        normed = (x_ref[rows, :].astype(jnp.float32) - mean) * inv_std
        pre_grad = convolve(sh, padded_ref, start, weight_ref, unit, True) * slope_ref[rows, :]
        pre_grad_ref[rows, :] = pre_grad
        return (sums[0] + fold_rows(pre_grad), sums[1] + fold_rows(pre_grad * normed))

    place_upstream(sh, up_ref, padded_ref)
    if sh.chunks == 1:
        sums = differentiate(0, (zero, zero))
    else:
        sums = lax.fori_loop(0, sh.chunks, differentiate, (zero, zero))
    sum_grad, sum_cross = column(sums[0]), column(sums[1])
    means = group_sums(stack_rows(factor * sum_grad, factor * sum_cross), sh.width) / sh.entries
    center, tilt = means[0:1], means[1:2]

    def finish(i):
        rows = pl.ds(chunk_start(i, sh.chunk), sh.chunk)
        normed = (x_ref[rows, :].astype(jnp.float32) - mean) * inv_std
        back = factor * pre_grad_ref[rows, :] - center - normed * tilt
        grad_ref[rows, :] = (up_ref[rows, :].astype(jnp.float32) + inv_std * back).astype(jnp.bfloat16)

    over_chunks(sh.chunks, finish)
    return stack_rows(sum_grad, sum_cross)


def weight_products(sh, padded_ref, act_ref, slab_ref, grad_ref, sums, unit, keep_ref, send_ref):
    core = lax.axis_index("segment") % PAIR
    space = lax.axis_index("space")
    first_row = space * sh.slab
    first_tap = jnp.minimum(first_row // sh.channels, 9 - sh.taps)
    offset = pl.multiple_of(first_row - first_tap * sh.channels, 8)
    for t in range(sh.taps):
        tap = first_tap + t
        row, col = 2 - tap // 3, 2 - tap % 3
        place = pl.ds(t * sh.channels, sh.channels)

        def product(i):
            start = chunk_start(i, sh.chunk)
            block = padded_ref[col, pl.ds(pl.multiple_of(start + row * sh.cols, 16), sh.chunk), :]
            return lax.dot_general(
                act_ref[pl.ds(start, sh.chunk), :],
                block,
                (((0,), (0,)), ((), ())),
                preferred_element_type=jnp.float32,
            )

        if sh.chunks == 1:
            slab_ref[place, :] = product(0)
        else:
            slab_ref[place, :] = jnp.zeros((sh.channels, sh.channels), jnp.float32)

            def accumulate(i):
                slab_ref[place, :] += product(i)

            over_chunks(sh.chunks, accumulate)
    mine = slab_ref[pl.ds(offset, sh.slab), :]
    rows = grad_ref[pl.ds(pl.multiple_of(space * sh.own_rows, sh.own_rows), sh.own_rows), :]

    def write(ref):
        ref[0 : sh.slab, :] = mine
        ref[sh.slab : sh.slab + sh.own_rows, :] = rows.astype(jnp.float32)
        ref[sh.slab + sh.own_rows : sh.pack, :] = sums

    @pl.when(core == unit)
    def _():
        write(keep_ref)

    @pl.when(core != unit)
    def _():
        write(send_ref)


def place_of():
    index = lax.axis_index("segment")
    return (index // PAIR, index % PAIR)


def unit_params(params_ref, unit):
    return (params_ref[2 * unit : 2 * unit + 1, :], params_ref[2 * unit + 1 : 2 * unit + 2, :])


def sinusoid_of(time, base):
    half = base // 2
    lanes = lax.broadcasted_iota(jnp.int32, (time.shape[0], base), 1)
    power = jnp.where(lanes < half, lanes, lanes - half).astype(jnp.float32)
    angle = time * jnp.exp(-math.log(10000.0) * power / half)
    turns = jnp.floor(angle * (2.0 / math.pi) + 0.5)
    rest = ((angle - turns * 1.5703125) - turns * 4.83751296997e-4) - turns * 7.54978995489e-8
    square = rest * rest
    sine = rest + rest * square * (
        -1.6666654611e-1 + square * (8.3321608736e-3 - square * 1.9515295891e-4)
    )
    cosine = 1.0 - 0.5 * square + square * square * (
        4.166664568298827e-2 + square * (-1.388731625493765e-3 + square * 2.443315711809948e-5)
    )
    quarter = turns.astype(jnp.int32) + jnp.where(lanes < half, 1, 0)
    value = jnp.where(quarter % 2 == 1, cosine, sine)
    return jnp.where((quarter // 2) % 2 == 1, -value, value).astype(jnp.bfloat16)


def start_all(pairs, sems):
    copies = [pltpu.make_async_copy(a, b, sems.at[i]) for i, (a, b) in enumerate(pairs)]
    for copy in copies:
        copy.start()
    return copies


def embed_kernel(times_ref, labels_ref, table_hbm, time_weight_hbm, embedded_ref, table_ref, time_weight_ref, sems):
    pairs = [(time_weight_hbm, time_weight_ref)]
    pairs += [(table_hbm.at[pl.ds(labels_ref[i] // 8, 1)], table_ref.at[pl.ds(i, 1)]) for i in range(PAIR)]
    copies = start_all(pairs, sems)
    spot = lax.broadcasted_iota(jnp.int32, (16, 1), 0)
    time = jnp.where(spot % 2 == 0, times_ref[0], times_ref[1]).astype(jnp.float32)
    sinusoid = sinusoid_of(time, time_weight_ref.shape[0])

    def label_row(image):
        block = table_ref[image].astype(jnp.float32)
        row = lax.broadcasted_iota(jnp.int32, block.shape, 0)
        return column(jnp.where(row == labels_ref[image] % 8, block, 0.0))

    for copy in copies:
        copy.wait()
    timed = jnp.dot(sinusoid, time_weight_ref[...], preferred_element_type=jnp.float32)
    timed = timed + jnp.where(spot % 2 == 0, label_row(0), label_row(1))
    embedded_ref[...] = (timed * sigmoid(timed)).astype(jnp.bfloat16)


def modulate_kernel(embedded_hbm, mod_weight_hbm, bias_hbm, gain_hbm, keep_ref, send_ref, *scratch):
    embedded_ref, mod_weight_ref, bias_ref, gain_ref, sems = scratch
    core = lax.axis_index("segment") % PAIR
    copies = start_all(zip((embedded_hbm, mod_weight_hbm, bias_hbm, gain_hbm), scratch[:4]), sems)
    for copy in copies:
        copy.wait()
    modulation = jnp.dot(embedded_ref[...], mod_weight_ref[...], preferred_element_type=jnp.float32) + bias_ref[...]
    channels = gain_ref.shape[1]
    factor = gain_ref[...] * (1.0 + modulation[:, :channels])
    shift = modulation[:, channels:]
    first = stack_rows(factor[0:1], shift[0:1])
    second = stack_rows(factor[1:2], shift[1:2])
    keep_ref[...] = jnp.where(core == 0, first, second)
    send_ref[...] = jnp.where(core == 0, second, first)


def layout_kernel(own_any, other_any, mod_keep_any, mod_other_any, weights_ref, params_ref, mods_ref, sems):
    core = lax.axis_index("segment") % PAIR
    pairs = [(mod_keep_any, mods_ref.at[core]), (mod_other_any, mods_ref.at[1 - core])]
    pairs += [(own_any, weights_ref.at[core]), (other_any, weights_ref.at[1 - core])]
    copies = start_all(pairs, sems)
    for copy in copies[:PAIR]:
        copy.wait()
    params_ref[0:2, :] = mods_ref[0, 0:2, :]
    params_ref[2:4, :] = mods_ref[1, 0:2, :]
    params_ref[4:8, :] = jnp.zeros((4, params_ref.shape[1]), jnp.float32)
    for copy in copies[PAIR:]:
        copy.wait()


def assemble(sh, blocks_ref, order, image_ref):
    space = lax.axis_index("space")
    for k, bits in enumerate(order):
        start = pl.multiple_of((space ^ bits) * sh.own_rows, sh.own_rows)
        image_ref[pl.ds(start, sh.own_rows), :] = blocks_ref[k]


def forward_kernel(sh, active_stage, orders, *refs):
    if orders:
        near_ref, far_ref, params_ref, weights, x_ref = refs[:5]
        assemble(sh, near_ref, orders[0], x_ref)
        assemble(sh, far_ref, orders[1], x_ref)
        refs = refs[5:]
    else:
        x_ref, params_ref, weights = refs[:3]
        refs = refs[3:]
    middle_ref, out_ref, padded_ref = refs
    stage, _ = place_of()

    @pl.when(stage == active_stage)
    def _():
        clear_edges(sh, padded_ref)
        forward_unit(sh, x_ref, middle_ref, unit_params(params_ref, 0), padded_ref, weights, 0)
        forward_unit(sh, middle_ref, out_ref, unit_params(params_ref, 1), padded_ref, weights, 1)


def note_kernel(sh, active_stage, x_ref, middle_ref, params_ref, *refs):
    act_ref, slope_ref, stats_ref = refs[-3:]
    stage, _ = place_of()

    @pl.when(stage == active_stage)
    def _():
        for unit, source in enumerate((x_ref, middle_ref)):
            stats = note_unit(sh, source, unit_params(params_ref, unit), act_ref.at[unit], slope_ref.at[unit])
            stats_ref[unit] = stack_rows(*stats)


def turn_kernel(sh, active_stage, x_ref, up_ref, params_ref, weights, *refs):
    grad_ref, between_ref, act_ref, sums_ref, padded_ref, pre_grad_ref, middle_ref, slope_ref = refs
    stage, _ = place_of()

    @pl.when(stage == active_stage)
    def _():
        clear_edges(sh, padded_ref)
        params = [unit_params(params_ref, unit) for unit in range(PAIR)]
        acts, slopes = [[ref.at[unit] for unit in range(PAIR)] for ref in (act_ref, slope_ref)]
        first = forward_unit(sh, x_ref, middle_ref, params[0], padded_ref, weights, 0, acts[0], slopes[0])
        second = note_unit(sh, middle_ref, params[1], acts[1], slopes[1])
        work = (padded_ref, pre_grad_ref, weights)
        known = (slopes[1], second)
        sums_ref[1] = backward_unit(sh, middle_ref, up_ref, between_ref, params[1], known, *work, 1)
        known = (slopes[0], first)
        sums_ref[0] = backward_unit(sh, x_ref, between_ref, grad_ref, params[0], known, *work, 0)


def products_kernel(sh, active_stage, up_ref, between_ref, grad_ref, act_ref, sums_ref, *refs):
    keep_ref, send_ref, padded_ref, slab_ref = refs
    stage, _ = place_of()

    @pl.when(stage == active_stage)
    def _():
        clear_edges(sh, padded_ref)
        for unit, above, below in ((1, up_ref, between_ref), (0, between_ref, grad_ref)):
            place_upstream(sh, above, padded_ref)
            outs = (keep_ref, send_ref)
            weight_products(sh, padded_ref, act_ref.at[unit], slab_ref, below, sums_ref[unit], unit, *outs)


def backward_kernel(sh, active_stage, *refs):
    x_ref, middle_ref, up_ref, params_ref, weights, act_ref, slope_ref, stats_ref = refs[:8]
    keep_ref, send_ref, grad_ref, padded_ref, pre_grad_ref, slab_ref, between_ref = refs[10:]
    stage, _ = place_of()

    @pl.when(stage == active_stage)
    def _():
        clear_edges(sh, padded_ref)
        for unit, x, above, below in ((1, middle_ref, up_ref, between_ref), (0, x_ref, between_ref, grad_ref)):
            stats = (stats_ref[unit, 0:1, :], stats_ref[unit, 1:2, :])
            known = (slope_ref.at[unit], stats)
            params = unit_params(params_ref, unit)
            sums = backward_unit(sh, x, above, below, params, known, padded_ref, pre_grad_ref, weights, unit)
            outs = (keep_ref, send_ref)
            weight_products(sh, padded_ref, act_ref.at[unit], slab_ref, below, sums, unit, *outs)


def finish_kernel(sh, keep_ref, other_ref, embedded_ref, gain_ref, grads_hbm, conv_hbm, mod_hbm, *scratch):
    grads_ref, conv_ref, mod_ref, sems = scratch
    core = lax.axis_index("segment") % PAIR
    base = sh.slab + sh.own_rows

    def mod_rows(ref):
        return jnp.concatenate([gain_ref[...] * ref[base + 1 : base + 2, :], ref[base : base + 1, :]], axis=1)

    own, other = mod_rows(keep_ref), mod_rows(other_ref)
    spot = lax.broadcasted_iota(jnp.int32, (16, own.shape[1]), 0)
    values = jnp.where(spot % 2 == core, own, other)
    high = values.astype(jnp.bfloat16).astype(jnp.float32)
    rest = values - high
    middle = rest.astype(jnp.bfloat16).astype(jnp.float32)
    low = rest - middle
    part = spot // 2
    pieces = jnp.where(part == 0, high, jnp.where(part == 1, middle, jnp.where(part == 2, low, 0.0)))
    pieces = pieces.astype(jnp.bfloat16)
    copies = []
    size = mod_ref.shape[0] // MOD_PARTS
    for k in range(MOD_PARTS):
        place = slice(k * size, (k + 1) * size)
        mod_ref[place, :] = lax.dot_general(
            embedded_ref[:, place],
            pieces,
            (((0,), (0,)), ((), ())),
            preferred_element_type=jnp.float32,
        )
        copies.append(pltpu.make_async_copy(mod_ref.at[place], mod_hbm.at[place], sems.at[k]))
        copies[-1].start()
    conv_ref[...] = keep_ref[0 : sh.slab, :] + other_ref[0 : sh.slab, :]
    copies.append(pltpu.make_async_copy(conv_ref, conv_hbm, sems.at[MOD_PARTS]))
    copies[-1].start()
    rows = slice(sh.slab, sh.slab + sh.own_rows)
    grads_ref[pl.ds(core, 1)] = keep_ref[rows, :].astype(jnp.bfloat16)[None]
    grads_ref[pl.ds(1 - core, 1)] = other_ref[rows, :].astype(jnp.bfloat16)[None]
    copies.append(pltpu.make_async_copy(grads_ref, grads_hbm, sems.at[MOD_PARTS + 1]))
    copies[-1].start()
    for copy in copies:
        copy.wait()


def shards(
    x_in,
    out_cotangent,
    timesteps,
    labels,
    time_weight,
    label_table,
    conv_weight,
    mod_weight,
    mod_bias,
    norm_gain,
):
    segments, spaces = lax.axis_size("segment"), lax.axis_size("space")
    stages = segments // PAIR
    stage, core = place_of()
    images, row_count, cols, channels = x_in.shape
    sh = Shape(row_count * spaces, cols, channels, spaces)
    f32, bf16 = jnp.float32, jnp.bfloat16

    def call(body, ins, outs, scratch=(), limit=CHAIN_LIMIT, cost=None, aliases={}):
        return pl.pallas_call(
            body,
            out_shape=outs,
            in_specs=ins,
            out_specs=[VMEM] * len(outs),
            scratch_shapes=list(scratch),
            input_output_aliases=aliases,
            compiler_params=pltpu.CompilerParams(vmem_limit_bytes=limit),
            cost_estimate=cost,
        )

    shape = jax.ShapeDtypeStruct
    swap = [(i, i ^ 1) for i in range(segments)]
    weight = conv_weight.reshape(9 * channels, channels)
    other_weight = lax.ppermute(weight, "segment", swap)
    ends = jnp.where(stage == 0, x_in, out_cotangent)
    near = lax.dynamic_index_in_dim(ends, core, 0, keepdims=False).reshape(1, sh.own_rows, channels)
    table = label_table.reshape(-1, 8, label_table.shape[1])
    width = time_weight.shape[1]
    some = pl.CostEstimate(flops=1 << 20, bytes_accessed=4 << 20, transcendentals=0)
    order, bit = [0], spaces // 2
    waiting = []
    while True:
        far = lax.ppermute(near, "space", [(i, i ^ bit) for i in range(spaces)])
        if not waiting:
            (embedded,) = call(
                embed_kernel,
                [SMEM, SMEM, ANY, ANY],
                [shape((16, width), bf16)],
                [
                    pltpu.VMEM((PAIR, 8, width), bf16),
                    pltpu.VMEM(time_weight.shape, bf16),
                    pltpu.SemaphoreType.DMA((PAIR + 1,)),
                ],
                PREPARE_LIMIT,
                some,
            )(timesteps, labels, table, time_weight)
            waiting = [embedded]
            far, embedded = lax.optimization_barrier((far, embedded))
        elif len(waiting) == 1:
            operands = (embedded, mod_weight[0], mod_bias, norm_gain)
            mod_keep, mod_send = call(
                modulate_kernel,
                [ANY] * 4,
                [shape((8, channels), f32)] * 2,
                [pltpu.VMEM(value.shape, value.dtype) for value in operands] + [pltpu.SemaphoreType.DMA((4,))],
                PREPARE_LIMIT,
                some,
            )(*operands)
            waiting.append(mod_keep)
            far, mod_keep, mod_send = lax.optimization_barrier((far, mod_keep, mod_send))
        far_order = [k ^ bit for k in order]
        if bit == 1:
            break
        near = jnp.concatenate([near, far])
        order, bit = order + far_order, bit // 2
    mod_other = lax.ppermute(mod_send, "segment", swap)
    weights, params = call(
        layout_kernel,
        [ANY] * 4,
        [shape((PAIR, 9 * channels, channels), bf16), shape((8, channels), f32)],
        [pltpu.VMEM((PAIR, 8, channels), f32), pltpu.SemaphoreType.DMA((2 * PAIR,))],
        cost=some,
    )(weight, other_weight, mod_keep, mod_other)

    image_shape = shape((sh.pixels, channels), bf16)
    pack_shape = shape((sh.pack, channels), f32)
    common = [pltpu.VMEM((3, sh.padded, channels), bf16)]

    def hop(value, source, target):
        pairs = [(PAIR * source + k, PAIR * target + k) for k in range(PAIR)]
        return lax.ppermute(value, "segment", pairs + [(b, a) for a, b in pairs])

    image, middle, out = call(
        functools.partial(forward_kernel, sh, 0, (order, far_order)),
        [VMEM] * 4,
        [image_shape] * 3,
        common,
    )(near, far, params, weights)
    entering, middles = [image, hop(out, 0, 1)], [middle]
    for active in range(1, stages - 1):
        middle, out = call(
            functools.partial(forward_kernel, sh, active, None),
            [VMEM] * 3,
            [image_shape, image_shape],
            common,
        )(entering[active], params, weights)
        middles.append(middle)
        entering.append(hop(out, active, active + 1))

    noted = []
    for active in range(stages - 1):
        noted = call(
            functools.partial(note_kernel, sh, active),
            [VMEM] * (3 + len(noted)),
            [
                shape((PAIR, sh.pixels, channels), bf16),
                shape((PAIR, sh.pixels, channels), f32),
                shape((PAIR, 8, channels), f32),
            ],
            cost=some,
            aliases={3 + k: k for k in range(len(noted))},
        )(entering[active], middles[active], params, *noted)

    work = common + [pltpu.VMEM((sh.pixels, channels), f32)]
    slab = [pltpu.VMEM((sh.taps * channels, channels), f32)]
    pair_shape = shape((PAIR, sh.pixels, channels), bf16)
    *grad, between, act, sums = call(
        functools.partial(turn_kernel, sh, stages - 1),
        [VMEM] * 4,
        [image_shape, image_shape, pair_shape, shape((PAIR, 8, channels), f32)],
        work + [pltpu.VMEM((sh.pixels, channels), bf16), pltpu.VMEM((PAIR, sh.pixels, channels), f32)],
    )(entering[stages - 1], image, params, weights)
    keep, send = call(
        functools.partial(products_kernel, sh, stages - 1),
        [VMEM] * 5,
        [pack_shape, pack_shape],
        common + slab,
        cost=some,
    )(image, between, grad[0], act, sums)
    for active in range(stages - 2, -1, -1):
        upstream = hop(grad[0], active + 1, active)
        last = active == 0
        spare = [pltpu.VMEM((sh.pixels, channels), bf16)]
        keep, send, *grad = call(
            functools.partial(backward_kernel, sh, active),
            [VMEM] * 10,
            [pack_shape, pack_shape] + ([] if last else [image_shape]),
            (spare if last else []) + work + slab + spare,
            aliases={8: 0, 9: 1},
        )(entering[active], middles[active], upstream, params, weights, *noted, keep, send)
    other = lax.ppermute(send, "segment", swap)
    finals = [
        ((images, sh.own_rows, channels), bf16),
        ((sh.slab, channels), f32),
        ((width, 2 * channels), f32),
    ]
    grads, conv_grad, mod_grad = pl.pallas_call(
        functools.partial(finish_kernel, sh),
        out_shape=[shape(*final) for final in finals],
        in_specs=[VMEM] * 4,
        out_specs=[ANY] * 3,
        scratch_shapes=[pltpu.VMEM(*final) for final in finals] + [pltpu.SemaphoreType.DMA((MOD_PARTS + 2,))],
        compiler_params=pltpu.CompilerParams(vmem_limit_bytes=CHAIN_LIMIT),
    )(keep, other, embedded, norm_gain)
    return (grads.reshape(1, images, row_count, cols, channels), conv_grad[None], mod_grad[None])


def solution(mesh):
    placed = (
        P(None, "space", None, None),
        P(None, "space", None, None),
        P(),
        P(),
        P(),
        P(),
        P("segment", None, None, None, None),
        P("segment", None, None),
        P("segment", None),
        P("segment", None),
    )
    return jax.shard_map(
        shards,
        mesh=mesh,
        in_specs=placed,
        out_specs=(
            P("segment", None, "space", None, None),
            P("segment", "space", None),
            P("segment", None, None),
        ),
        check_vma=False,
    )
```

```python
import functools
import math

import jax
import jax.numpy as jnp
from jax import lax
from jax.experimental import pallas as pl
from jax.experimental.pallas import tpu as pltpu
from jax.sharding import PartitionSpec as P

GROUPS = 32
EPSILON = 1e-05
PAIR = 2
MOD_PARTS = 4
PREPARE_LIMIT = 60 << 20
CHAIN_LIMIT = 48 << 20
VMEM = pl.BlockSpec(memory_space=pltpu.VMEM)
SMEM = pl.BlockSpec(memory_space=pltpu.SMEM)
ANY = pl.BlockSpec(memory_space=pl.ANY)


def sigmoid(values):
    return 1.0 / (1.0 + jnp.exp(-values))


def over_chunks(count, body):
    if count == 1:
        body(0)
    else:

        def step(i, carry):
            body(i)
            return carry

        lax.fori_loop(0, count, step, 0)


def chunk_start(i, size):
    return 0 if isinstance(i, int) else pl.multiple_of(i * size, size)


def fold_rows(values):
    return jnp.sum(values.reshape(values.shape[0] // 8, 8, values.shape[1]), axis=0)


def column(rows):
    return jnp.sum(rows, axis=0, keepdims=True)


def group_sums(rows, width):
    lanes = lax.broadcasted_iota(jnp.int32, rows.shape, 1)
    size = rows.shape[1]
    step = 1
    while step < width:
        ahead = pltpu.roll(rows, size - step, 1)
        behind = pltpu.roll(rows, step, 1)
        rows = rows + jnp.where((lanes & step) == 0, ahead, behind)
        step *= 2
    return rows


def stack_rows(first, second):
    spot = lax.broadcasted_iota(jnp.int32, (8, first.shape[1]), 0)
    return jnp.where(spot == 0, first, jnp.where(spot == 1, second, 0.0))


class Shape:
    def __init__(self, height, cols, channels, space_count):
        self.cols, self.channels = cols, channels
        self.pixels = height * cols
        self.chunk = cols * max(1, min(self.pixels, 256) // cols)
        self.chunks = self.pixels // self.chunk
        self.width = channels // GROUPS
        self.entries = float(self.pixels * self.width)
        self.padded = self.pixels + 2 * cols
        self.own_rows = height // space_count * cols
        self.slab = 9 * channels // space_count
        step = math.gcd(self.slab, channels)
        self.taps = min(9, -(-(channels - step + self.slab) // channels))
        self.pack = self.slab + self.own_rows + 8
        self.limit = (12 << 20) + self.pixels * channels * 40


def statistics(sh, x_ref):
    zero = jnp.zeros((8, sh.channels), jnp.float32)

    def add(i, sums):
        part = x_ref[pl.ds(chunk_start(i, sh.chunk), sh.chunk), :].astype(jnp.float32)
        return (sums[0] + fold_rows(part), sums[1] + fold_rows(part * part))

    if sh.chunks == 1:
        one, two = add(0, (zero, zero))
    else:
        one, two = lax.fori_loop(0, sh.chunks, add, (zero, zero))
    total = group_sums(stack_rows(column(one), column(two)), sh.width) / sh.entries
    mean = total[0:1]
    return (mean, lax.rsqrt(total[1:2] - mean * mean + EPSILON))


def clear_edges(sh, padded_ref):
    zero = jnp.zeros((3, sh.cols, sh.channels), padded_ref.dtype)
    padded_ref[:, 0 : sh.cols, :] = zero
    padded_ref[:, sh.pixels + sh.cols : sh.padded, :] = zero


def spread(sh, padded_ref, start, values):
    place = pl.ds(start + sh.cols, sh.chunk)
    spot = lax.broadcasted_iota(jnp.int32, values.shape, 0) % sh.cols
    padded_ref[0, place, :] = jnp.where(spot == 0, 0.0, pltpu.roll(values, 1, 0)).astype(jnp.bfloat16)
    padded_ref[1, place, :] = values.astype(jnp.bfloat16)
    padded_ref[2, place, :] = jnp.where(
        spot == sh.cols - 1, 0.0, pltpu.roll(values, sh.chunk - 1, 0)
    ).astype(jnp.bfloat16)


def convolve(sh, padded_ref, start, weight_ref, unit, backward):
    total = None
    for p in range(3):
        for q in range(3):
            row, col = (2 - p, 2 - q) if backward else (p, q)
            block = padded_ref[col, pl.ds(start + row * sh.cols, sh.chunk), :]
            tap = (3 * p + q) * sh.channels
            weight = weight_ref[unit, tap : tap + sh.channels, :]
            part = lax.dot_general(
                block,
                weight,
                (((1,), (1 if backward else 0,)), ((), ())),
                preferred_element_type=jnp.float32,
            )
            total = part if total is None else total + part
    return total


def activation(sh, x_ref, place, stats, params):
    (mean, inv_std), (factor, shift) = stats, params
    pre = (x_ref[place, :].astype(jnp.float32) - mean) * inv_std * factor + shift
    sigma = sigmoid(pre)
    return pre * sigma, sigma * (1.0 + pre * (1.0 - sigma))


def note_unit(sh, x_ref, params, act_ref, slope_ref, turned=False):
    stats = statistics(sh, x_ref)

    def activate(i):
        place = pl.ds(chunk_start(i, sh.chunk), sh.chunk)
        values, slope = activation(sh, x_ref, place, stats, params)
        if turned:
            act_ref[:, place] = values.T.astype(jnp.bfloat16)
        else:
            act_ref[place, :] = values.astype(jnp.bfloat16)
        slope_ref[place, :] = slope

    over_chunks(sh.chunks, activate)
    return stats


def forward_unit(sh, x_ref, out_ref, params, padded_ref, weight_ref, unit, act_ref=None, slope_ref=None):
    stats = statistics(sh, x_ref)

    def activate(i):
        start = chunk_start(i, sh.chunk)
        place = pl.ds(start, sh.chunk)
        values, slope = activation(sh, x_ref, place, stats, params)
        spread(sh, padded_ref, start, values)
        if act_ref is not None:
            act_ref[place, :] = values.astype(jnp.bfloat16)
            slope_ref[place, :] = slope

    def produce(i):
        start = chunk_start(i, sh.chunk)
        inputs = x_ref[pl.ds(start, sh.chunk), :].astype(jnp.float32)
        z = convolve(sh, padded_ref, start, weight_ref, unit, False)
        out_ref[pl.ds(start, sh.chunk), :] = (inputs + z).astype(jnp.bfloat16)

    over_chunks(sh.chunks, activate)
    over_chunks(sh.chunks, produce)
    return stats


def own_place(sh):
    return pl.ds(pl.multiple_of(lax.axis_index("space") * sh.own_rows, sh.own_rows), sh.own_rows)


def place_upstream(sh, up_ref, padded_ref):
    def place(i):
        start = chunk_start(i, sh.chunk)
        spread(sh, padded_ref, start, up_ref[pl.ds(start, sh.chunk), :].astype(jnp.float32))

    over_chunks(sh.chunks, place)


def backward_unit(sh, x_ref, up_ref, grad_ref, params, known, padded_ref, pre_grad_ref, weight_ref, unit, own=False, placed=False):
    slope_ref, (mean, inv_std) = known
    factor, _ = params
    zero = jnp.zeros((8, sh.channels), jnp.float32)

    def differentiate(i, sums):
        start = chunk_start(i, sh.chunk)
        rows = pl.ds(start, sh.chunk)
        normed = (x_ref[rows, :].astype(jnp.float32) - mean) * inv_std
        pre_grad = convolve(sh, padded_ref, start, weight_ref, unit, True) * slope_ref[rows, :]
        pre_grad_ref[rows, :] = pre_grad
        return (sums[0] + fold_rows(pre_grad), sums[1] + fold_rows(pre_grad * normed))

    if not placed:
        place_upstream(sh, up_ref, padded_ref)
    if sh.chunks == 1:
        sums = differentiate(0, (zero, zero))
    else:
        sums = lax.fori_loop(0, sh.chunks, differentiate, (zero, zero))
    sum_grad, sum_cross = column(sums[0]), column(sums[1])
    means = group_sums(stack_rows(factor * sum_grad, factor * sum_cross), sh.width) / sh.entries
    center, tilt = means[0:1], means[1:2]

    def finish(rows):
        normed = (x_ref[rows, :].astype(jnp.float32) - mean) * inv_std
        back = factor * pre_grad_ref[rows, :] - center - normed * tilt
        grad_ref[rows, :] = (up_ref[rows, :].astype(jnp.float32) + inv_std * back).astype(jnp.bfloat16)

    if own:
        finish(own_place(sh))
    else:
        over_chunks(sh.chunks, lambda i: finish(pl.ds(chunk_start(i, sh.chunk), sh.chunk)))
    return stack_rows(sum_grad, sum_cross)


def weight_products(sh, padded_ref, act_ref, slab_ref, grad_ref, sums, unit, keep_ref, send_ref, turned=False):
    core = lax.axis_index("segment") % PAIR
    space = lax.axis_index("space")
    first_row = space * sh.slab
    first_tap = jnp.minimum(first_row // sh.channels, 9 - sh.taps)
    offset = pl.multiple_of(first_row - first_tap * sh.channels, 8)
    for t in range(sh.taps):
        tap = first_tap + t
        row, col = 2 - tap // 3, 2 - tap % 3
        place = pl.ds(t * sh.channels, sh.channels)

        def product(i):
            start = chunk_start(i, sh.chunk)
            block = padded_ref[col, pl.ds(pl.multiple_of(start + row * sh.cols, 16), sh.chunk), :]
            here = pl.ds(start, sh.chunk)
            return lax.dot_general(
                act_ref[:, here] if turned else act_ref[here, :],
                block,
                (((1 if turned else 0,), (0,)), ((), ())),
                preferred_element_type=jnp.float32,
            )

        if sh.chunks == 1:
            slab_ref[place, :] = product(0)
        else:
            slab_ref[place, :] = jnp.zeros((sh.channels, sh.channels), jnp.float32)

            def accumulate(i):
                slab_ref[place, :] += product(i)

            over_chunks(sh.chunks, accumulate)
    mine = slab_ref[pl.ds(offset, sh.slab), :]
    rows = grad_ref[own_place(sh), :]

    def write(ref):
        ref[0 : sh.slab, :] = mine
        ref[sh.slab : sh.slab + sh.own_rows, :] = rows.astype(jnp.float32)
        ref[sh.slab + sh.own_rows : sh.pack, :] = sums

    @pl.when(core == unit)
    def _():
        write(keep_ref)

    @pl.when(core != unit)
    def _():
        write(send_ref)


def place_of():
    index = lax.axis_index("segment")
    return (index // PAIR, index % PAIR)


def unit_params(params_ref, unit):
    return (params_ref[2 * unit : 2 * unit + 1, :], params_ref[2 * unit + 1 : 2 * unit + 2, :])


def sinusoid_of(time, base):
    half = base // 2
    lanes = lax.broadcasted_iota(jnp.int32, (time.shape[0], base), 1)
    power = jnp.where(lanes < half, lanes, lanes - half).astype(jnp.float32)
    angle = time * jnp.exp(-math.log(10000.0) * power / half)
    turns = jnp.floor(angle * (2.0 / math.pi) + 0.5)
    rest = ((angle - turns * 1.5703125) - turns * 4.83751296997e-4) - turns * 7.54978995489e-8
    square = rest * rest
    sine = rest + rest * square * (
        -1.6666654611e-1 + square * (8.3321608736e-3 - square * 1.9515295891e-4)
    )
    cosine = 1.0 - 0.5 * square + square * square * (
        4.166664568298827e-2 + square * (-1.388731625493765e-3 + square * 2.443315711809948e-5)
    )
    quarter = turns.astype(jnp.int32) + jnp.where(lanes < half, 1, 0)
    value = jnp.where(quarter % 2 == 1, cosine, sine)
    return jnp.where((quarter // 2) % 2 == 1, -value, value).astype(jnp.bfloat16)


def start_all(pairs, sems):
    copies = [pltpu.make_async_copy(a, b, sems.at[i]) for i, (a, b) in enumerate(pairs)]
    for copy in copies:
        copy.start()
    return copies


def embed_kernel(times_ref, labels_ref, table_hbm, time_weight_hbm, embedded_ref, table_ref, time_weight_ref, sems):
    pairs = [(time_weight_hbm, time_weight_ref)]
    pairs += [(table_hbm.at[pl.ds(labels_ref[i] // 8, 1)], table_ref.at[pl.ds(i, 1)]) for i in range(PAIR)]
    copies = start_all(pairs, sems)
    spot = lax.broadcasted_iota(jnp.int32, (16, 1), 0)
    time = jnp.where(spot % 2 == 0, times_ref[0], times_ref[1]).astype(jnp.float32)
    sinusoid = sinusoid_of(time, time_weight_ref.shape[0])

    def label_row(image):
        block = table_ref[image].astype(jnp.float32)
        row = lax.broadcasted_iota(jnp.int32, block.shape, 0)
        return column(jnp.where(row == labels_ref[image] % 8, block, 0.0))

    for copy in copies:
        copy.wait()
    timed = jnp.dot(sinusoid, time_weight_ref[...], preferred_element_type=jnp.float32)
    timed = timed + jnp.where(spot % 2 == 0, label_row(0), label_row(1))
    embedded_ref[...] = (timed * sigmoid(timed)).astype(jnp.bfloat16)


def modulate_kernel(embedded_hbm, mod_weight_hbm, bias_hbm, gain_hbm, keep_ref, send_ref, *scratch):
    embedded_ref, mod_weight_ref, bias_ref, gain_ref, sems = scratch
    core = lax.axis_index("segment") % PAIR
    copies = start_all(zip((embedded_hbm, mod_weight_hbm, bias_hbm, gain_hbm), scratch[:4]), sems)
    for copy in copies:
        copy.wait()
    modulation = jnp.dot(embedded_ref[...], mod_weight_ref[...], preferred_element_type=jnp.float32) + bias_ref[...]
    channels = gain_ref.shape[1]
    factor = gain_ref[...] * (1.0 + modulation[:, :channels])
    shift = modulation[:, channels:]
    first = stack_rows(factor[0:1], shift[0:1])
    second = stack_rows(factor[1:2], shift[1:2])
    keep_ref[...] = jnp.where(core == 0, first, second)
    send_ref[...] = jnp.where(core == 0, second, first)


def layout_kernel(own_any, other_any, mod_keep_any, mod_other_any, weights_ref, params_ref, mods_ref, sems):
    core = lax.axis_index("segment") % PAIR
    pairs = [(mod_keep_any, mods_ref.at[core]), (mod_other_any, mods_ref.at[1 - core])]
    pairs += [(own_any, weights_ref.at[core]), (other_any, weights_ref.at[1 - core])]
    copies = start_all(pairs, sems)
    for copy in copies[:PAIR]:
        copy.wait()
    params_ref[0:2, :] = mods_ref[0, 0:2, :]
    params_ref[2:4, :] = mods_ref[1, 0:2, :]
    params_ref[4:8, :] = jnp.zeros((4, params_ref.shape[1]), jnp.float32)
    for copy in copies[PAIR:]:
        copy.wait()


def assemble(sh, blocks_ref, order, image_ref):
    space = lax.axis_index("space")
    for k, bits in enumerate(order):
        start = pl.multiple_of((space ^ bits) * sh.own_rows, sh.own_rows)
        image_ref[pl.ds(start, sh.own_rows), :] = blocks_ref[k]


def forward_kernel(sh, active_stage, orders, *refs):
    if orders:
        near_ref, far_ref, params_ref, weights, x_ref = refs[:5]
        assemble(sh, near_ref, orders[0], x_ref)
        assemble(sh, far_ref, orders[1], x_ref)
        refs = refs[5:]
    else:
        x_ref, params_ref, weights = refs[:3]
        refs = refs[3:]
    middle_ref, out_ref, padded_ref = refs
    stage, _ = place_of()

    @pl.when(stage == active_stage)
    def _():
        clear_edges(sh, padded_ref)
        forward_unit(sh, x_ref, middle_ref, unit_params(params_ref, 0), padded_ref, weights, 0)
        forward_unit(sh, middle_ref, out_ref, unit_params(params_ref, 1), padded_ref, weights, 1)


def note_kernel(sh, active_stage, x_ref, middle_ref, params_ref, *refs):
    act_ref, slope_ref, stats_ref = refs[-3:]
    stage, _ = place_of()

    @pl.when(stage == active_stage)
    def _():
        for unit, source in enumerate((x_ref, middle_ref)):
            stats = note_unit(sh, source, unit_params(params_ref, unit), act_ref.at[unit], slope_ref.at[unit], True)
            stats_ref[unit] = stack_rows(*stats)


def lay_kernel(sh, active_stage, up_ref, padded_ref):
    stage, _ = place_of()

    @pl.when(stage == active_stage)
    def _():
        clear_edges(sh, padded_ref)
        place_upstream(sh, up_ref, padded_ref)


def turn_kernel(sh, active_stage, x_ref, up_ref, laid_ref, params_ref, weights, *refs):
    grad_ref, between_ref, act_ref, sums_ref, padded_ref, pre_grad_ref, middle_ref, slope_ref = refs
    stage, _ = place_of()

    @pl.when(stage == active_stage)
    def _():
        clear_edges(sh, padded_ref)
        params = [unit_params(params_ref, unit) for unit in range(PAIR)]
        acts, slopes = [[ref.at[unit] for unit in range(PAIR)] for ref in (act_ref, slope_ref)]
        first = forward_unit(sh, x_ref, middle_ref, params[0], padded_ref, weights, 0, acts[0], slopes[0])
        second = note_unit(sh, middle_ref, params[1], acts[1], slopes[1])
        work = (pre_grad_ref, weights)
        known = (slopes[1], second)
        sums_ref[1] = backward_unit(
            sh, middle_ref, up_ref, between_ref, params[1], known, laid_ref, *work, 1, placed=True
        )
        known = (slopes[0], first)
        sums_ref[0] = backward_unit(sh, x_ref, between_ref, grad_ref, params[0], known, padded_ref, *work, 0)


def products_kernel(sh, active_stage, laid_ref, between_ref, grad_ref, act_ref, sums_ref, *refs):
    keep_ref, send_ref, padded_ref, slab_ref = refs
    stage, _ = place_of()

    @pl.when(stage == active_stage)
    def _():
        clear_edges(sh, padded_ref)
        place_upstream(sh, between_ref, padded_ref)
        for unit, above, below in ((1, laid_ref, between_ref), (0, padded_ref, grad_ref)):
            outs = (keep_ref, send_ref)
            weight_products(sh, above, act_ref.at[unit], slab_ref, below, sums_ref[unit], unit, *outs)


def backward_kernel(sh, active_stage, *refs):
    x_ref, middle_ref, up_ref, params_ref, weights, act_ref, slope_ref, stats_ref = refs[:8]
    keep_ref, send_ref, grad_ref, padded_ref, pre_grad_ref, slab_ref, between_ref = refs[10:]
    stage, _ = place_of()

    @pl.when(stage == active_stage)
    def _():
        clear_edges(sh, padded_ref)
        for unit, x, above, below in ((1, middle_ref, up_ref, between_ref), (0, x_ref, between_ref, grad_ref)):
            stats = (stats_ref[unit, 0:1, :], stats_ref[unit, 1:2, :])
            known = (slope_ref.at[unit], stats)
            params = unit_params(params_ref, unit)
            own = unit == 0 and active_stage == 0
            sums = backward_unit(sh, x, above, below, params, known, padded_ref, pre_grad_ref, weights, unit, own)
            outs = (keep_ref, send_ref)
            weight_products(sh, padded_ref, act_ref.at[unit], slab_ref, below, sums, unit, *outs, turned=True)


def finish_kernel(sh, keep_ref, other_ref, embedded_ref, gain_ref, grads_hbm, conv_hbm, mod_hbm, *scratch):
    grads_ref, conv_ref, mod_ref, sems = scratch
    core = lax.axis_index("segment") % PAIR
    base = sh.slab + sh.own_rows

    def mod_rows(ref):
        return jnp.concatenate([gain_ref[...] * ref[base + 1 : base + 2, :], ref[base : base + 1, :]], axis=1)

    own, other = mod_rows(keep_ref), mod_rows(other_ref)
    spot = lax.broadcasted_iota(jnp.int32, (16, own.shape[1]), 0)
    values = jnp.where(spot % 2 == core, own, other)
    high = values.astype(jnp.bfloat16).astype(jnp.float32)
    rest = values - high
    middle = rest.astype(jnp.bfloat16).astype(jnp.float32)
    low = rest - middle
    part = spot // 2
    pieces = jnp.where(part == 0, high, jnp.where(part == 1, middle, jnp.where(part == 2, low, 0.0)))
    pieces = pieces.astype(jnp.bfloat16)
    copies = []
    size = mod_ref.shape[0] // MOD_PARTS
    for k in range(MOD_PARTS):
        place = slice(k * size, (k + 1) * size)
        mod_ref[place, :] = lax.dot_general(
            embedded_ref[:, place],
            pieces,
            (((0,), (0,)), ((), ())),
            preferred_element_type=jnp.float32,
        )
        copies.append(pltpu.make_async_copy(mod_ref.at[place], mod_hbm.at[place], sems.at[k]))
        copies[-1].start()
    conv_ref[...] = keep_ref[0 : sh.slab, :] + other_ref[0 : sh.slab, :]
    copies.append(pltpu.make_async_copy(conv_ref, conv_hbm, sems.at[MOD_PARTS]))
    copies[-1].start()
    rows = slice(sh.slab, sh.slab + sh.own_rows)
    grads_ref[pl.ds(core, 1)] = keep_ref[rows, :].astype(jnp.bfloat16)[None]
    grads_ref[pl.ds(1 - core, 1)] = other_ref[rows, :].astype(jnp.bfloat16)[None]
    copies.append(pltpu.make_async_copy(grads_ref, grads_hbm, sems.at[MOD_PARTS + 1]))
    copies[-1].start()
    for copy in copies:
        copy.wait()


def shards(
    x_in,
    out_cotangent,
    timesteps,
    labels,
    time_weight,
    label_table,
    conv_weight,
    mod_weight,
    mod_bias,
    norm_gain,
):
    segments, spaces = lax.axis_size("segment"), lax.axis_size("space")
    stages = segments // PAIR
    stage, core = place_of()
    images, row_count, cols, channels = x_in.shape
    sh = Shape(row_count * spaces, cols, channels, spaces)
    f32, bf16 = jnp.float32, jnp.bfloat16

    def call(body, ins, outs, scratch=(), limit=CHAIN_LIMIT, cost=None, aliases={}):
        return pl.pallas_call(
            body,
            out_shape=outs,
            in_specs=ins,
            out_specs=[VMEM] * len(outs),
            scratch_shapes=list(scratch),
            input_output_aliases=aliases,
            compiler_params=pltpu.CompilerParams(vmem_limit_bytes=limit),
            cost_estimate=cost,
        )

    shape = jax.ShapeDtypeStruct
    swap = [(i, i ^ 1) for i in range(segments)]
    weight = conv_weight.reshape(9 * channels, channels)
    other_weight = lax.ppermute(weight, "segment", swap)
    ends = jnp.where(stage == 0, x_in, out_cotangent)
    near = lax.dynamic_index_in_dim(ends, core, 0, keepdims=False).reshape(1, sh.own_rows, channels)
    table = label_table.reshape(-1, 8, label_table.shape[1])
    width = time_weight.shape[1]
    some = pl.CostEstimate(flops=1 << 20, bytes_accessed=4 << 20, transcendentals=0)
    order, bit = [0], spaces // 2
    waiting = []
    while True:
        far = lax.ppermute(near, "space", [(i, i ^ bit) for i in range(spaces)])
        if not waiting:
            (embedded,) = call(
                embed_kernel,
                [SMEM, SMEM, ANY, ANY],
                [shape((16, width), bf16)],
                [
                    pltpu.VMEM((PAIR, 8, width), bf16),
                    pltpu.VMEM(time_weight.shape, bf16),
                    pltpu.SemaphoreType.DMA((PAIR + 1,)),
                ],
                PREPARE_LIMIT,
                some,
            )(timesteps, labels, table, time_weight)
            waiting = [embedded]
            far, embedded = lax.optimization_barrier((far, embedded))
        elif len(waiting) == 1:
            operands = (embedded, mod_weight[0], mod_bias, norm_gain)
            mod_keep, mod_send = call(
                modulate_kernel,
                [ANY] * 4,
                [shape((8, channels), f32)] * 2,
                [pltpu.VMEM(value.shape, value.dtype) for value in operands] + [pltpu.SemaphoreType.DMA((4,))],
                PREPARE_LIMIT,
                some,
            )(*operands)
            waiting.append(mod_keep)
            far, mod_keep, mod_send = lax.optimization_barrier((far, mod_keep, mod_send))
        far_order = [k ^ bit for k in order]
        if bit == 1:
            break
        near = jnp.concatenate([near, far])
        order, bit = order + far_order, bit // 2
    mod_other = lax.ppermute(mod_send, "segment", swap)
    weights, params = call(
        layout_kernel,
        [ANY] * 4,
        [shape((PAIR, 9 * channels, channels), bf16), shape((8, channels), f32)],
        [pltpu.VMEM((PAIR, 8, channels), f32), pltpu.SemaphoreType.DMA((2 * PAIR,))],
        cost=some,
    )(weight, other_weight, mod_keep, mod_other)

    image_shape = shape((sh.pixels, channels), bf16)
    pack_shape = shape((sh.pack, channels), f32)
    common = [pltpu.VMEM((3, sh.padded, channels), bf16)]

    def hop(value, source, target):
        pairs = [(PAIR * source + k, PAIR * target + k) for k in range(PAIR)]
        return lax.ppermute(value, "segment", pairs + [(b, a) for a, b in pairs])

    image, middle, out = call(
        functools.partial(forward_kernel, sh, 0, (order, far_order)),
        [VMEM] * 4,
        [image_shape] * 3,
        common,
    )(near, far, params, weights)
    entering, middles = [image, hop(out, 0, 1)], [middle]
    for active in range(1, stages - 1):
        middle, out = call(
            functools.partial(forward_kernel, sh, active, None),
            [VMEM] * 3,
            [image_shape, image_shape],
            common,
        )(entering[active], params, weights)
        middles.append(middle)
        entering.append(hop(out, active, active + 1))

    noted = []
    for active in range(stages - 1):
        noted = call(
            functools.partial(note_kernel, sh, active),
            [VMEM] * (3 + len(noted)),
            [
                shape((PAIR, channels, sh.pixels), bf16),
                shape((PAIR, sh.pixels, channels), f32),
                shape((PAIR, 8, channels), f32),
            ],
            cost=some,
            aliases={3 + k: k for k in range(len(noted))},
        )(entering[active], middles[active], params, *noted)

    work = common + [pltpu.VMEM((sh.pixels, channels), f32)]
    slab = [pltpu.VMEM((sh.taps * channels, channels), f32)]
    pair_shape = shape((PAIR, sh.pixels, channels), bf16)
    (laid,) = call(
        functools.partial(lay_kernel, sh, stages - 1),
        [VMEM],
        [shape((3, sh.padded, channels), bf16)],
        cost=some,
    )(image)
    *grad, between, act, sums = call(
        functools.partial(turn_kernel, sh, stages - 1),
        [VMEM] * 5,
        [image_shape, image_shape, pair_shape, shape((PAIR, 8, channels), f32)],
        work + [pltpu.VMEM((sh.pixels, channels), bf16), pltpu.VMEM((PAIR, sh.pixels, channels), f32)],
    )(entering[stages - 1], image, laid, params, weights)
    keep, send = call(
        functools.partial(products_kernel, sh, stages - 1),
        [VMEM] * 5,
        [pack_shape, pack_shape],
        common + slab,
        cost=some,
    )(laid, between, grad[0], act, sums)
    for active in range(stages - 2, -1, -1):
        upstream = hop(grad[0], active + 1, active)
        last = active == 0
        spare = [pltpu.VMEM((sh.pixels, channels), bf16)]
        keep, send, *grad = call(
            functools.partial(backward_kernel, sh, active),
            [VMEM] * 10,
            [pack_shape, pack_shape] + ([] if last else [image_shape]),
            (spare if last else []) + work + slab + spare,
            aliases={8: 0, 9: 1},
        )(entering[active], middles[active], upstream, params, weights, *noted, keep, send)
    other = lax.ppermute(send, "segment", swap)
    finals = [
        ((images, sh.own_rows, channels), bf16),
        ((sh.slab, channels), f32),
        ((width, 2 * channels), f32),
    ]
    grads, conv_grad, mod_grad = pl.pallas_call(
        functools.partial(finish_kernel, sh),
        out_shape=[shape(*final) for final in finals],
        in_specs=[VMEM] * 4,
        out_specs=[ANY] * 3,
        scratch_shapes=[pltpu.VMEM(*final) for final in finals] + [pltpu.SemaphoreType.DMA((MOD_PARTS + 2,))],
        compiler_params=pltpu.CompilerParams(vmem_limit_bytes=CHAIN_LIMIT),
    )(keep, other, embedded, norm_gain)
    return (grads.reshape(1, images, row_count, cols, channels), conv_grad[None], mod_grad[None])


def solution(mesh):
    placed = (
        P(None, "space", None, None),
        P(None, "space", None, None),
        P(),
        P(),
        P(),
        P(),
        P("segment", None, None, None, None),
        P("segment", None, None),
        P("segment", None),
        P("segment", None),
    )
    return jax.shard_map(
        shards,
        mesh=mesh,
        in_specs=placed,
        out_specs=(
            P("segment", None, "space", None, None),
            P("segment", "space", None),
            P("segment", None, None),
        ),
        check_vma=False,
    )
```

```python
import functools
import math

import jax
import jax.numpy as jnp
from jax import lax
from jax.experimental import pallas as pl
from jax.experimental.pallas import tpu as pltpu
from jax.sharding import PartitionSpec as P

GROUPS = 32
EPSILON = 1e-05
PAIR = 2
BLOCK = 128
MOD_PARTS = 4
PREPARE_LIMIT = 60 << 20
CHAIN_LIMIT = 48 << 20
VMEM = pl.BlockSpec(memory_space=pltpu.VMEM)
SMEM = pl.BlockSpec(memory_space=pltpu.SMEM)
ANY = pl.BlockSpec(memory_space=pl.ANY)


def sigmoid(values):
    return 1.0 / (1.0 + jnp.exp(-values))


def over_chunks(count, body):
    if count == 1:
        body(0)
    else:

        def step(i, carry):
            body(i)
            return carry

        lax.fori_loop(0, count, step, 0)


def chunk_start(i, size):
    return 0 if isinstance(i, int) else pl.multiple_of(i * size, size)


def fold_rows(values):
    return jnp.sum(values.reshape(values.shape[0] // 8, 8, values.shape[1]), axis=0)


def column(rows):
    return jnp.sum(rows, axis=0, keepdims=True)


def group_sums(rows, width):
    lanes = lax.broadcasted_iota(jnp.int32, rows.shape, 1)
    size = rows.shape[1]
    step = 1
    while step < width:
        ahead = pltpu.roll(rows, size - step, 1)
        behind = pltpu.roll(rows, step, 1)
        rows = rows + jnp.where((lanes & step) == 0, ahead, behind)
        step *= 2
    return rows


def stack_rows(first, second):
    spot = lax.broadcasted_iota(jnp.int32, (8, first.shape[1]), 0)
    return jnp.where(spot == 0, first, jnp.where(spot == 1, second, 0.0))


class Shape:
    def __init__(self, height, cols, channels, space_count):
        self.cols, self.channels = cols, channels
        self.pixels = height * cols
        self.chunk = cols * max(1, min(self.pixels, 256) // cols)
        self.chunks = self.pixels // self.chunk
        self.width = channels // GROUPS
        self.entries = float(self.pixels * self.width)
        self.padded = self.pixels + 2 * cols
        self.own_rows = height // space_count * cols
        self.slab = 9 * channels // space_count
        step = math.gcd(self.slab, channels)
        self.taps = min(9, -(-(channels - step + self.slab) // channels))
        self.pack = self.slab + self.own_rows + 8
        self.limit = (12 << 20) + self.pixels * channels * 40


def statistics(sh, x_ref):
    zero = jnp.zeros((8, sh.channels), jnp.float32)

    def add(i, sums):
        part = x_ref[pl.ds(chunk_start(i, sh.chunk), sh.chunk), :].astype(jnp.float32)
        return (sums[0] + fold_rows(part), sums[1] + fold_rows(part * part))

    if sh.chunks == 1:
        one, two = add(0, (zero, zero))
    else:
        one, two = lax.fori_loop(0, sh.chunks, add, (zero, zero))
    total = group_sums(stack_rows(column(one), column(two)), sh.width) / sh.entries
    mean = total[0:1]
    return (mean, lax.rsqrt(total[1:2] - mean * mean + EPSILON))


def clear_edges(sh, padded_ref):
    zero = jnp.zeros((3, sh.cols, sh.channels), padded_ref.dtype)
    padded_ref[:, 0 : sh.cols, :] = zero
    padded_ref[:, sh.pixels + sh.cols : sh.padded, :] = zero


def spread(sh, padded_ref, start, values):
    place = pl.ds(start + sh.cols, sh.chunk)
    spot = lax.broadcasted_iota(jnp.int32, values.shape, 0) % sh.cols
    padded_ref[0, place, :] = jnp.where(spot == 0, 0.0, pltpu.roll(values, 1, 0)).astype(jnp.bfloat16)
    padded_ref[1, place, :] = values.astype(jnp.bfloat16)
    padded_ref[2, place, :] = jnp.where(
        spot == sh.cols - 1, 0.0, pltpu.roll(values, sh.chunk - 1, 0)
    ).astype(jnp.bfloat16)


def convolve(sh, padded_ref, start, weight_ref, unit, backward):
    size = min(BLOCK, sh.chunk)
    totals = []
    for first in range(0, sh.chunk, size):
        total = None
        for p in range(3):
            for q in range(3):
                row, col = (2 - p, 2 - q) if backward else (p, q)
                block = padded_ref[col, pl.ds(start + first + row * sh.cols, size), :]
                tap = (3 * p + q) * sh.channels
                weight = weight_ref[unit, tap : tap + sh.channels, :]
                part = lax.dot_general(
                    block,
                    weight,
                    (((1,), (1 if backward else 0,)), ((), ())),
                    preferred_element_type=jnp.float32,
                )
                total = part if total is None else total + part
        totals.append(total)
    return totals[0] if len(totals) == 1 else jnp.concatenate(totals, axis=0)


def activation(sh, x_ref, place, stats, params):
    (mean, inv_std), (factor, shift) = stats, params
    pre = (x_ref[place, :].astype(jnp.float32) - mean) * inv_std * factor + shift
    sigma = sigmoid(pre)
    return pre * sigma, sigma * (1.0 + pre * (1.0 - sigma))


def note_unit(sh, x_ref, params, act_ref, slope_ref, turned=False):
    stats = statistics(sh, x_ref)

    def activate(i):
        place = pl.ds(chunk_start(i, sh.chunk), sh.chunk)
        values, slope = activation(sh, x_ref, place, stats, params)
        if turned:
            act_ref[:, place] = values.T.astype(jnp.bfloat16)
        else:
            act_ref[place, :] = values.astype(jnp.bfloat16)
        slope_ref[place, :] = slope

    over_chunks(sh.chunks, activate)
    return stats


def forward_unit(sh, x_ref, out_ref, params, padded_ref, weight_ref, unit, act_ref=None, slope_ref=None):
    stats = statistics(sh, x_ref)

    def activate(i):
        start = chunk_start(i, sh.chunk)
        place = pl.ds(start, sh.chunk)
        values, slope = activation(sh, x_ref, place, stats, params)
        spread(sh, padded_ref, start, values)
        if act_ref is not None:
            act_ref[place, :] = values.astype(jnp.bfloat16)
            slope_ref[place, :] = slope

    def produce(i):
        start = chunk_start(i, sh.chunk)
        inputs = x_ref[pl.ds(start, sh.chunk), :].astype(jnp.float32)
        z = convolve(sh, padded_ref, start, weight_ref, unit, False)
        out_ref[pl.ds(start, sh.chunk), :] = (inputs + z).astype(jnp.bfloat16)

    over_chunks(sh.chunks, activate)
    over_chunks(sh.chunks, produce)
    return stats


def own_place(sh):
    return pl.ds(pl.multiple_of(lax.axis_index("space") * sh.own_rows, sh.own_rows), sh.own_rows)


def place_upstream(sh, up_ref, padded_ref):
    def place(i):
        start = chunk_start(i, sh.chunk)
        spread(sh, padded_ref, start, up_ref[pl.ds(start, sh.chunk), :].astype(jnp.float32))

    over_chunks(sh.chunks, place)


def backward_unit(sh, x_ref, up_ref, grad_ref, params, known, padded_ref, pre_grad_ref, weight_ref, unit, own=False, placed=False):
    slope_ref, (mean, inv_std) = known
    factor, _ = params
    zero = jnp.zeros((8, sh.channels), jnp.float32)

    def differentiate(i, sums):
        start = chunk_start(i, sh.chunk)
        rows = pl.ds(start, sh.chunk)
        normed = (x_ref[rows, :].astype(jnp.float32) - mean) * inv_std
        pre_grad = convolve(sh, padded_ref, start, weight_ref, unit, True) * slope_ref[rows, :]
        pre_grad_ref[rows, :] = pre_grad
        return (sums[0] + fold_rows(pre_grad), sums[1] + fold_rows(pre_grad * normed))

    if not placed:
        place_upstream(sh, up_ref, padded_ref)
    if sh.chunks == 1:
        sums = differentiate(0, (zero, zero))
    else:
        sums = lax.fori_loop(0, sh.chunks, differentiate, (zero, zero))
    sum_grad, sum_cross = column(sums[0]), column(sums[1])
    means = group_sums(stack_rows(factor * sum_grad, factor * sum_cross), sh.width) / sh.entries
    center, tilt = means[0:1], means[1:2]

    def finish(rows):
        normed = (x_ref[rows, :].astype(jnp.float32) - mean) * inv_std
        back = factor * pre_grad_ref[rows, :] - center - normed * tilt
        grad_ref[rows, :] = (up_ref[rows, :].astype(jnp.float32) + inv_std * back).astype(jnp.bfloat16)

    if own:
        finish(own_place(sh))
    else:
        over_chunks(sh.chunks, lambda i: finish(pl.ds(chunk_start(i, sh.chunk), sh.chunk)))
    return stack_rows(sum_grad, sum_cross)


def weight_products(sh, padded_ref, act_ref, slab_ref, grad_ref, sums, unit, keep_ref, send_ref, turned=False):
    core = lax.axis_index("segment") % PAIR
    space = lax.axis_index("space")
    first_row = space * sh.slab
    first_tap = jnp.minimum(first_row // sh.channels, 9 - sh.taps)
    offset = pl.multiple_of(first_row - first_tap * sh.channels, 8)
    for t in range(sh.taps):
        tap = first_tap + t
        row, col = 2 - tap // 3, 2 - tap % 3
        place = pl.ds(t * sh.channels, sh.channels)

        def product(i):
            start = chunk_start(i, sh.chunk)
            block = padded_ref[col, pl.ds(pl.multiple_of(start + row * sh.cols, 16), sh.chunk), :]
            here = pl.ds(start, sh.chunk)
            return lax.dot_general(
                act_ref[:, here] if turned else act_ref[here, :],
                block,
                (((1 if turned else 0,), (0,)), ((), ())),
                preferred_element_type=jnp.float32,
            )

        if sh.chunks == 1:
            slab_ref[place, :] = product(0)
        else:
            slab_ref[place, :] = jnp.zeros((sh.channels, sh.channels), jnp.float32)

            def accumulate(i):
                slab_ref[place, :] += product(i)

            over_chunks(sh.chunks, accumulate)
    mine = slab_ref[pl.ds(offset, sh.slab), :]
    rows = grad_ref[own_place(sh), :]

    def write(ref):
        ref[0 : sh.slab, :] = mine
        ref[sh.slab : sh.slab + sh.own_rows, :] = rows.astype(jnp.float32)
        ref[sh.slab + sh.own_rows : sh.pack, :] = sums

    @pl.when(core == unit)
    def _():
        write(keep_ref)

    @pl.when(core != unit)
    def _():
        write(send_ref)


def place_of():
    index = lax.axis_index("segment")
    return (index // PAIR, index % PAIR)


def unit_params(params_ref, unit):
    return (params_ref[2 * unit : 2 * unit + 1, :], params_ref[2 * unit + 1 : 2 * unit + 2, :])


def sinusoid_of(time, base):
    half = base // 2
    lanes = lax.broadcasted_iota(jnp.int32, (time.shape[0], base), 1)
    power = jnp.where(lanes < half, lanes, lanes - half).astype(jnp.float32)
    angle = time * jnp.exp(-math.log(10000.0) * power / half)
    turns = jnp.floor(angle * (2.0 / math.pi) + 0.5)
    rest = ((angle - turns * 1.5703125) - turns * 4.83751296997e-4) - turns * 7.54978995489e-8
    square = rest * rest
    sine = rest + rest * square * (
        -1.6666654611e-1 + square * (8.3321608736e-3 - square * 1.9515295891e-4)
    )
    cosine = 1.0 - 0.5 * square + square * square * (
        4.166664568298827e-2 + square * (-1.388731625493765e-3 + square * 2.443315711809948e-5)
    )
    quarter = turns.astype(jnp.int32) + jnp.where(lanes < half, 1, 0)
    value = jnp.where(quarter % 2 == 1, cosine, sine)
    return jnp.where((quarter // 2) % 2 == 1, -value, value).astype(jnp.bfloat16)


def start_all(pairs, sems):
    copies = [pltpu.make_async_copy(a, b, sems.at[i]) for i, (a, b) in enumerate(pairs)]
    for copy in copies:
        copy.start()
    return copies


def embed_kernel(times_ref, labels_ref, table_hbm, time_weight_hbm, embedded_ref, table_ref, time_weight_ref, sems):
    pairs = [(time_weight_hbm, time_weight_ref)]
    pairs += [(table_hbm.at[pl.ds(labels_ref[i] // 8, 1)], table_ref.at[pl.ds(i, 1)]) for i in range(PAIR)]
    copies = start_all(pairs, sems)
    spot = lax.broadcasted_iota(jnp.int32, (16, 1), 0)
    time = jnp.where(spot % 2 == 0, times_ref[0], times_ref[1]).astype(jnp.float32)
    sinusoid = sinusoid_of(time, time_weight_ref.shape[0])

    def label_row(image):
        block = table_ref[image].astype(jnp.float32)
        row = lax.broadcasted_iota(jnp.int32, block.shape, 0)
        return column(jnp.where(row == labels_ref[image] % 8, block, 0.0))

    for copy in copies:
        copy.wait()
    timed = jnp.dot(sinusoid, time_weight_ref[...], preferred_element_type=jnp.float32)
    timed = timed + jnp.where(spot % 2 == 0, label_row(0), label_row(1))
    embedded_ref[...] = (timed * sigmoid(timed)).astype(jnp.bfloat16)


def modulate_kernel(embedded_hbm, mod_weight_hbm, bias_hbm, gain_hbm, keep_ref, send_ref, *scratch):
    embedded_ref, mod_weight_ref, bias_ref, gain_ref, sems = scratch
    core = lax.axis_index("segment") % PAIR
    copies = start_all(zip((embedded_hbm, mod_weight_hbm, bias_hbm, gain_hbm), scratch[:4]), sems)
    for copy in copies:
        copy.wait()
    modulation = jnp.dot(embedded_ref[...], mod_weight_ref[...], preferred_element_type=jnp.float32) + bias_ref[...]
    channels = gain_ref.shape[1]
    factor = gain_ref[...] * (1.0 + modulation[:, :channels])
    shift = modulation[:, channels:]
    first = stack_rows(factor[0:1], shift[0:1])
    second = stack_rows(factor[1:2], shift[1:2])
    keep_ref[...] = jnp.where(core == 0, first, second)
    send_ref[...] = jnp.where(core == 0, second, first)


def layout_kernel(own_any, other_any, mod_keep_any, mod_other_any, weights_ref, params_ref, mods_ref, sems):
    core = lax.axis_index("segment") % PAIR
    pairs = [(mod_keep_any, mods_ref.at[core]), (mod_other_any, mods_ref.at[1 - core])]
    pairs += [(own_any, weights_ref.at[core]), (other_any, weights_ref.at[1 - core])]
    copies = start_all(pairs, sems)
    for copy in copies[:PAIR]:
        copy.wait()
    params_ref[0:2, :] = mods_ref[0, 0:2, :]
    params_ref[2:4, :] = mods_ref[1, 0:2, :]
    params_ref[4:8, :] = jnp.zeros((4, params_ref.shape[1]), jnp.float32)
    for copy in copies[PAIR:]:
        copy.wait()


def assemble(sh, blocks_ref, order, image_ref):
    space = lax.axis_index("space")
    for k, bits in enumerate(order):
        start = pl.multiple_of((space ^ bits) * sh.own_rows, sh.own_rows)
        image_ref[pl.ds(start, sh.own_rows), :] = blocks_ref[k]


def forward_kernel(sh, active_stage, orders, *refs):
    if orders:
        near_ref, far_ref, params_ref, weights, x_ref = refs[:5]
        assemble(sh, near_ref, orders[0], x_ref)
        assemble(sh, far_ref, orders[1], x_ref)
        refs = refs[5:]
    else:
        x_ref, params_ref, weights = refs[:3]
        refs = refs[3:]
    middle_ref, out_ref, padded_ref = refs
    stage, _ = place_of()

    @pl.when(stage == active_stage)
    def _():
        clear_edges(sh, padded_ref)
        forward_unit(sh, x_ref, middle_ref, unit_params(params_ref, 0), padded_ref, weights, 0)
        forward_unit(sh, middle_ref, out_ref, unit_params(params_ref, 1), padded_ref, weights, 1)


def note_kernel(sh, active_stage, x_ref, middle_ref, params_ref, *refs):
    act_ref, slope_ref, stats_ref = refs[-3:]
    stage, _ = place_of()

    @pl.when(stage == active_stage)
    def _():
        for unit, source in enumerate((x_ref, middle_ref)):
            stats = note_unit(sh, source, unit_params(params_ref, unit), act_ref.at[unit], slope_ref.at[unit], True)
            stats_ref[unit] = stack_rows(*stats)


def lay_kernel(sh, active_stage, up_ref, padded_ref):
    stage, _ = place_of()

    @pl.when(stage == active_stage)
    def _():
        clear_edges(sh, padded_ref)
        place_upstream(sh, up_ref, padded_ref)


def turn_kernel(sh, active_stage, x_ref, up_ref, laid_ref, params_ref, weights, *refs):
    grad_ref, between_ref, act_ref, sums_ref, padded_ref, pre_grad_ref, middle_ref, slope_ref = refs
    stage, _ = place_of()

    @pl.when(stage == active_stage)
    def _():
        clear_edges(sh, padded_ref)
        params = [unit_params(params_ref, unit) for unit in range(PAIR)]
        acts, slopes = [[ref.at[unit] for unit in range(PAIR)] for ref in (act_ref, slope_ref)]
        first = forward_unit(sh, x_ref, middle_ref, params[0], padded_ref, weights, 0, acts[0], slopes[0])
        second = note_unit(sh, middle_ref, params[1], acts[1], slopes[1])
        work = (pre_grad_ref, weights)
        known = (slopes[1], second)
        sums_ref[1] = backward_unit(
            sh, middle_ref, up_ref, between_ref, params[1], known, laid_ref, *work, 1, placed=True
        )
        known = (slopes[0], first)
        sums_ref[0] = backward_unit(sh, x_ref, between_ref, grad_ref, params[0], known, padded_ref, *work, 0)


def products_kernel(sh, active_stage, laid_ref, between_ref, grad_ref, act_ref, sums_ref, *refs):
    keep_ref, send_ref, padded_ref, slab_ref = refs
    stage, _ = place_of()

    @pl.when(stage == active_stage)
    def _():
        clear_edges(sh, padded_ref)
        place_upstream(sh, between_ref, padded_ref)
        for unit, above, below in ((1, laid_ref, between_ref), (0, padded_ref, grad_ref)):
            outs = (keep_ref, send_ref)
            weight_products(sh, above, act_ref.at[unit], slab_ref, below, sums_ref[unit], unit, *outs)


def backward_kernel(sh, active_stage, *refs):
    x_ref, middle_ref, up_ref, params_ref, weights, act_ref, slope_ref, stats_ref = refs[:8]
    keep_ref, send_ref, grad_ref, padded_ref, pre_grad_ref, slab_ref, between_ref = refs[10:]
    stage, _ = place_of()

    @pl.when(stage == active_stage)
    def _():
        clear_edges(sh, padded_ref)
        for unit, x, above, below in ((1, middle_ref, up_ref, between_ref), (0, x_ref, between_ref, grad_ref)):
            stats = (stats_ref[unit, 0:1, :], stats_ref[unit, 1:2, :])
            known = (slope_ref.at[unit], stats)
            params = unit_params(params_ref, unit)
            own = unit == 0 and active_stage == 0
            sums = backward_unit(sh, x, above, below, params, known, padded_ref, pre_grad_ref, weights, unit, own)
            outs = (keep_ref, send_ref)
            weight_products(sh, padded_ref, act_ref.at[unit], slab_ref, below, sums, unit, *outs, turned=True)


def finish_kernel(sh, keep_ref, other_ref, embedded_ref, gain_ref, grads_hbm, conv_hbm, mod_hbm, *scratch):
    grads_ref, conv_ref, mod_ref, sems = scratch
    core = lax.axis_index("segment") % PAIR
    base = sh.slab + sh.own_rows

    def mod_rows(ref):
        return jnp.concatenate([gain_ref[...] * ref[base + 1 : base + 2, :], ref[base : base + 1, :]], axis=1)

    own, other = mod_rows(keep_ref), mod_rows(other_ref)
    spot = lax.broadcasted_iota(jnp.int32, (16, own.shape[1]), 0)
    values = jnp.where(spot % 2 == core, own, other)
    high = values.astype(jnp.bfloat16).astype(jnp.float32)
    rest = values - high
    middle = rest.astype(jnp.bfloat16).astype(jnp.float32)
    low = rest - middle
    part = spot // 2
    pieces = jnp.where(part == 0, high, jnp.where(part == 1, middle, jnp.where(part == 2, low, 0.0)))
    pieces = pieces.astype(jnp.bfloat16)
    copies = []
    size = mod_ref.shape[0] // MOD_PARTS
    for k in range(MOD_PARTS):
        place = slice(k * size, (k + 1) * size)
        mod_ref[place, :] = lax.dot_general(
            embedded_ref[:, place],
            pieces,
            (((0,), (0,)), ((), ())),
            preferred_element_type=jnp.float32,
        )
        copies.append(pltpu.make_async_copy(mod_ref.at[place], mod_hbm.at[place], sems.at[k]))
        copies[-1].start()
    conv_ref[...] = keep_ref[0 : sh.slab, :] + other_ref[0 : sh.slab, :]
    copies.append(pltpu.make_async_copy(conv_ref, conv_hbm, sems.at[MOD_PARTS]))
    copies[-1].start()
    rows = slice(sh.slab, sh.slab + sh.own_rows)
    grads_ref[pl.ds(core, 1)] = keep_ref[rows, :].astype(jnp.bfloat16)[None]
    grads_ref[pl.ds(1 - core, 1)] = other_ref[rows, :].astype(jnp.bfloat16)[None]
    copies.append(pltpu.make_async_copy(grads_ref, grads_hbm, sems.at[MOD_PARTS + 1]))
    copies[-1].start()
    for copy in copies:
        copy.wait()


def shards(
    x_in,
    out_cotangent,
    timesteps,
    labels,
    time_weight,
    label_table,
    conv_weight,
    mod_weight,
    mod_bias,
    norm_gain,
):
    segments, spaces = lax.axis_size("segment"), lax.axis_size("space")
    stages = segments // PAIR
    stage, core = place_of()
    images, row_count, cols, channels = x_in.shape
    sh = Shape(row_count * spaces, cols, channels, spaces)
    f32, bf16 = jnp.float32, jnp.bfloat16

    def call(body, ins, outs, scratch=(), limit=CHAIN_LIMIT, cost=None, aliases={}):
        return pl.pallas_call(
            body,
            out_shape=outs,
            in_specs=ins,
            out_specs=[VMEM] * len(outs),
            scratch_shapes=list(scratch),
            input_output_aliases=aliases,
            compiler_params=pltpu.CompilerParams(vmem_limit_bytes=limit),
            cost_estimate=cost,
        )

    shape = jax.ShapeDtypeStruct
    swap = [(i, i ^ 1) for i in range(segments)]
    weight = conv_weight.reshape(9 * channels, channels)
    other_weight = lax.ppermute(weight, "segment", swap)
    ends = jnp.where(stage == 0, x_in, out_cotangent)
    near = lax.dynamic_index_in_dim(ends, core, 0, keepdims=False).reshape(1, sh.own_rows, channels)
    table = label_table.reshape(-1, 8, label_table.shape[1])
    width = time_weight.shape[1]
    some = pl.CostEstimate(flops=1 << 20, bytes_accessed=4 << 20, transcendentals=0)
    order, bit = [0], spaces // 2
    waiting = []
    while True:
        far = lax.ppermute(near, "space", [(i, i ^ bit) for i in range(spaces)])
        if not waiting:
            (embedded,) = call(
                embed_kernel,
                [SMEM, SMEM, ANY, ANY],
                [shape((16, width), bf16)],
                [
                    pltpu.VMEM((PAIR, 8, width), bf16),
                    pltpu.VMEM(time_weight.shape, bf16),
                    pltpu.SemaphoreType.DMA((PAIR + 1,)),
                ],
                PREPARE_LIMIT,
                some,
            )(timesteps, labels, table, time_weight)
            waiting = [embedded]
            far, embedded = lax.optimization_barrier((far, embedded))
        elif len(waiting) == 1:
            operands = (embedded, mod_weight[0], mod_bias, norm_gain)
            mod_keep, mod_send = call(
                modulate_kernel,
                [ANY] * 4,
                [shape((8, channels), f32)] * 2,
                [pltpu.VMEM(value.shape, value.dtype) for value in operands] + [pltpu.SemaphoreType.DMA((4,))],
                PREPARE_LIMIT,
                some,
            )(*operands)
            waiting.append(mod_keep)
            far, mod_keep, mod_send = lax.optimization_barrier((far, mod_keep, mod_send))
        far_order = [k ^ bit for k in order]
        if bit == 1:
            break
        near = jnp.concatenate([near, far])
        order, bit = order + far_order, bit // 2
    mod_other = lax.ppermute(mod_send, "segment", swap)
    weights, params = call(
        layout_kernel,
        [ANY] * 4,
        [shape((PAIR, 9 * channels, channels), bf16), shape((8, channels), f32)],
        [pltpu.VMEM((PAIR, 8, channels), f32), pltpu.SemaphoreType.DMA((2 * PAIR,))],
        cost=some,
    )(weight, other_weight, mod_keep, mod_other)

    image_shape = shape((sh.pixels, channels), bf16)
    pack_shape = shape((sh.pack, channels), f32)
    common = [pltpu.VMEM((3, sh.padded, channels), bf16)]

    def hop(value, source, target):
        pairs = [(PAIR * source + k, PAIR * target + k) for k in range(PAIR)]
        return lax.ppermute(value, "segment", pairs + [(b, a) for a, b in pairs])

    image, middle, out = call(
        functools.partial(forward_kernel, sh, 0, (order, far_order)),
        [VMEM] * 4,
        [image_shape] * 3,
        common,
    )(near, far, params, weights)
    entering, middles = [image, hop(out, 0, 1)], [middle]
    for active in range(1, stages - 1):
        middle, out = call(
            functools.partial(forward_kernel, sh, active, None),
            [VMEM] * 3,
            [image_shape, image_shape],
            common,
        )(entering[active], params, weights)
        middles.append(middle)
        entering.append(hop(out, active, active + 1))

    noted = []
    for active in range(stages - 1):
        noted = call(
            functools.partial(note_kernel, sh, active),
            [VMEM] * (3 + len(noted)),
            [
                shape((PAIR, channels, sh.pixels), bf16),
                shape((PAIR, sh.pixels, channels), f32),
                shape((PAIR, 8, channels), f32),
            ],
            cost=some,
            aliases={3 + k: k for k in range(len(noted))},
        )(entering[active], middles[active], params, *noted)

    work = common + [pltpu.VMEM((sh.pixels, channels), f32)]
    slab = [pltpu.VMEM((sh.taps * channels, channels), f32)]
    pair_shape = shape((PAIR, sh.pixels, channels), bf16)
    (laid,) = call(
        functools.partial(lay_kernel, sh, stages - 1),
        [VMEM],
        [shape((3, sh.padded, channels), bf16)],
        cost=some,
    )(image)
    *grad, between, act, sums = call(
        functools.partial(turn_kernel, sh, stages - 1),
        [VMEM] * 5,
        [image_shape, image_shape, pair_shape, shape((PAIR, 8, channels), f32)],
        work + [pltpu.VMEM((sh.pixels, channels), bf16), pltpu.VMEM((PAIR, sh.pixels, channels), f32)],
    )(entering[stages - 1], image, laid, params, weights)
    keep, send = call(
        functools.partial(products_kernel, sh, stages - 1),
        [VMEM] * 5,
        [pack_shape, pack_shape],
        common + slab,
        cost=some,
    )(laid, between, grad[0], act, sums)
    for active in range(stages - 2, -1, -1):
        upstream = hop(grad[0], active + 1, active)
        last = active == 0
        spare = [pltpu.VMEM((sh.pixels, channels), bf16)]
        keep, send, *grad = call(
            functools.partial(backward_kernel, sh, active),
            [VMEM] * 10,
            [pack_shape, pack_shape] + ([] if last else [image_shape]),
            (spare if last else []) + work + slab + spare,
            aliases={8: 0, 9: 1},
        )(entering[active], middles[active], upstream, params, weights, *noted, keep, send)
    other = lax.ppermute(send, "segment", swap)
    finals = [
        ((images, sh.own_rows, channels), bf16),
        ((sh.slab, channels), f32),
        ((width, 2 * channels), f32),
    ]
    grads, conv_grad, mod_grad = pl.pallas_call(
        functools.partial(finish_kernel, sh),
        out_shape=[shape(*final) for final in finals],
        in_specs=[VMEM] * 4,
        out_specs=[ANY] * 3,
        scratch_shapes=[pltpu.VMEM(*final) for final in finals] + [pltpu.SemaphoreType.DMA((MOD_PARTS + 2,))],
        compiler_params=pltpu.CompilerParams(vmem_limit_bytes=CHAIN_LIMIT),
    )(keep, other, embedded, norm_gain)
    return (grads.reshape(1, images, row_count, cols, channels), conv_grad[None], mod_grad[None])


def solution(mesh):
    placed = (
        P(None, "space", None, None),
        P(None, "space", None, None),
        P(),
        P(),
        P(),
        P(),
        P("segment", None, None, None, None),
        P("segment", None, None),
        P("segment", None),
        P("segment", None),
    )
    return jax.shard_map(
        shards,
        mesh=mesh,
        in_specs=placed,
        out_specs=(
            P("segment", None, "space", None, None),
            P("segment", "space", None),
            P("segment", None, None),
        ),
        check_vma=False,
    )
```

```python
import functools
import math

import jax
import jax.numpy as jnp
from jax import lax
from jax.experimental import pallas as pl
from jax.experimental.pallas import tpu as pltpu
from jax.sharding import PartitionSpec as P

GROUPS = 32
EPSILON = 1e-05
PAIR = 2
BLOCK = 128
MOD_PARTS = 4
PREPARE_LIMIT = 60 << 20
CHAIN_LIMIT = 48 << 20
VMEM = pl.BlockSpec(memory_space=pltpu.VMEM)
SMEM = pl.BlockSpec(memory_space=pltpu.SMEM)
ANY = pl.BlockSpec(memory_space=pl.ANY)


def sigmoid(values):
    return 1.0 / (1.0 + jnp.exp(-values))


def over_chunks(count, body):
    if count == 1:
        body(0)
    else:

        def step(i, carry):
            body(i)
            return carry

        lax.fori_loop(0, count, step, 0)


def chunk_start(i, size):
    return 0 if isinstance(i, int) else pl.multiple_of(i * size, size)


def fold_rows(values):
    return jnp.sum(values.reshape(values.shape[0] // 8, 8, values.shape[1]), axis=0)


def column(rows):
    return jnp.sum(rows, axis=0, keepdims=True)


def group_sums(rows, width):
    lanes = lax.broadcasted_iota(jnp.int32, rows.shape, 1)
    size = rows.shape[1]
    step = 1
    while step < width:
        ahead = pltpu.roll(rows, size - step, 1)
        behind = pltpu.roll(rows, step, 1)
        rows = rows + jnp.where((lanes & step) == 0, ahead, behind)
        step *= 2
    return rows


def stack_rows(first, second):
    spot = lax.broadcasted_iota(jnp.int32, (8, first.shape[1]), 0)
    return jnp.where(spot == 0, first, jnp.where(spot == 1, second, 0.0))


class Shape:
    def __init__(self, height, cols, channels, space_count):
        self.cols, self.channels = cols, channels
        self.pixels = height * cols
        self.chunk = cols * max(1, min(self.pixels, 256) // cols)
        self.chunks = self.pixels // self.chunk
        self.width = channels // GROUPS
        self.entries = float(self.pixels * self.width)
        self.padded = self.pixels + 2 * cols
        self.own_rows = height // space_count * cols
        self.slab = 9 * channels // space_count
        step = math.gcd(self.slab, channels)
        self.taps = min(9, -(-(channels - step + self.slab) // channels))
        self.pack = self.slab + self.own_rows + 8
        self.limit = (12 << 20) + self.pixels * channels * 40


def statistics(sh, x_ref):
    zero = jnp.zeros((8, sh.channels), jnp.float32)

    def add(i, sums):
        part = x_ref[pl.ds(chunk_start(i, sh.chunk), sh.chunk), :].astype(jnp.float32)
        return (sums[0] + fold_rows(part), sums[1] + fold_rows(part * part))

    if sh.chunks == 1:
        one, two = add(0, (zero, zero))
    else:
        one, two = lax.fori_loop(0, sh.chunks, add, (zero, zero))
    total = group_sums(stack_rows(column(one), column(two)), sh.width) / sh.entries
    mean = total[0:1]
    return (mean, lax.rsqrt(total[1:2] - mean * mean + EPSILON))


def clear_edges(sh, padded_ref):
    zero = jnp.zeros((3, sh.cols, sh.channels), padded_ref.dtype)
    padded_ref[:, 0 : sh.cols, :] = zero
    padded_ref[:, sh.pixels + sh.cols : sh.padded, :] = zero


def spread(sh, padded_ref, start, values):
    place = pl.ds(start + sh.cols, sh.chunk)
    spot = lax.broadcasted_iota(jnp.int32, values.shape, 0) % sh.cols
    padded_ref[0, place, :] = jnp.where(spot == 0, 0.0, pltpu.roll(values, 1, 0)).astype(jnp.bfloat16)
    padded_ref[1, place, :] = values.astype(jnp.bfloat16)
    padded_ref[2, place, :] = jnp.where(
        spot == sh.cols - 1, 0.0, pltpu.roll(values, sh.chunk - 1, 0)
    ).astype(jnp.bfloat16)


def convolve(sh, padded_ref, start, weight_ref, unit, backward):
    size = min(BLOCK, sh.chunk)
    totals = []
    for first in range(0, sh.chunk, size):
        total = None
        for p in range(3):
            for q in range(3):
                row, col = (2 - p, 2 - q) if backward else (p, q)
                block = padded_ref[col, pl.ds(start + first + row * sh.cols, size), :]
                tap = (3 * p + q) * sh.channels
                weight = weight_ref[unit, tap : tap + sh.channels, :]
                part = lax.dot_general(
                    block,
                    weight,
                    (((1,), (0,)), ((), ())),
                    preferred_element_type=jnp.float32,
                )
                total = part if total is None else total + part
        totals.append(total)
    return totals[0] if len(totals) == 1 else jnp.concatenate(totals, axis=0)


def activation(sh, x_ref, place, stats, params):
    (mean, inv_std), (factor, shift) = stats, params
    pre = (x_ref[place, :].astype(jnp.float32) - mean) * inv_std * factor + shift
    sigma = sigmoid(pre)
    return pre * sigma, sigma * (1.0 + pre * (1.0 - sigma))


def note_unit(sh, x_ref, params, act_ref, slope_ref, turned=False):
    stats = statistics(sh, x_ref)

    def activate(i):
        place = pl.ds(chunk_start(i, sh.chunk), sh.chunk)
        values, slope = activation(sh, x_ref, place, stats, params)
        if turned:
            act_ref[:, place] = values.T.astype(jnp.bfloat16)
        else:
            act_ref[place, :] = values.astype(jnp.bfloat16)
        slope_ref[place, :] = slope

    over_chunks(sh.chunks, activate)
    return stats


def forward_unit(sh, x_ref, out_ref, params, padded_ref, weight_ref, unit, act_ref=None, slope_ref=None):
    stats = statistics(sh, x_ref)

    def activate(i):
        start = chunk_start(i, sh.chunk)
        place = pl.ds(start, sh.chunk)
        values, slope = activation(sh, x_ref, place, stats, params)
        spread(sh, padded_ref, start, values)
        if act_ref is not None:
            act_ref[place, :] = values.astype(jnp.bfloat16)
            slope_ref[place, :] = slope

    def produce(i):
        start = chunk_start(i, sh.chunk)
        inputs = x_ref[pl.ds(start, sh.chunk), :].astype(jnp.float32)
        z = convolve(sh, padded_ref, start, weight_ref, unit, False)
        out_ref[pl.ds(start, sh.chunk), :] = (inputs + z).astype(jnp.bfloat16)

    over_chunks(sh.chunks, activate)
    over_chunks(sh.chunks, produce)
    return stats


def own_place(sh):
    return pl.ds(pl.multiple_of(lax.axis_index("space") * sh.own_rows, sh.own_rows), sh.own_rows)


def place_upstream(sh, up_ref, padded_ref):
    def place(i):
        start = chunk_start(i, sh.chunk)
        spread(sh, padded_ref, start, up_ref[pl.ds(start, sh.chunk), :].astype(jnp.float32))

    over_chunks(sh.chunks, place)


def backward_unit(sh, x_ref, up_ref, grad_ref, params, known, padded_ref, pre_grad_ref, weight_ref, unit, own=False, placed=False):
    slope_ref, (mean, inv_std) = known
    factor, _ = params
    zero = jnp.zeros((8, sh.channels), jnp.float32)

    def differentiate(i, sums):
        start = chunk_start(i, sh.chunk)
        rows = pl.ds(start, sh.chunk)
        normed = (x_ref[rows, :].astype(jnp.float32) - mean) * inv_std
        pre_grad = convolve(sh, padded_ref, start, weight_ref, unit, True) * slope_ref[rows, :]
        pre_grad_ref[rows, :] = pre_grad
        return (sums[0] + fold_rows(pre_grad), sums[1] + fold_rows(pre_grad * normed))

    if not placed:
        place_upstream(sh, up_ref, padded_ref)
    if sh.chunks == 1:
        sums = differentiate(0, (zero, zero))
    else:
        sums = lax.fori_loop(0, sh.chunks, differentiate, (zero, zero))
    sum_grad, sum_cross = column(sums[0]), column(sums[1])
    means = group_sums(stack_rows(factor * sum_grad, factor * sum_cross), sh.width) / sh.entries
    center, tilt = means[0:1], means[1:2]

    def finish(rows):
        normed = (x_ref[rows, :].astype(jnp.float32) - mean) * inv_std
        back = factor * pre_grad_ref[rows, :] - center - normed * tilt
        grad_ref[rows, :] = (up_ref[rows, :].astype(jnp.float32) + inv_std * back).astype(jnp.bfloat16)

    if own:
        finish(own_place(sh))
    else:
        over_chunks(sh.chunks, lambda i: finish(pl.ds(chunk_start(i, sh.chunk), sh.chunk)))
    return stack_rows(sum_grad, sum_cross)


def weight_products(sh, padded_ref, act_ref, slab_ref, grad_ref, sums, unit, keep_ref, send_ref, turned=False):
    core = lax.axis_index("segment") % PAIR
    space = lax.axis_index("space")
    first_row = space * sh.slab
    first_tap = jnp.minimum(first_row // sh.channels, 9 - sh.taps)
    offset = pl.multiple_of(first_row - first_tap * sh.channels, 8)
    for t in range(sh.taps):
        tap = first_tap + t
        row, col = 2 - tap // 3, 2 - tap % 3
        place = pl.ds(t * sh.channels, sh.channels)

        def product(i):
            start = chunk_start(i, sh.chunk)
            block = padded_ref[col, pl.ds(pl.multiple_of(start + row * sh.cols, 16), sh.chunk), :]
            here = pl.ds(start, sh.chunk)
            return lax.dot_general(
                act_ref[:, here] if turned else act_ref[here, :],
                block,
                (((1 if turned else 0,), (0,)), ((), ())),
                preferred_element_type=jnp.float32,
            )

        if sh.chunks == 1:
            slab_ref[place, :] = product(0)
        else:
            slab_ref[place, :] = jnp.zeros((sh.channels, sh.channels), jnp.float32)

            def accumulate(i):
                slab_ref[place, :] += product(i)

            over_chunks(sh.chunks, accumulate)
    mine = slab_ref[pl.ds(offset, sh.slab), :]
    rows = grad_ref[own_place(sh), :]

    def write(ref):
        ref[0 : sh.slab, :] = mine
        ref[sh.slab : sh.slab + sh.own_rows, :] = rows.astype(jnp.float32)
        ref[sh.slab + sh.own_rows : sh.pack, :] = sums

    @pl.when(core == unit)
    def _():
        write(keep_ref)

    @pl.when(core != unit)
    def _():
        write(send_ref)


def place_of():
    index = lax.axis_index("segment")
    return (index // PAIR, index % PAIR)


def unit_params(params_ref, unit):
    return (params_ref[2 * unit : 2 * unit + 1, :], params_ref[2 * unit + 1 : 2 * unit + 2, :])


def sinusoid_of(time, base):
    half = base // 2
    lanes = lax.broadcasted_iota(jnp.int32, (time.shape[0], base), 1)
    power = jnp.where(lanes < half, lanes, lanes - half).astype(jnp.float32)
    angle = time * jnp.exp(-math.log(10000.0) * power / half)
    turns = jnp.floor(angle * (2.0 / math.pi) + 0.5)
    rest = ((angle - turns * 1.5703125) - turns * 4.83751296997e-4) - turns * 7.54978995489e-8
    square = rest * rest
    sine = rest + rest * square * (
        -1.6666654611e-1 + square * (8.3321608736e-3 - square * 1.9515295891e-4)
    )
    cosine = 1.0 - 0.5 * square + square * square * (
        4.166664568298827e-2 + square * (-1.388731625493765e-3 + square * 2.443315711809948e-5)
    )
    quarter = turns.astype(jnp.int32) + jnp.where(lanes < half, 1, 0)
    value = jnp.where(quarter % 2 == 1, cosine, sine)
    return jnp.where((quarter // 2) % 2 == 1, -value, value).astype(jnp.bfloat16)


def start_all(pairs, sems):
    copies = [pltpu.make_async_copy(a, b, sems.at[i]) for i, (a, b) in enumerate(pairs)]
    for copy in copies:
        copy.start()
    return copies


def embed_kernel(times_ref, labels_ref, table_hbm, time_weight_hbm, embedded_ref, table_ref, time_weight_ref, sems):
    pairs = [(time_weight_hbm, time_weight_ref)]
    pairs += [(table_hbm.at[pl.ds(labels_ref[i] // 8, 1)], table_ref.at[pl.ds(i, 1)]) for i in range(PAIR)]
    copies = start_all(pairs, sems)
    spot = lax.broadcasted_iota(jnp.int32, (16, 1), 0)
    time = jnp.where(spot % 2 == 0, times_ref[0], times_ref[1]).astype(jnp.float32)
    sinusoid = sinusoid_of(time, time_weight_ref.shape[0])

    def label_row(image):
        block = table_ref[image].astype(jnp.float32)
        row = lax.broadcasted_iota(jnp.int32, block.shape, 0)
        return column(jnp.where(row == labels_ref[image] % 8, block, 0.0))

    for copy in copies:
        copy.wait()
    timed = jnp.dot(sinusoid, time_weight_ref[...], preferred_element_type=jnp.float32)
    timed = timed + jnp.where(spot % 2 == 0, label_row(0), label_row(1))
    embedded_ref[...] = (timed * sigmoid(timed)).astype(jnp.bfloat16)


def modulate_kernel(embedded_hbm, mod_weight_hbm, bias_hbm, gain_hbm, keep_ref, send_ref, *scratch):
    embedded_ref, mod_weight_ref, bias_ref, gain_ref, sems = scratch
    core = lax.axis_index("segment") % PAIR
    copies = start_all(zip((embedded_hbm, mod_weight_hbm, bias_hbm, gain_hbm), scratch[:4]), sems)
    for copy in copies:
        copy.wait()
    modulation = jnp.dot(embedded_ref[...], mod_weight_ref[...], preferred_element_type=jnp.float32) + bias_ref[...]
    channels = gain_ref.shape[1]
    factor = gain_ref[...] * (1.0 + modulation[:, :channels])
    shift = modulation[:, channels:]
    first = stack_rows(factor[0:1], shift[0:1])
    second = stack_rows(factor[1:2], shift[1:2])
    keep_ref[...] = jnp.where(core == 0, first, second)
    send_ref[...] = jnp.where(core == 0, second, first)


def layout_kernel(own_any, other_any, mod_keep_any, mod_other_any, weights_ref, params_ref, mods_ref, sems):
    core = lax.axis_index("segment") % PAIR
    pairs = [(mod_keep_any, mods_ref.at[core]), (mod_other_any, mods_ref.at[1 - core])]
    pairs += [(own_any, weights_ref.at[core]), (other_any, weights_ref.at[1 - core])]
    copies = start_all(pairs, sems)
    for copy in copies[:PAIR]:
        copy.wait()
    params_ref[0:2, :] = mods_ref[0, 0:2, :]
    params_ref[2:4, :] = mods_ref[1, 0:2, :]
    params_ref[4:8, :] = jnp.zeros((4, params_ref.shape[1]), jnp.float32)
    for copy in copies[PAIR:]:
        copy.wait()


def assemble(sh, blocks_ref, order, image_ref):
    space = lax.axis_index("space")
    for k, bits in enumerate(order):
        start = pl.multiple_of((space ^ bits) * sh.own_rows, sh.own_rows)
        image_ref[pl.ds(start, sh.own_rows), :] = blocks_ref[k]


def forward_kernel(sh, active_stage, orders, *refs):
    if orders:
        near_ref, far_ref, params_ref, weights, x_ref = refs[:5]
        assemble(sh, near_ref, orders[0], x_ref)
        assemble(sh, far_ref, orders[1], x_ref)
        refs = refs[5:]
    else:
        x_ref, params_ref, weights = refs[:3]
        refs = refs[3:]
    middle_ref, out_ref, padded_ref = refs
    stage, _ = place_of()

    @pl.when(stage == active_stage)
    def _():
        clear_edges(sh, padded_ref)
        forward_unit(sh, x_ref, middle_ref, unit_params(params_ref, 0), padded_ref, weights, 0)
        forward_unit(sh, middle_ref, out_ref, unit_params(params_ref, 1), padded_ref, weights, 1)


def note_kernel(sh, active_stage, x_ref, middle_ref, params_ref, *refs):
    act_ref, slope_ref, stats_ref = refs[-3:]
    stage, _ = place_of()

    @pl.when(stage == active_stage)
    def _():
        for unit, source in enumerate((x_ref, middle_ref)):
            stats = note_unit(sh, source, unit_params(params_ref, unit), act_ref.at[unit], slope_ref.at[unit], True)
            stats_ref[unit] = stack_rows(*stats)


def lay_kernel(sh, active_stage, up_ref, weights_ref, padded_ref, turned_ref):
    stage, _ = place_of()

    @pl.when(stage == active_stage)
    def _():
        clear_edges(sh, padded_ref)
        place_upstream(sh, up_ref, padded_ref)

    for unit in range(PAIR):
        for tap in range(9):
            place = slice(tap * sh.channels, (tap + 1) * sh.channels)
            turned_ref[unit, place, :] = weights_ref[unit, place, :].astype(jnp.float32).T.astype(jnp.bfloat16)


def turn_kernel(sh, active_stage, x_ref, up_ref, laid_ref, params_ref, weights, turned, *refs):
    grad_ref, between_ref, act_ref, sums_ref, padded_ref, pre_grad_ref, middle_ref, slope_ref = refs
    stage, _ = place_of()

    @pl.when(stage == active_stage)
    def _():
        clear_edges(sh, padded_ref)
        params = [unit_params(params_ref, unit) for unit in range(PAIR)]
        acts, slopes = [[ref.at[unit] for unit in range(PAIR)] for ref in (act_ref, slope_ref)]
        first = forward_unit(sh, x_ref, middle_ref, params[0], padded_ref, weights, 0, acts[0], slopes[0])
        second = note_unit(sh, middle_ref, params[1], acts[1], slopes[1])
        work = (pre_grad_ref, turned)
        known = (slopes[1], second)
        sums_ref[1] = backward_unit(
            sh, middle_ref, up_ref, between_ref, params[1], known, laid_ref, *work, 1, placed=True
        )
        known = (slopes[0], first)
        sums_ref[0] = backward_unit(sh, x_ref, between_ref, grad_ref, params[0], known, padded_ref, *work, 0)


def products_kernel(sh, active_stage, laid_ref, between_ref, grad_ref, act_ref, sums_ref, *refs):
    keep_ref, send_ref, padded_ref, slab_ref = refs
    stage, _ = place_of()

    @pl.when(stage == active_stage)
    def _():
        clear_edges(sh, padded_ref)
        place_upstream(sh, between_ref, padded_ref)
        for unit, above, below in ((1, laid_ref, between_ref), (0, padded_ref, grad_ref)):
            outs = (keep_ref, send_ref)
            weight_products(sh, above, act_ref.at[unit], slab_ref, below, sums_ref[unit], unit, *outs)


def backward_kernel(sh, active_stage, *refs):
    x_ref, middle_ref, up_ref, params_ref, weights, act_ref, slope_ref, stats_ref = refs[:8]
    keep_ref, send_ref, grad_ref, padded_ref, pre_grad_ref, slab_ref, between_ref = refs[10:]
    stage, _ = place_of()

    @pl.when(stage == active_stage)
    def _():
        clear_edges(sh, padded_ref)
        for unit, x, above, below in ((1, middle_ref, up_ref, between_ref), (0, x_ref, between_ref, grad_ref)):
            stats = (stats_ref[unit, 0:1, :], stats_ref[unit, 1:2, :])
            known = (slope_ref.at[unit], stats)
            params = unit_params(params_ref, unit)
            own = unit == 0 and active_stage == 0
            sums = backward_unit(sh, x, above, below, params, known, padded_ref, pre_grad_ref, weights, unit, own)
            outs = (keep_ref, send_ref)
            weight_products(sh, padded_ref, act_ref.at[unit], slab_ref, below, sums, unit, *outs, turned=True)


def finish_kernel(sh, keep_ref, other_ref, embedded_ref, gain_ref, grads_hbm, conv_hbm, mod_hbm, *scratch):
    grads_ref, conv_ref, mod_ref, sems = scratch
    core = lax.axis_index("segment") % PAIR
    base = sh.slab + sh.own_rows

    def mod_rows(ref):
        return jnp.concatenate([gain_ref[...] * ref[base + 1 : base + 2, :], ref[base : base + 1, :]], axis=1)

    own, other = mod_rows(keep_ref), mod_rows(other_ref)
    spot = lax.broadcasted_iota(jnp.int32, (16, own.shape[1]), 0)
    values = jnp.where(spot % 2 == core, own, other)
    high = values.astype(jnp.bfloat16).astype(jnp.float32)
    rest = values - high
    middle = rest.astype(jnp.bfloat16).astype(jnp.float32)
    low = rest - middle
    part = spot // 2
    pieces = jnp.where(part == 0, high, jnp.where(part == 1, middle, jnp.where(part == 2, low, 0.0)))
    pieces = pieces.astype(jnp.bfloat16)
    copies = []
    size = mod_ref.shape[0] // MOD_PARTS
    for k in range(MOD_PARTS):
        place = slice(k * size, (k + 1) * size)
        mod_ref[place, :] = lax.dot_general(
            embedded_ref[:, place],
            pieces,
            (((0,), (0,)), ((), ())),
            preferred_element_type=jnp.float32,
        )
        copies.append(pltpu.make_async_copy(mod_ref.at[place], mod_hbm.at[place], sems.at[k]))
        copies[-1].start()
    conv_ref[...] = keep_ref[0 : sh.slab, :] + other_ref[0 : sh.slab, :]
    copies.append(pltpu.make_async_copy(conv_ref, conv_hbm, sems.at[MOD_PARTS]))
    copies[-1].start()
    rows = slice(sh.slab, sh.slab + sh.own_rows)
    grads_ref[pl.ds(core, 1)] = keep_ref[rows, :].astype(jnp.bfloat16)[None]
    grads_ref[pl.ds(1 - core, 1)] = other_ref[rows, :].astype(jnp.bfloat16)[None]
    copies.append(pltpu.make_async_copy(grads_ref, grads_hbm, sems.at[MOD_PARTS + 1]))
    copies[-1].start()
    for copy in copies:
        copy.wait()


def shards(
    x_in,
    out_cotangent,
    timesteps,
    labels,
    time_weight,
    label_table,
    conv_weight,
    mod_weight,
    mod_bias,
    norm_gain,
):
    segments, spaces = lax.axis_size("segment"), lax.axis_size("space")
    stages = segments // PAIR
    stage, core = place_of()
    images, row_count, cols, channels = x_in.shape
    sh = Shape(row_count * spaces, cols, channels, spaces)
    f32, bf16 = jnp.float32, jnp.bfloat16

    def call(body, ins, outs, scratch=(), limit=CHAIN_LIMIT, cost=None, aliases={}):
        return pl.pallas_call(
            body,
            out_shape=outs,
            in_specs=ins,
            out_specs=[VMEM] * len(outs),
            scratch_shapes=list(scratch),
            input_output_aliases=aliases,
            compiler_params=pltpu.CompilerParams(vmem_limit_bytes=limit),
            cost_estimate=cost,
        )

    shape = jax.ShapeDtypeStruct
    swap = [(i, i ^ 1) for i in range(segments)]
    weight = conv_weight.reshape(9 * channels, channels)
    other_weight = lax.ppermute(weight, "segment", swap)
    ends = jnp.where(stage == 0, x_in, out_cotangent)
    near = lax.dynamic_index_in_dim(ends, core, 0, keepdims=False).reshape(1, sh.own_rows, channels)
    table = label_table.reshape(-1, 8, label_table.shape[1])
    width = time_weight.shape[1]
    some = pl.CostEstimate(flops=1 << 20, bytes_accessed=4 << 20, transcendentals=0)
    order, bit = [0], spaces // 2
    waiting = []
    while True:
        far = lax.ppermute(near, "space", [(i, i ^ bit) for i in range(spaces)])
        if not waiting:
            (embedded,) = call(
                embed_kernel,
                [SMEM, SMEM, ANY, ANY],
                [shape((16, width), bf16)],
                [
                    pltpu.VMEM((PAIR, 8, width), bf16),
                    pltpu.VMEM(time_weight.shape, bf16),
                    pltpu.SemaphoreType.DMA((PAIR + 1,)),
                ],
                PREPARE_LIMIT,
                some,
            )(timesteps, labels, table, time_weight)
            waiting = [embedded]
            far, embedded = lax.optimization_barrier((far, embedded))
        elif len(waiting) == 1:
            operands = (embedded, mod_weight[0], mod_bias, norm_gain)
            mod_keep, mod_send = call(
                modulate_kernel,
                [ANY] * 4,
                [shape((8, channels), f32)] * 2,
                [pltpu.VMEM(value.shape, value.dtype) for value in operands] + [pltpu.SemaphoreType.DMA((4,))],
                PREPARE_LIMIT,
                some,
            )(*operands)
            waiting.append(mod_keep)
            far, mod_keep, mod_send = lax.optimization_barrier((far, mod_keep, mod_send))
        far_order = [k ^ bit for k in order]
        if bit == 1:
            break
        near = jnp.concatenate([near, far])
        order, bit = order + far_order, bit // 2
    mod_other = lax.ppermute(mod_send, "segment", swap)
    weights, params = call(
        layout_kernel,
        [ANY] * 4,
        [shape((PAIR, 9 * channels, channels), bf16), shape((8, channels), f32)],
        [pltpu.VMEM((PAIR, 8, channels), f32), pltpu.SemaphoreType.DMA((2 * PAIR,))],
        cost=some,
    )(weight, other_weight, mod_keep, mod_other)

    image_shape = shape((sh.pixels, channels), bf16)
    pack_shape = shape((sh.pack, channels), f32)
    common = [pltpu.VMEM((3, sh.padded, channels), bf16)]

    def hop(value, source, target):
        pairs = [(PAIR * source + k, PAIR * target + k) for k in range(PAIR)]
        return lax.ppermute(value, "segment", pairs + [(b, a) for a, b in pairs])

    image, middle, out = call(
        functools.partial(forward_kernel, sh, 0, (order, far_order)),
        [VMEM] * 4,
        [image_shape] * 3,
        common,
    )(near, far, params, weights)
    entering, middles = [image, hop(out, 0, 1)], [middle]
    for active in range(1, stages - 1):
        middle, out = call(
            functools.partial(forward_kernel, sh, active, None),
            [VMEM] * 3,
            [image_shape, image_shape],
            common,
        )(entering[active], params, weights)
        middles.append(middle)
        entering.append(hop(out, active, active + 1))

    noted = []
    for active in range(stages - 1):
        noted = call(
            functools.partial(note_kernel, sh, active),
            [VMEM] * (3 + len(noted)),
            [
                shape((PAIR, channels, sh.pixels), bf16),
                shape((PAIR, sh.pixels, channels), f32),
                shape((PAIR, 8, channels), f32),
            ],
            cost=some,
            aliases={3 + k: k for k in range(len(noted))},
        )(entering[active], middles[active], params, *noted)

    work = common + [pltpu.VMEM((sh.pixels, channels), f32)]
    slab = [pltpu.VMEM((sh.taps * channels, channels), f32)]
    pair_shape = shape((PAIR, sh.pixels, channels), bf16)
    laid, turned = call(
        functools.partial(lay_kernel, sh, stages - 1),
        [VMEM] * 2,
        [shape((3, sh.padded, channels), bf16), shape((PAIR, 9 * channels, channels), bf16)],
        cost=some,
    )(image, weights)
    *grad, between, act, sums = call(
        functools.partial(turn_kernel, sh, stages - 1),
        [VMEM] * 6,
        [image_shape, image_shape, pair_shape, shape((PAIR, 8, channels), f32)],
        work + [pltpu.VMEM((sh.pixels, channels), bf16), pltpu.VMEM((PAIR, sh.pixels, channels), f32)],
    )(entering[stages - 1], image, laid, params, weights, turned)
    keep, send = call(
        functools.partial(products_kernel, sh, stages - 1),
        [VMEM] * 5,
        [pack_shape, pack_shape],
        common + slab,
        cost=some,
    )(laid, between, grad[0], act, sums)
    for active in range(stages - 2, -1, -1):
        upstream = hop(grad[0], active + 1, active)
        last = active == 0
        spare = [pltpu.VMEM((sh.pixels, channels), bf16)]
        keep, send, *grad = call(
            functools.partial(backward_kernel, sh, active),
            [VMEM] * 10,
            [pack_shape, pack_shape] + ([] if last else [image_shape]),
            (spare if last else []) + work + slab + spare,
            aliases={8: 0, 9: 1},
        )(entering[active], middles[active], upstream, params, turned, *noted, keep, send)
    other = lax.ppermute(send, "segment", swap)
    finals = [
        ((images, sh.own_rows, channels), bf16),
        ((sh.slab, channels), f32),
        ((width, 2 * channels), f32),
    ]
    grads, conv_grad, mod_grad = pl.pallas_call(
        functools.partial(finish_kernel, sh),
        out_shape=[shape(*final) for final in finals],
        in_specs=[VMEM] * 4,
        out_specs=[ANY] * 3,
        scratch_shapes=[pltpu.VMEM(*final) for final in finals] + [pltpu.SemaphoreType.DMA((MOD_PARTS + 2,))],
        compiler_params=pltpu.CompilerParams(vmem_limit_bytes=CHAIN_LIMIT),
    )(keep, other, embedded, norm_gain)
    return (grads.reshape(1, images, row_count, cols, channels), conv_grad[None], mod_grad[None])


def solution(mesh):
    placed = (
        P(None, "space", None, None),
        P(None, "space", None, None),
        P(),
        P(),
        P(),
        P(),
        P("segment", None, None, None, None),
        P("segment", None, None),
        P("segment", None),
        P("segment", None),
    )
    return jax.shard_map(
        shards,
        mesh=mesh,
        in_specs=placed,
        out_specs=(
            P("segment", None, "space", None, None),
            P("segment", "space", None),
            P("segment", None, None),
        ),
        check_vma=False,
    )
```

```python
import functools
import math

import jax
import jax.numpy as jnp
from jax import lax
from jax.experimental import pallas as pl
from jax.experimental.pallas import tpu as pltpu
from jax.sharding import PartitionSpec as P

GROUPS = 32
EPSILON = 1e-05
PAIR = 2
BLOCK = 64
MOD_PARTS = 4
PREPARE_LIMIT = 60 << 20
CHAIN_LIMIT = 48 << 20
VMEM = pl.BlockSpec(memory_space=pltpu.VMEM)
SMEM = pl.BlockSpec(memory_space=pltpu.SMEM)
ANY = pl.BlockSpec(memory_space=pl.ANY)


def sigmoid(values):
    return 1.0 / (1.0 + jnp.exp(-values))


def over_chunks(count, body):
    if count == 1:
        body(0)
    else:

        def step(i, carry):
            body(i)
            return carry

        lax.fori_loop(0, count, step, 0)


def chunk_start(i, size):
    return 0 if isinstance(i, int) else pl.multiple_of(i * size, size)


def fold_rows(values):
    return jnp.sum(values.reshape(values.shape[0] // 8, 8, values.shape[1]), axis=0)


def column(rows):
    return jnp.sum(rows, axis=0, keepdims=True)


def group_sums(rows, width):
    lanes = lax.broadcasted_iota(jnp.int32, rows.shape, 1)
    size = rows.shape[1]
    step = 1
    while step < width:
        ahead = pltpu.roll(rows, size - step, 1)
        behind = pltpu.roll(rows, step, 1)
        rows = rows + jnp.where((lanes & step) == 0, ahead, behind)
        step *= 2
    return rows


def stack_rows(first, second):
    spot = lax.broadcasted_iota(jnp.int32, (8, first.shape[1]), 0)
    return jnp.where(spot == 0, first, jnp.where(spot == 1, second, 0.0))


class Shape:
    def __init__(self, height, cols, channels, space_count):
        self.cols, self.channels = cols, channels
        self.pixels = height * cols
        self.chunk = cols * max(1, min(self.pixels, 256) // cols)
        self.chunks = self.pixels // self.chunk
        self.width = channels // GROUPS
        self.entries = float(self.pixels * self.width)
        self.padded = self.pixels + 2 * cols
        self.own_rows = height // space_count * cols
        self.slab = 9 * channels // space_count
        step = math.gcd(self.slab, channels)
        self.taps = min(9, -(-(channels - step + self.slab) // channels))
        self.pack = self.slab + self.own_rows + 8
        self.limit = (12 << 20) + self.pixels * channels * 40


def statistics(sh, x_ref):
    zero = jnp.zeros((8, sh.channels), jnp.float32)

    def add(i, sums):
        part = x_ref[pl.ds(chunk_start(i, sh.chunk), sh.chunk), :].astype(jnp.float32)
        return (sums[0] + fold_rows(part), sums[1] + fold_rows(part * part))

    if sh.chunks == 1:
        one, two = add(0, (zero, zero))
    else:
        one, two = lax.fori_loop(0, sh.chunks, add, (zero, zero))
    total = group_sums(stack_rows(column(one), column(two)), sh.width) / sh.entries
    mean = total[0:1]
    return (mean, lax.rsqrt(total[1:2] - mean * mean + EPSILON))


def clear_edges(sh, padded_ref):
    zero = jnp.zeros((3, sh.cols, sh.channels), padded_ref.dtype)
    padded_ref[:, 0 : sh.cols, :] = zero
    padded_ref[:, sh.pixels + sh.cols : sh.padded, :] = zero


def spread(sh, padded_ref, start, values):
    place = pl.ds(start + sh.cols, sh.chunk)
    spot = lax.broadcasted_iota(jnp.int32, values.shape, 0) % sh.cols
    padded_ref[0, place, :] = jnp.where(spot == 0, 0.0, pltpu.roll(values, 1, 0)).astype(jnp.bfloat16)
    padded_ref[1, place, :] = values.astype(jnp.bfloat16)
    padded_ref[2, place, :] = jnp.where(
        spot == sh.cols - 1, 0.0, pltpu.roll(values, sh.chunk - 1, 0)
    ).astype(jnp.bfloat16)


def convolve(sh, padded_ref, start, weight_ref, unit, backward):
    size = min(BLOCK, sh.chunk)
    totals = []
    for first in range(0, sh.chunk, size):
        total = None
        for p in range(3):
            for q in range(3):
                row, col = (2 - p, 2 - q) if backward else (p, q)
                block = padded_ref[col, pl.ds(start + first + row * sh.cols, size), :]
                tap = (3 * p + q) * sh.channels
                weight = weight_ref[unit, tap : tap + sh.channels, :]
                part = lax.dot_general(
                    block,
                    weight,
                    (((1,), (0,)), ((), ())),
                    preferred_element_type=jnp.float32,
                )
                total = part if total is None else total + part
        totals.append(total)
    return totals[0] if len(totals) == 1 else jnp.concatenate(totals, axis=0)


def activation(sh, x_ref, place, stats, params):
    (mean, inv_std), (factor, shift) = stats, params
    pre = (x_ref[place, :].astype(jnp.float32) - mean) * inv_std * factor + shift
    sigma = sigmoid(pre)
    return pre * sigma, sigma * (1.0 + pre * (1.0 - sigma))


def note_unit(sh, x_ref, params, act_ref, slope_ref, turned=False):
    stats = statistics(sh, x_ref)

    def activate(i):
        place = pl.ds(chunk_start(i, sh.chunk), sh.chunk)
        values, slope = activation(sh, x_ref, place, stats, params)
        if turned:
            act_ref[:, place] = values.T.astype(jnp.bfloat16)
        else:
            act_ref[place, :] = values.astype(jnp.bfloat16)
        slope_ref[place, :] = slope

    over_chunks(sh.chunks, activate)
    return stats


def forward_unit(sh, x_ref, out_ref, params, padded_ref, weight_ref, unit, act_ref=None, slope_ref=None):
    stats = statistics(sh, x_ref)

    def activate(i):
        start = chunk_start(i, sh.chunk)
        place = pl.ds(start, sh.chunk)
        values, slope = activation(sh, x_ref, place, stats, params)
        spread(sh, padded_ref, start, values)
        if act_ref is not None:
            act_ref[place, :] = values.astype(jnp.bfloat16)
            slope_ref[place, :] = slope

    def produce(i):
        start = chunk_start(i, sh.chunk)
        inputs = x_ref[pl.ds(start, sh.chunk), :].astype(jnp.float32)
        z = convolve(sh, padded_ref, start, weight_ref, unit, False)
        out_ref[pl.ds(start, sh.chunk), :] = (inputs + z).astype(jnp.bfloat16)

    over_chunks(sh.chunks, activate)
    over_chunks(sh.chunks, produce)
    return stats


def own_place(sh):
    return pl.ds(pl.multiple_of(lax.axis_index("space") * sh.own_rows, sh.own_rows), sh.own_rows)


def place_upstream(sh, up_ref, padded_ref):
    def place(i):
        start = chunk_start(i, sh.chunk)
        spread(sh, padded_ref, start, up_ref[pl.ds(start, sh.chunk), :].astype(jnp.float32))

    over_chunks(sh.chunks, place)


def backward_unit(sh, x_ref, up_ref, grad_ref, params, known, padded_ref, pre_grad_ref, weight_ref, unit, own=False, placed=False):
    slope_ref, (mean, inv_std) = known
    factor, _ = params
    zero = jnp.zeros((8, sh.channels), jnp.float32)

    def differentiate(i, sums):
        start = chunk_start(i, sh.chunk)
        rows = pl.ds(start, sh.chunk)
        normed = (x_ref[rows, :].astype(jnp.float32) - mean) * inv_std
        pre_grad = convolve(sh, padded_ref, start, weight_ref, unit, True) * slope_ref[rows, :]
        pre_grad_ref[rows, :] = pre_grad
        return (sums[0] + fold_rows(pre_grad), sums[1] + fold_rows(pre_grad * normed))

    if not placed:
        place_upstream(sh, up_ref, padded_ref)
    if sh.chunks == 1:
        sums = differentiate(0, (zero, zero))
    else:
        sums = lax.fori_loop(0, sh.chunks, differentiate, (zero, zero))
    sum_grad, sum_cross = column(sums[0]), column(sums[1])
    means = group_sums(stack_rows(factor * sum_grad, factor * sum_cross), sh.width) / sh.entries
    center, tilt = means[0:1], means[1:2]

    def finish(rows):
        normed = (x_ref[rows, :].astype(jnp.float32) - mean) * inv_std
        back = factor * pre_grad_ref[rows, :] - center - normed * tilt
        grad_ref[rows, :] = (up_ref[rows, :].astype(jnp.float32) + inv_std * back).astype(jnp.bfloat16)

    if own:
        finish(own_place(sh))
    else:
        over_chunks(sh.chunks, lambda i: finish(pl.ds(chunk_start(i, sh.chunk), sh.chunk)))
    return stack_rows(sum_grad, sum_cross)


def weight_products(sh, padded_ref, act_ref, slab_ref, grad_ref, sums, unit, keep_ref, send_ref, turned=False):
    core = lax.axis_index("segment") % PAIR
    space = lax.axis_index("space")
    first_row = space * sh.slab
    first_tap = jnp.minimum(first_row // sh.channels, 9 - sh.taps)
    offset = pl.multiple_of(first_row - first_tap * sh.channels, 8)
    for t in range(sh.taps):
        tap = first_tap + t
        row, col = 2 - tap // 3, 2 - tap % 3
        place = pl.ds(t * sh.channels, sh.channels)

        def product(i):
            start = chunk_start(i, sh.chunk)
            block = padded_ref[col, pl.ds(pl.multiple_of(start + row * sh.cols, 16), sh.chunk), :]
            here = pl.ds(start, sh.chunk)
            return lax.dot_general(
                act_ref[:, here] if turned else act_ref[here, :],
                block,
                (((1 if turned else 0,), (0,)), ((), ())),
                preferred_element_type=jnp.float32,
            )

        if sh.chunks == 1:
            slab_ref[place, :] = product(0)
        else:
            slab_ref[place, :] = jnp.zeros((sh.channels, sh.channels), jnp.float32)

            def accumulate(i):
                slab_ref[place, :] += product(i)

            over_chunks(sh.chunks, accumulate)
    mine = slab_ref[pl.ds(offset, sh.slab), :]
    rows = grad_ref[own_place(sh), :]

    def write(ref):
        ref[0 : sh.slab, :] = mine
        ref[sh.slab : sh.slab + sh.own_rows, :] = rows.astype(jnp.float32)
        ref[sh.slab + sh.own_rows : sh.pack, :] = sums

    @pl.when(core == unit)
    def _():
        write(keep_ref)

    @pl.when(core != unit)
    def _():
        write(send_ref)


def place_of():
    index = lax.axis_index("segment")
    return (index // PAIR, index % PAIR)


def unit_params(params_ref, unit):
    return (params_ref[2 * unit : 2 * unit + 1, :], params_ref[2 * unit + 1 : 2 * unit + 2, :])


def sinusoid_of(time, base):
    half = base // 2
    lanes = lax.broadcasted_iota(jnp.int32, (time.shape[0], base), 1)
    power = jnp.where(lanes < half, lanes, lanes - half).astype(jnp.float32)
    angle = time * jnp.exp(-math.log(10000.0) * power / half)
    turns = jnp.floor(angle * (2.0 / math.pi) + 0.5)
    rest = ((angle - turns * 1.5703125) - turns * 4.83751296997e-4) - turns * 7.54978995489e-8
    square = rest * rest
    sine = rest + rest * square * (
        -1.6666654611e-1 + square * (8.3321608736e-3 - square * 1.9515295891e-4)
    )
    cosine = 1.0 - 0.5 * square + square * square * (
        4.166664568298827e-2 + square * (-1.388731625493765e-3 + square * 2.443315711809948e-5)
    )
    quarter = turns.astype(jnp.int32) + jnp.where(lanes < half, 1, 0)
    value = jnp.where(quarter % 2 == 1, cosine, sine)
    return jnp.where((quarter // 2) % 2 == 1, -value, value).astype(jnp.bfloat16)


def start_all(pairs, sems):
    copies = [pltpu.make_async_copy(a, b, sems.at[i]) for i, (a, b) in enumerate(pairs)]
    for copy in copies:
        copy.start()
    return copies


def embed_kernel(times_ref, labels_ref, table_hbm, time_weight_hbm, *refs):
    embedded_ref, turned_ref, table_ref, time_weight_ref, sems = refs
    pairs = [(time_weight_hbm, time_weight_ref)]
    pairs += [(table_hbm.at[pl.ds(labels_ref[i] // 8, 1)], table_ref.at[pl.ds(i, 1)]) for i in range(PAIR)]
    copies = start_all(pairs, sems)
    spot = lax.broadcasted_iota(jnp.int32, (16, 1), 0)
    time = jnp.where(spot % 2 == 0, times_ref[0], times_ref[1]).astype(jnp.float32)
    sinusoid = sinusoid_of(time, time_weight_ref.shape[0])

    def label_row(image):
        block = table_ref[image].astype(jnp.float32)
        row = lax.broadcasted_iota(jnp.int32, block.shape, 0)
        return column(jnp.where(row == labels_ref[image] % 8, block, 0.0))

    for copy in copies:
        copy.wait()
    timed = jnp.dot(sinusoid, time_weight_ref[...], preferred_element_type=jnp.float32)
    timed = timed + jnp.where(spot % 2 == 0, label_row(0), label_row(1))
    embedded = timed * sigmoid(timed)
    embedded_ref[...] = embedded.astype(jnp.bfloat16)
    turned_ref[...] = embedded.T.astype(jnp.bfloat16)


def modulate_kernel(embedded_hbm, mod_weight_hbm, bias_hbm, gain_hbm, keep_ref, send_ref, *scratch):
    embedded_ref, mod_weight_ref, bias_ref, gain_ref, sems = scratch
    core = lax.axis_index("segment") % PAIR
    copies = start_all(zip((embedded_hbm, mod_weight_hbm, bias_hbm, gain_hbm), scratch[:4]), sems)
    for copy in copies:
        copy.wait()
    modulation = jnp.dot(embedded_ref[...], mod_weight_ref[...], preferred_element_type=jnp.float32) + bias_ref[...]
    channels = gain_ref.shape[1]
    factor = gain_ref[...] * (1.0 + modulation[:, :channels])
    shift = modulation[:, channels:]
    first = stack_rows(factor[0:1], shift[0:1])
    second = stack_rows(factor[1:2], shift[1:2])
    keep_ref[...] = jnp.where(core == 0, first, second)
    send_ref[...] = jnp.where(core == 0, second, first)


def layout_kernel(own_any, other_any, mod_keep_any, mod_other_any, weights_ref, params_ref, mods_ref, sems):
    core = lax.axis_index("segment") % PAIR
    pairs = [(mod_keep_any, mods_ref.at[core]), (mod_other_any, mods_ref.at[1 - core])]
    pairs += [(own_any, weights_ref.at[core]), (other_any, weights_ref.at[1 - core])]
    copies = start_all(pairs, sems)
    for copy in copies[:PAIR]:
        copy.wait()
    params_ref[0:2, :] = mods_ref[0, 0:2, :]
    params_ref[2:4, :] = mods_ref[1, 0:2, :]
    params_ref[4:8, :] = jnp.zeros((4, params_ref.shape[1]), jnp.float32)
    for copy in copies[PAIR:]:
        copy.wait()


def assemble(sh, blocks_ref, order, image_ref):
    space = lax.axis_index("space")
    for k, bits in enumerate(order):
        start = pl.multiple_of((space ^ bits) * sh.own_rows, sh.own_rows)
        image_ref[pl.ds(start, sh.own_rows), :] = blocks_ref[k]


def forward_kernel(sh, active_stage, orders, *refs):
    if orders:
        near_ref, far_ref, params_ref, weights, x_ref = refs[:5]
        assemble(sh, near_ref, orders[0], x_ref)
        assemble(sh, far_ref, orders[1], x_ref)
        refs = refs[5:]
    else:
        x_ref, params_ref, weights = refs[:3]
        refs = refs[3:]
    middle_ref, out_ref, padded_ref = refs
    stage, _ = place_of()

    @pl.when(stage == active_stage)
    def _():
        clear_edges(sh, padded_ref)
        forward_unit(sh, x_ref, middle_ref, unit_params(params_ref, 0), padded_ref, weights, 0)
        forward_unit(sh, middle_ref, out_ref, unit_params(params_ref, 1), padded_ref, weights, 1)


def note_kernel(sh, active_stage, x_ref, middle_ref, params_ref, *refs):
    act_ref, slope_ref, stats_ref = refs[-3:]
    stage, _ = place_of()

    @pl.when(stage == active_stage)
    def _():
        for unit, source in enumerate((x_ref, middle_ref)):
            stats = note_unit(sh, source, unit_params(params_ref, unit), act_ref.at[unit], slope_ref.at[unit], True)
            stats_ref[unit] = stack_rows(*stats)


def lay_kernel(sh, active_stage, up_ref, weights_ref, padded_ref, turned_ref):
    stage, _ = place_of()

    @pl.when(stage == active_stage)
    def _():
        clear_edges(sh, padded_ref)
        place_upstream(sh, up_ref, padded_ref)

    for unit in range(PAIR):
        for tap in range(9):
            place = slice(tap * sh.channels, (tap + 1) * sh.channels)
            turned_ref[unit, place, :] = weights_ref[unit, place, :].astype(jnp.float32).T.astype(jnp.bfloat16)


def turn_kernel(sh, active_stage, x_ref, up_ref, laid_ref, params_ref, weights, turned, *refs):
    grad_ref, between_ref, act_ref, sums_ref, padded_ref, pre_grad_ref, middle_ref, slope_ref = refs
    stage, _ = place_of()

    @pl.when(stage == active_stage)
    def _():
        clear_edges(sh, padded_ref)
        params = [unit_params(params_ref, unit) for unit in range(PAIR)]
        acts, slopes = [[ref.at[unit] for unit in range(PAIR)] for ref in (act_ref, slope_ref)]
        first = forward_unit(sh, x_ref, middle_ref, params[0], padded_ref, weights, 0, acts[0], slopes[0])
        second = note_unit(sh, middle_ref, params[1], acts[1], slopes[1])
        work = (pre_grad_ref, turned)
        known = (slopes[1], second)
        sums_ref[1] = backward_unit(
            sh, middle_ref, up_ref, between_ref, params[1], known, laid_ref, *work, 1, placed=True
        )
        known = (slopes[0], first)
        sums_ref[0] = backward_unit(sh, x_ref, between_ref, grad_ref, params[0], known, padded_ref, *work, 0)


def products_kernel(sh, active_stage, laid_ref, between_ref, grad_ref, act_ref, sums_ref, *refs):
    keep_ref, send_ref, padded_ref, slab_ref = refs
    stage, _ = place_of()

    @pl.when(stage == active_stage)
    def _():
        clear_edges(sh, padded_ref)
        place_upstream(sh, between_ref, padded_ref)
        for unit, above, below in ((1, laid_ref, between_ref), (0, padded_ref, grad_ref)):
            outs = (keep_ref, send_ref)
            weight_products(sh, above, act_ref.at[unit], slab_ref, below, sums_ref[unit], unit, *outs)


def backward_kernel(sh, active_stage, *refs):
    x_ref, middle_ref, up_ref, params_ref, weights, act_ref, slope_ref, stats_ref = refs[:8]
    keep_ref, send_ref, grad_ref, padded_ref, pre_grad_ref, slab_ref, between_ref = refs[10:]
    stage, _ = place_of()

    @pl.when(stage == active_stage)
    def _():
        clear_edges(sh, padded_ref)
        for unit, x, above, below in ((1, middle_ref, up_ref, between_ref), (0, x_ref, between_ref, grad_ref)):
            stats = (stats_ref[unit, 0:1, :], stats_ref[unit, 1:2, :])
            known = (slope_ref.at[unit], stats)
            params = unit_params(params_ref, unit)
            own = unit == 0 and active_stage == 0
            sums = backward_unit(sh, x, above, below, params, known, padded_ref, pre_grad_ref, weights, unit, own)
            outs = (keep_ref, send_ref)
            weight_products(sh, padded_ref, act_ref.at[unit], slab_ref, below, sums, unit, *outs, turned=True)


def finish_kernel(sh, keep_ref, other_ref, embedded_ref, gain_ref, grads_hbm, conv_hbm, mod_hbm, *scratch):
    grads_ref, conv_ref, mod_ref, sems = scratch
    core = lax.axis_index("segment") % PAIR
    base = sh.slab + sh.own_rows

    def mod_rows(ref):
        return jnp.concatenate([gain_ref[...] * ref[base + 1 : base + 2, :], ref[base : base + 1, :]], axis=1)

    own, other = mod_rows(keep_ref), mod_rows(other_ref)
    spot = lax.broadcasted_iota(jnp.int32, (16, own.shape[1]), 0)
    values = jnp.where(spot % 2 == core, own, other)
    high = values.astype(jnp.bfloat16).astype(jnp.float32)
    rest = values - high
    middle = rest.astype(jnp.bfloat16).astype(jnp.float32)
    low = rest - middle
    part = spot // 2
    pieces = jnp.where(part == 0, high, jnp.where(part == 1, middle, jnp.where(part == 2, low, 0.0)))
    pieces = pieces.astype(jnp.bfloat16)
    copies = []
    size = mod_ref.shape[0] // MOD_PARTS
    for k in range(MOD_PARTS):
        place = slice(k * size, (k + 1) * size)
        mod_ref[place, :] = lax.dot_general(
            embedded_ref[place, :],
            pieces,
            (((1,), (0,)), ((), ())),
            preferred_element_type=jnp.float32,
        )
        copies.append(pltpu.make_async_copy(mod_ref.at[place], mod_hbm.at[place], sems.at[k]))
        copies[-1].start()
    conv_ref[...] = keep_ref[0 : sh.slab, :] + other_ref[0 : sh.slab, :]
    copies.append(pltpu.make_async_copy(conv_ref, conv_hbm, sems.at[MOD_PARTS]))
    copies[-1].start()
    rows = slice(sh.slab, sh.slab + sh.own_rows)
    grads_ref[pl.ds(core, 1)] = keep_ref[rows, :].astype(jnp.bfloat16)[None]
    grads_ref[pl.ds(1 - core, 1)] = other_ref[rows, :].astype(jnp.bfloat16)[None]
    copies.append(pltpu.make_async_copy(grads_ref, grads_hbm, sems.at[MOD_PARTS + 1]))
    copies[-1].start()
    for copy in copies:
        copy.wait()


def shards(
    x_in,
    out_cotangent,
    timesteps,
    labels,
    time_weight,
    label_table,
    conv_weight,
    mod_weight,
    mod_bias,
    norm_gain,
):
    segments, spaces = lax.axis_size("segment"), lax.axis_size("space")
    stages = segments // PAIR
    stage, core = place_of()
    images, row_count, cols, channels = x_in.shape
    sh = Shape(row_count * spaces, cols, channels, spaces)
    f32, bf16 = jnp.float32, jnp.bfloat16

    def call(body, ins, outs, scratch=(), limit=CHAIN_LIMIT, cost=None, aliases={}):
        return pl.pallas_call(
            body,
            out_shape=outs,
            in_specs=ins,
            out_specs=[VMEM] * len(outs),
            scratch_shapes=list(scratch),
            input_output_aliases=aliases,
            compiler_params=pltpu.CompilerParams(vmem_limit_bytes=limit),
            cost_estimate=cost,
        )

    shape = jax.ShapeDtypeStruct
    swap = [(i, i ^ 1) for i in range(segments)]
    weight = conv_weight.reshape(9 * channels, channels)
    other_weight = lax.ppermute(weight, "segment", swap)
    ends = jnp.where(stage == 0, x_in, out_cotangent)
    near = lax.dynamic_index_in_dim(ends, core, 0, keepdims=False).reshape(1, sh.own_rows, channels)
    table = label_table.reshape(-1, 8, label_table.shape[1])
    width = time_weight.shape[1]
    some = pl.CostEstimate(flops=1 << 20, bytes_accessed=4 << 20, transcendentals=0)
    order, bit = [0], spaces // 2
    waiting = []
    while True:
        far = lax.ppermute(near, "space", [(i, i ^ bit) for i in range(spaces)])
        if not waiting:
            embedded, turned_embedded = call(
                embed_kernel,
                [SMEM, SMEM, ANY, ANY],
                [shape((16, width), bf16), shape((width, 16), bf16)],
                [
                    pltpu.VMEM((PAIR, 8, width), bf16),
                    pltpu.VMEM(time_weight.shape, bf16),
                    pltpu.SemaphoreType.DMA((PAIR + 1,)),
                ],
                PREPARE_LIMIT,
                some,
            )(timesteps, labels, table, time_weight)
            waiting = [embedded]
            far, embedded = lax.optimization_barrier((far, embedded))
        elif len(waiting) == 1:
            operands = (embedded, mod_weight[0], mod_bias, norm_gain)
            mod_keep, mod_send = call(
                modulate_kernel,
                [ANY] * 4,
                [shape((8, channels), f32)] * 2,
                [pltpu.VMEM(value.shape, value.dtype) for value in operands] + [pltpu.SemaphoreType.DMA((4,))],
                PREPARE_LIMIT,
                some,
            )(*operands)
            waiting.append(mod_keep)
            far, mod_keep, mod_send = lax.optimization_barrier((far, mod_keep, mod_send))
        far_order = [k ^ bit for k in order]
        if bit == 1:
            break
        near = jnp.concatenate([near, far])
        order, bit = order + far_order, bit // 2
    mod_other = lax.ppermute(mod_send, "segment", swap)
    weights, params = call(
        layout_kernel,
        [ANY] * 4,
        [shape((PAIR, 9 * channels, channels), bf16), shape((8, channels), f32)],
        [pltpu.VMEM((PAIR, 8, channels), f32), pltpu.SemaphoreType.DMA((2 * PAIR,))],
        cost=some,
    )(weight, other_weight, mod_keep, mod_other)

    image_shape = shape((sh.pixels, channels), bf16)
    pack_shape = shape((sh.pack, channels), f32)
    common = [pltpu.VMEM((3, sh.padded, channels), bf16)]

    def hop(value, source, target):
        pairs = [(PAIR * source + k, PAIR * target + k) for k in range(PAIR)]
        return lax.ppermute(value, "segment", pairs + [(b, a) for a, b in pairs])

    image, middle, out = call(
        functools.partial(forward_kernel, sh, 0, (order, far_order)),
        [VMEM] * 4,
        [image_shape] * 3,
        common,
    )(near, far, params, weights)
    entering, middles = [image, hop(out, 0, 1)], [middle]
    for active in range(1, stages - 1):
        middle, out = call(
            functools.partial(forward_kernel, sh, active, None),
            [VMEM] * 3,
            [image_shape, image_shape],
            common,
        )(entering[active], params, weights)
        middles.append(middle)
        entering.append(hop(out, active, active + 1))

    noted = []
    for active in range(stages - 1):
        noted = call(
            functools.partial(note_kernel, sh, active),
            [VMEM] * (3 + len(noted)),
            [
                shape((PAIR, channels, sh.pixels), bf16),
                shape((PAIR, sh.pixels, channels), f32),
                shape((PAIR, 8, channels), f32),
            ],
            cost=some,
            aliases={3 + k: k for k in range(len(noted))},
        )(entering[active], middles[active], params, *noted)

    work = common + [pltpu.VMEM((sh.pixels, channels), f32)]
    slab = [pltpu.VMEM((sh.taps * channels, channels), f32)]
    pair_shape = shape((PAIR, sh.pixels, channels), bf16)
    laid, turned = call(
        functools.partial(lay_kernel, sh, stages - 1),
        [VMEM] * 2,
        [shape((3, sh.padded, channels), bf16), shape((PAIR, 9 * channels, channels), bf16)],
        cost=some,
    )(image, weights)
    *grad, between, act, sums = call(
        functools.partial(turn_kernel, sh, stages - 1),
        [VMEM] * 6,
        [image_shape, image_shape, pair_shape, shape((PAIR, 8, channels), f32)],
        work + [pltpu.VMEM((sh.pixels, channels), bf16), pltpu.VMEM((PAIR, sh.pixels, channels), f32)],
    )(entering[stages - 1], image, laid, params, weights, turned)
    keep, send = call(
        functools.partial(products_kernel, sh, stages - 1),
        [VMEM] * 5,
        [pack_shape, pack_shape],
        common + slab,
        cost=some,
    )(laid, between, grad[0], act, sums)
    for active in range(stages - 2, -1, -1):
        upstream = hop(grad[0], active + 1, active)
        last = active == 0
        spare = [pltpu.VMEM((sh.pixels, channels), bf16)]
        keep, send, *grad = call(
            functools.partial(backward_kernel, sh, active),
            [VMEM] * 10,
            [pack_shape, pack_shape] + ([] if last else [image_shape]),
            (spare if last else []) + work + slab + spare,
            aliases={8: 0, 9: 1},
        )(entering[active], middles[active], upstream, params, turned, *noted, keep, send)
    other = lax.ppermute(send, "segment", swap)
    finals = [
        ((images, sh.own_rows, channels), bf16),
        ((sh.slab, channels), f32),
        ((width, 2 * channels), f32),
    ]
    grads, conv_grad, mod_grad = pl.pallas_call(
        functools.partial(finish_kernel, sh),
        out_shape=[shape(*final) for final in finals],
        in_specs=[VMEM] * 4,
        out_specs=[ANY] * 3,
        scratch_shapes=[pltpu.VMEM(*final) for final in finals] + [pltpu.SemaphoreType.DMA((MOD_PARTS + 2,))],
        compiler_params=pltpu.CompilerParams(vmem_limit_bytes=CHAIN_LIMIT),
    )(keep, other, turned_embedded, norm_gain)
    return (grads.reshape(1, images, row_count, cols, channels), conv_grad[None], mod_grad[None])


def solution(mesh):
    placed = (
        P(None, "space", None, None),
        P(None, "space", None, None),
        P(),
        P(),
        P(),
        P(),
        P("segment", None, None, None, None),
        P("segment", None, None),
        P("segment", None),
        P("segment", None),
    )
    return jax.shard_map(
        shards,
        mesh=mesh,
        in_specs=placed,
        out_specs=(
            P("segment", None, "space", None, None),
            P("segment", "space", None),
            P("segment", None, None),
        ),
        check_vma=False,
    )
```

```python
import functools
import math

import jax
import jax.numpy as jnp
from jax import lax
from jax.experimental import pallas as pl
from jax.experimental.pallas import tpu as pltpu
from jax.sharding import PartitionSpec as P

GROUPS = 32
EPSILON = 1e-05
PAIR = 2
BLOCK = 128
MOD_PARTS = 4
PREPARE_LIMIT = 60 << 20
CHAIN_LIMIT = 48 << 20
VMEM = pl.BlockSpec(memory_space=pltpu.VMEM)
SMEM = pl.BlockSpec(memory_space=pltpu.SMEM)
ANY = pl.BlockSpec(memory_space=pl.ANY)


def sigmoid(values):
    return 1.0 / (1.0 + jnp.exp(-values))


def over_chunks(count, body):
    if count == 1:
        body(0)
    else:

        def step(i, carry):
            body(i)
            return carry

        lax.fori_loop(0, count, step, 0)


def chunk_start(i, size):
    return 0 if isinstance(i, int) else pl.multiple_of(i * size, size)


def fold_rows(values):
    return jnp.sum(values.reshape(values.shape[0] // 8, 8, values.shape[1]), axis=0)


def column(rows):
    return jnp.sum(rows, axis=0, keepdims=True)


def group_sums(rows, width):
    lanes = lax.broadcasted_iota(jnp.int32, rows.shape, 1)
    size = rows.shape[1]
    step = 1
    while step < width:
        ahead = pltpu.roll(rows, size - step, 1)
        behind = pltpu.roll(rows, step, 1)
        rows = rows + jnp.where((lanes & step) == 0, ahead, behind)
        step *= 2
    return rows


def stack_rows(first, second):
    spot = lax.broadcasted_iota(jnp.int32, (8, first.shape[1]), 0)
    return jnp.where(spot == 0, first, jnp.where(spot == 1, second, 0.0))


class Shape:
    def __init__(self, height, cols, channels, space_count):
        self.cols, self.channels = cols, channels
        self.pixels = height * cols
        self.chunk = cols * max(1, min(self.pixels, 256) // cols)
        self.chunks = self.pixels // self.chunk
        self.width = channels // GROUPS
        self.entries = float(self.pixels * self.width)
        self.padded = self.pixels + 2 * cols
        self.own_rows = height // space_count * cols
        self.slab = 9 * channels // space_count
        step = math.gcd(self.slab, channels)
        self.taps = min(9, -(-(channels - step + self.slab) // channels))
        self.pack = self.slab + self.own_rows + 8
        self.limit = (12 << 20) + self.pixels * channels * 40


def statistics(sh, x_ref):
    zero = jnp.zeros((8, sh.channels), jnp.float32)

    def add(i, sums):
        part = x_ref[pl.ds(chunk_start(i, sh.chunk), sh.chunk), :].astype(jnp.float32)
        return (sums[0] + fold_rows(part), sums[1] + fold_rows(part * part))

    if sh.chunks == 1:
        one, two = add(0, (zero, zero))
    else:
        one, two = lax.fori_loop(0, sh.chunks, add, (zero, zero))
    total = group_sums(stack_rows(column(one), column(two)), sh.width) / sh.entries
    mean = total[0:1]
    return (mean, lax.rsqrt(total[1:2] - mean * mean + EPSILON))


def clear_edges(sh, padded_ref):
    zero = jnp.zeros((3, sh.cols, sh.channels), padded_ref.dtype)
    padded_ref[:, 0 : sh.cols, :] = zero
    padded_ref[:, sh.pixels + sh.cols : sh.padded, :] = zero


def spread(sh, padded_ref, start, values):
    place = pl.ds(start + sh.cols, sh.chunk)
    spot = lax.broadcasted_iota(jnp.int32, values.shape, 0) % sh.cols
    padded_ref[0, place, :] = jnp.where(spot == 0, 0.0, pltpu.roll(values, 1, 0)).astype(jnp.bfloat16)
    padded_ref[1, place, :] = values.astype(jnp.bfloat16)
    padded_ref[2, place, :] = jnp.where(
        spot == sh.cols - 1, 0.0, pltpu.roll(values, sh.chunk - 1, 0)
    ).astype(jnp.bfloat16)


def convolve(sh, padded_ref, start, weight_ref, unit, backward):
    size = min(BLOCK, sh.chunk)
    totals = []
    for first in range(0, sh.chunk, size):
        total = None
        for p in range(3):
            for q in range(3):
                row, col = (2 - p, 2 - q) if backward else (p, q)
                block = padded_ref[col, pl.ds(start + first + row * sh.cols, size), :]
                tap = (3 * p + q) * sh.channels
                weight = weight_ref[unit, tap : tap + sh.channels, :]
                part = lax.dot_general(
                    block,
                    weight,
                    (((1,), (0,)), ((), ())),
                    preferred_element_type=jnp.float32,
                )
                total = part if total is None else total + part
        totals.append(total)
    return totals[0] if len(totals) == 1 else jnp.concatenate(totals, axis=0)


def activation(sh, x_ref, place, stats, params):
    (mean, inv_std), (factor, shift) = stats, params
    pre = (x_ref[place, :].astype(jnp.float32) - mean) * inv_std * factor + shift
    sigma = sigmoid(pre)
    return pre * sigma, sigma * (1.0 + pre * (1.0 - sigma))


def note_unit(sh, x_ref, params, act_ref, slope_ref, turned=False):
    stats = statistics(sh, x_ref)

    def activate(i):
        place = pl.ds(chunk_start(i, sh.chunk), sh.chunk)
        values, slope = activation(sh, x_ref, place, stats, params)
        if turned:
            act_ref[:, place] = values.T.astype(jnp.bfloat16)
        else:
            act_ref[place, :] = values.astype(jnp.bfloat16)
        slope_ref[place, :] = slope

    over_chunks(sh.chunks, activate)
    return stats


def forward_unit(sh, x_ref, out_ref, params, padded_ref, weight_ref, unit, act_ref=None, slope_ref=None):
    stats = statistics(sh, x_ref)

    def activate(i):
        start = chunk_start(i, sh.chunk)
        place = pl.ds(start, sh.chunk)
        values, slope = activation(sh, x_ref, place, stats, params)
        spread(sh, padded_ref, start, values)
        if act_ref is not None:
            act_ref[place, :] = values.astype(jnp.bfloat16)
            slope_ref[place, :] = slope

    def produce(i):
        start = chunk_start(i, sh.chunk)
        inputs = x_ref[pl.ds(start, sh.chunk), :].astype(jnp.float32)
        z = convolve(sh, padded_ref, start, weight_ref, unit, False)
        out_ref[pl.ds(start, sh.chunk), :] = (inputs + z).astype(jnp.bfloat16)

    over_chunks(sh.chunks, activate)
    over_chunks(sh.chunks, produce)
    return stats


def own_place(sh):
    return pl.ds(pl.multiple_of(lax.axis_index("space") * sh.own_rows, sh.own_rows), sh.own_rows)


def place_upstream(sh, up_ref, padded_ref):
    def place(i):
        start = chunk_start(i, sh.chunk)
        spread(sh, padded_ref, start, up_ref[pl.ds(start, sh.chunk), :].astype(jnp.float32))

    over_chunks(sh.chunks, place)


def backward_unit(sh, x_ref, up_ref, grad_ref, params, known, padded_ref, pre_grad_ref, weight_ref, unit, own=False, placed=False):
    slope_ref, (mean, inv_std) = known
    factor, _ = params
    zero = jnp.zeros((8, sh.channels), jnp.float32)

    def differentiate(i, sums):
        start = chunk_start(i, sh.chunk)
        rows = pl.ds(start, sh.chunk)
        normed = (x_ref[rows, :].astype(jnp.float32) - mean) * inv_std
        pre_grad = convolve(sh, padded_ref, start, weight_ref, unit, True) * slope_ref[rows, :]
        pre_grad_ref[rows, :] = pre_grad
        return (sums[0] + fold_rows(pre_grad), sums[1] + fold_rows(pre_grad * normed))

    if not placed:
        place_upstream(sh, up_ref, padded_ref)
    if sh.chunks == 1:
        sums = differentiate(0, (zero, zero))
    else:
        sums = lax.fori_loop(0, sh.chunks, differentiate, (zero, zero))
    sum_grad, sum_cross = column(sums[0]), column(sums[1])
    means = group_sums(stack_rows(factor * sum_grad, factor * sum_cross), sh.width) / sh.entries
    center, tilt = means[0:1], means[1:2]

    def finish(rows):
        normed = (x_ref[rows, :].astype(jnp.float32) - mean) * inv_std
        back = factor * pre_grad_ref[rows, :] - center - normed * tilt
        grad_ref[rows, :] = (up_ref[rows, :].astype(jnp.float32) + inv_std * back).astype(jnp.bfloat16)

    if own:
        finish(own_place(sh))
    else:
        over_chunks(sh.chunks, lambda i: finish(pl.ds(chunk_start(i, sh.chunk), sh.chunk)))
    return stack_rows(sum_grad, sum_cross)


def slab_place(sh):
    first_row = lax.axis_index("space") * sh.slab
    first_tap = jnp.minimum(first_row // sh.channels, 9 - sh.taps)
    return (first_tap, pl.multiple_of(first_row - first_tap * sh.channels, 8))


def weight_products(sh, padded_ref, act_ref, slab_ref, turned=False):
    first_tap, _ = slab_place(sh)
    for t in range(sh.taps):
        tap = first_tap + t
        row, col = 2 - tap // 3, 2 - tap % 3
        place = pl.ds(t * sh.channels, sh.channels)

        def product(i):
            start = chunk_start(i, sh.chunk)
            block = padded_ref[col, pl.ds(pl.multiple_of(start + row * sh.cols, 16), sh.chunk), :]
            here = pl.ds(start, sh.chunk)
            return lax.dot_general(
                act_ref[:, here] if turned else act_ref[here, :],
                block,
                (((1 if turned else 0,), (0,)), ((), ())),
                preferred_element_type=jnp.float32,
            )

        if sh.chunks == 1:
            slab_ref[place, :] = product(0)
        else:
            slab_ref[place, :] = jnp.zeros((sh.channels, sh.channels), jnp.float32)

            def accumulate(i):
                slab_ref[place, :] += product(i)

            over_chunks(sh.chunks, accumulate)


def write_pack(sh, slab_ref, grad_ref, sums, unit, keep_ref, send_ref):
    core = lax.axis_index("segment") % PAIR
    _, offset = slab_place(sh)
    mine = slab_ref[pl.ds(offset, sh.slab), :]
    rows = grad_ref[own_place(sh), :]

    def write(ref):
        ref[0 : sh.slab, :] = mine
        ref[sh.slab : sh.slab + sh.own_rows, :] = rows.astype(jnp.float32)
        ref[sh.slab + sh.own_rows : sh.pack, :] = sums

    @pl.when(core == unit)
    def _():
        write(keep_ref)

    @pl.when(core != unit)
    def _():
        write(send_ref)


def place_of():
    index = lax.axis_index("segment")
    return (index // PAIR, index % PAIR)


def unit_params(params_ref, unit):
    return (params_ref[2 * unit : 2 * unit + 1, :], params_ref[2 * unit + 1 : 2 * unit + 2, :])


def sinusoid_of(time, base):
    half = base // 2
    lanes = lax.broadcasted_iota(jnp.int32, (time.shape[0], base), 1)
    power = jnp.where(lanes < half, lanes, lanes - half).astype(jnp.float32)
    angle = time * jnp.exp(-math.log(10000.0) * power / half)
    turns = jnp.floor(angle * (2.0 / math.pi) + 0.5)
    rest = ((angle - turns * 1.5703125) - turns * 4.83751296997e-4) - turns * 7.54978995489e-8
    square = rest * rest
    sine = rest + rest * square * (
        -1.6666654611e-1 + square * (8.3321608736e-3 - square * 1.9515295891e-4)
    )
    cosine = 1.0 - 0.5 * square + square * square * (
        4.166664568298827e-2 + square * (-1.388731625493765e-3 + square * 2.443315711809948e-5)
    )
    quarter = turns.astype(jnp.int32) + jnp.where(lanes < half, 1, 0)
    value = jnp.where(quarter % 2 == 1, cosine, sine)
    return jnp.where((quarter // 2) % 2 == 1, -value, value).astype(jnp.bfloat16)


def start_all(pairs, sems):
    copies = [pltpu.make_async_copy(a, b, sems.at[i]) for i, (a, b) in enumerate(pairs)]
    for copy in copies:
        copy.start()
    return copies


def embed_kernel(times_ref, labels_ref, table_hbm, time_weight_hbm, *refs):
    embedded_ref, turned_ref, table_ref, time_weight_ref, sems = refs
    pairs = [(time_weight_hbm, time_weight_ref)]
    pairs += [(table_hbm.at[pl.ds(labels_ref[i] // 8, 1)], table_ref.at[pl.ds(i, 1)]) for i in range(PAIR)]
    copies = start_all(pairs, sems)
    spot = lax.broadcasted_iota(jnp.int32, (16, 1), 0)
    time = jnp.where(spot % 2 == 0, times_ref[0], times_ref[1]).astype(jnp.float32)
    sinusoid = sinusoid_of(time, time_weight_ref.shape[0])

    def label_row(image):
        block = table_ref[image].astype(jnp.float32)
        row = lax.broadcasted_iota(jnp.int32, block.shape, 0)
        return column(jnp.where(row == labels_ref[image] % 8, block, 0.0))

    for copy in copies:
        copy.wait()
    timed = jnp.dot(sinusoid, time_weight_ref[...], preferred_element_type=jnp.float32)
    timed = timed + jnp.where(spot % 2 == 0, label_row(0), label_row(1))
    embedded = timed * sigmoid(timed)
    embedded_ref[...] = embedded.astype(jnp.bfloat16)
    turned_ref[...] = embedded.T.astype(jnp.bfloat16)


def modulate_kernel(embedded_hbm, mod_weight_hbm, bias_hbm, gain_hbm, keep_ref, send_ref, *scratch):
    embedded_ref, mod_weight_ref, bias_ref, gain_ref, sems = scratch
    core = lax.axis_index("segment") % PAIR
    copies = start_all(zip((embedded_hbm, mod_weight_hbm, bias_hbm, gain_hbm), scratch[:4]), sems)
    for copy in copies:
        copy.wait()
    modulation = jnp.dot(embedded_ref[...], mod_weight_ref[...], preferred_element_type=jnp.float32) + bias_ref[...]
    channels = gain_ref.shape[1]
    factor = gain_ref[...] * (1.0 + modulation[:, :channels])
    shift = modulation[:, channels:]
    first = stack_rows(factor[0:1], shift[0:1])
    second = stack_rows(factor[1:2], shift[1:2])
    keep_ref[...] = jnp.where(core == 0, first, second)
    send_ref[...] = jnp.where(core == 0, second, first)


def layout_kernel(own_any, other_any, mod_keep_any, mod_other_any, weights_ref, params_ref, mods_ref, sems):
    core = lax.axis_index("segment") % PAIR
    pairs = [(mod_keep_any, mods_ref.at[core]), (mod_other_any, mods_ref.at[1 - core])]
    pairs += [(own_any, weights_ref.at[core]), (other_any, weights_ref.at[1 - core])]
    copies = start_all(pairs, sems)
    for copy in copies[:PAIR]:
        copy.wait()
    params_ref[0:2, :] = mods_ref[0, 0:2, :]
    params_ref[2:4, :] = mods_ref[1, 0:2, :]
    params_ref[4:8, :] = jnp.zeros((4, params_ref.shape[1]), jnp.float32)
    for copy in copies[PAIR:]:
        copy.wait()


def assemble(sh, blocks_ref, order, image_ref):
    space = lax.axis_index("space")
    for k, bits in enumerate(order):
        start = pl.multiple_of((space ^ bits) * sh.own_rows, sh.own_rows)
        image_ref[pl.ds(start, sh.own_rows), :] = blocks_ref[k]


def forward_kernel(sh, active_stage, orders, *refs):
    if orders:
        near_ref, far_ref, params_ref, weights, x_ref = refs[:5]
        assemble(sh, near_ref, orders[0], x_ref)
        assemble(sh, far_ref, orders[1], x_ref)
        refs = refs[5:]
    else:
        x_ref, params_ref, weights = refs[:3]
        refs = refs[3:]
    middle_ref, out_ref, padded_ref = refs
    stage, _ = place_of()

    @pl.when(stage == active_stage)
    def _():
        clear_edges(sh, padded_ref)
        forward_unit(sh, x_ref, middle_ref, unit_params(params_ref, 0), padded_ref, weights, 0)
        forward_unit(sh, middle_ref, out_ref, unit_params(params_ref, 1), padded_ref, weights, 1)


def note_kernel(sh, active_stage, x_ref, middle_ref, params_ref, *refs):
    act_ref, slope_ref, stats_ref = refs[-3:]
    stage, _ = place_of()

    @pl.when(stage == active_stage)
    def _():
        for unit, source in enumerate((x_ref, middle_ref)):
            stats = note_unit(sh, source, unit_params(params_ref, unit), act_ref.at[unit], slope_ref.at[unit], True)
            stats_ref[unit] = stack_rows(*stats)


def lay_kernel(sh, active_stage, up_ref, weights_ref, padded_ref, turned_ref):
    stage, _ = place_of()

    @pl.when(stage == active_stage)
    def _():
        clear_edges(sh, padded_ref)
        place_upstream(sh, up_ref, padded_ref)

    for unit in range(PAIR):
        for tap in range(9):
            place = slice(tap * sh.channels, (tap + 1) * sh.channels)
            turned_ref[unit, place, :] = weights_ref[unit, place, :].astype(jnp.float32).T.astype(jnp.bfloat16)


def turn_kernel(sh, active_stage, x_ref, up_ref, laid_ref, params_ref, weights, turned, *refs):
    grad_ref, between_ref, act_ref, sums_ref, padded_ref, pre_grad_ref, middle_ref, slope_ref = refs
    stage, _ = place_of()

    @pl.when(stage == active_stage)
    def _():
        clear_edges(sh, padded_ref)
        params = [unit_params(params_ref, unit) for unit in range(PAIR)]
        acts, slopes = [[ref.at[unit] for unit in range(PAIR)] for ref in (act_ref, slope_ref)]
        first = forward_unit(sh, x_ref, middle_ref, params[0], padded_ref, weights, 0, acts[0], slopes[0])
        second = note_unit(sh, middle_ref, params[1], acts[1], slopes[1])
        work = (pre_grad_ref, turned)
        known = (slopes[1], second)
        sums_ref[1] = backward_unit(
            sh, middle_ref, up_ref, between_ref, params[1], known, laid_ref, *work, 1, placed=True
        )
        known = (slopes[0], first)
        sums_ref[0] = backward_unit(sh, x_ref, between_ref, grad_ref, params[0], known, padded_ref, *work, 0)


def products_kernel(sh, active_stage, laid_ref, between_ref, grad_ref, act_ref, sums_ref, *refs):
    keep_ref, send_ref, padded_ref, slab_ref = refs
    stage, _ = place_of()

    @pl.when(stage == active_stage)
    def _():
        clear_edges(sh, padded_ref)
        place_upstream(sh, between_ref, padded_ref)
        for unit, above, below in ((1, laid_ref, between_ref), (0, padded_ref, grad_ref)):
            weight_products(sh, above, act_ref.at[unit], slab_ref)
            write_pack(sh, slab_ref, below, sums_ref[unit], unit, keep_ref, send_ref)


def backward_kernel(sh, active_stage, *refs):
    x_ref, middle_ref, up_ref, params_ref, weights, act_ref, slope_ref, stats_ref = refs[:8]
    keep_ref, send_ref, grad_ref, padded_ref, pre_grad_ref, slab_ref, between_ref, second_ref, other_slab_ref = refs[10:]
    stage, _ = place_of()

    @pl.when(stage == active_stage)
    def _():
        clear_edges(sh, padded_ref)
        clear_edges(sh, second_ref)
        packs = []
        for unit, x, above, below, shifted, slab in (
            (1, middle_ref, up_ref, between_ref, second_ref, other_slab_ref),
            (0, x_ref, between_ref, grad_ref, padded_ref, slab_ref),
        ):
            known = (slope_ref.at[unit], (stats_ref[unit, 0:1, :], stats_ref[unit, 1:2, :]))
            params = unit_params(params_ref, unit)
            own = unit == 0 and active_stage == 0
            sums = backward_unit(sh, x, above, below, params, known, shifted, pre_grad_ref, weights, unit, own)
            weight_products(sh, shifted, act_ref.at[unit], slab, turned=True)
            packs.append((slab, below, sums, unit))
        for pack in packs:
            write_pack(sh, *pack, keep_ref, send_ref)


def finish_kernel(sh, keep_ref, other_ref, embedded_ref, gain_ref, grads_hbm, conv_hbm, mod_hbm, *scratch):
    grads_ref, conv_ref, mod_ref, sems = scratch
    core = lax.axis_index("segment") % PAIR
    base = sh.slab + sh.own_rows

    def mod_rows(ref):
        return jnp.concatenate([gain_ref[...] * ref[base + 1 : base + 2, :], ref[base : base + 1, :]], axis=1)

    own, other = mod_rows(keep_ref), mod_rows(other_ref)
    spot = lax.broadcasted_iota(jnp.int32, (16, own.shape[1]), 0)
    values = jnp.where(spot % 2 == core, own, other)
    high = values.astype(jnp.bfloat16).astype(jnp.float32)
    rest = values - high
    middle = rest.astype(jnp.bfloat16).astype(jnp.float32)
    low = rest - middle
    part = spot // 2
    pieces = jnp.where(part == 0, high, jnp.where(part == 1, middle, jnp.where(part == 2, low, 0.0)))
    pieces = pieces.astype(jnp.bfloat16)
    copies = []
    size = mod_ref.shape[0] // MOD_PARTS
    for k in range(MOD_PARTS):
        place = slice(k * size, (k + 1) * size)
        mod_ref[place, :] = lax.dot_general(
            embedded_ref[place, :],
            pieces,
            (((1,), (0,)), ((), ())),
            preferred_element_type=jnp.float32,
        )
        copies.append(pltpu.make_async_copy(mod_ref.at[place], mod_hbm.at[place], sems.at[k]))
        copies[-1].start()
    conv_ref[...] = keep_ref[0 : sh.slab, :] + other_ref[0 : sh.slab, :]
    copies.append(pltpu.make_async_copy(conv_ref, conv_hbm, sems.at[MOD_PARTS]))
    copies[-1].start()
    rows = slice(sh.slab, sh.slab + sh.own_rows)
    grads_ref[pl.ds(core, 1)] = keep_ref[rows, :].astype(jnp.bfloat16)[None]
    grads_ref[pl.ds(1 - core, 1)] = other_ref[rows, :].astype(jnp.bfloat16)[None]
    copies.append(pltpu.make_async_copy(grads_ref, grads_hbm, sems.at[MOD_PARTS + 1]))
    copies[-1].start()
    for copy in copies:
        copy.wait()


def shards(
    x_in,
    out_cotangent,
    timesteps,
    labels,
    time_weight,
    label_table,
    conv_weight,
    mod_weight,
    mod_bias,
    norm_gain,
):
    segments, spaces = lax.axis_size("segment"), lax.axis_size("space")
    stages = segments // PAIR
    stage, core = place_of()
    images, row_count, cols, channels = x_in.shape
    sh = Shape(row_count * spaces, cols, channels, spaces)
    f32, bf16 = jnp.float32, jnp.bfloat16

    def call(body, ins, outs, scratch=(), limit=CHAIN_LIMIT, cost=None, aliases={}):
        return pl.pallas_call(
            body,
            out_shape=outs,
            in_specs=ins,
            out_specs=[VMEM] * len(outs),
            scratch_shapes=list(scratch),
            input_output_aliases=aliases,
            compiler_params=pltpu.CompilerParams(vmem_limit_bytes=limit),
            cost_estimate=cost,
        )

    shape = jax.ShapeDtypeStruct
    swap = [(i, i ^ 1) for i in range(segments)]
    weight = conv_weight.reshape(9 * channels, channels)
    other_weight = lax.ppermute(weight, "segment", swap)
    ends = jnp.where(stage == 0, x_in, out_cotangent)
    near = lax.dynamic_index_in_dim(ends, core, 0, keepdims=False).reshape(1, sh.own_rows, channels)
    table = label_table.reshape(-1, 8, label_table.shape[1])
    width = time_weight.shape[1]
    some = pl.CostEstimate(flops=1 << 20, bytes_accessed=4 << 20, transcendentals=0)
    order, bit = [0], spaces // 2
    waiting = []
    while True:
        far = lax.ppermute(near, "space", [(i, i ^ bit) for i in range(spaces)])
        if not waiting:
            embedded, turned_embedded = call(
                embed_kernel,
                [SMEM, SMEM, ANY, ANY],
                [shape((16, width), bf16), shape((width, 16), bf16)],
                [
                    pltpu.VMEM((PAIR, 8, width), bf16),
                    pltpu.VMEM(time_weight.shape, bf16),
                    pltpu.SemaphoreType.DMA((PAIR + 1,)),
                ],
                PREPARE_LIMIT,
                some,
            )(timesteps, labels, table, time_weight)
            waiting = [embedded]
            far, embedded = lax.optimization_barrier((far, embedded))
        elif len(waiting) == 1:
            operands = (embedded, mod_weight[0], mod_bias, norm_gain)
            mod_keep, mod_send = call(
                modulate_kernel,
                [ANY] * 4,
                [shape((8, channels), f32)] * 2,
                [pltpu.VMEM(value.shape, value.dtype) for value in operands] + [pltpu.SemaphoreType.DMA((4,))],
                PREPARE_LIMIT,
                some,
            )(*operands)
            waiting.append(mod_keep)
            far, mod_keep, mod_send = lax.optimization_barrier((far, mod_keep, mod_send))
        far_order = [k ^ bit for k in order]
        if bit == 1:
            break
        near = jnp.concatenate([near, far])
        order, bit = order + far_order, bit // 2
    mod_other = lax.ppermute(mod_send, "segment", swap)
    weights, params = call(
        layout_kernel,
        [ANY] * 4,
        [shape((PAIR, 9 * channels, channels), bf16), shape((8, channels), f32)],
        [pltpu.VMEM((PAIR, 8, channels), f32), pltpu.SemaphoreType.DMA((2 * PAIR,))],
        cost=some,
    )(weight, other_weight, mod_keep, mod_other)

    image_shape = shape((sh.pixels, channels), bf16)
    pack_shape = shape((sh.pack, channels), f32)
    common = [pltpu.VMEM((3, sh.padded, channels), bf16)]

    def hop(value, source, target):
        pairs = [(PAIR * source + k, PAIR * target + k) for k in range(PAIR)]
        return lax.ppermute(value, "segment", pairs + [(b, a) for a, b in pairs])

    image, middle, out = call(
        functools.partial(forward_kernel, sh, 0, (order, far_order)),
        [VMEM] * 4,
        [image_shape] * 3,
        common,
    )(near, far, params, weights)
    entering, middles = [image, hop(out, 0, 1)], [middle]
    for active in range(1, stages - 1):
        middle, out = call(
            functools.partial(forward_kernel, sh, active, None),
            [VMEM] * 3,
            [image_shape, image_shape],
            common,
        )(entering[active], params, weights)
        middles.append(middle)
        entering.append(hop(out, active, active + 1))

    noted = []
    for active in range(stages - 1):
        noted = call(
            functools.partial(note_kernel, sh, active),
            [VMEM] * (3 + len(noted)),
            [
                shape((PAIR, channels, sh.pixels), bf16),
                shape((PAIR, sh.pixels, channels), f32),
                shape((PAIR, 8, channels), f32),
            ],
            cost=some,
            aliases={3 + k: k for k in range(len(noted))},
        )(entering[active], middles[active], params, *noted)

    work = common + [pltpu.VMEM((sh.pixels, channels), f32)]
    slab = [pltpu.VMEM((sh.taps * channels, channels), f32)]
    pair_shape = shape((PAIR, sh.pixels, channels), bf16)
    laid, turned = call(
        functools.partial(lay_kernel, sh, stages - 1),
        [VMEM] * 2,
        [shape((3, sh.padded, channels), bf16), shape((PAIR, 9 * channels, channels), bf16)],
        cost=some,
    )(image, weights)
    *grad, between, act, sums = call(
        functools.partial(turn_kernel, sh, stages - 1),
        [VMEM] * 6,
        [image_shape, image_shape, pair_shape, shape((PAIR, 8, channels), f32)],
        work + [pltpu.VMEM((sh.pixels, channels), bf16), pltpu.VMEM((PAIR, sh.pixels, channels), f32)],
    )(entering[stages - 1], image, laid, params, weights, turned)
    keep, send = call(
        functools.partial(products_kernel, sh, stages - 1),
        [VMEM] * 5,
        [pack_shape, pack_shape],
        common + slab,
        cost=some,
    )(laid, between, grad[0], act, sums)
    for active in range(stages - 2, -1, -1):
        upstream = hop(grad[0], active + 1, active)
        last = active == 0
        spare = [pltpu.VMEM((sh.pixels, channels), bf16)]
        keep, send, *grad = call(
            functools.partial(backward_kernel, sh, active),
            [VMEM] * 10,
            [pack_shape, pack_shape] + ([] if last else [image_shape]),
            (spare if last else []) + work + slab + spare + common + slab,
            aliases={8: 0, 9: 1},
        )(entering[active], middles[active], upstream, params, turned, *noted, keep, send)
    other = lax.ppermute(send, "segment", swap)
    finals = [
        ((images, sh.own_rows, channels), bf16),
        ((sh.slab, channels), f32),
        ((width, 2 * channels), f32),
    ]
    grads, conv_grad, mod_grad = pl.pallas_call(
        functools.partial(finish_kernel, sh),
        out_shape=[shape(*final) for final in finals],
        in_specs=[VMEM] * 4,
        out_specs=[ANY] * 3,
        scratch_shapes=[pltpu.VMEM(*final) for final in finals] + [pltpu.SemaphoreType.DMA((MOD_PARTS + 2,))],
        compiler_params=pltpu.CompilerParams(vmem_limit_bytes=CHAIN_LIMIT),
    )(keep, other, turned_embedded, norm_gain)
    return (grads.reshape(1, images, row_count, cols, channels), conv_grad[None], mod_grad[None])


def solution(mesh):
    placed = (
        P(None, "space", None, None),
        P(None, "space", None, None),
        P(),
        P(),
        P(),
        P(),
        P("segment", None, None, None, None),
        P("segment", None, None),
        P("segment", None),
        P("segment", None),
    )
    return jax.shard_map(
        shards,
        mesh=mesh,
        in_specs=placed,
        out_specs=(
            P("segment", None, "space", None, None),
            P("segment", "space", None),
            P("segment", None, None),
        ),
        check_vma=False,
    )
```

```python
import functools
import math

import jax
import jax.numpy as jnp
from jax import lax
from jax.experimental import pallas as pl
from jax.experimental.pallas import tpu as pltpu
from jax.sharding import PartitionSpec as P

GROUPS = 32
EPSILON = 1e-05
PAIR = 2
BLOCK = 128
MOD_PARTS = 4
PREPARE_LIMIT = 60 << 20
CHAIN_LIMIT = 48 << 20
VMEM = pl.BlockSpec(memory_space=pltpu.VMEM)
SMEM = pl.BlockSpec(memory_space=pltpu.SMEM)
ANY = pl.BlockSpec(memory_space=pl.ANY)


def sigmoid(values):
    return 1.0 / (1.0 + jnp.exp(-values))


def over_chunks(count, body):
    if count == 1:
        body(0)
    else:

        def step(i, carry):
            body(i)
            return carry

        lax.fori_loop(0, count, step, 0)


def chunk_start(i, size):
    return 0 if isinstance(i, int) else pl.multiple_of(i * size, size)


def fold_rows(values):
    return jnp.sum(values.reshape(values.shape[0] // 8, 8, values.shape[1]), axis=0)


def column(rows):
    return jnp.sum(rows, axis=0, keepdims=True)


def group_sums(rows, width):
    lanes = lax.broadcasted_iota(jnp.int32, rows.shape, 1)
    size = rows.shape[1]
    step = 1
    while step < width:
        ahead = pltpu.roll(rows, size - step, 1)
        behind = pltpu.roll(rows, step, 1)
        rows = rows + jnp.where((lanes & step) == 0, ahead, behind)
        step *= 2
    return rows


def stack_rows(first, second):
    spot = lax.broadcasted_iota(jnp.int32, (8, first.shape[1]), 0)
    return jnp.where(spot == 0, first, jnp.where(spot == 1, second, 0.0))


class Shape:
    def __init__(self, height, cols, channels, space_count):
        self.cols, self.channels = cols, channels
        self.pixels = height * cols
        self.chunk = cols * max(1, min(self.pixels, 256) // cols)
        self.chunks = self.pixels // self.chunk
        self.width = channels // GROUPS
        self.entries = float(self.pixels * self.width)
        self.padded = self.pixels + 2 * cols
        self.own_rows = height // space_count * cols
        self.slab = 9 * channels // space_count
        step = math.gcd(self.slab, channels)
        self.taps = min(9, -(-(channels - step + self.slab) // channels))
        self.pack = self.slab + self.own_rows + 8
        self.limit = (12 << 20) + self.pixels * channels * 40


def statistics(sh, x_ref):
    zero = jnp.zeros((8, sh.channels), jnp.float32)

    def add(i, sums):
        part = x_ref[pl.ds(chunk_start(i, sh.chunk), sh.chunk), :].astype(jnp.float32)
        return (sums[0] + fold_rows(part), sums[1] + fold_rows(part * part))

    if sh.chunks == 1:
        one, two = add(0, (zero, zero))
    else:
        one, two = lax.fori_loop(0, sh.chunks, add, (zero, zero))
    total = group_sums(stack_rows(column(one), column(two)), sh.width) / sh.entries
    mean = total[0:1]
    return (mean, lax.rsqrt(total[1:2] - mean * mean + EPSILON))


def clear_edges(sh, padded_ref):
    zero = jnp.zeros((3, sh.cols, sh.channels), padded_ref.dtype)
    padded_ref[:, 0 : sh.cols, :] = zero
    padded_ref[:, sh.pixels + sh.cols : sh.padded, :] = zero


def spread(sh, padded_ref, start, values):
    place = pl.ds(start + sh.cols, sh.chunk)
    spot = lax.broadcasted_iota(jnp.int32, values.shape, 0) % sh.cols
    padded_ref[0, place, :] = jnp.where(spot == 0, 0.0, pltpu.roll(values, 1, 0)).astype(jnp.bfloat16)
    padded_ref[1, place, :] = values.astype(jnp.bfloat16)
    padded_ref[2, place, :] = jnp.where(
        spot == sh.cols - 1, 0.0, pltpu.roll(values, sh.chunk - 1, 0)
    ).astype(jnp.bfloat16)


def convolve(sh, padded_ref, start, size, weight_ref, unit, backward):
    total = None
    for p in range(3):
        for q in range(3):
            row, col = (2 - p, 2 - q) if backward else (p, q)
            block = padded_ref[col, pl.ds(start + row * sh.cols, size), :]
            tap = (3 * p + q) * sh.channels
            weight = weight_ref[unit, tap : tap + sh.channels, :]
            part = jnp.dot(block, weight, preferred_element_type=jnp.float32)
            total = part if total is None else total + part
    return total


def activation(sh, x_ref, place, stats, params):
    (mean, inv_std), (factor, shift) = stats, params
    pre = (x_ref[place, :].astype(jnp.float32) - mean) * inv_std * factor + shift
    sigma = sigmoid(pre)
    return pre * sigma, sigma * (1.0 + pre * (1.0 - sigma))


def note_unit(sh, x_ref, params, act_ref, slope_ref, turned=False):
    stats = statistics(sh, x_ref)

    def activate(i):
        place = pl.ds(chunk_start(i, sh.chunk), sh.chunk)
        values, slope = activation(sh, x_ref, place, stats, params)
        if turned:
            act_ref[:, place] = values.T.astype(jnp.bfloat16)
        else:
            act_ref[place, :] = values.astype(jnp.bfloat16)
        slope_ref[place, :] = slope

    over_chunks(sh.chunks, activate)
    return stats


def forward_unit(sh, x_ref, out_ref, params, padded_ref, weight_ref, unit, act_ref=None, slope_ref=None):
    stats = statistics(sh, x_ref)

    def activate(i):
        start = chunk_start(i, sh.chunk)
        place = pl.ds(start, sh.chunk)
        values, slope = activation(sh, x_ref, place, stats, params)
        spread(sh, padded_ref, start, values)
        if act_ref is not None:
            act_ref[place, :] = values.astype(jnp.bfloat16)
            slope_ref[place, :] = slope

    def produce(i):
        size = min(BLOCK, sh.chunk)
        for first in range(0, sh.chunk, size):
            start = chunk_start(i, sh.chunk) + first
            inputs = x_ref[pl.ds(start, size), :].astype(jnp.float32)
            z = convolve(sh, padded_ref, start, size, weight_ref, unit, False)
            out_ref[pl.ds(start, size), :] = (inputs + z).astype(jnp.bfloat16)

    over_chunks(sh.chunks, activate)
    over_chunks(sh.chunks, produce)
    return stats


def own_place(sh):
    return pl.ds(pl.multiple_of(lax.axis_index("space") * sh.own_rows, sh.own_rows), sh.own_rows)


def place_upstream(sh, up_ref, padded_ref):
    def place(i):
        start = chunk_start(i, sh.chunk)
        spread(sh, padded_ref, start, up_ref[pl.ds(start, sh.chunk), :].astype(jnp.float32))

    over_chunks(sh.chunks, place)


def backward_unit(sh, x_ref, up_ref, grad_ref, params, known, padded_ref, pre_grad_ref, weight_ref, unit, own=False, placed=False):
    slope_ref, (mean, inv_std) = known
    factor, _ = params
    zero = jnp.zeros((8, sh.channels), jnp.float32)

    def differentiate(i, sums):
        size = min(BLOCK, sh.chunk)
        for first in range(0, sh.chunk, size):
            start = chunk_start(i, sh.chunk) + first
            rows = pl.ds(start, size)
            normed = (x_ref[rows, :].astype(jnp.float32) - mean) * inv_std
            pre_grad = convolve(sh, padded_ref, start, size, weight_ref, unit, True) * slope_ref[rows, :]
            pre_grad_ref[rows, :] = pre_grad
            sums = (sums[0] + fold_rows(pre_grad), sums[1] + fold_rows(pre_grad * normed))
        return sums

    if not placed:
        place_upstream(sh, up_ref, padded_ref)
    if sh.chunks == 1:
        sums = differentiate(0, (zero, zero))
    else:
        sums = lax.fori_loop(0, sh.chunks, differentiate, (zero, zero))
    sum_grad, sum_cross = column(sums[0]), column(sums[1])
    means = group_sums(stack_rows(factor * sum_grad, factor * sum_cross), sh.width) / sh.entries
    center, tilt = means[0:1], means[1:2]

    def finish(rows):
        normed = (x_ref[rows, :].astype(jnp.float32) - mean) * inv_std
        back = factor * pre_grad_ref[rows, :] - center - normed * tilt
        grad_ref[rows, :] = (up_ref[rows, :].astype(jnp.float32) + inv_std * back).astype(jnp.bfloat16)

    if own:
        finish(own_place(sh))
    else:
        over_chunks(sh.chunks, lambda i: finish(pl.ds(chunk_start(i, sh.chunk), sh.chunk)))
    return stack_rows(sum_grad, sum_cross)


def weight_products(sh, padded_ref, act_ref, slab_ref, grad_ref, sums, unit, keep_ref, send_ref, turned=False):
    core = lax.axis_index("segment") % PAIR
    space = lax.axis_index("space")
    first_row = space * sh.slab
    first_tap = jnp.minimum(first_row // sh.channels, 9 - sh.taps)
    offset = pl.multiple_of(first_row - first_tap * sh.channels, 8)
    for t in range(sh.taps):
        tap = first_tap + t
        row, col = 2 - tap // 3, 2 - tap % 3
        place = pl.ds(t * sh.channels, sh.channels)

        def product(i):
            start = chunk_start(i, sh.chunk)
            block = padded_ref[col, pl.ds(pl.multiple_of(start + row * sh.cols, 16), sh.chunk), :]
            here = pl.ds(start, sh.chunk)
            return lax.dot_general(
                act_ref[:, here] if turned else act_ref[here, :],
                block,
                (((1 if turned else 0,), (0,)), ((), ())),
                preferred_element_type=jnp.float32,
            )

        if sh.chunks == 1:
            slab_ref[place, :] = product(0)
        else:
            slab_ref[place, :] = jnp.zeros((sh.channels, sh.channels), jnp.float32)

            def accumulate(i):
                slab_ref[place, :] += product(i)

            over_chunks(sh.chunks, accumulate)
    mine = slab_ref[pl.ds(offset, sh.slab), :]
    rows = grad_ref[own_place(sh), :]

    def write(ref):
        ref[0 : sh.slab, :] = mine
        ref[sh.slab : sh.slab + sh.own_rows, :] = rows.astype(jnp.float32)
        ref[sh.slab + sh.own_rows : sh.pack, :] = sums

    @pl.when(core == unit)
    def _():
        write(keep_ref)

    @pl.when(core != unit)
    def _():
        write(send_ref)


def place_of():
    index = lax.axis_index("segment")
    return (index // PAIR, index % PAIR)


def unit_params(params_ref, unit):
    return (params_ref[2 * unit : 2 * unit + 1, :], params_ref[2 * unit + 1 : 2 * unit + 2, :])


def sinusoid_of(time, base):
    half = base // 2
    lanes = lax.broadcasted_iota(jnp.int32, (time.shape[0], base), 1)
    power = jnp.where(lanes < half, lanes, lanes - half).astype(jnp.float32)
    angle = time * jnp.exp(-math.log(10000.0) * power / half)
    turns = jnp.floor(angle * (2.0 / math.pi) + 0.5)
    rest = ((angle - turns * 1.5703125) - turns * 4.83751296997e-4) - turns * 7.54978995489e-8
    square = rest * rest
    sine = rest + rest * square * (
        -1.6666654611e-1 + square * (8.3321608736e-3 - square * 1.9515295891e-4)
    )
    cosine = 1.0 - 0.5 * square + square * square * (
        4.166664568298827e-2 + square * (-1.388731625493765e-3 + square * 2.443315711809948e-5)
    )
    quarter = turns.astype(jnp.int32) + jnp.where(lanes < half, 1, 0)
    value = jnp.where(quarter % 2 == 1, cosine, sine)
    return jnp.where((quarter // 2) % 2 == 1, -value, value).astype(jnp.bfloat16)


def start_all(pairs, sems):
    copies = [pltpu.make_async_copy(a, b, sems.at[i]) for i, (a, b) in enumerate(pairs)]
    for copy in copies:
        copy.start()
    return copies


def embed_kernel(times_ref, labels_ref, table_hbm, time_weight_hbm, embedded_ref, table_ref, time_weight_ref, sems):
    pairs = [(time_weight_hbm, time_weight_ref)]
    pairs += [(table_hbm.at[pl.ds(labels_ref[i] // 8, 1)], table_ref.at[pl.ds(i, 1)]) for i in range(PAIR)]
    copies = start_all(pairs, sems)
    spot = lax.broadcasted_iota(jnp.int32, (16, 1), 0)
    time = jnp.where(spot % 2 == 0, times_ref[0], times_ref[1]).astype(jnp.float32)
    sinusoid = sinusoid_of(time, time_weight_ref.shape[0])

    def label_row(image):
        block = table_ref[image].astype(jnp.float32)
        row = lax.broadcasted_iota(jnp.int32, block.shape, 0)
        return column(jnp.where(row == labels_ref[image] % 8, block, 0.0))

    for copy in copies:
        copy.wait()
    timed = jnp.dot(sinusoid, time_weight_ref[...], preferred_element_type=jnp.float32)
    timed = timed + jnp.where(spot % 2 == 0, label_row(0), label_row(1))
    embedded_ref[...] = (timed * sigmoid(timed)).astype(jnp.bfloat16)


def modulate_kernel(embedded_hbm, mod_weight_hbm, bias_hbm, gain_hbm, keep_ref, send_ref, *scratch):
    embedded_ref, mod_weight_ref, bias_ref, gain_ref, sems = scratch
    core = lax.axis_index("segment") % PAIR
    copies = start_all(zip((embedded_hbm, mod_weight_hbm, bias_hbm, gain_hbm), scratch[:4]), sems)
    for copy in copies:
        copy.wait()
    modulation = jnp.dot(embedded_ref[...], mod_weight_ref[...], preferred_element_type=jnp.float32) + bias_ref[...]
    channels = gain_ref.shape[1]
    factor = gain_ref[...] * (1.0 + modulation[:, :channels])
    shift = modulation[:, channels:]
    first = stack_rows(factor[0:1], shift[0:1])
    second = stack_rows(factor[1:2], shift[1:2])
    keep_ref[...] = jnp.where(core == 0, first, second)
    send_ref[...] = jnp.where(core == 0, second, first)


def layout_kernel(own_any, other_any, mod_keep_any, mod_other_any, weights_ref, params_ref, mods_ref, sems):
    core = lax.axis_index("segment") % PAIR
    pairs = [(mod_keep_any, mods_ref.at[core]), (mod_other_any, mods_ref.at[1 - core])]
    pairs += [(own_any, weights_ref.at[core]), (other_any, weights_ref.at[1 - core])]
    copies = start_all(pairs, sems)
    for copy in copies[:PAIR]:
        copy.wait()
    params_ref[0:2, :] = mods_ref[0, 0:2, :]
    params_ref[2:4, :] = mods_ref[1, 0:2, :]
    params_ref[4:8, :] = jnp.zeros((4, params_ref.shape[1]), jnp.float32)
    for copy in copies[PAIR:]:
        copy.wait()


def assemble(sh, blocks_ref, order, image_ref):
    space = lax.axis_index("space")
    for k, bits in enumerate(order):
        start = pl.multiple_of((space ^ bits) * sh.own_rows, sh.own_rows)
        image_ref[pl.ds(start, sh.own_rows), :] = blocks_ref[k]


def forward_kernel(sh, active_stage, orders, *refs):
    if orders:
        near_ref, far_ref, params_ref, weights, x_ref = refs[:5]
        assemble(sh, near_ref, orders[0], x_ref)
        assemble(sh, far_ref, orders[1], x_ref)
        refs = refs[5:]
    else:
        x_ref, params_ref, weights = refs[:3]
        refs = refs[3:]
    middle_ref, out_ref, padded_ref = refs
    stage, _ = place_of()

    @pl.when(stage == active_stage)
    def _():
        clear_edges(sh, padded_ref)
        forward_unit(sh, x_ref, middle_ref, unit_params(params_ref, 0), padded_ref, weights, 0)
        forward_unit(sh, middle_ref, out_ref, unit_params(params_ref, 1), padded_ref, weights, 1)


def note_kernel(sh, active_stage, x_ref, middle_ref, params_ref, *refs):
    act_ref, slope_ref, stats_ref = refs[-3:]
    stage, _ = place_of()

    @pl.when(stage == active_stage)
    def _():
        for unit, source in enumerate((x_ref, middle_ref)):
            stats = note_unit(sh, source, unit_params(params_ref, unit), act_ref.at[unit], slope_ref.at[unit], True)
            stats_ref[unit] = stack_rows(*stats)


def lay_kernel(sh, active_stage, up_ref, weights_ref, padded_ref, turned_ref):
    stage, _ = place_of()

    @pl.when(stage == active_stage)
    def _():
        clear_edges(sh, padded_ref)
        place_upstream(sh, up_ref, padded_ref)

    for unit in range(PAIR):
        for tap in range(9):
            place = slice(tap * sh.channels, (tap + 1) * sh.channels)
            turned_ref[unit, place, :] = weights_ref[unit, place, :].astype(jnp.float32).T.astype(jnp.bfloat16)


def turn_kernel(sh, active_stage, x_ref, up_ref, laid_ref, params_ref, weights, turned, *refs):
    grad_ref, between_ref, act_ref, sums_ref, padded_ref, pre_grad_ref, middle_ref, slope_ref = refs
    stage, _ = place_of()

    @pl.when(stage == active_stage)
    def _():
        clear_edges(sh, padded_ref)
        params = [unit_params(params_ref, unit) for unit in range(PAIR)]
        acts, slopes = [[ref.at[unit] for unit in range(PAIR)] for ref in (act_ref, slope_ref)]
        first = forward_unit(sh, x_ref, middle_ref, params[0], padded_ref, weights, 0, acts[0], slopes[0])
        second = note_unit(sh, middle_ref, params[1], acts[1], slopes[1])
        work = (pre_grad_ref, turned)
        known = (slopes[1], second)
        sums_ref[1] = backward_unit(
            sh, middle_ref, up_ref, between_ref, params[1], known, laid_ref, *work, 1, placed=True
        )
        known = (slopes[0], first)
        sums_ref[0] = backward_unit(sh, x_ref, between_ref, grad_ref, params[0], known, padded_ref, *work, 0)


def products_kernel(sh, active_stage, laid_ref, between_ref, grad_ref, act_ref, sums_ref, *refs):
    keep_ref, send_ref, padded_ref, slab_ref = refs
    stage, _ = place_of()

    @pl.when(stage == active_stage)
    def _():
        clear_edges(sh, padded_ref)
        place_upstream(sh, between_ref, padded_ref)
        for unit, above, below in ((1, laid_ref, between_ref), (0, padded_ref, grad_ref)):
            outs = (keep_ref, send_ref)
            weight_products(sh, above, act_ref.at[unit], slab_ref, below, sums_ref[unit], unit, *outs)


def backward_kernel(sh, active_stage, *refs):
    x_ref, middle_ref, up_ref, params_ref, weights, act_ref, slope_ref, stats_ref = refs[:8]
    keep_ref, send_ref, grad_ref, padded_ref, pre_grad_ref, slab_ref, between_ref = refs[10:]
    stage, _ = place_of()

    @pl.when(stage == active_stage)
    def _():
        clear_edges(sh, padded_ref)
        for unit, x, above, below in ((1, middle_ref, up_ref, between_ref), (0, x_ref, between_ref, grad_ref)):
            stats = (stats_ref[unit, 0:1, :], stats_ref[unit, 1:2, :])
            known = (slope_ref.at[unit], stats)
            params = unit_params(params_ref, unit)
            own = unit == 0 and active_stage == 0
            sums = backward_unit(sh, x, above, below, params, known, padded_ref, pre_grad_ref, weights, unit, own)
            outs = (keep_ref, send_ref)
            weight_products(sh, padded_ref, act_ref.at[unit], slab_ref, below, sums, unit, *outs, turned=True)


def finish_kernel(sh, keep_ref, other_ref, embedded_ref, gain_ref, grads_hbm, conv_hbm, mod_hbm, *scratch):
    grads_ref, conv_ref, mod_ref, sems = scratch
    core = lax.axis_index("segment") % PAIR
    base = sh.slab + sh.own_rows

    def mod_rows(ref):
        return jnp.concatenate([gain_ref[...] * ref[base + 1 : base + 2, :], ref[base : base + 1, :]], axis=1)

    own, other = mod_rows(keep_ref), mod_rows(other_ref)
    spot = lax.broadcasted_iota(jnp.int32, (16, own.shape[1]), 0)
    values = jnp.where(spot % 2 == core, own, other)
    high = values.astype(jnp.bfloat16).astype(jnp.float32)
    rest = values - high
    middle = rest.astype(jnp.bfloat16).astype(jnp.float32)
    low = rest - middle
    part = spot // 2
    pieces = jnp.where(part == 0, high, jnp.where(part == 1, middle, jnp.where(part == 2, low, 0.0)))
    pieces = pieces.astype(jnp.bfloat16)
    copies = []
    size = mod_ref.shape[0] // MOD_PARTS
    for k in range(MOD_PARTS):
        place = slice(k * size, (k + 1) * size)
        mod_ref[place, :] = lax.dot_general(
            embedded_ref[:, place],
            pieces,
            (((0,), (0,)), ((), ())),
            preferred_element_type=jnp.float32,
        )
        copies.append(pltpu.make_async_copy(mod_ref.at[place], mod_hbm.at[place], sems.at[k]))
        copies[-1].start()
    conv_ref[...] = keep_ref[0 : sh.slab, :] + other_ref[0 : sh.slab, :]
    copies.append(pltpu.make_async_copy(conv_ref, conv_hbm, sems.at[MOD_PARTS]))
    copies[-1].start()
    rows = slice(sh.slab, sh.slab + sh.own_rows)
    grads_ref[pl.ds(core, 1)] = keep_ref[rows, :].astype(jnp.bfloat16)[None]
    grads_ref[pl.ds(1 - core, 1)] = other_ref[rows, :].astype(jnp.bfloat16)[None]
    copies.append(pltpu.make_async_copy(grads_ref, grads_hbm, sems.at[MOD_PARTS + 1]))
    copies[-1].start()
    for copy in copies:
        copy.wait()


def shards(
    x_in,
    out_cotangent,
    timesteps,
    labels,
    time_weight,
    label_table,
    conv_weight,
    mod_weight,
    mod_bias,
    norm_gain,
):
    segments, spaces = lax.axis_size("segment"), lax.axis_size("space")
    stages = segments // PAIR
    stage, core = place_of()
    images, row_count, cols, channels = x_in.shape
    sh = Shape(row_count * spaces, cols, channels, spaces)
    f32, bf16 = jnp.float32, jnp.bfloat16

    def call(body, ins, outs, scratch=(), limit=CHAIN_LIMIT, cost=None, aliases={}):
        return pl.pallas_call(
            body,
            out_shape=outs,
            in_specs=ins,
            out_specs=[VMEM] * len(outs),
            scratch_shapes=list(scratch),
            input_output_aliases=aliases,
            compiler_params=pltpu.CompilerParams(vmem_limit_bytes=limit),
            cost_estimate=cost,
        )

    shape = jax.ShapeDtypeStruct
    swap = [(i, i ^ 1) for i in range(segments)]
    weight = conv_weight.reshape(9 * channels, channels)
    other_weight = lax.ppermute(weight, "segment", swap)
    ends = jnp.where(stage == 0, x_in, out_cotangent)
    near = lax.dynamic_index_in_dim(ends, core, 0, keepdims=False).reshape(1, sh.own_rows, channels)
    table = label_table.reshape(-1, 8, label_table.shape[1])
    width = time_weight.shape[1]
    some = pl.CostEstimate(flops=1 << 20, bytes_accessed=4 << 20, transcendentals=0)
    order, bit = [0], spaces // 2
    waiting = []
    while True:
        far = lax.ppermute(near, "space", [(i, i ^ bit) for i in range(spaces)])
        if not waiting:
            (embedded,) = call(
                embed_kernel,
                [SMEM, SMEM, ANY, ANY],
                [shape((16, width), bf16)],
                [
                    pltpu.VMEM((PAIR, 8, width), bf16),
                    pltpu.VMEM(time_weight.shape, bf16),
                    pltpu.SemaphoreType.DMA((PAIR + 1,)),
                ],
                PREPARE_LIMIT,
                some,
            )(timesteps, labels, table, time_weight)
            waiting = [embedded]
            far, embedded = lax.optimization_barrier((far, embedded))
        elif len(waiting) == 1:
            operands = (embedded, mod_weight[0], mod_bias, norm_gain)
            mod_keep, mod_send = call(
                modulate_kernel,
                [ANY] * 4,
                [shape((8, channels), f32)] * 2,
                [pltpu.VMEM(value.shape, value.dtype) for value in operands] + [pltpu.SemaphoreType.DMA((4,))],
                PREPARE_LIMIT,
                some,
            )(*operands)
            waiting.append(mod_keep)
            far, mod_keep, mod_send = lax.optimization_barrier((far, mod_keep, mod_send))
        far_order = [k ^ bit for k in order]
        if bit == 1:
            break
        near = jnp.concatenate([near, far])
        order, bit = order + far_order, bit // 2
    mod_other = lax.ppermute(mod_send, "segment", swap)
    weights, params = call(
        layout_kernel,
        [ANY] * 4,
        [shape((PAIR, 9 * channels, channels), bf16), shape((8, channels), f32)],
        [pltpu.VMEM((PAIR, 8, channels), f32), pltpu.SemaphoreType.DMA((2 * PAIR,))],
        cost=some,
    )(weight, other_weight, mod_keep, mod_other)

    image_shape = shape((sh.pixels, channels), bf16)
    pack_shape = shape((sh.pack, channels), f32)
    common = [pltpu.VMEM((3, sh.padded, channels), bf16)]

    def hop(value, source, target):
        pairs = [(PAIR * source + k, PAIR * target + k) for k in range(PAIR)]
        return lax.ppermute(value, "segment", pairs + [(b, a) for a, b in pairs])

    image, middle, out = call(
        functools.partial(forward_kernel, sh, 0, (order, far_order)),
        [VMEM] * 4,
        [image_shape] * 3,
        common,
    )(near, far, params, weights)
    entering, middles = [image, hop(out, 0, 1)], [middle]
    for active in range(1, stages - 1):
        middle, out = call(
            functools.partial(forward_kernel, sh, active, None),
            [VMEM] * 3,
            [image_shape, image_shape],
            common,
        )(entering[active], params, weights)
        middles.append(middle)
        entering.append(hop(out, active, active + 1))

    noted = []
    for active in range(stages - 1):
        noted = call(
            functools.partial(note_kernel, sh, active),
            [VMEM] * (3 + len(noted)),
            [
                shape((PAIR, channels, sh.pixels), bf16),
                shape((PAIR, sh.pixels, channels), f32),
                shape((PAIR, 8, channels), f32),
            ],
            cost=some,
            aliases={3 + k: k for k in range(len(noted))},
        )(entering[active], middles[active], params, *noted)

    work = common + [pltpu.VMEM((sh.pixels, channels), f32)]
    slab = [pltpu.VMEM((sh.taps * channels, channels), f32)]
    pair_shape = shape((PAIR, sh.pixels, channels), bf16)
    laid, turned = call(
        functools.partial(lay_kernel, sh, stages - 1),
        [VMEM] * 2,
        [shape((3, sh.padded, channels), bf16), shape((PAIR, 9 * channels, channels), bf16)],
        cost=some,
    )(image, weights)
    *grad, between, act, sums = call(
        functools.partial(turn_kernel, sh, stages - 1),
        [VMEM] * 6,
        [image_shape, image_shape, pair_shape, shape((PAIR, 8, channels), f32)],
        work + [pltpu.VMEM((sh.pixels, channels), bf16), pltpu.VMEM((PAIR, sh.pixels, channels), f32)],
    )(entering[stages - 1], image, laid, params, weights, turned)
    keep, send = call(
        functools.partial(products_kernel, sh, stages - 1),
        [VMEM] * 5,
        [pack_shape, pack_shape],
        common + slab,
        cost=some,
    )(laid, between, grad[0], act, sums)
    for active in range(stages - 2, -1, -1):
        upstream = hop(grad[0], active + 1, active)
        last = active == 0
        spare = [pltpu.VMEM((sh.pixels, channels), bf16)]
        keep, send, *grad = call(
            functools.partial(backward_kernel, sh, active),
            [VMEM] * 10,
            [pack_shape, pack_shape] + ([] if last else [image_shape]),
            (spare if last else []) + work + slab + spare,
            aliases={8: 0, 9: 1},
        )(entering[active], middles[active], upstream, params, turned, *noted, keep, send)
    other = lax.ppermute(send, "segment", swap)
    finals = [
        ((images, sh.own_rows, channels), bf16),
        ((sh.slab, channels), f32),
        ((width, 2 * channels), f32),
    ]
    grads, conv_grad, mod_grad = pl.pallas_call(
        functools.partial(finish_kernel, sh),
        out_shape=[shape(*final) for final in finals],
        in_specs=[VMEM] * 4,
        out_specs=[ANY] * 3,
        scratch_shapes=[pltpu.VMEM(*final) for final in finals] + [pltpu.SemaphoreType.DMA((MOD_PARTS + 2,))],
        compiler_params=pltpu.CompilerParams(vmem_limit_bytes=CHAIN_LIMIT),
    )(keep, other, embedded, norm_gain)
    return (grads.reshape(1, images, row_count, cols, channels), conv_grad[None], mod_grad[None])


def solution(mesh):
    placed = (
        P(None, "space", None, None),
        P(None, "space", None, None),
        P(),
        P(),
        P(),
        P(),
        P("segment", None, None, None, None),
        P("segment", None, None),
        P("segment", None),
        P("segment", None),
    )
    return jax.shard_map(
        shards,
        mesh=mesh,
        in_specs=placed,
        out_specs=(
            P("segment", None, "space", None, None),
            P("segment", "space", None),
            P("segment", None, None),
        ),
        check_vma=False,
    )
```

```python
import functools
import math

import jax
import jax.numpy as jnp
from jax import lax
from jax.experimental import pallas as pl
from jax.experimental.pallas import tpu as pltpu
from jax.sharding import PartitionSpec as P

GROUPS = 32
EPSILON = 1e-05
PAIR = 2
BLOCK = 128
MOD_PARTS = 4
PREPARE_LIMIT = 60 << 20
CHAIN_LIMIT = 48 << 20
VMEM = pl.BlockSpec(memory_space=pltpu.VMEM)
SMEM = pl.BlockSpec(memory_space=pltpu.SMEM)
ANY = pl.BlockSpec(memory_space=pl.ANY)


def sigmoid(values):
    return 1.0 / (1.0 + jnp.exp(-values))


def over_chunks(count, body):
    if count == 1:
        body(0)
    else:

        def step(i, carry):
            body(i)
            return carry

        lax.fori_loop(0, count, step, 0)


def chunk_start(i, size):
    return 0 if isinstance(i, int) else pl.multiple_of(i * size, size)


def fold_rows(values):
    return jnp.sum(values.reshape(values.shape[0] // 8, 8, values.shape[1]), axis=0)


def column(rows):
    return jnp.sum(rows, axis=0, keepdims=True)


def group_sums(rows, width):
    lanes = lax.broadcasted_iota(jnp.int32, rows.shape, 1)
    size = rows.shape[1]
    step = 1
    while step < width:
        ahead = pltpu.roll(rows, size - step, 1)
        behind = pltpu.roll(rows, step, 1)
        rows = rows + jnp.where((lanes & step) == 0, ahead, behind)
        step *= 2
    return rows


def stack_rows(first, second):
    spot = lax.broadcasted_iota(jnp.int32, (8, first.shape[1]), 0)
    return jnp.where(spot == 0, first, jnp.where(spot == 1, second, 0.0))


class Shape:
    def __init__(self, height, cols, channels, space_count):
        self.cols, self.channels = cols, channels
        self.pixels = height * cols
        self.chunk = cols * max(1, min(self.pixels, 256) // cols)
        self.chunks = self.pixels // self.chunk
        self.width = channels // GROUPS
        self.entries = float(self.pixels * self.width)
        self.padded = self.pixels + 2 * cols
        self.own_rows = height // space_count * cols
        self.slab = 9 * channels // space_count
        step = math.gcd(self.slab, channels)
        self.taps = min(9, -(-(channels - step + self.slab) // channels))
        self.pack = self.slab + self.own_rows + 8
        self.limit = (12 << 20) + self.pixels * channels * 40


def statistics(sh, x_ref):
    zero = jnp.zeros((8, sh.channels), jnp.float32)

    def add(i, sums):
        part = x_ref[pl.ds(chunk_start(i, sh.chunk), sh.chunk), :].astype(jnp.float32)
        return (sums[0] + fold_rows(part), sums[1] + fold_rows(part * part))

    if sh.chunks == 1:
        one, two = add(0, (zero, zero))
    else:
        one, two = lax.fori_loop(0, sh.chunks, add, (zero, zero))
    total = group_sums(stack_rows(column(one), column(two)), sh.width) / sh.entries
    mean = total[0:1]
    return (mean, lax.rsqrt(total[1:2] - mean * mean + EPSILON))


def clear_edges(sh, padded_ref):
    zero = jnp.zeros((3, sh.cols, sh.channels), padded_ref.dtype)
    padded_ref[:, 0 : sh.cols, :] = zero
    padded_ref[:, sh.pixels + sh.cols : sh.padded, :] = zero


def spread(sh, padded_ref, start, values):
    place = pl.ds(start + sh.cols, sh.chunk)
    spot = lax.broadcasted_iota(jnp.int32, values.shape, 0) % sh.cols
    padded_ref[0, place, :] = jnp.where(spot == 0, 0.0, pltpu.roll(values, 1, 0)).astype(jnp.bfloat16)
    padded_ref[1, place, :] = values.astype(jnp.bfloat16)
    padded_ref[2, place, :] = jnp.where(
        spot == sh.cols - 1, 0.0, pltpu.roll(values, sh.chunk - 1, 0)
    ).astype(jnp.bfloat16)


def convolve(sh, padded_ref, start, size, weight_ref, unit, backward):
    total = None
    for p in range(3):
        for q in range(3):
            row, col = (2 - p, 2 - q) if backward else (p, q)
            block = padded_ref[col, pl.ds(start + row * sh.cols, size), :]
            tap = (3 * p + q) * sh.channels
            weight = weight_ref[unit, tap : tap + sh.channels, :]
            part = jnp.dot(block, weight, preferred_element_type=jnp.float32)
            total = part if total is None else total + part
    return total


def activation(sh, x_ref, place, stats, params):
    (mean, inv_std), (factor, shift) = stats, params
    pre = (x_ref[place, :].astype(jnp.float32) - mean) * inv_std * factor + shift
    sigma = sigmoid(pre)
    return pre * sigma, sigma * (1.0 + pre * (1.0 - sigma))


def note_unit(sh, x_ref, params, act_ref, slope_ref, turned=False):
    stats = statistics(sh, x_ref)

    def activate(i):
        place = pl.ds(chunk_start(i, sh.chunk), sh.chunk)
        values, slope = activation(sh, x_ref, place, stats, params)
        if turned:
            act_ref[:, place] = values.T.astype(jnp.bfloat16)
        else:
            act_ref[place, :] = values.astype(jnp.bfloat16)
        slope_ref[place, :] = slope

    over_chunks(sh.chunks, activate)
    return stats


def forward_unit(sh, x_ref, out_ref, params, padded_ref, weight_ref, unit, act_ref=None, slope_ref=None):
    stats = statistics(sh, x_ref)

    def activate(i):
        start = chunk_start(i, sh.chunk)
        place = pl.ds(start, sh.chunk)
        values, slope = activation(sh, x_ref, place, stats, params)
        spread(sh, padded_ref, start, values)
        if act_ref is not None:
            act_ref[place, :] = values.astype(jnp.bfloat16)
            slope_ref[place, :] = slope

    def produce(i):
        size = min(BLOCK, sh.chunk)
        for first in range(0, sh.chunk, size):
            start = chunk_start(i, sh.chunk) + first
            inputs = x_ref[pl.ds(start, size), :].astype(jnp.float32)
            z = convolve(sh, padded_ref, start, size, weight_ref, unit, False)
            out_ref[pl.ds(start, size), :] = (inputs + z).astype(jnp.bfloat16)

    over_chunks(sh.chunks, activate)
    over_chunks(sh.chunks, produce)
    return stats


def own_place(sh):
    return pl.ds(pl.multiple_of(lax.axis_index("space") * sh.own_rows, sh.own_rows), sh.own_rows)


def place_upstream(sh, up_ref, padded_ref):
    def place(i):
        start = chunk_start(i, sh.chunk)
        spread(sh, padded_ref, start, up_ref[pl.ds(start, sh.chunk), :].astype(jnp.float32))

    over_chunks(sh.chunks, place)


def backward_unit(sh, x_ref, up_ref, grad_ref, params, known, padded_ref, pre_grad_ref, weight_ref, unit, own=False, placed=False):
    slope_ref, (mean, inv_std) = known
    factor, _ = params
    zero = jnp.zeros((8, sh.channels), jnp.float32)

    def differentiate(i, sums):
        size = min(BLOCK, sh.chunk)
        for first in range(0, sh.chunk, size):
            start = chunk_start(i, sh.chunk) + first
            rows = pl.ds(start, size)
            normed = (x_ref[rows, :].astype(jnp.float32) - mean) * inv_std
            pre_grad = convolve(sh, padded_ref, start, size, weight_ref, unit, True) * slope_ref[rows, :]
            pre_grad_ref[rows, :] = pre_grad
            sums = (sums[0] + fold_rows(pre_grad), sums[1] + fold_rows(pre_grad * normed))
        return sums

    if not placed:
        place_upstream(sh, up_ref, padded_ref)
    if sh.chunks == 1:
        sums = differentiate(0, (zero, zero))
    else:
        sums = lax.fori_loop(0, sh.chunks, differentiate, (zero, zero))
    sum_grad, sum_cross = column(sums[0]), column(sums[1])
    means = group_sums(stack_rows(factor * sum_grad, factor * sum_cross), sh.width) / sh.entries
    center, tilt = means[0:1], means[1:2]

    def finish(rows):
        normed = (x_ref[rows, :].astype(jnp.float32) - mean) * inv_std
        back = factor * pre_grad_ref[rows, :] - center - normed * tilt
        grad_ref[rows, :] = (up_ref[rows, :].astype(jnp.float32) + inv_std * back).astype(jnp.bfloat16)

    if own:
        finish(own_place(sh))
    else:
        over_chunks(sh.chunks, lambda i: finish(pl.ds(chunk_start(i, sh.chunk), sh.chunk)))
    return stack_rows(sum_grad, sum_cross)


def weight_products(sh, padded_ref, act_ref, slab_ref, grad_ref, sums, unit, keep_ref, send_ref, turned=False):
    core = lax.axis_index("segment") % PAIR
    space = lax.axis_index("space")
    first_row = space * sh.slab
    first_tap = jnp.minimum(first_row // sh.channels, 9 - sh.taps)
    offset = pl.multiple_of(first_row - first_tap * sh.channels, 8)
    for t in range(sh.taps):
        tap = first_tap + t
        row, col = 2 - tap // 3, 2 - tap % 3
        place = pl.ds(t * sh.channels, sh.channels)

        def product(i):
            start = chunk_start(i, sh.chunk)
            block = padded_ref[col, pl.ds(pl.multiple_of(start + row * sh.cols, 16), sh.chunk), :]
            here = pl.ds(start, sh.chunk)
            return lax.dot_general(
                act_ref[:, here] if turned else act_ref[here, :],
                block,
                (((1 if turned else 0,), (0,)), ((), ())),
                preferred_element_type=jnp.float32,
            )

        if sh.chunks == 1:
            slab_ref[place, :] = product(0)
        else:
            slab_ref[place, :] = jnp.zeros((sh.channels, sh.channels), jnp.float32)

            def accumulate(i):
                slab_ref[place, :] += product(i)

            over_chunks(sh.chunks, accumulate)
    mine = slab_ref[pl.ds(offset, sh.slab), :]
    rows = grad_ref[own_place(sh), :]

    def write(ref):
        ref[0 : sh.slab, :] = mine
        ref[sh.slab : sh.slab + sh.own_rows, :] = rows.astype(jnp.float32)
        ref[sh.slab + sh.own_rows : sh.pack, :] = sums

    @pl.when(core == unit)
    def _():
        write(keep_ref)

    @pl.when(core != unit)
    def _():
        write(send_ref)


def place_of():
    index = lax.axis_index("segment")
    return (index // PAIR, index % PAIR)


def unit_params(params_ref, unit):
    return (params_ref[2 * unit : 2 * unit + 1, :], params_ref[2 * unit + 1 : 2 * unit + 2, :])


def sinusoid_of(time, base):
    half = base // 2
    lanes = lax.broadcasted_iota(jnp.int32, (time.shape[0], base), 1)
    power = jnp.where(lanes < half, lanes, lanes - half).astype(jnp.float32)
    angle = time * jnp.exp(-math.log(10000.0) * power / half)
    turns = jnp.floor(angle * (2.0 / math.pi) + 0.5)
    rest = ((angle - turns * 1.5703125) - turns * 4.83751296997e-4) - turns * 7.54978995489e-8
    square = rest * rest
    sine = rest + rest * square * (
        -1.6666654611e-1 + square * (8.3321608736e-3 - square * 1.9515295891e-4)
    )
    cosine = 1.0 - 0.5 * square + square * square * (
        4.166664568298827e-2 + square * (-1.388731625493765e-3 + square * 2.443315711809948e-5)
    )
    quarter = turns.astype(jnp.int32) + jnp.where(lanes < half, 1, 0)
    value = jnp.where(quarter % 2 == 1, cosine, sine)
    return jnp.where((quarter // 2) % 2 == 1, -value, value).astype(jnp.bfloat16)


def start_all(pairs, sems):
    copies = [pltpu.make_async_copy(a, b, sems.at[i]) for i, (a, b) in enumerate(pairs)]
    for copy in copies:
        copy.start()
    return copies


def embed_kernel(times_ref, labels_ref, table_hbm, time_weight_hbm, *refs):
    embedded_ref, turned_ref, table_ref, time_weight_ref, sems = refs
    pairs = [(time_weight_hbm, time_weight_ref)]
    pairs += [(table_hbm.at[pl.ds(labels_ref[i] // 8, 1)], table_ref.at[pl.ds(i, 1)]) for i in range(PAIR)]
    copies = start_all(pairs, sems)
    spot = lax.broadcasted_iota(jnp.int32, (16, 1), 0)
    time = jnp.where(spot % 2 == 0, times_ref[0], times_ref[1]).astype(jnp.float32)
    sinusoid = sinusoid_of(time, time_weight_ref.shape[0])

    def label_row(image):
        block = table_ref[image].astype(jnp.float32)
        row = lax.broadcasted_iota(jnp.int32, block.shape, 0)
        return column(jnp.where(row == labels_ref[image] % 8, block, 0.0))

    for copy in copies:
        copy.wait()
    timed = jnp.dot(sinusoid, time_weight_ref[...], preferred_element_type=jnp.float32)
    timed = timed + jnp.where(spot % 2 == 0, label_row(0), label_row(1))
    embedded = timed * sigmoid(timed)
    embedded_ref[...] = embedded.astype(jnp.bfloat16)
    turned_ref[...] = embedded.T.astype(jnp.bfloat16)


def modulate_kernel(embedded_hbm, mod_weight_hbm, bias_hbm, gain_hbm, keep_ref, send_ref, *scratch):
    embedded_ref, mod_weight_ref, bias_ref, gain_ref, sems = scratch
    core = lax.axis_index("segment") % PAIR
    copies = start_all(zip((embedded_hbm, mod_weight_hbm, bias_hbm, gain_hbm), scratch[:4]), sems)
    for copy in copies:
        copy.wait()
    modulation = jnp.dot(embedded_ref[...], mod_weight_ref[...], preferred_element_type=jnp.float32) + bias_ref[...]
    channels = gain_ref.shape[1]
    factor = gain_ref[...] * (1.0 + modulation[:, :channels])
    shift = modulation[:, channels:]
    first = stack_rows(factor[0:1], shift[0:1])
    second = stack_rows(factor[1:2], shift[1:2])
    keep_ref[...] = jnp.where(core == 0, first, second)
    send_ref[...] = jnp.where(core == 0, second, first)


def layout_kernel(own_any, other_any, mod_keep_any, mod_other_any, weights_ref, params_ref, mods_ref, sems):
    core = lax.axis_index("segment") % PAIR
    pairs = [(mod_keep_any, mods_ref.at[core]), (mod_other_any, mods_ref.at[1 - core])]
    pairs += [(own_any, weights_ref.at[core]), (other_any, weights_ref.at[1 - core])]
    copies = start_all(pairs, sems)
    for copy in copies[:PAIR]:
        copy.wait()
    params_ref[0:2, :] = mods_ref[0, 0:2, :]
    params_ref[2:4, :] = mods_ref[1, 0:2, :]
    params_ref[4:8, :] = jnp.zeros((4, params_ref.shape[1]), jnp.float32)
    for copy in copies[PAIR:]:
        copy.wait()


def assemble(sh, blocks_ref, order, image_ref):
    space = lax.axis_index("space")
    for k, bits in enumerate(order):
        start = pl.multiple_of((space ^ bits) * sh.own_rows, sh.own_rows)
        image_ref[pl.ds(start, sh.own_rows), :] = blocks_ref[k]


def forward_kernel(sh, active_stage, orders, *refs):
    if orders:
        near_ref, far_ref, params_ref, weights, x_ref = refs[:5]
        assemble(sh, near_ref, orders[0], x_ref)
        assemble(sh, far_ref, orders[1], x_ref)
        refs = refs[5:]
    else:
        x_ref, params_ref, weights = refs[:3]
        refs = refs[3:]
    middle_ref, out_ref, padded_ref = refs
    stage, _ = place_of()

    @pl.when(stage == active_stage)
    def _():
        clear_edges(sh, padded_ref)
        forward_unit(sh, x_ref, middle_ref, unit_params(params_ref, 0), padded_ref, weights, 0)
        forward_unit(sh, middle_ref, out_ref, unit_params(params_ref, 1), padded_ref, weights, 1)


def note_kernel(sh, active_stage, x_ref, middle_ref, params_ref, *refs):
    act_ref, slope_ref, stats_ref = refs[-3:]
    stage, _ = place_of()

    @pl.when(stage == active_stage)
    def _():
        for unit, source in enumerate((x_ref, middle_ref)):
            stats = note_unit(sh, source, unit_params(params_ref, unit), act_ref.at[unit], slope_ref.at[unit], True)
            stats_ref[unit] = stack_rows(*stats)


def lay_kernel(sh, active_stage, up_ref, weights_ref, padded_ref, turned_ref):
    stage, _ = place_of()

    @pl.when(stage == active_stage)
    def _():
        clear_edges(sh, padded_ref)
        place_upstream(sh, up_ref, padded_ref)

    for unit in range(PAIR):
        for tap in range(9):
            place = slice(tap * sh.channels, (tap + 1) * sh.channels)
            turned_ref[unit, place, :] = weights_ref[unit, place, :].astype(jnp.float32).T.astype(jnp.bfloat16)


def turn_kernel(sh, active_stage, x_ref, up_ref, laid_ref, params_ref, weights, turned, *refs):
    grad_ref, between_ref, act_ref, sums_ref, padded_ref, pre_grad_ref, middle_ref, slope_ref = refs
    stage, _ = place_of()

    @pl.when(stage == active_stage)
    def _():
        clear_edges(sh, padded_ref)
        params = [unit_params(params_ref, unit) for unit in range(PAIR)]
        acts, slopes = [[ref.at[unit] for unit in range(PAIR)] for ref in (act_ref, slope_ref)]
        first = forward_unit(sh, x_ref, middle_ref, params[0], padded_ref, weights, 0, acts[0], slopes[0])
        second = note_unit(sh, middle_ref, params[1], acts[1], slopes[1])
        work = (pre_grad_ref, turned)
        known = (slopes[1], second)
        sums_ref[1] = backward_unit(
            sh, middle_ref, up_ref, between_ref, params[1], known, laid_ref, *work, 1, placed=True
        )
        known = (slopes[0], first)
        sums_ref[0] = backward_unit(sh, x_ref, between_ref, grad_ref, params[0], known, padded_ref, *work, 0)


def products_kernel(sh, active_stage, laid_ref, between_ref, grad_ref, act_ref, sums_ref, *refs):
    keep_ref, send_ref, padded_ref, slab_ref = refs
    stage, _ = place_of()

    @pl.when(stage == active_stage)
    def _():
        clear_edges(sh, padded_ref)
        place_upstream(sh, between_ref, padded_ref)
        for unit, above, below in ((1, laid_ref, between_ref), (0, padded_ref, grad_ref)):
            outs = (keep_ref, send_ref)
            weight_products(sh, above, act_ref.at[unit], slab_ref, below, sums_ref[unit], unit, *outs)


def backward_kernel(sh, active_stage, *refs):
    x_ref, middle_ref, up_ref, params_ref, weights, act_ref, slope_ref, stats_ref = refs[:8]
    keep_ref, send_ref, grad_ref, padded_ref, pre_grad_ref, slab_ref, between_ref = refs[10:]
    stage, _ = place_of()

    @pl.when(stage == active_stage)
    def _():
        clear_edges(sh, padded_ref)
        for unit, x, above, below in ((1, middle_ref, up_ref, between_ref), (0, x_ref, between_ref, grad_ref)):
            stats = (stats_ref[unit, 0:1, :], stats_ref[unit, 1:2, :])
            known = (slope_ref.at[unit], stats)
            params = unit_params(params_ref, unit)
            own = unit == 0 and active_stage == 0
            sums = backward_unit(sh, x, above, below, params, known, padded_ref, pre_grad_ref, weights, unit, own)
            outs = (keep_ref, send_ref)
            weight_products(sh, padded_ref, act_ref.at[unit], slab_ref, below, sums, unit, *outs, turned=True)


def finish_kernel(sh, keep_ref, other_ref, embedded_ref, gain_ref, grads_hbm, conv_hbm, mod_hbm, *scratch):
    grads_ref, conv_ref, mod_ref, sems = scratch
    core = lax.axis_index("segment") % PAIR
    base = sh.slab + sh.own_rows

    def mod_rows(ref):
        return jnp.concatenate([gain_ref[...] * ref[base + 1 : base + 2, :], ref[base : base + 1, :]], axis=1)

    own, other = mod_rows(keep_ref), mod_rows(other_ref)
    spot = lax.broadcasted_iota(jnp.int32, (16, own.shape[1]), 0)
    values = jnp.where(spot % 2 == core, own, other)
    high = values.astype(jnp.bfloat16).astype(jnp.float32)
    rest = values - high
    middle = rest.astype(jnp.bfloat16).astype(jnp.float32)
    low = rest - middle
    part = spot // 2
    pieces = jnp.where(part == 0, high, jnp.where(part == 1, middle, jnp.where(part == 2, low, 0.0)))
    pieces = pieces.astype(jnp.bfloat16)
    copies = []
    size = mod_ref.shape[0] // MOD_PARTS
    for k in range(MOD_PARTS):
        place = slice(k * size, (k + 1) * size)
        mod_ref[place, :] = lax.dot_general(
            embedded_ref[place, :],
            pieces,
            (((1,), (0,)), ((), ())),
            preferred_element_type=jnp.float32,
        )
        copies.append(pltpu.make_async_copy(mod_ref.at[place], mod_hbm.at[place], sems.at[k]))
        copies[-1].start()
    conv_ref[...] = keep_ref[0 : sh.slab, :] + other_ref[0 : sh.slab, :]
    copies.append(pltpu.make_async_copy(conv_ref, conv_hbm, sems.at[MOD_PARTS]))
    copies[-1].start()
    rows = slice(sh.slab, sh.slab + sh.own_rows)
    grads_ref[pl.ds(core, 1)] = keep_ref[rows, :].astype(jnp.bfloat16)[None]
    grads_ref[pl.ds(1 - core, 1)] = other_ref[rows, :].astype(jnp.bfloat16)[None]
    copies.append(pltpu.make_async_copy(grads_ref, grads_hbm, sems.at[MOD_PARTS + 1]))
    copies[-1].start()
    for copy in copies:
        copy.wait()


def shards(
    x_in,
    out_cotangent,
    timesteps,
    labels,
    time_weight,
    label_table,
    conv_weight,
    mod_weight,
    mod_bias,
    norm_gain,
):
    segments, spaces = lax.axis_size("segment"), lax.axis_size("space")
    stages = segments // PAIR
    stage, core = place_of()
    images, row_count, cols, channels = x_in.shape
    sh = Shape(row_count * spaces, cols, channels, spaces)
    f32, bf16 = jnp.float32, jnp.bfloat16

    def call(body, ins, outs, scratch=(), limit=CHAIN_LIMIT, cost=None, aliases={}):
        return pl.pallas_call(
            body,
            out_shape=outs,
            in_specs=ins,
            out_specs=[VMEM] * len(outs),
            scratch_shapes=list(scratch),
            input_output_aliases=aliases,
            compiler_params=pltpu.CompilerParams(vmem_limit_bytes=limit),
            cost_estimate=cost,
        )

    shape = jax.ShapeDtypeStruct
    swap = [(i, i ^ 1) for i in range(segments)]
    weight = conv_weight.reshape(9 * channels, channels)
    other_weight = lax.ppermute(weight, "segment", swap)
    ends = jnp.where(stage == 0, x_in, out_cotangent)
    near = lax.dynamic_index_in_dim(ends, core, 0, keepdims=False).reshape(1, sh.own_rows, channels)
    table = label_table.reshape(-1, 8, label_table.shape[1])
    width = time_weight.shape[1]
    some = pl.CostEstimate(flops=1 << 20, bytes_accessed=4 << 20, transcendentals=0)
    order, bit = [0], spaces // 2
    waiting = []
    while True:
        far = lax.ppermute(near, "space", [(i, i ^ bit) for i in range(spaces)])
        if not waiting:
            embedded, turned_embedded = call(
                embed_kernel,
                [SMEM, SMEM, ANY, ANY],
                [shape((16, width), bf16), shape((width, 16), bf16)],
                [
                    pltpu.VMEM((PAIR, 8, width), bf16),
                    pltpu.VMEM(time_weight.shape, bf16),
                    pltpu.SemaphoreType.DMA((PAIR + 1,)),
                ],
                PREPARE_LIMIT,
                some,
            )(timesteps, labels, table, time_weight)
            waiting = [embedded]
            far, embedded = lax.optimization_barrier((far, embedded))
        elif len(waiting) == 1:
            operands = (embedded, mod_weight[0], mod_bias, norm_gain)
            mod_keep, mod_send = call(
                modulate_kernel,
                [ANY] * 4,
                [shape((8, channels), f32)] * 2,
                [pltpu.VMEM(value.shape, value.dtype) for value in operands] + [pltpu.SemaphoreType.DMA((4,))],
                PREPARE_LIMIT,
                some,
            )(*operands)
            waiting.append(mod_keep)
            far, mod_keep, mod_send = lax.optimization_barrier((far, mod_keep, mod_send))
        far_order = [k ^ bit for k in order]
        if bit == 1:
            break
        near = jnp.concatenate([near, far])
        order, bit = order + far_order, bit // 2
    mod_other = lax.ppermute(mod_send, "segment", swap)
    weights, params = call(
        layout_kernel,
        [ANY] * 4,
        [shape((PAIR, 9 * channels, channels), bf16), shape((8, channels), f32)],
        [pltpu.VMEM((PAIR, 8, channels), f32), pltpu.SemaphoreType.DMA((2 * PAIR,))],
        cost=some,
    )(weight, other_weight, mod_keep, mod_other)

    image_shape = shape((sh.pixels, channels), bf16)
    pack_shape = shape((sh.pack, channels), f32)
    common = [pltpu.VMEM((3, sh.padded, channels), bf16)]

    def hop(value, source, target):
        pairs = [(PAIR * source + k, PAIR * target + k) for k in range(PAIR)]
        return lax.ppermute(value, "segment", pairs + [(b, a) for a, b in pairs])

    image, middle, out = call(
        functools.partial(forward_kernel, sh, 0, (order, far_order)),
        [VMEM] * 4,
        [image_shape] * 3,
        common,
    )(near, far, params, weights)
    entering, middles = [image, hop(out, 0, 1)], [middle]
    for active in range(1, stages - 1):
        middle, out = call(
            functools.partial(forward_kernel, sh, active, None),
            [VMEM] * 3,
            [image_shape, image_shape],
            common,
        )(entering[active], params, weights)
        middles.append(middle)
        entering.append(hop(out, active, active + 1))

    noted = []
    for active in range(stages - 1):
        noted = call(
            functools.partial(note_kernel, sh, active),
            [VMEM] * (3 + len(noted)),
            [
                shape((PAIR, channels, sh.pixels), bf16),
                shape((PAIR, sh.pixels, channels), f32),
                shape((PAIR, 8, channels), f32),
            ],
            cost=some,
            aliases={3 + k: k for k in range(len(noted))},
        )(entering[active], middles[active], params, *noted)

    work = common + [pltpu.VMEM((sh.pixels, channels), f32)]
    slab = [pltpu.VMEM((sh.taps * channels, channels), f32)]
    pair_shape = shape((PAIR, sh.pixels, channels), bf16)
    laid, turned = call(
        functools.partial(lay_kernel, sh, stages - 1),
        [VMEM] * 2,
        [shape((3, sh.padded, channels), bf16), shape((PAIR, 9 * channels, channels), bf16)],
        cost=some,
    )(image, weights)
    *grad, between, act, sums = call(
        functools.partial(turn_kernel, sh, stages - 1),
        [VMEM] * 6,
        [image_shape, image_shape, pair_shape, shape((PAIR, 8, channels), f32)],
        work + [pltpu.VMEM((sh.pixels, channels), bf16), pltpu.VMEM((PAIR, sh.pixels, channels), f32)],
    )(entering[stages - 1], image, laid, params, weights, turned)
    keep, send = call(
        functools.partial(products_kernel, sh, stages - 1),
        [VMEM] * 5,
        [pack_shape, pack_shape],
        common + slab,
        cost=some,
    )(laid, between, grad[0], act, sums)
    for active in range(stages - 2, -1, -1):
        upstream = hop(grad[0], active + 1, active)
        last = active == 0
        spare = [pltpu.VMEM((sh.pixels, channels), bf16)]
        keep, send, *grad = call(
            functools.partial(backward_kernel, sh, active),
            [VMEM] * 10,
            [pack_shape, pack_shape] + ([] if last else [image_shape]),
            (spare if last else []) + work + slab + spare,
            aliases={8: 0, 9: 1},
        )(entering[active], middles[active], upstream, params, turned, *noted, keep, send)
    other = lax.ppermute(send, "segment", swap)
    finals = [
        ((images, sh.own_rows, channels), bf16),
        ((sh.slab, channels), f32),
        ((width, 2 * channels), f32),
    ]
    grads, conv_grad, mod_grad = pl.pallas_call(
        functools.partial(finish_kernel, sh),
        out_shape=[shape(*final) for final in finals],
        in_specs=[VMEM] * 4,
        out_specs=[ANY] * 3,
        scratch_shapes=[pltpu.VMEM(*final) for final in finals] + [pltpu.SemaphoreType.DMA((MOD_PARTS + 2,))],
        compiler_params=pltpu.CompilerParams(vmem_limit_bytes=CHAIN_LIMIT),
    )(keep, other, turned_embedded, norm_gain)
    return (grads.reshape(1, images, row_count, cols, channels), conv_grad[None], mod_grad[None])


def solution(mesh):
    placed = (
        P(None, "space", None, None),
        P(None, "space", None, None),
        P(),
        P(),
        P(),
        P(),
        P("segment", None, None, None, None),
        P("segment", None, None),
        P("segment", None),
        P("segment", None),
    )
    return jax.shard_map(
        shards,
        mesh=mesh,
        in_specs=placed,
        out_specs=(
            P("segment", None, "space", None, None),
            P("segment", "space", None),
            P("segment", None, None),
        ),
        check_vma=False,
    )
```
